128 devices in a mesh: row: 16 (over z, y_hi, core), col: 8 (over y_lo, x).
Axes of the slice: x: 4, y: 4 (y_hi: 2, y_lo: 2; y = y_hi * 2 + y_lo), z: 4, core: 2. Of those that a mesh axis runs over, the one named last changes fastest.
Arguments:
- query_rows: bfloat16 [8192, 8192], P('row', 'col'), may hold values from -100 to 100
- key_rows: bfloat16 [8192, 1024], P('row', 'col'), may hold values from -4 to 4
- value_rows: bfloat16 [8192, 1024], P('row', 'col'), may hold values from -6 to 6
- output_grad: bfloat16 [8192, 8192], P('row', 'col'), may hold values from -6 to 6
- out_proj: bfloat16 [8192, 8192], P('row', 'col'), may hold values from -0.0625 to 0.0625
- segment_ids: int32 [8192], replicated, may hold values from 0 to 3, as said below
Outputs:
- query_grad: bfloat16 [8192, 8192], P('row', 'col')
- key_grad: bfloat16 [8192, 1024], P('row', 'col')
- value_grad: bfloat16 [8192, 1024], P('row', 'col')
- proj_grad: bfloat16 [8192, 8192], P('row', 'col')
The draws below stay inside these ranges and needn't reach their ends.
Inputs may be any that keep to these rules, and one draw needn't show every extreme that they name: `segment_ids`: ids never fall and start at 0 with token 0. Exactly three tokens have an id one more than their predecessor's; they lie in three different aligned blocks of 512 tokens and are never a block's first token.
All inputs are finite; a program needn't handle non-finite values.
Results may differ from the reference program's by a relative error of at most 0.017.
Values may be sent and summed in bfloat16 or wider, within the bound.
No kernel may reach another device: no remote copies, remote signals or barrier semaphores. Data moves between devices by JAX's collectives and lax.ppermute only.
A program may use at most 192 MiB of HBM per device.

```python
import math
import jax
import jax.numpy as jnp
from jax import lax

D = 8192
HQ = 64
KV = 8
HD = 128
TOK_DEV = 512
TOKENS = 8192


def shared_keys(key):
    base = jax.random.normal(key, (TOKENS, KV, HD), jnp.float32)
    return jnp.clip(base, -4.0, 4.0)


def draw_key_rows(key, part):
    base = shared_keys(key)
    return base.reshape(TOKENS, KV * HD).astype(jnp.bfloat16)


def draw_query_rows(key, part):
    key = jax.random.fold_in(key, 2)
    fresh = jnp.clip(jax.random.normal(key, (TOKENS, HQ, HD), jnp.float32), -6.0, 6.0)
    return fresh.reshape(TOKENS, HQ * HD).astype(jnp.bfloat16)


def draw_segment_ids(key, part):
    key = jax.random.fold_in(key, 7)
    block_key, offset_key = jax.random.split(key)
    block_count = TOKENS // TOK_DEV
    picked = jax.random.permutation(block_key, block_count)[:3].astype(jnp.int32)
    offsets = jax.random.randint(offset_key, (3,), 1, TOK_DEV, dtype=jnp.int32)
    starts = picked * TOK_DEV + offsets
    positions = jnp.arange(TOKENS, dtype=jnp.int32)
    return jnp.sum((positions[:, None] >= starts[None, :]).astype(jnp.int32), axis=1)


def with_spikes(drawn, key, source, target, blocks, factor):
    owner, partner = [(jnp.arange(drawn.shape[dim]) // (drawn.shape[dim] // blocks)).reshape([-1 if axis == dim else 1 for axis in range(drawn.ndim)]) for dim in (source, target)]
    chosen = jax.random.permutation(key, blocks)[partner]
    strong = (owner == chosen) | (owner == (partner + blocks // 2) % blocks)
    return jnp.where(strong, factor * drawn, drawn)


def block_scale(stream_key, dims, shards, smallest, high):
    def one(dim, parts):
        steps = jax.random.uniform(jax.random.fold_in(jax.random.fold_in(stream_key, 6), dim), (parts,), jnp.float32, smallest / len(shards), high / len(shards))
        return jnp.repeat(jnp.exp(steps), dims[dim] // parts).reshape((-1,) + (1,) * (len(dims) - dim - 1))

    level = one(*shards[0])
    for cut in shards[1:]:
        level = level * one(*cut)
    return level


def bell_draw(own_key, dims, deviation, reach, cuts=(), kind=jnp.bfloat16):
    level = block_scale(own_key, dims, cuts, -0.22, 0.18) if cuts else 1.0
    entries = jax.random.normal(own_key, dims, jnp.float32) * deviation * level
    return jnp.minimum(jnp.maximum(entries, -reach), reach).astype(kind)


def heavy_noise(own_key, extent, spread, limit, cuts, heavy, held_as=jnp.bfloat16):
    values = spread * jax.random.normal(own_key, extent, jnp.float32)
    if cuts:
        values = values * block_scale(own_key, extent, cuts, -0.22, 0.18)
    return jnp.clip(with_spikes(values, jax.random.fold_in(own_key, 3), *heavy), -limit, limit).astype(held_as)


def setup_inputs(seed: int = 0) -> dict:
    keys = jax.random.split(jax.random.key(seed), 7)
    query_rows = draw_query_rows(jax.random.fold_in(keys[6], 71), 0)
    key_rows = draw_key_rows(jax.random.fold_in(keys[6], 71), 0)
    value_rows = bell_draw(keys[2], (TOKENS, KV * HD), 1.0, 6.0, ((0, 16), (1, 8)))
    output_grad = heavy_noise(keys[3], (TOKENS, D), 1.0, 6.0, ((0, 16), (1, 8)), (0, 1, 16, 2.0))
    out_proj = bell_draw(keys[4], (D, HQ * HD), (HQ * HD) ** -0.5, 0.0625, ((0, 16), (1, 8)))
    segment_ids = draw_segment_ids(jax.random.fold_in(keys[6], 71), 0)
    return {"query_rows": query_rows, "key_rows": key_rows, "value_rows": value_rows, "output_grad": output_grad, "out_proj": out_proj, "segment_ids": segment_ids}


def allowed_mask(segment_ids, block, count):
    query_pos = block * count + jnp.arange(count, dtype=jnp.int32)
    key_pos = (block - 1) * count + jnp.arange(2 * count, dtype=jnp.int32)
    seg_query = lax.dynamic_slice_in_dim(segment_ids, (block * count).astype(jnp.int32), count, 0)
    seg_earlier = lax.dynamic_slice_in_dim(segment_ids, (jnp.maximum(block - 1, 0) * count).astype(jnp.int32), count, 0)
    seg_keys = jnp.concatenate([seg_earlier, seg_query], 0)
    same_list = seg_keys[None, :] == seg_query[:, None]
    causal = key_pos[None, :] <= query_pos[:, None]
    present = key_pos[None, :] >= 0
    return same_list & causal & present

def block_pass(query_blk, key_pair, value_pair, grad_blk, allowed):
    head_count = query_blk.shape[1] // HD
    group_count = key_pair.shape[1] // HD
    per_group = head_count // group_count
    score_scale = 1.0 / math.sqrt(HD)

    def one_head(head_index):
        kv_index = head_index // per_group
        query_head = lax.dynamic_slice_in_dim(query_blk, head_index * HD, HD, 1)
        key_head = lax.dynamic_slice_in_dim(key_pair, kv_index * HD, HD, 1)
        value_head = lax.dynamic_slice_in_dim(value_pair, kv_index * HD, HD, 1)
        grad_head = lax.dynamic_slice_in_dim(grad_blk, head_index * HD, HD, 1)
        scores = lax.dot_general(query_head, key_head, (((1,), (1,)), ((), ())), preferred_element_type=jnp.float32) * score_scale
        scores = jnp.where(allowed, scores, -jnp.inf)
        row_top = lax.optimization_barrier(jnp.max(scores, axis=1, keepdims=True))
        expo = jnp.exp(scores - row_top)
        attn_probs = expo / lax.optimization_barrier(jnp.sum(expo, axis=1, keepdims=True))
        probs_low = attn_probs.astype(jnp.bfloat16)
        out_head = jnp.dot(probs_low, value_head, preferred_element_type=jnp.float32).astype(jnp.bfloat16)
        dprobs = lax.dot_general(grad_head, value_head, (((1,), (1,)), ((), ())), preferred_element_type=jnp.float32)
        row_delta = lax.optimization_barrier(jnp.sum(attn_probs * dprobs, axis=1, keepdims=True))
        dscore = (attn_probs * (dprobs - row_delta)).astype(jnp.bfloat16)
        dquery = jnp.dot(dscore, key_head, preferred_element_type=jnp.float32) * score_scale
        dkey = lax.dot_general(dscore, query_head, (((0,), (0,)), ((), ())), preferred_element_type=jnp.float32) * score_scale
        dvalue = lax.dot_general(probs_low, grad_head, (((0,), (0,)), ((), ())), preferred_element_type=jnp.float32)
        return (out_head, dquery, dkey, dvalue)
    out_heads, dquery_heads, dkey_heads, dvalue_heads = lax.map(one_head, jnp.arange(head_count, dtype=jnp.int32))
    count = query_blk.shape[0]
    attn_out = jnp.transpose(out_heads, (1, 0, 2)).reshape(count, head_count * HD)
    dquery_all = jnp.transpose(dquery_heads, (1, 0, 2)).reshape(count, head_count * HD)
    dkey_all = lax.optimization_barrier(jnp.sum(dkey_heads.reshape(group_count, per_group, 2 * count, HD), axis=1))
    dvalue_all = lax.optimization_barrier(jnp.sum(dvalue_heads.reshape(group_count, per_group, 2 * count, HD), axis=1))
    dkey_all = jnp.transpose(dkey_all, (1, 0, 2)).reshape(2 * count, group_count * HD)
    dvalue_all = jnp.transpose(dvalue_all, (1, 0, 2)).reshape(2 * count, group_count * HD)
    return (attn_out, dquery_all, dkey_all, dvalue_all)

def reference(query_rows, key_rows, value_rows, output_grad, out_proj, segment_ids):
    block_count = TOKENS // TOK_DEV
    attn_grad = jnp.dot(output_grad, out_proj, preferred_element_type=jnp.float32).astype(jnp.bfloat16)

    def per_block(block):
        start = (block * TOK_DEV).astype(jnp.int32)
        earlier = (jnp.maximum(block - 1, 0) * TOK_DEV).astype(jnp.int32)
        query_blk = lax.dynamic_slice_in_dim(query_rows, start, TOK_DEV, 0)
        grad_blk = lax.dynamic_slice_in_dim(attn_grad, start, TOK_DEV, 0)
        key_pair = jnp.concatenate([lax.dynamic_slice_in_dim(key_rows, earlier, TOK_DEV, 0), lax.dynamic_slice_in_dim(key_rows, start, TOK_DEV, 0)], 0)
        value_pair = jnp.concatenate([lax.dynamic_slice_in_dim(value_rows, earlier, TOK_DEV, 0), lax.dynamic_slice_in_dim(value_rows, start, TOK_DEV, 0)], 0)
        allowed = allowed_mask(segment_ids, block, TOK_DEV)
        attn_out, dquery_all, dkey_all, dvalue_all = block_pass(query_blk, key_pair, value_pair, grad_blk, allowed)
        return (attn_out, dquery_all.astype(jnp.bfloat16), dkey_all, dvalue_all)
    attn_outs, dquery_blocks, dkey_blocks, dvalue_blocks = lax.map(per_block, jnp.arange(block_count, dtype=jnp.int32))
    query_grad = dquery_blocks.reshape(TOKENS, HQ * HD)
    zero_block = jnp.zeros((1, TOK_DEV, KV * HD), jnp.float32)
    key_next = jnp.concatenate([dkey_blocks[1:, :TOK_DEV], zero_block], 0)
    value_next = jnp.concatenate([dvalue_blocks[1:, :TOK_DEV], zero_block], 0)
    key_grad = (dkey_blocks[:, TOK_DEV:] + key_next).astype(jnp.bfloat16).reshape(TOKENS, KV * HD)
    value_grad = (dvalue_blocks[:, TOK_DEV:] + value_next).astype(jnp.bfloat16).reshape(TOKENS, KV * HD)
    grad_blocks = output_grad.reshape(block_count, TOK_DEV, D)

    def add_block(total, pair):
        grad_one, out_one = pair
        term = lax.dot_general(grad_one, out_one, (((0,), (0,)), ((), ())), preferred_element_type=jnp.float32)
        term_low = lax.optimization_barrier(term.astype(jnp.bfloat16))
        return (total + term_low.astype(jnp.float32), None)
    proj_total, _ = lax.scan(add_block, jnp.zeros((D, HQ * HD), jnp.float32), (grad_blocks, attn_outs))
    proj_grad = proj_total.astype(jnp.bfloat16)
    return (query_grad, key_grad, value_grad, proj_grad)
```

```python
import functools
import math

import jax
import jax.numpy as jnp
from jax import lax
from jax.experimental import pallas as pl
from jax.experimental.pallas import tpu as pltpu
from jax.sharding import PartitionSpec as P

HD = 128
SCALE = 1.0 / math.sqrt(HD)
NEG = -1e30
BF = jnp.bfloat16
F32 = jnp.float32

ZN, YN, KN, LN, XN = 4, 2, 2, 2, 4


def move_row(value, dz=0, dyh=0, dk=0):
    pairs = []
    for z in range(ZN):
        for y in range(YN):
            for k in range(KN):
                source = (z * YN + y) * KN + k
                target = ((z + dz) % ZN * YN + (y + dyh) % YN) * KN + (k + dk) % KN
                pairs.append((source, target))
    return lax.ppermute(value, "row", pairs)


def move_col(value, dx=0, dyl=0):
    pairs = []
    for y in range(LN):
        for x in range(XN):
            pairs.append((y * XN + x, (y + dyl) % LN * XN + (x + dx) % XN))
    return lax.ppermute(value, "col", pairs)


def passed_along(value, axis, steps):
    count = lax.axis_size(axis)
    first, last = (max(0, -steps), min(count, count - steps))
    return lax.ppermute(value, axis, [(source, source + steps) for source in range(first, last)])


def tied(values, *others):
    held = lax.optimization_barrier((tuple(values), tuple(others)))
    return held[0]


def params(mib, **kw):
    return pltpu.CompilerParams(vmem_limit_bytes=mib * 1024 * 1024, **kw)


def fill_bias(bias_ref, segq, segk, first_block, count):
    key = lax.broadcasted_iota(jnp.int32, (2 * count, count), 0)
    query = lax.broadcasted_iota(jnp.int32, (2 * count, count), 1)
    ok = (key <= query + count) & (segk == segq) & (key >= first_block * count)
    bias_ref[...] = jnp.where(ok, 0.0, NEG).astype(F32)


def chunk_list(count, width):
    return [(i * width, count + (i + 1) * width) for i in range(count // width)]


def fwd_kernel(meta_ref, q_ref, k_ref, vt_ref, segq_ref, segk_ref, out_ref, top_ref, sum_ref, bias_ref):
    count = q_ref.shape[0]

    @pl.when(pl.program_id(0) == 0)
    def _():
        fill_bias(bias_ref, segq_ref[...], segk_ref[...], meta_ref[0], count)

    for start, keys in chunk_list(count, 256):
        cols = slice(start, start + 256)
        s = lax.dot_general(
            k_ref[:keys, :], q_ref[cols, :], (((1,), (1,)), ((), ())), preferred_element_type=F32
        )
        s = s * SCALE + bias_ref[:keys, cols]
        top = jnp.max(s, axis=0, keepdims=True)
        e = jnp.exp(s - top)
        total = jnp.sum(e, axis=0, keepdims=True)
        inv = 1.0 / total
        p = (e * inv).astype(BF)
        a = jnp.dot(vt_ref[:, :keys], p, preferred_element_type=F32)
        out_ref[cols, :] = a.T.astype(BF)
        top_ref[0, :, cols] = top
        sum_ref[0, :, cols] = inv


def attend(query, key_pair, vt, segq, segk, first):
    count, width = query.shape
    heads = width // HD
    whole = lambda shape: pl.BlockSpec(shape, lambda h, m: (0,) * len(shape))
    head = pl.BlockSpec((count, HD), lambda h, m: (0, h))
    stat = pl.BlockSpec((1, 1, count), lambda h, m: (h, 0, 0))
    return pl.pallas_call(
        fwd_kernel,
        grid_spec=pltpu.PrefetchScalarGridSpec(
            num_scalar_prefetch=1,
            grid=(heads,),
            in_specs=[
                head,
                whole((2 * count, HD)),
                whole((HD, 2 * count)),
                whole((1, count)),
                whole((2 * count, 1)),
            ],
            out_specs=[head, stat, stat],
            scratch_shapes=[pltpu.VMEM((2 * count, count), F32)],
        ),
        out_shape=[
            jax.ShapeDtypeStruct((count, width), BF),
            jax.ShapeDtypeStruct((heads, 1, count), F32),
            jax.ShapeDtypeStruct((heads, 1, count), F32),
        ],
        compiler_params=params(40),
        cost_estimate=pl.CostEstimate(
            flops=heads * 4 * 2 * 2 * count * count * HD,
            bytes_accessed=8 * 2**20,
            transcendentals=heads * 2 * count * count,
        ),
        name="attend",
    )(first, query, key_pair, vt, segq, segk)


def bwd_kernel(
    meta_ref, q_ref, g_ref, k_ref, kt_ref, v_ref, segq_ref, segk_ref, top_ref, sum_ref,
    dq_ref, dk_ref, dv_ref, bias_ref,
):
    count = q_ref.shape[0]

    @pl.when(pl.program_id(0) == 0)
    def _():
        fill_bias(bias_ref, segq_ref[...], segk_ref[...], meta_ref[0], count)
        dk_ref[...] = jnp.zeros_like(dk_ref)
        dv_ref[...] = jnp.zeros_like(dv_ref)

    for start, keys in chunk_list(count, 256):
        cols = slice(start, start + 256)
        q = q_ref[cols, :]
        g = g_ref[cols, :]
        s = lax.dot_general(
            k_ref[:keys, :], q, (((1,), (1,)), ((), ())), preferred_element_type=F32
        )
        s = s * SCALE + bias_ref[:keys, cols]
        p = jnp.exp(s - top_ref[0, :, cols]) * sum_ref[0, :, cols]
        dp = lax.dot_general(
            v_ref[:keys, :], g, (((1,), (1,)), ((), ())), preferred_element_type=F32
        )
        delta = jnp.sum(p * dp, axis=0, keepdims=True)
        ds = (p * (dp - delta)).astype(BF)
        dq = jnp.dot(kt_ref[:, :keys], ds, preferred_element_type=F32) * SCALE
        dq_ref[cols, :] = dq.T.astype(BF)
        dk_ref[:keys, :] += jnp.dot(ds, q, preferred_element_type=F32)
        dv_ref[:keys, :] += jnp.dot(p.astype(BF), g, preferred_element_type=F32)

    @pl.when(pl.program_id(0) == pl.num_programs(0) - 1)
    def _():
        dk_ref[...] = dk_ref[...] * SCALE


def attend_back(query, grad, key_pair, kt, value_pair, segq, segk, first, top, total):
    count, width = query.shape
    heads = width // HD
    whole = lambda shape: pl.BlockSpec(shape, lambda h, m: (0,) * len(shape))
    head = pl.BlockSpec((count, HD), lambda h, m: (0, h))
    stat = pl.BlockSpec((1, 1, count), lambda h, m: (h, 0, 0))
    pair = whole((2 * count, HD))
    return pl.pallas_call(
        bwd_kernel,
        grid_spec=pltpu.PrefetchScalarGridSpec(
            num_scalar_prefetch=1,
            grid=(heads,),
            in_specs=[
                head,
                head,
                pair,
                whole((HD, 2 * count)),
                pair,
                whole((1, count)),
                whole((2 * count, 1)),
                stat,
                stat,
            ],
            out_specs=[head, pair, pair],
            scratch_shapes=[pltpu.VMEM((2 * count, count), F32)],
        ),
        out_shape=[
            jax.ShapeDtypeStruct((count, width), BF),
            jax.ShapeDtypeStruct((2 * count, HD), F32),
            jax.ShapeDtypeStruct((2 * count, HD), F32),
        ],
        compiler_params=params(40),
        cost_estimate=pl.CostEstimate(
            flops=heads * 10 * 2 * 2 * count * count * HD,
            bytes_accessed=12 * 2**20,
            transcendentals=heads * 2 * count * count,
        ),
        name="attend_back",
    )(first, query, grad, key_pair, kt, value_pair, segq, segk, top, total)


def load_pieces(meta_ref, refs, plan, buffer, sems):
    copies = []
    for n, (ref_at, source, block, start, rows) in enumerate(plan):
        copies.append(
            pltpu.make_async_copy(
                refs[ref_at].at[pl.ds(source, rows)],
                buffer.at[meta_ref[block], pl.ds(start, rows)],
                sems.at[n],
            )
        )
    for copy in copies:
        copy.start()
    return copies


def proj_kernel(plan, n_in, meta_ref, *refs):
    pieces, a_ref = refs[:n_in], refs[n_in]
    out_ref = refs[n_in + 1]
    buffer, sems = refs[n_in + 2:]
    step = pl.program_id(0)

    @pl.when(step == 0)
    def _():
        for copy in load_pieces(meta_ref, pieces, plan, buffer, sems):
            copy.wait()

    block = buffer[meta_ref[8 + step]]
    out_ref[0] = lax.dot_general(
        block, a_ref[...], (((0,), (0,)), ((), ())), preferred_element_type=F32
    ).astype(BF)


def project(pieces, plan, meta, a_pair, first, count):
    tokens, width = a_pair.shape
    depth = pieces[0].shape[1]
    kernel = functools.partial(proj_kernel, plan, len(pieces))
    return pl.pallas_call(
        kernel,
        grid_spec=pltpu.PrefetchScalarGridSpec(
            num_scalar_prefetch=1,
            grid=(count,),
            in_specs=[pl.BlockSpec(memory_space=pl.ANY)] * len(pieces)
            + [pl.BlockSpec((tokens, width), lambda j, m: (0, 0))],
            out_specs=pl.BlockSpec((1, depth, width), lambda j, m: (j, 0, 0)),
            scratch_shapes=[
                pltpu.VMEM((8, tokens, depth), BF),
                pltpu.SemaphoreType.DMA((len(plan),)),
            ],
        ),
        out_shape=jax.ShapeDtypeStruct((count, depth, width), BF),
        compiler_params=params(44),
        cost_estimate=pl.CostEstimate(
            flops=2 * count * tokens * depth * width,
            bytes_accessed=(8 + 2 + count) * 2**20,
            transcendentals=0,
        ),
        name="project",
    )(jnp.concatenate([meta[:8], meta[8 + first:]]), *pieces, a_pair)


def grad_kernel(gplan, wplan, n_g, n_w, meta_ref, *refs):
    g_in, w_in = refs[:n_g], refs[n_g:n_g + n_w]
    own_ref, other_ref = refs[n_g + n_w:n_g + n_w + 2]
    gbuf, wbuf, total, gsems, wsems = refs[n_g + n_w + 2:]
    step = pl.program_id(0)
    half = own_ref.shape[0]

    @pl.when(step == 0)
    def _():
        copies = load_pieces(meta_ref, g_in, gplan, gbuf, gsems)
        copies += load_pieces(meta_ref, w_in, wplan, wbuf, wsems)
        for copy in copies:
            copy.wait()
        total[...] = jnp.dot(gbuf[0], wbuf[0], preferred_element_type=F32)

    @pl.when(step > 0)
    def _():
        total[...] += jnp.dot(gbuf[step], wbuf[step], preferred_element_type=F32)

    @pl.when(step == 7)
    def _():
        own_ref[...] = total[:half, :]
        other_ref[...] = total[half:, :].astype(BF)


def attn_grad_part(g_pieces, gplan, w_pieces, wplan, meta):
    tokens, depth = g_pieces[0].shape
    width = w_pieces[0].shape[1]
    half = tokens // 2
    kernel = functools.partial(grad_kernel, gplan, wplan, len(g_pieces), len(w_pieces))
    whole = pl.BlockSpec((half, width), lambda j, m: (0, 0))
    return pl.pallas_call(
        kernel,
        grid_spec=pltpu.PrefetchScalarGridSpec(
            num_scalar_prefetch=1,
            grid=(8,),
            in_specs=[pl.BlockSpec(memory_space=pl.ANY)] * (len(g_pieces) + len(w_pieces)),
            out_specs=[whole, whole],
            scratch_shapes=[
                pltpu.VMEM((8, tokens, depth), BF),
                pltpu.VMEM((8, depth, width), BF),
                pltpu.VMEM((tokens, width), F32),
                pltpu.SemaphoreType.DMA((len(gplan),)),
                pltpu.SemaphoreType.DMA((len(wplan),)),
            ],
        ),
        out_shape=[
            jax.ShapeDtypeStruct((half, width), F32),
            jax.ShapeDtypeStruct((half, width), BF),
        ],
        compiler_params=params(48),
        cost_estimate=pl.CostEstimate(
            flops=16 * tokens * depth * width,
            bytes_accessed=20 * 2**20,
            transcendentals=0,
        ),
        name="attn_grad",
    )(meta, *g_pieces, *w_pieces)


def add_up(*terms):
    total = terms[0].astype(F32)
    for term in terms[1:]:
        total = total + term.astype(F32)
    return total.astype(BF)


def local(query_rows, key_rows, value_rows, output_grad, out_proj, segment_ids):
    count = query_rows.shape[0]
    half_d = output_grad.shape[1] // 2
    row, col = lax.axis_index("row"), lax.axis_index("col")
    z, yh, k = row // 4, row // 2 % 2, row % 2
    yl, x = col // 4, col % 4

    def gblock(dyl, dx):
        return (yl + dyl) % 2 * 4 + (x + dx) % 4

    def wblock(dz, dy):
        return (z + dz) % 4 * 2 + (yh + dy) % 2

    def ints(*values):
        return jnp.stack([jnp.asarray(v, jnp.int32) for v in values])

    g_keep = lax.dynamic_slice_in_dim(output_grad, k * half_d, half_d, 1)
    g_give = lax.dynamic_slice_in_dim(output_grad, (1 - k) * half_d, half_d, 1)
    g0 = jnp.concatenate([g_keep, move_row(g_give, dk=1)], 0)
    kv = jnp.concatenate([key_rows, value_rows], 1)
    kv_earlier = passed_along(kv, "row", 1)

    gxm = move_col(g0, dx=1)
    gxp = move_col(g0, dx=-1)
    gy = move_col(g0, dyl=1)
    wzm = move_row(out_proj, dz=1)
    wzp = move_row(out_proj, dz=-1)

    kv_pair = jnp.concatenate([kv_earlier, kv], 0)
    key_pair, value_pair = kv_pair[:, :HD], kv_pair[:, HD:]
    key_t, value_t = key_pair.T, value_pair.T
    seg_query = lax.dynamic_slice_in_dim(segment_ids, row * count, count, 0)
    seg_earlier = lax.dynamic_slice_in_dim(
        segment_ids, jnp.maximum(row - 1, 0) * count, count, 0
    )
    segk = jnp.concatenate([seg_earlier, seg_query], 0)[:, None]
    segq = seg_query[None, :]
    first = ints(row == 0)
    (query_held,) = tied((query_rows,), g0)
    attn_out, top, total = attend(query_held, key_pair, value_t, segq, segk, first)
    a_other = move_row(attn_out, dk=1)
    a_pair = jnp.concatenate([attn_out, a_other], 0)

    gxm, gxp, gy, wzm, wzp, a_pair = tied((gxm, gxp, gy, wzm, wzp, a_pair))

    h = g0.shape[0] // 2
    hw = out_proj.shape[0] // 2
    gyxm = move_col(gy, dx=1)
    gyxp = move_col(gy, dx=-1)
    wom = move_row(wzm[:hw], dz=1)
    wop = move_row(wzp[hw:], dz=-1)
    wy = move_row(out_proj, dyh=1)

    gyxm, gyxp, wom, wop, wy = tied((gyxm, gyxp, wom, wop, wy))

    gom = move_col(jnp.concatenate([gxm[:h], gyxm[:h]], 0), dx=1)
    gop = move_col(jnp.concatenate([gxp[h:], gyxp[h:]], 0), dx=-1)
    wyzm = move_row(wy, dz=1)
    wyzp = move_row(wy, dz=-1)

    gom, gop, wyzm, wyzp = tied((gom, gop, wyzm, wyzp))

    wyom = move_row(wyzm[:hw], dz=1)
    wyop = move_row(wyzp[hw:], dz=-1)

    g_pieces = [g0, gxm, gxp, gy, gyxm, gyxp, gom, gop]
    gplan = [(i, 0, i, 0, 2 * h) for i in range(6)] + [
        (6, 0, 6, 0, h),
        (6, h, 7, 0, h),
        (7, 0, 6, h, h),
        (7, h, 7, h, h),
    ]
    g_order = ints(
        gblock(0, 0), gblock(0, -1), gblock(0, 1), gblock(1, 0),
        gblock(1, -1), gblock(1, 1), gblock(0, 2), gblock(1, 2),
        wblock(2, 1), wblock(2, 0), wblock(1, 1), wblock(-1, 1),
        wblock(1, 0), wblock(-1, 0), wblock(0, 1), wblock(0, 0),
    )
    far = project(g_pieces, gplan, g_order, a_pair, 0, 2)
    fm = move_row(jnp.concatenate([far[0, :hw], far[1, :hw]], 0), dz=1)
    fp = move_row(jnp.concatenate([far[0, hw:], far[1, hw:]], 0), dz=-1)
    near = project(g_pieces, gplan, g_order, a_pair, 2, 6)

    w_pieces = [out_proj, wzm, wzp, wy, wyzm, wyzp, wom, wop, wyom, wyop]
    wplan = [(i, 0, i, 0, 2 * hw) for i in range(6)] + [
        (6, 0, 6, 0, hw),
        (7, 0, 6, hw, hw),
        (8, 0, 7, 0, hw),
        (9, 0, 7, hw, hw),
    ]
    w_order = ints(
        wblock(0, 0), wblock(-1, 0), wblock(1, 0), wblock(0, 1),
        wblock(-1, 1), wblock(1, 1), wblock(2, 0), wblock(2, 1),
    )
    meta = jnp.concatenate([g_order[:8], w_order])
    wplan = [(i, s, b + 8, t, n) for i, s, b, t, n in wplan]
    grad_own, grad_give = attn_grad_part(g_pieces, gplan, w_pieces, wplan, meta)
    grad_got = move_row(grad_give, dk=1)
    attn_grad = (grad_own + grad_got.astype(F32)).astype(BF)

    fm, fp, near = tied((fm, fp, near))

    up = lambda block, extra: jnp.concatenate([add_up(block[:hw], extra), block[hw:]], 0)
    down = lambda block, extra: jnp.concatenate([block[:hw], add_up(block[hw:], extra)], 0)
    sup1 = move_row(up(near[0], fm[:hw]), dz=1)
    sdn1 = move_row(down(near[1], fp[:hw]), dz=-1)

    query_grad, dkey, dvalue = attend_back(
        query_rows, attn_grad, key_pair, key_t, value_pair, segq, segk, first, top, total
    )
    back = passed_along(
        jnp.concatenate([dkey[:count], dvalue[:count]], 1).astype(BF), "row", -1
    ).astype(F32)

    sup1, sdn1, = tied((sup1, sdn1))

    other = move_row(add_up(near[4], sup1, sdn1), dyh=1)
    sup0 = move_row(up(near[2], fm[hw:]), dz=1)
    sdn0 = move_row(down(near[3], fp[hw:]), dz=-1)
    proj_grad = add_up(near[5], sup0, sdn0, other)

    key_grad = (dkey[count:] + back[:, :HD]).astype(BF)
    value_grad = (dvalue[count:] + back[:, HD:]).astype(BF)
    return (query_grad, key_grad, value_grad, proj_grad)


def solution(mesh):
    placed = (
        P("row", "col"),
        P("row", "col"),
        P("row", "col"),
        P("row", "col"),
        P("row", "col"),
        P(),
    )
    return jax.shard_map(
        local,
        mesh=mesh,
        in_specs=placed,
        out_specs=(P("row", "col"), P("row", "col"), P("row", "col"), P("row", "col")),
        check_vma=False,
    )
```

```python
import functools
import math

import jax
import jax.numpy as jnp
from jax import lax
from jax.experimental import pallas as pl
from jax.experimental.pallas import tpu as pltpu
from jax.sharding import PartitionSpec as P

HD = 128
SCALE = 1.0 / math.sqrt(HD)
NEG = -1e30
BF = jnp.bfloat16
F32 = jnp.float32

ZN, YN, KN, LN, XN = 4, 2, 2, 2, 4


def move_row(value, dz=0, dyh=0, dk=0):
    pairs = []
    for z in range(ZN):
        for y in range(YN):
            for k in range(KN):
                source = (z * YN + y) * KN + k
                target = ((z + dz) % ZN * YN + (y + dyh) % YN) * KN + (k + dk) % KN
                pairs.append((source, target))
    return lax.ppermute(value, "row", pairs)


def move_col(value, dx=0, dyl=0):
    pairs = []
    for y in range(LN):
        for x in range(XN):
            pairs.append((y * XN + x, (y + dyl) % LN * XN + (x + dx) % XN))
    return lax.ppermute(value, "col", pairs)


def passed_along(value, axis, steps):
    count = lax.axis_size(axis)
    first, last = (max(0, -steps), min(count, count - steps))
    return lax.ppermute(value, axis, [(source, source + steps) for source in range(first, last)])


def tied(values, *others):
    held = lax.optimization_barrier((tuple(values), tuple(others)))
    return held[0]


def params(mib, **kw):
    return pltpu.CompilerParams(vmem_limit_bytes=mib * 1024 * 1024, **kw)


def fill_bias(bias_ref, segq, segk, first_block, count):
    key = lax.broadcasted_iota(jnp.int32, (2 * count, count), 0)
    query = lax.broadcasted_iota(jnp.int32, (2 * count, count), 1)
    ok = (key <= query + count) & (segk == segq) & (key >= first_block * count)
    bias_ref[...] = jnp.where(ok, 0.0, NEG).astype(F32)


def chunk_list(count, width):
    return [(i * width, count + (i + 1) * width) for i in range(count // width)]


def fwd_kernel(meta_ref, q_ref, k_ref, vt_ref, segq_ref, segk_ref, out_ref, top_ref, sum_ref, bias_ref):
    count = q_ref.shape[0]

    @pl.when(pl.program_id(0) == 0)
    def _():
        fill_bias(bias_ref, segq_ref[...], segk_ref[...], meta_ref[0], count)

    for start, keys in chunk_list(count, 256):
        cols = slice(start, start + 256)
        s = lax.dot_general(
            k_ref[:keys, :], q_ref[cols, :], (((1,), (1,)), ((), ())), preferred_element_type=F32
        )
        s = s * SCALE + bias_ref[:keys, cols]
        top = jnp.max(s, axis=0, keepdims=True)
        e = jnp.exp(s - top)
        total = jnp.sum(e, axis=0, keepdims=True)
        inv = 1.0 / total
        p = (e * inv).astype(BF)
        a = jnp.dot(vt_ref[:, :keys], p, preferred_element_type=F32)
        out_ref[cols, :] = a.T.astype(BF)
        top_ref[0, :, cols] = top
        sum_ref[0, :, cols] = inv


def attend(query, key_pair, vt, segq, segk, first):
    count, width = query.shape
    heads = width // HD
    whole = lambda shape: pl.BlockSpec(shape, lambda h, m: (0,) * len(shape))
    head = pl.BlockSpec((count, HD), lambda h, m: (0, h))
    stat = pl.BlockSpec((1, 1, count), lambda h, m: (h, 0, 0))
    return pl.pallas_call(
        fwd_kernel,
        grid_spec=pltpu.PrefetchScalarGridSpec(
            num_scalar_prefetch=1,
            grid=(heads,),
            in_specs=[
                head,
                whole((2 * count, HD)),
                whole((HD, 2 * count)),
                whole((1, count)),
                whole((2 * count, 1)),
            ],
            out_specs=[head, stat, stat],
            scratch_shapes=[pltpu.VMEM((2 * count, count), F32)],
        ),
        out_shape=[
            jax.ShapeDtypeStruct((count, width), BF),
            jax.ShapeDtypeStruct((heads, 1, count), F32),
            jax.ShapeDtypeStruct((heads, 1, count), F32),
        ],
        compiler_params=params(40),
        cost_estimate=pl.CostEstimate(
            flops=heads * 4 * 2 * 2 * count * count * HD,
            bytes_accessed=8 * 2**20,
            transcendentals=heads * 2 * count * count,
        ),
        name="attend",
    )(first, query, key_pair, vt, segq, segk)


def bwd_kernel(
    meta_ref, q_ref, g_ref, k_ref, kt_ref, v_ref, segq_ref, segk_ref, top_ref, sum_ref,
    dq_ref, dk_ref, dv_ref, bias_ref,
):
    count = q_ref.shape[0]

    @pl.when(pl.program_id(0) == 0)
    def _():
        fill_bias(bias_ref, segq_ref[...], segk_ref[...], meta_ref[0], count)
        dk_ref[...] = jnp.zeros_like(dk_ref)
        dv_ref[...] = jnp.zeros_like(dv_ref)

    for start, keys in chunk_list(count, 256):
        cols = slice(start, start + 256)
        q = q_ref[cols, :]
        g = g_ref[cols, :]
        s = lax.dot_general(
            k_ref[:keys, :], q, (((1,), (1,)), ((), ())), preferred_element_type=F32
        )
        s = s * SCALE + bias_ref[:keys, cols]
        p = jnp.exp(s - top_ref[0, :, cols]) * sum_ref[0, :, cols]
        dp = lax.dot_general(
            v_ref[:keys, :], g, (((1,), (1,)), ((), ())), preferred_element_type=F32
        )
        delta = jnp.sum(p * dp, axis=0, keepdims=True)
        ds = (p * (dp - delta)).astype(BF)
        dq = jnp.dot(kt_ref[:, :keys], ds, preferred_element_type=F32) * SCALE
        dq_ref[cols, :] = dq.T.astype(BF)
        dk_ref[:keys, :] += jnp.dot(ds, q, preferred_element_type=F32)
        dv_ref[:keys, :] += jnp.dot(p.astype(BF), g, preferred_element_type=F32)

    @pl.when(pl.program_id(0) == pl.num_programs(0) - 1)
    def _():
        dk_ref[...] = dk_ref[...] * SCALE


def attend_back(query, grad, key_pair, kt, value_pair, segq, segk, first, top, total):
    count, width = query.shape
    heads = width // HD
    whole = lambda shape: pl.BlockSpec(shape, lambda h, m: (0,) * len(shape))
    head = pl.BlockSpec((count, HD), lambda h, m: (0, h))
    stat = pl.BlockSpec((1, 1, count), lambda h, m: (h, 0, 0))
    pair = whole((2 * count, HD))
    return pl.pallas_call(
        bwd_kernel,
        grid_spec=pltpu.PrefetchScalarGridSpec(
            num_scalar_prefetch=1,
            grid=(heads,),
            in_specs=[
                head,
                head,
                pair,
                whole((HD, 2 * count)),
                pair,
                whole((1, count)),
                whole((2 * count, 1)),
                stat,
                stat,
            ],
            out_specs=[head, pair, pair],
            scratch_shapes=[pltpu.VMEM((2 * count, count), F32)],
        ),
        out_shape=[
            jax.ShapeDtypeStruct((count, width), BF),
            jax.ShapeDtypeStruct((2 * count, HD), F32),
            jax.ShapeDtypeStruct((2 * count, HD), F32),
        ],
        compiler_params=params(40),
        cost_estimate=pl.CostEstimate(
            flops=heads * 10 * 2 * 2 * count * count * HD,
            bytes_accessed=12 * 2**20,
            transcendentals=heads * 2 * count * count,
        ),
        name="attend_back",
    )(first, query, grad, key_pair, kt, value_pair, segq, segk, top, total)


def proj_kernel(split, n_blocks, n_in, held, meta_ref, *refs):
    pieces, a_ref = refs[:n_in], refs[n_in]
    out_ref = refs[n_in + 1 + held]
    step = pl.program_id(0)
    h = a_ref.shape[0] // 2
    over_tokens = (((0,), (0,)), ((), ()))

    def store(value):
        value = value.astype(BF)
        rows = value.shape[0] // 2
        out_ref[0, 0] = value[:rows]
        out_ref[1, 0] = value[rows:]

    for j in range(n_blocks):

        @pl.when(step == j)
        def _():
            if split:
                part = slice(j * h, (j + 1) * h)
                store(
                    lax.dot_general(
                        pieces[0][part, :], a_ref[:h, :], over_tokens, preferred_element_type=F32
                    )
                    + lax.dot_general(
                        pieces[1][part, :], a_ref[h:, :], over_tokens, preferred_element_type=F32
                    )
                )
            else:
                store(
                    lax.dot_general(
                        pieces[j][...], a_ref[...], over_tokens, preferred_element_type=F32
                    )
                )


def project(pieces, split, a_pair, blocks, buffer):
    tokens, width = a_pair.shape
    depth = pieces[0].shape[1]
    n_blocks = 2 if split else len(pieces)
    held = int(buffer is not None)
    whole = lambda shape: pl.BlockSpec(shape, lambda j, m: (0,) * len(shape))
    operands = (*pieces, a_pair) + ((buffer,) if held else ())
    return pl.pallas_call(
        functools.partial(proj_kernel, split, n_blocks, len(pieces), held),
        grid_spec=pltpu.PrefetchScalarGridSpec(
            num_scalar_prefetch=1,
            grid=(n_blocks,),
            in_specs=[whole((tokens, depth))] * len(pieces)
            + [whole((tokens, width))]
            + [pl.BlockSpec(memory_space=pl.ANY)] * held,
            out_specs=pl.BlockSpec((2, 1, depth // 2, width), lambda j, m: (0, m[j], 0, 0)),
        ),
        out_shape=jax.ShapeDtypeStruct((2, 8, depth // 2, width), BF),
        input_output_aliases={len(pieces) + 2: 0} if held else {},
        compiler_params=params(40),
        cost_estimate=pl.CostEstimate(
            flops=2 * n_blocks * tokens * depth * width,
            bytes_accessed=(2 * n_blocks + 2) * 2**20,
            transcendentals=0,
        ),
        name="project",
    )(blocks, *operands)


def grad_kernel(gplan, wplan, n_g, n_w, meta_ref, *refs):
    g_in, w_in = refs[:n_g], refs[n_g:n_g + n_w]
    own_ref, other_ref = refs[n_g + n_w:n_g + n_w + 2]
    gbuf, wbuf, total, gsems, wsems = refs[n_g + n_w + 2:]
    step = pl.program_id(0)
    half = own_ref.shape[0]
    gh, wh = gbuf.shape[1] // 2, wbuf.shape[1] // 2

    def g_copy(n):
        ref, source, block, part = gplan[n]
        return pltpu.make_async_copy(
            g_in[ref].at[pl.ds(source, gh)], gbuf.at[block, pl.ds(part * gh, gh)], gsems.at[n]
        )

    def w_copy(n):
        ref, source, block, part = wplan[n]
        place = meta_ref[8 + block]
        return pltpu.make_async_copy(
            w_in[ref].at[pl.ds(source, wh)],
            wbuf.at[place, pl.ds(part * wh, wh)],
            wsems.at[part, place],
        )

    @pl.when(step == 0)
    def _():
        for n in range(16):
            w_copy(n).start()
            g_copy(n).start()

    for j in range(8):

        @pl.when(step == j)
        def _():
            for n in range(16):
                if gplan[n][2] == j:
                    g_copy(n).wait()

    place = meta_ref[step]
    for part in range(2):
        pltpu.make_async_copy(
            w_in[0].at[pl.ds(0, wh)], wbuf.at[place, pl.ds(part * wh, wh)], wsems.at[part, place]
        ).wait()

    @pl.when(step == 0)
    def _():
        total[...] = jnp.dot(gbuf[step], wbuf[place], preferred_element_type=F32)

    @pl.when(step > 0)
    def _():
        total[...] += jnp.dot(gbuf[step], wbuf[place], preferred_element_type=F32)

    @pl.when(step == 7)
    def _():
        own_ref[...] = total[:half, :]
        other_ref[...] = total[half:, :].astype(BF)


def attn_grad_part(g_pieces, gplan, w_pieces, wplan, meta):
    tokens, depth = g_pieces[0].shape
    width = w_pieces[0].shape[1]
    half = tokens // 2
    kernel = functools.partial(grad_kernel, gplan, wplan, len(g_pieces), len(w_pieces))
    whole = pl.BlockSpec((half, width), lambda j, m: (0, 0))
    return pl.pallas_call(
        kernel,
        grid_spec=pltpu.PrefetchScalarGridSpec(
            num_scalar_prefetch=1,
            grid=(8,),
            in_specs=[pl.BlockSpec(memory_space=pl.ANY)] * (len(g_pieces) + len(w_pieces)),
            out_specs=[whole, whole],
            scratch_shapes=[
                pltpu.VMEM((8, tokens, depth), BF),
                pltpu.VMEM((8, depth, width), BF),
                pltpu.VMEM((tokens, width), F32),
                pltpu.SemaphoreType.DMA((16,)),
                pltpu.SemaphoreType.DMA((2, 8)),
            ],
        ),
        out_shape=[
            jax.ShapeDtypeStruct((half, width), F32),
            jax.ShapeDtypeStruct((half, width), BF),
        ],
        compiler_params=params(48),
        cost_estimate=pl.CostEstimate(
            flops=16 * tokens * depth * width,
            bytes_accessed=20 * 2**20,
            transcendentals=0,
        ),
        name="attn_grad",
    )(meta, *g_pieces, *w_pieces)


def add_kernel(n_blocks, plan, meta_ref, *refs):
    blocks = refs[:n_blocks]
    n_out = len(plan)
    terms = refs[n_blocks:len(refs) - n_out]
    for out_ref, (block, part, extra) in zip(refs[len(refs) - n_out:], plan):
        if part is None:
            for p in range(2):
                value = blocks[block][p, 0]
                added = [e if isinstance(e, int) else e[0] for e in extra if isinstance(e, int) or e[1] == p]
                if added:
                    value = value.astype(F32)
                    for e in added:
                        term = terms[e]
                        value = value + (term[p] if term.shape[0] == 2 else term[0]).astype(F32)
                out_ref[p] = value.astype(BF)
        else:
            value = blocks[block][part, 0].astype(F32)
            for e in extra:
                value = value + terms[e][part].astype(F32)
            out_ref[0] = value.astype(BF)


def add_blocks(buffer, blocks, terms, plan):
    _, _, rows, width = buffer.shape
    n_blocks = blocks.shape[0]
    place = lambda n: pl.BlockSpec((2, 1, rows, width), lambda i, m: (0, m[n], 0, 0))
    whole = lambda shape: pl.BlockSpec(shape, lambda i, m: (0,) * len(shape))
    shapes = [(2 if part is None else 1, rows, width) for _, part, _ in plan]
    return pl.pallas_call(
        functools.partial(add_kernel, n_blocks, plan),
        grid_spec=pltpu.PrefetchScalarGridSpec(
            num_scalar_prefetch=1,
            grid=(1,),
            in_specs=[place(n) for n in range(n_blocks)] + [whole(t.shape) for t in terms],
            out_specs=[whole(shape) for shape in shapes],
        ),
        out_shape=[jax.ShapeDtypeStruct(shape, BF) for shape in shapes],
        compiler_params=params(32),
        cost_estimate=pl.CostEstimate(
            flops=2**21, bytes_accessed=5 * 2**20, transcendentals=0
        ),
        name="add_blocks",
    )(blocks, *([buffer] * n_blocks), *terms)


def local(query_rows, key_rows, value_rows, output_grad, out_proj, segment_ids):
    count = query_rows.shape[0]
    half_d = output_grad.shape[1] // 2
    row, col = lax.axis_index("row"), lax.axis_index("col")
    z, yh, k = row // 4, row // 2 % 2, row % 2
    yl, x = col // 4, col % 4

    def gblock(dyl, dx):
        return (yl + dyl) % 2 * 4 + (x + dx) % 4

    def wblock(dz, dy):
        return (z + dz) % 4 * 2 + (yh + dy) % 2

    def ints(*values):
        return jnp.stack([jnp.asarray(v, jnp.int32) for v in values])

    g_keep = lax.dynamic_slice_in_dim(output_grad, k * half_d, half_d, 1)
    g_give = lax.dynamic_slice_in_dim(output_grad, (1 - k) * half_d, half_d, 1)
    g0 = jnp.concatenate([g_keep, move_row(g_give, dk=1)], 0)
    kv = jnp.concatenate([key_rows, value_rows], 1)
    kv_earlier = passed_along(kv, "row", 1)

    gxm = move_col(g0, dx=1)
    gxp = move_col(g0, dx=-1)
    gy = move_col(g0, dyl=1)
    wzm = move_row(out_proj, dz=1)
    wzp = move_row(out_proj, dz=-1)

    kv_pair = jnp.concatenate([kv_earlier, kv], 0)
    key_pair, value_pair = kv_pair[:, :HD], kv_pair[:, HD:]
    key_t, value_t = key_pair.T, value_pair.T
    seg_query = lax.dynamic_slice_in_dim(segment_ids, row * count, count, 0)
    seg_earlier = lax.dynamic_slice_in_dim(
        segment_ids, jnp.maximum(row - 1, 0) * count, count, 0
    )
    segk = jnp.concatenate([seg_earlier, seg_query], 0)[:, None]
    segq = seg_query[None, :]
    first = ints(row == 0)
    (query_held,) = tied((query_rows,), g0)
    attn_out, top, total = attend(query_held, key_pair, value_t, segq, segk, first)

    gxm, gxp, gy, wzm, wzp, attn_out = tied((gxm, gxp, gy, wzm, wzp, attn_out))

    h = g0.shape[0] // 2
    hw = out_proj.shape[0] // 2
    a_other = move_row(attn_out, dk=1)
    gyxm = move_col(gy, dx=1)
    gyxp = move_col(gy, dx=-1)
    wom = move_row(wzm[:hw], dz=1)
    wop = move_row(wzp[hw:], dz=-1)
    wy = move_row(out_proj, dyh=1)

    a_pair = jnp.concatenate([attn_out, a_other], 0)
    proj = project(
        [g0, gxm, gxp, gy],
        False,
        a_pair,
        ints(gblock(0, 0), gblock(0, -1), gblock(0, 1), gblock(1, 0)),
        None,
    )

    gyxm, gyxp, wom, wop, wy, proj = tied((gyxm, gyxp, wom, wop, wy, proj))

    gom = move_col(jnp.concatenate([gxm[:h], gyxm[:h]], 0), dx=1)
    gop = move_col(jnp.concatenate([gxp[h:], gyxp[h:]], 0), dx=-1)
    wyzm = move_row(wy, dz=1)
    wyzp = move_row(wy, dz=-1)
    wyo = move_row(jnp.concatenate([wom, wop], 0), dyh=1)

    proj = project([gyxm, gyxp], False, a_pair, ints(gblock(1, -1), gblock(1, 1)), proj)

    gom, gop, wyzm, wyzp, wyo, proj = tied((gom, gop, wyzm, wyzp, wyo, proj))

    proj = project([gom, gop], True, a_pair, ints(gblock(0, 2), gblock(1, 2)), proj)

    def block_at(dz, dy):
        return lax.dynamic_slice_in_dim(proj, wblock(dz, dy), 1, 1)[:, 0]

    rup = move_row(block_at(1, 1), dz=1)
    rdn = move_row(block_at(-1, 1), dz=-1)
    ry = move_row(block_at(2, 1), dyh=1)

    g_pieces = [g0, gxm, gxp, gy, gyxm, gyxp, gom, gop]
    gplan = [(i, p * h, i, p) for i in range(6) for p in range(2)] + [
        (6, 0, 6, 0),
        (6, h, 7, 0),
        (7, 0, 6, 1),
        (7, h, 7, 1),
    ]
    w_pieces = [out_proj, wzm, wzp, wy, wyzm, wyzp, wyo, wom, wop]
    wplan = [(i, p * hw, i, p) for i in range(7) for p in range(2)] + [(7, 0, 7, 0), (8, 0, 7, 1)]
    meta = ints(
        gblock(0, 0), gblock(0, -1), gblock(0, 1), gblock(1, 0),
        gblock(1, -1), gblock(1, 1), gblock(0, 2), gblock(1, 2),
        wblock(0, 0), wblock(-1, 0), wblock(1, 0), wblock(0, 1),
        wblock(-1, 1), wblock(1, 1), wblock(2, 1), wblock(2, 0),
    )
    (meta,) = tied((meta,), proj)
    grad_own, grad_give = attn_grad_part(g_pieces, gplan, w_pieces, wplan, meta)

    rup, rdn, ry, grad_own, grad_give = tied((rup, rdn, ry, grad_own, grad_give))

    across, far_up, far_dn = add_blocks(
        proj,
        ints(wblock(0, 1), wblock(2, 0)),
        [rup, rdn, ry],
        [(0, None, (0, 1)), (1, 0, (2,)), (1, 1, (2,))],
    )
    fup = move_row(far_up, dz=1)
    fdn = move_row(far_dn, dz=-1)
    across = move_row(across, dyh=1)
    grad_got = move_row(grad_give, dk=1)
    attn_grad = (grad_own + grad_got.astype(F32)).astype(BF)

    fup, fdn, attn_grad = tied((fup, fdn, attn_grad))

    near_up, near_dn = add_blocks(
        proj,
        ints(wblock(1, 0), wblock(-1, 0)),
        [fup, fdn],
        [(0, None, ((0, 0),)), (1, None, ((1, 1),))],
    )
    nup = move_row(near_up, dz=1)
    ndn = move_row(near_dn, dz=-1)

    (attn_grad,) = tied((attn_grad,), near_up)
    query_grad, dkey, dvalue = attend_back(
        query_rows, attn_grad, key_pair, key_t, value_pair, segq, segk, first, top, total
    )
    back = passed_along(
        jnp.concatenate([dkey[:count], dvalue[:count]], 1).astype(BF), "row", -1
    ).astype(F32)
    key_grad = (dkey[count:] + back[:, :HD]).astype(BF)
    value_grad = (dvalue[count:] + back[:, HD:]).astype(BF)

    (proj_grad,) = add_blocks(
        proj, ints(wblock(0, 0)), [nup, ndn, across], [(0, None, (0, 1, 2))]
    )
    return (query_grad, key_grad, value_grad, proj_grad.reshape(2 * hw, out_proj.shape[1]))


def solution(mesh):
    placed = (
        P("row", "col"),
        P("row", "col"),
        P("row", "col"),
        P("row", "col"),
        P("row", "col"),
        P(),
    )
    return jax.shard_map(
        local,
        mesh=mesh,
        in_specs=placed,
        out_specs=(P("row", "col"), P("row", "col"), P("row", "col"), P("row", "col")),
        check_vma=False,
    )
```

```python
import functools
import math

import jax
import jax.numpy as jnp
from jax import lax
from jax.experimental import pallas as pl
from jax.experimental.pallas import tpu as pltpu
from jax.sharding import PartitionSpec as P

HD = 128
SCALE = 1.0 / math.sqrt(HD)
NEG = -1e30
BF = jnp.bfloat16
F32 = jnp.float32

ZN, YN, KN, LN, XN = 4, 2, 2, 2, 4


def move_row(value, dz=0, dyh=0, dk=0):
    pairs = []
    for z in range(ZN):
        for y in range(YN):
            for k in range(KN):
                source = (z * YN + y) * KN + k
                target = ((z + dz) % ZN * YN + (y + dyh) % YN) * KN + (k + dk) % KN
                pairs.append((source, target))
    return lax.ppermute(value, "row", pairs)


def move_col(value, dx=0, dyl=0):
    pairs = []
    for y in range(LN):
        for x in range(XN):
            pairs.append((y * XN + x, (y + dyl) % LN * XN + (x + dx) % XN))
    return lax.ppermute(value, "col", pairs)


def passed_along(value, axis, steps):
    count = lax.axis_size(axis)
    first, last = (max(0, -steps), min(count, count - steps))
    return lax.ppermute(value, axis, [(source, source + steps) for source in range(first, last)])


def tied(values, *others):
    held = lax.optimization_barrier((tuple(values), tuple(others)))
    return held[0]


def params(mib, **kw):
    return pltpu.CompilerParams(vmem_limit_bytes=mib * 1024 * 1024, **kw)


def fill_bias(bias_ref, segq, segk, first_block, count):
    key = lax.broadcasted_iota(jnp.int32, (2 * count, count), 0)
    query = lax.broadcasted_iota(jnp.int32, (2 * count, count), 1)
    ok = (key <= query + count) & (segk == segq) & (key >= first_block * count)
    bias_ref[...] = jnp.where(ok, 0.0, NEG).astype(F32)


def chunk_list(count, width):
    return [(i * width, count + (i + 1) * width) for i in range(count // width)]


def fwd_kernel(meta_ref, q_ref, k_ref, vt_ref, segq_ref, segk_ref, out_ref, top_ref, sum_ref, bias_ref):
    count = q_ref.shape[0]

    @pl.when(pl.program_id(0) == 0)
    def _():
        fill_bias(bias_ref, segq_ref[...], segk_ref[...], meta_ref[0], count)

    for start, keys in chunk_list(count, 256):
        cols = slice(start, start + 256)
        s = lax.dot_general(
            k_ref[:keys, :], q_ref[cols, :], (((1,), (1,)), ((), ())), preferred_element_type=F32
        )
        s = s * SCALE + bias_ref[:keys, cols]
        top = jnp.max(s, axis=0, keepdims=True)
        e = jnp.exp(s - top)
        total = jnp.sum(e, axis=0, keepdims=True)
        inv = 1.0 / total
        p = (e * inv).astype(BF)
        a = jnp.dot(vt_ref[:, :keys], p, preferred_element_type=F32)
        out_ref[cols, :] = a.T.astype(BF)
        top_ref[0, :, cols] = top
        sum_ref[0, :, cols] = inv


def attend(query, key_pair, vt, segq, segk, first):
    count, width = query.shape
    heads = width // HD
    whole = lambda shape: pl.BlockSpec(shape, lambda h, m: (0,) * len(shape))
    head = pl.BlockSpec((count, HD), lambda h, m: (0, h))
    stat = pl.BlockSpec((1, 1, count), lambda h, m: (h, 0, 0))
    return pl.pallas_call(
        fwd_kernel,
        grid_spec=pltpu.PrefetchScalarGridSpec(
            num_scalar_prefetch=1,
            grid=(heads,),
            in_specs=[
                head,
                whole((2 * count, HD)),
                whole((HD, 2 * count)),
                whole((1, count)),
                whole((2 * count, 1)),
            ],
            out_specs=[head, stat, stat],
            scratch_shapes=[pltpu.VMEM((2 * count, count), F32)],
        ),
        out_shape=[
            jax.ShapeDtypeStruct((count, width), BF),
            jax.ShapeDtypeStruct((heads, 1, count), F32),
            jax.ShapeDtypeStruct((heads, 1, count), F32),
        ],
        compiler_params=params(53),
        cost_estimate=pl.CostEstimate(
            flops=heads * 4 * 2 * 2 * count * count * HD,
            bytes_accessed=8 * 2**20,
            transcendentals=heads * 2 * count * count,
        ),
        name="attend",
    )(first, query, key_pair, vt, segq, segk)


def bwd_kernel(
    meta_ref, q_ref, g_ref, k_ref, kt_ref, v_ref, segq_ref, segk_ref, top_ref, sum_ref,
    dq_ref, dk_ref, dv_ref, bias_ref,
):
    count = q_ref.shape[0]

    @pl.when(pl.program_id(0) == 0)
    def _():
        fill_bias(bias_ref, segq_ref[...], segk_ref[...], meta_ref[0], count)
        dk_ref[...] = jnp.zeros_like(dk_ref)
        dv_ref[...] = jnp.zeros_like(dv_ref)

    for start, keys in chunk_list(count, 256):
        cols = slice(start, start + 256)
        q = q_ref[cols, :]
        g = g_ref[cols, :]
        s = lax.dot_general(
            k_ref[:keys, :], q, (((1,), (1,)), ((), ())), preferred_element_type=F32
        )
        s = s * SCALE + bias_ref[:keys, cols]
        p = jnp.exp(s - top_ref[0, :, cols]) * sum_ref[0, :, cols]
        dp = lax.dot_general(
            v_ref[:keys, :], g, (((1,), (1,)), ((), ())), preferred_element_type=F32
        )
        delta = jnp.sum(p * dp, axis=0, keepdims=True)
        ds = (p * (dp - delta)).astype(BF)
        dq = jnp.dot(kt_ref[:, :keys], ds, preferred_element_type=F32) * SCALE
        dq_ref[cols, :] = dq.T.astype(BF)
        dk_ref[:keys, :] += jnp.dot(ds, q, preferred_element_type=F32)
        dv_ref[:keys, :] += jnp.dot(p.astype(BF), g, preferred_element_type=F32)

    @pl.when(pl.program_id(0) == pl.num_programs(0) - 1)
    def _():
        dk_ref[...] = dk_ref[...] * SCALE


def attend_back(query, grad, key_pair, kt, value_pair, segq, segk, first, top, total):
    count, width = query.shape
    heads = width // HD
    whole = lambda shape: pl.BlockSpec(shape, lambda h, m: (0,) * len(shape))
    head = pl.BlockSpec((count, HD), lambda h, m: (0, h))
    stat = pl.BlockSpec((1, 1, count), lambda h, m: (h, 0, 0))
    pair = whole((2 * count, HD))
    return pl.pallas_call(
        bwd_kernel,
        grid_spec=pltpu.PrefetchScalarGridSpec(
            num_scalar_prefetch=1,
            grid=(heads,),
            in_specs=[
                head,
                head,
                pair,
                whole((HD, 2 * count)),
                pair,
                whole((1, count)),
                whole((2 * count, 1)),
                stat,
                stat,
            ],
            out_specs=[head, pair, pair],
            scratch_shapes=[pltpu.VMEM((2 * count, count), F32)],
        ),
        out_shape=[
            jax.ShapeDtypeStruct((count, width), BF),
            jax.ShapeDtypeStruct((2 * count, HD), F32),
            jax.ShapeDtypeStruct((2 * count, HD), F32),
        ],
        compiler_params=params(53),
        cost_estimate=pl.CostEstimate(
            flops=heads * 10 * 2 * 2 * count * count * HD,
            bytes_accessed=12 * 2**20,
            transcendentals=heads * 2 * count * count,
        ),
        name="attend_back",
    )(first, query, grad, key_pair, kt, value_pair, segq, segk, top, total)


def proj_kernel(n_in, held, meta_ref, *refs):
    pieces, a_ref = refs[:n_in], refs[n_in]
    out_ref = refs[n_in + 1 + held]
    step = pl.program_id(0)
    rows = out_ref.shape[2]

    for j in range(n_in):

        @pl.when(step == j)
        def _():
            value = lax.dot_general(
                pieces[j][...], a_ref[...], (((0,), (0,)), ((), ())), preferred_element_type=F32
            ).astype(BF)
            out_ref[0, 0] = value[:rows]
            out_ref[1, 0] = value[rows:]


def project(pieces, a_pair, blocks, buffer):
    tokens, width = a_pair.shape
    depth = pieces[0].shape[1]
    n_blocks = len(pieces)
    held = int(buffer is not None)
    whole = lambda shape: pl.BlockSpec(shape, lambda j, m: (0,) * len(shape))
    operands = (*pieces, a_pair) + ((buffer,) if held else ())
    return pl.pallas_call(
        functools.partial(proj_kernel, n_blocks, held),
        grid_spec=pltpu.PrefetchScalarGridSpec(
            num_scalar_prefetch=1,
            grid=(n_blocks,),
            in_specs=[whole((tokens, depth))] * len(pieces)
            + [whole((tokens, width))]
            + [pl.BlockSpec(memory_space=pl.ANY)] * held,
            out_specs=pl.BlockSpec((2, 1, depth // 2, width), lambda j, m: (0, m[j], 0, 0)),
        ),
        out_shape=jax.ShapeDtypeStruct((2, 8, depth // 2, width), BF),
        input_output_aliases={len(pieces) + 2: 0} if held else {},
        compiler_params=params(53),
        cost_estimate=pl.CostEstimate(
            flops=2 * n_blocks * tokens * depth * width,
            bytes_accessed=(2 * n_blocks + 2) * 2**20,
            transcendentals=0,
        ),
        name="project",
    )(blocks, *operands)


def grad_kernel(gplan, wplan, n_g, n_w, meta_ref, *refs):
    g_in, w_in = refs[:n_g], refs[n_g:n_g + n_w]
    own_ref, other_ref = refs[n_g + n_w:n_g + n_w + 2]
    gbuf, wbuf, total, gsems, wsems = refs[n_g + n_w + 2:]
    step = pl.program_id(0)
    half = own_ref.shape[0]
    gh, wh = gbuf.shape[1] // 2, wbuf.shape[1] // 2

    def g_copy(n):
        ref, source, block, part = gplan[n]
        return pltpu.make_async_copy(
            g_in[ref].at[pl.ds(source, gh)], gbuf.at[block, pl.ds(part * gh, gh)], gsems.at[n]
        )

    def w_copy(n):
        ref, source, block, part = wplan[n]
        place = meta_ref[8 + block]
        return pltpu.make_async_copy(
            w_in[ref].at[pl.ds(source, wh)],
            wbuf.at[place, pl.ds(part * wh, wh)],
            wsems.at[part, place],
        )

    @pl.when(step == 0)
    def _():
        for n in range(16):
            w_copy(n).start()
            g_copy(n).start()

    for j in range(8):

        @pl.when(step == j)
        def _():
            for n in range(16):
                if gplan[n][2] == j:
                    g_copy(n).wait()

    place = meta_ref[step]
    for part in range(2):
        pltpu.make_async_copy(
            w_in[0].at[pl.ds(0, wh)], wbuf.at[place, pl.ds(part * wh, wh)], wsems.at[part, place]
        ).wait()

    @pl.when(step == 0)
    def _():
        total[...] = jnp.dot(gbuf[step], wbuf[place], preferred_element_type=F32)

    @pl.when(step > 0)
    def _():
        total[...] += jnp.dot(gbuf[step], wbuf[place], preferred_element_type=F32)

    @pl.when(step == 7)
    def _():
        own_ref[...] = total[:half, :]
        other_ref[...] = total[half:, :].astype(BF)


def attn_grad_part(g_pieces, gplan, w_pieces, wplan, meta):
    tokens, depth = g_pieces[0].shape
    width = w_pieces[0].shape[1]
    half = tokens // 2
    kernel = functools.partial(grad_kernel, gplan, wplan, len(g_pieces), len(w_pieces))
    whole = pl.BlockSpec((half, width), lambda j, m: (0, 0))
    return pl.pallas_call(
        kernel,
        grid_spec=pltpu.PrefetchScalarGridSpec(
            num_scalar_prefetch=1,
            grid=(8,),
            in_specs=[pl.BlockSpec(memory_space=pl.ANY)] * (len(g_pieces) + len(w_pieces)),
            out_specs=[whole, whole],
            scratch_shapes=[
                pltpu.VMEM((8, tokens, depth), BF),
                pltpu.VMEM((8, depth, width), BF),
                pltpu.VMEM((tokens, width), F32),
                pltpu.SemaphoreType.DMA((16,)),
                pltpu.SemaphoreType.DMA((2, 8)),
            ],
        ),
        out_shape=[
            jax.ShapeDtypeStruct((half, width), F32),
            jax.ShapeDtypeStruct((half, width), BF),
        ],
        compiler_params=params(53),
        cost_estimate=pl.CostEstimate(
            flops=16 * tokens * depth * width,
            bytes_accessed=20 * 2**20,
            transcendentals=0,
        ),
        name="attn_grad",
    )(meta, *g_pieces, *w_pieces)


def add_kernel(n_terms, plan, meta_ref, buffer_ref, *refs):
    terms, outs = refs[:n_terms], refs[n_terms:n_terms + len(plan)]
    blocks, sems = refs[n_terms + len(plan):]
    copies = [
        pltpu.make_async_copy(buffer_ref.at[:, meta_ref[n]], blocks.at[n], sems.at[n])
        for n in range(blocks.shape[0])
    ]
    for copy in copies:
        copy.start()
    for copy in copies:
        copy.wait()
    for out_ref, (block, half, extra) in zip(outs, plan):
        for place, part in enumerate((0, 1) if half is None else (half,)):
            value = blocks[block, part].astype(F32)
            for term, at in extra:
                if at is None:
                    value = value + terms[term][part].astype(F32)
                elif at == part:
                    value = value + terms[term][0].astype(F32)
            out_ref[place] = value.astype(BF)


def add_blocks(buffer, blocks, terms, plan):
    _, _, rows, width = buffer.shape
    whole = lambda shape: pl.BlockSpec(shape, lambda i, m: (0,) * len(shape))
    shapes = [(2 if half is None else 1, rows, width) for _, half, _ in plan]
    return pl.pallas_call(
        functools.partial(add_kernel, len(terms), plan),
        grid_spec=pltpu.PrefetchScalarGridSpec(
            num_scalar_prefetch=1,
            grid=(1,),
            in_specs=[pl.BlockSpec(memory_space=pl.ANY)] + [whole(t.shape) for t in terms],
            out_specs=[whole(shape) for shape in shapes],
            scratch_shapes=[
                pltpu.VMEM((blocks.shape[0], 2, rows, width), BF),
                pltpu.SemaphoreType.DMA((blocks.shape[0],)),
            ],
        ),
        out_shape=[jax.ShapeDtypeStruct(shape, BF) for shape in shapes],
        compiler_params=params(53),
        cost_estimate=pl.CostEstimate(
            flops=2**21, bytes_accessed=5 * 2**20, transcendentals=0
        ),
        name="add_blocks",
    )(blocks, buffer, *terms)


def local(query_rows, key_rows, value_rows, output_grad, out_proj, segment_ids):
    count = query_rows.shape[0]
    half_d = output_grad.shape[1] // 2
    row, col = lax.axis_index("row"), lax.axis_index("col")
    z, yh, k = row // 4, row // 2 % 2, row % 2
    yl, x = col // 4, col % 4

    def gblock(dyl, dx):
        return (yl + dyl) % 2 * 4 + (x + dx) % 4

    def wblock(dz, dy):
        return (z + dz) % 4 * 2 + (yh + dy) % 2

    def ints(*values):
        return jnp.stack([jnp.asarray(v, jnp.int32) for v in values])

    g_keep = lax.dynamic_slice_in_dim(output_grad, k * half_d, half_d, 1)
    g_give = lax.dynamic_slice_in_dim(output_grad, (1 - k) * half_d, half_d, 1)
    g0 = jnp.concatenate([g_keep, move_row(g_give, dk=1)], 0)
    kv = jnp.concatenate([key_rows, value_rows], 1)
    kv_earlier = passed_along(kv, "row", 1)

    gxm = move_col(g0, dx=1)
    gxp = move_col(g0, dx=-1)
    gy = move_col(g0, dyl=1)
    wzm = move_row(out_proj, dz=1)
    wzp = move_row(out_proj, dz=-1)

    kv_pair = jnp.concatenate([kv_earlier, kv], 0)
    key_pair, value_pair = kv_pair[:, :HD], kv_pair[:, HD:]
    key_t, value_t = key_pair.T, value_pair.T
    seg_query = lax.dynamic_slice_in_dim(segment_ids, row * count, count, 0)
    seg_earlier = lax.dynamic_slice_in_dim(
        segment_ids, jnp.maximum(row - 1, 0) * count, count, 0
    )
    segk = jnp.concatenate([seg_earlier, seg_query], 0)[:, None]
    segq = seg_query[None, :]
    first = ints(row == 0)
    (query_held,) = tied((query_rows,), g0)
    attn_out, top, total = attend(query_held, key_pair, value_t, segq, segk, first)

    gxm, gxp, gy, wzm, wzp, attn_out = tied((gxm, gxp, gy, wzm, wzp, attn_out))

    h = g0.shape[0] // 2
    hw = out_proj.shape[0] // 2
    gyxm = move_col(gy, dx=1)
    gyxp = move_col(gy, dx=-1)
    a_other = move_row(attn_out, dk=1)
    wo = move_row(wzm, dz=1)
    wy = move_row(out_proj, dyh=1)

    a_pair = jnp.concatenate([attn_out, a_other], 0)
    proj = project(
        [g0, gxm, gxp, gy],
        a_pair,
        ints(gblock(0, 0), gblock(0, -1), gblock(0, 1), gblock(1, 0)),
        None,
    )

    gyxm, gyxp, wo, wy, proj = tied((gyxm, gyxp, wo, wy, proj))

    go = move_col(gxm, dx=1)
    gyo = move_col(gyxp, dx=-1)
    wyzm = move_row(wy, dz=1)
    wyzp = move_row(wy, dz=-1)
    wyo = move_row(wo, dyh=1)

    proj = project([gyxm, gyxp], a_pair, ints(gblock(1, -1), gblock(1, 1)), proj)

    go, gyo, wyzm, wyzp, wyo, proj = tied((go, gyo, wyzm, wyzp, wyo, proj))

    proj = project([go, gyo], a_pair, ints(gblock(0, 2), gblock(1, 2)), proj)

    give_up, give_dn, give_far = add_blocks(
        proj,
        ints(wblock(1, 1), wblock(-1, 1), wblock(2, 1)),
        [],
        [(0, None, ()), (1, None, ()), (2, None, ())],
    )
    rup = move_row(give_up, dz=1)
    rdn = move_row(give_dn, dz=-1)
    ry = move_row(give_far, dyh=1)

    g_pieces = [g0, gxm, gxp, gy, gyxm, gyxp, go, gyo]
    gplan = [(i, p * h, i, p) for i in range(8) for p in range(2)]
    w_pieces = [out_proj, wzm, wzp, wy, wyzm, wyzp, wyo, wo]
    wplan = [(i, p * hw, i, p) for i in range(8) for p in range(2)]
    meta = ints(
        gblock(0, 0), gblock(0, -1), gblock(0, 1), gblock(1, 0),
        gblock(1, -1), gblock(1, 1), gblock(0, 2), gblock(1, 2),
        wblock(0, 0), wblock(-1, 0), wblock(1, 0), wblock(0, 1),
        wblock(-1, 1), wblock(1, 1), wblock(2, 1), wblock(2, 0),
    )
    (meta,) = tied((meta,), give_up)
    grad_own, grad_give = attn_grad_part(g_pieces, gplan, w_pieces, wplan, meta)

    rup, rdn, ry, grad_own, grad_give = tied((rup, rdn, ry, grad_own, grad_give))

    across, far_up, far_dn = add_blocks(
        proj,
        ints(wblock(0, 1), wblock(2, 0)),
        [rup, rdn, ry],
        [(0, None, ((0, None), (1, None))), (1, 0, ((2, None),)), (1, 1, ((2, None),))],
    )
    fup = move_row(far_up, dz=1)
    fdn = move_row(far_dn, dz=-1)
    across = move_row(across, dyh=1)
    grad_got = move_row(grad_give, dk=1)
    attn_grad = (grad_own + grad_got.astype(F32)).astype(BF)

    fup, fdn, attn_grad = tied((fup, fdn, attn_grad))

    near_up, near_dn = add_blocks(
        proj,
        ints(wblock(1, 0), wblock(-1, 0)),
        [fup, fdn],
        [(0, None, ((0, 0),)), (1, None, ((1, 1),))],
    )
    nup = move_row(near_up, dz=1)
    ndn = move_row(near_dn, dz=-1)

    (attn_grad,) = tied((attn_grad,), near_up)
    query_grad, dkey, dvalue = attend_back(
        query_rows, attn_grad, key_pair, key_t, value_pair, segq, segk, first, top, total
    )
    back = passed_along(
        jnp.concatenate([dkey[:count], dvalue[:count]], 1).astype(BF), "row", -1
    ).astype(F32)
    key_grad = (dkey[count:] + back[:, :HD]).astype(BF)
    value_grad = (dvalue[count:] + back[:, HD:]).astype(BF)

    (proj_grad,) = add_blocks(
        proj, ints(wblock(0, 0)), [nup, ndn, across], [(0, None, ((0, None), (1, None), (2, None)))]
    )
    return (query_grad, key_grad, value_grad, proj_grad.reshape(2 * hw, out_proj.shape[1]))


def solution(mesh):
    placed = (
        P("row", "col"),
        P("row", "col"),
        P("row", "col"),
        P("row", "col"),
        P("row", "col"),
        P(),
    )
    return jax.shard_map(
        local,
        mesh=mesh,
        in_specs=placed,
        out_specs=(P("row", "col"), P("row", "col"), P("row", "col"), P("row", "col")),
        check_vma=False,
    )
```

```python
import functools
import math

import jax
import jax.numpy as jnp
from jax import lax
from jax.experimental import pallas as pl
from jax.experimental.pallas import tpu as pltpu
from jax.sharding import PartitionSpec as P

HD = 128
SCALE = 1.0 / math.sqrt(HD)
NEG = -1e30
BF = jnp.bfloat16
F32 = jnp.float32

ZN, YN, KN, LN, XN = 4, 2, 2, 2, 4


def move_row(value, dz=0, dyh=0, dk=0):
    pairs = []
    for z in range(ZN):
        for y in range(YN):
            for k in range(KN):
                source = (z * YN + y) * KN + k
                target = ((z + dz) % ZN * YN + (y + dyh) % YN) * KN + (k + dk) % KN
                pairs.append((source, target))
    return lax.ppermute(value, "row", pairs)


def move_col(value, dx=0, dyl=0):
    pairs = []
    for y in range(LN):
        for x in range(XN):
            pairs.append((y * XN + x, (y + dyl) % LN * XN + (x + dx) % XN))
    return lax.ppermute(value, "col", pairs)


def passed_along(value, axis, steps):
    count = lax.axis_size(axis)
    first, last = (max(0, -steps), min(count, count - steps))
    return lax.ppermute(value, axis, [(source, source + steps) for source in range(first, last)])


def tied(values, *others):
    held = lax.optimization_barrier((tuple(values), tuple(others)))
    return held[0]


def params(mib, **kw):
    return pltpu.CompilerParams(vmem_limit_bytes=mib * 1024 * 1024, **kw)


def fill_bias(bias_ref, segq, segk, first_block, count):
    key = lax.broadcasted_iota(jnp.int32, (2 * count, count), 0)
    query = lax.broadcasted_iota(jnp.int32, (2 * count, count), 1)
    ok = (key <= query + count) & (segk == segq) & (key >= first_block * count)
    bias_ref[...] = jnp.where(ok, 0.0, NEG).astype(F32)


def chunk_list(count, width):
    return [(i * width, count + (i + 1) * width) for i in range(count // width)]


def fwd_kernel(meta_ref, q_ref, k_ref, vt_ref, segq_ref, segk_ref, out_ref, top_ref, sum_ref, bias_ref):
    count = q_ref.shape[0]

    @pl.when(pl.program_id(0) == 0)
    def _():
        fill_bias(bias_ref, segq_ref[...], segk_ref[...], meta_ref[0], count)

    for start, keys in chunk_list(count, 256):
        cols = slice(start, start + 256)
        s = lax.dot_general(
            k_ref[:keys, :], q_ref[cols, :], (((1,), (1,)), ((), ())), preferred_element_type=F32
        )
        s = s * SCALE + bias_ref[:keys, cols]
        top = jnp.max(s, axis=0, keepdims=True)
        e = jnp.exp(s - top)
        total = jnp.sum(e, axis=0, keepdims=True)
        inv = 1.0 / total
        p = (e * inv).astype(BF)
        a = jnp.dot(vt_ref[:, :keys], p, preferred_element_type=F32)
        out_ref[cols, :] = a.T.astype(BF)
        top_ref[0, :, cols] = top
        sum_ref[0, :, cols] = inv


def attend(query, key_pair, vt, segq, segk, first):
    count, width = query.shape
    heads = width // HD
    whole = lambda shape: pl.BlockSpec(shape, lambda h, m: (0,) * len(shape))
    head = pl.BlockSpec((count, HD), lambda h, m: (0, h))
    stat = pl.BlockSpec((1, 1, count), lambda h, m: (h, 0, 0))
    return pl.pallas_call(
        fwd_kernel,
        grid_spec=pltpu.PrefetchScalarGridSpec(
            num_scalar_prefetch=1,
            grid=(heads,),
            in_specs=[
                head,
                whole((2 * count, HD)),
                whole((HD, 2 * count)),
                whole((1, count)),
                whole((2 * count, 1)),
            ],
            out_specs=[head, stat, stat],
            scratch_shapes=[pltpu.VMEM((2 * count, count), F32)],
        ),
        out_shape=[
            jax.ShapeDtypeStruct((count, width), BF),
            jax.ShapeDtypeStruct((heads, 1, count), F32),
            jax.ShapeDtypeStruct((heads, 1, count), F32),
        ],
        compiler_params=params(16),
        cost_estimate=pl.CostEstimate(
            flops=heads * 4 * 2 * 2 * count * count * HD,
            bytes_accessed=8 * 2**20,
            transcendentals=heads * 2 * count * count,
        ),
        name="attend",
    )(first, query, key_pair, vt, segq, segk)


def bwd_kernel(
    meta_ref, q_ref, g_ref, k_ref, kt_ref, v_ref, segq_ref, segk_ref, top_ref, sum_ref,
    dq_ref, dk_ref, dv_ref, bias_ref,
):
    count = q_ref.shape[0]

    @pl.when(pl.program_id(0) == 0)
    def _():
        fill_bias(bias_ref, segq_ref[...], segk_ref[...], meta_ref[0], count)
        dk_ref[...] = jnp.zeros_like(dk_ref)
        dv_ref[...] = jnp.zeros_like(dv_ref)

    for start, keys in chunk_list(count, 256):
        cols = slice(start, start + 256)
        q = q_ref[cols, :]
        g = g_ref[cols, :]
        s = lax.dot_general(
            k_ref[:keys, :], q, (((1,), (1,)), ((), ())), preferred_element_type=F32
        )
        s = s * SCALE + bias_ref[:keys, cols]
        p = jnp.exp(s - top_ref[0, :, cols]) * sum_ref[0, :, cols]
        dp = lax.dot_general(
            v_ref[:keys, :], g, (((1,), (1,)), ((), ())), preferred_element_type=F32
        )
        delta = jnp.sum(p * dp, axis=0, keepdims=True)
        ds = (p * (dp - delta)).astype(BF)
        dq = jnp.dot(kt_ref[:, :keys], ds, preferred_element_type=F32) * SCALE
        dq_ref[cols, :] = dq.T.astype(BF)
        dk_ref[:keys, :] += jnp.dot(ds, q, preferred_element_type=F32)
        dv_ref[:keys, :] += jnp.dot(p.astype(BF), g, preferred_element_type=F32)

    @pl.when(pl.program_id(0) == pl.num_programs(0) - 1)
    def _():
        dk_ref[...] = dk_ref[...] * SCALE


def attend_back(query, grad, key_pair, kt, value_pair, segq, segk, first, top, total):
    count, width = query.shape
    heads = width // HD
    whole = lambda shape: pl.BlockSpec(shape, lambda h, m: (0,) * len(shape))
    head = pl.BlockSpec((count, HD), lambda h, m: (0, h))
    stat = pl.BlockSpec((1, 1, count), lambda h, m: (h, 0, 0))
    pair = whole((2 * count, HD))
    return pl.pallas_call(
        bwd_kernel,
        grid_spec=pltpu.PrefetchScalarGridSpec(
            num_scalar_prefetch=1,
            grid=(heads,),
            in_specs=[
                head,
                head,
                pair,
                whole((HD, 2 * count)),
                pair,
                whole((1, count)),
                whole((2 * count, 1)),
                stat,
                stat,
            ],
            out_specs=[head, pair, pair],
            scratch_shapes=[pltpu.VMEM((2 * count, count), F32)],
        ),
        out_shape=[
            jax.ShapeDtypeStruct((count, width), BF),
            jax.ShapeDtypeStruct((2 * count, HD), F32),
            jax.ShapeDtypeStruct((2 * count, HD), F32),
        ],
        compiler_params=params(22),
        cost_estimate=pl.CostEstimate(
            flops=heads * 10 * 2 * 2 * count * count * HD,
            bytes_accessed=12 * 2**20,
            transcendentals=heads * 2 * count * count,
        ),
        name="attend_back",
    )(first, query, grad, key_pair, kt, value_pair, segq, segk, top, total)


def proj_kernel(n_in, held, meta_ref, *refs):
    pieces, a_ref = refs[:n_in], refs[n_in]
    refs = refs[n_in + 1 + held:]
    buffer_ref, taken = refs[0], refs[1:-3]
    done, sems, take_sems = refs[-3:]
    step = pl.program_id(0)
    rows = done.shape[2]

    def put(j):
        return pltpu.make_async_copy(done.at[j], buffer_ref.at[:, meta_ref[j]], sems.at[j])

    for j in range(n_in):

        @pl.when(step == j)
        def _():
            value = lax.dot_general(
                pieces[j][...], a_ref[...], (((0,), (0,)), ((), ())), preferred_element_type=F32
            ).astype(BF)
            done[j, 0] = value[:rows]
            done[j, 1] = value[rows:]
            put(j).start()

    @pl.when(step == n_in - 1)
    def _():
        for j in range(n_in):
            put(j).wait()
        takes = [
            pltpu.make_async_copy(buffer_ref.at[:, meta_ref[n_in + i]], ref, take_sems.at[i])
            for i, ref in enumerate(taken)
        ]
        for take in takes:
            take.start()
        for take in takes:
            take.wait()


def project(pieces, a_pair, blocks, buffer, n_taken=0):
    tokens, width = a_pair.shape
    depth = pieces[0].shape[1]
    n_blocks = len(pieces)
    held = int(buffer is not None)
    here = pl.BlockSpec(memory_space=pltpu.VMEM)
    there = pl.BlockSpec(memory_space=pltpu.HBM)
    operands = (*pieces, a_pair) + ((buffer,) if held else ())
    shape = (2, depth // 2, width)
    out = pl.pallas_call(
        functools.partial(proj_kernel, n_blocks, held),
        grid_spec=pltpu.PrefetchScalarGridSpec(
            num_scalar_prefetch=1,
            grid=(n_blocks,),
            in_specs=[here] * (n_blocks + 1) + [there] * held,
            out_specs=[there] + [here] * n_taken,
            scratch_shapes=[
                pltpu.VMEM((n_blocks, *shape), BF),
                pltpu.SemaphoreType.DMA((n_blocks,)),
                pltpu.SemaphoreType.DMA((max(n_taken, 1),)),
            ],
        ),
        out_shape=[jax.ShapeDtypeStruct((2, 8, depth // 2, width), BF)]
        + [jax.ShapeDtypeStruct(shape, BF)] * n_taken,
        input_output_aliases={n_blocks + 2: 0} if held else {},
        compiler_params=params(16),
        cost_estimate=pl.CostEstimate(
            flops=2 * n_blocks * tokens * depth * width,
            bytes_accessed=(2 * n_blocks + 2) * 2**20,
            transcendentals=0,
        ),
        name="project",
    )(blocks, *operands)
    return out if n_taken else out[0]


def grad_kernel(gplan, wplan, n_g, n_w, meta_ref, *refs):
    g_in, w_in = refs[:n_g], refs[n_g:n_g + n_w]
    own_ref, other_ref = refs[n_g + n_w:n_g + n_w + 2]
    gbuf, wbuf, total, gsems, wsems = refs[n_g + n_w + 2:]
    step = pl.program_id(0)
    half = own_ref.shape[0]
    gh, wh = gbuf.shape[1] // 2, wbuf.shape[1] // 2

    def g_copy(n):
        ref, source, block, part = gplan[n]
        return pltpu.make_async_copy(
            g_in[ref].at[pl.ds(source, gh)], gbuf.at[block, pl.ds(part * gh, gh)], gsems.at[n]
        )

    def w_copy(n):
        ref, source, block, part = wplan[n]
        place = meta_ref[8 + block]
        return pltpu.make_async_copy(
            w_in[ref].at[pl.ds(source, wh)],
            wbuf.at[place, pl.ds(part * wh, wh)],
            wsems.at[part, place],
        )

    @pl.when(step == 0)
    def _():
        for n in range(16):
            w_copy(n).start()
            g_copy(n).start()

    for j in range(8):

        @pl.when(step == j)
        def _():
            for n in range(16):
                if gplan[n][2] == j:
                    g_copy(n).wait()

    place = meta_ref[step]
    for part in range(2):
        pltpu.make_async_copy(
            w_in[0].at[pl.ds(0, wh)], wbuf.at[place, pl.ds(part * wh, wh)], wsems.at[part, place]
        ).wait()

    @pl.when(step == 0)
    def _():
        total[...] = jnp.dot(gbuf[step], wbuf[place], preferred_element_type=F32)

    @pl.when(step > 0)
    def _():
        total[...] += jnp.dot(gbuf[step], wbuf[place], preferred_element_type=F32)

    @pl.when(step == 7)
    def _():
        own_ref[...] = total[:half, :]
        other_ref[...] = total[half:, :].astype(BF)


def attn_grad_part(g_pieces, gplan, w_pieces, wplan, meta):
    tokens, depth = g_pieces[0].shape
    width = w_pieces[0].shape[1]
    half = tokens // 2
    kernel = functools.partial(grad_kernel, gplan, wplan, len(g_pieces), len(w_pieces))
    whole = pl.BlockSpec((half, width), lambda j, m: (0, 0))
    return pl.pallas_call(
        kernel,
        grid_spec=pltpu.PrefetchScalarGridSpec(
            num_scalar_prefetch=1,
            grid=(8,),
            in_specs=[pl.BlockSpec(memory_space=pltpu.HBM)] * (len(g_pieces) + len(w_pieces)),
            out_specs=[whole, whole],
            scratch_shapes=[
                pltpu.VMEM((8, tokens, depth), BF),
                pltpu.VMEM((8, depth, width), BF),
                pltpu.VMEM((tokens, width), F32),
                pltpu.SemaphoreType.DMA((16,)),
                pltpu.SemaphoreType.DMA((2, 8)),
            ],
        ),
        out_shape=[
            jax.ShapeDtypeStruct((half, width), F32),
            jax.ShapeDtypeStruct((half, width), BF),
        ],
        compiler_params=params(34),
        cost_estimate=pl.CostEstimate(
            flops=16 * tokens * depth * width,
            bytes_accessed=20 * 2**20,
            transcendentals=0,
        ),
        name="attn_grad",
    )(meta, *g_pieces, *w_pieces)


def add_kernel(n_terms, plan, meta_ref, buffer_ref, *refs):
    terms, outs = refs[:n_terms], refs[n_terms:n_terms + len(plan)]
    blocks, sems = refs[n_terms + len(plan):]
    copies = [
        pltpu.make_async_copy(buffer_ref.at[:, meta_ref[n]], blocks.at[n], sems.at[n])
        for n in range(blocks.shape[0])
    ]
    for copy in copies:
        copy.start()
    for copy in copies:
        copy.wait()
    for out_ref, (block, half, extra) in zip(outs, plan):
        for place, part in enumerate((0, 1) if half is None else (half,)):
            value = blocks[block, part].astype(F32)
            for term, at in extra:
                if at is None:
                    value = value + terms[term][part].astype(F32)
                elif at == part:
                    value = value + terms[term][0].astype(F32)
            out_ref[place] = value.astype(BF)


def add_blocks(buffer, blocks, terms, plan):
    _, _, rows, width = buffer.shape
    here = pl.BlockSpec(memory_space=pltpu.VMEM)
    shapes = [(2 if half is None else 1, rows, width) for _, half, _ in plan]
    return pl.pallas_call(
        functools.partial(add_kernel, len(terms), plan),
        grid_spec=pltpu.PrefetchScalarGridSpec(
            num_scalar_prefetch=1,
            grid=(1,),
            in_specs=[pl.BlockSpec(memory_space=pltpu.HBM)] + [here] * len(terms),
            out_specs=[here] * len(plan),
            scratch_shapes=[
                pltpu.VMEM((blocks.shape[0], 2, rows, width), BF),
                pltpu.SemaphoreType.DMA((blocks.shape[0],)),
            ],
        ),
        out_shape=[jax.ShapeDtypeStruct(shape, BF) for shape in shapes],
        compiler_params=params(12),
        cost_estimate=pl.CostEstimate(
            flops=2**21, bytes_accessed=5 * 2**20, transcendentals=0
        ),
        name="add_blocks",
    )(blocks, buffer, *terms)


def local(query_rows, key_rows, value_rows, output_grad, out_proj, segment_ids):
    count = query_rows.shape[0]
    half_d = output_grad.shape[1] // 2
    row, col = lax.axis_index("row"), lax.axis_index("col")
    z, yh, k = row // 4, row // 2 % 2, row % 2
    yl, x = col // 4, col % 4

    def gblock(dyl, dx):
        return (yl + dyl) % 2 * 4 + (x + dx) % 4

    def wblock(dz, dy):
        return (z + dz) % 4 * 2 + (yh + dy) % 2

    def ints(*values):
        return jnp.stack([jnp.asarray(v, jnp.int32) for v in values])

    g_keep = lax.dynamic_slice_in_dim(output_grad, k * half_d, half_d, 1)
    g_give = lax.dynamic_slice_in_dim(output_grad, (1 - k) * half_d, half_d, 1)
    g0 = jnp.concatenate([g_keep, move_row(g_give, dk=1)], 0)
    kv = jnp.concatenate([key_rows, value_rows], 1)
    (kv,) = tied((kv,), g0)
    kv_earlier = passed_along(kv, "row", 1)

    gxm = move_col(g0, dx=1)
    gxp = move_col(g0, dx=-1)
    gy = move_col(g0, dyl=1)
    wzm = move_row(out_proj, dz=1)
    wzp = move_row(out_proj, dz=-1)

    kv_pair = jnp.concatenate([kv_earlier, kv], 0)
    key_pair, value_pair = kv_pair[:, :HD], kv_pair[:, HD:]
    key_t, value_t = key_pair.T, value_pair.T
    seg_query = lax.dynamic_slice_in_dim(segment_ids, row * count, count, 0)
    seg_earlier = lax.dynamic_slice_in_dim(
        segment_ids, jnp.maximum(row - 1, 0) * count, count, 0
    )
    segk = jnp.concatenate([seg_earlier, seg_query], 0)[:, None]
    segq = seg_query[None, :]
    first = ints(row == 0)
    (query_held,) = tied((query_rows,), g0)
    attn_out, top, total = attend(query_held, key_pair, value_t, segq, segk, first)

    gxm, gxp, gy, wzm, wzp, attn_out = tied((gxm, gxp, gy, wzm, wzp, attn_out))

    h = g0.shape[0] // 2
    hw = out_proj.shape[0] // 2
    gyxm = move_col(gy, dx=1)
    gyxp = move_col(gy, dx=-1)
    a_other = move_row(attn_out, dk=1)
    wo = move_row(wzm, dz=1)
    wy = move_row(out_proj, dyh=1)

    a_pair = jnp.concatenate([attn_out, a_other], 0)
    proj = project(
        [g0, gxm, gxp, gy],
        a_pair,
        ints(gblock(0, 0), gblock(0, -1), gblock(0, 1), gblock(1, 0)),
        None,
    )

    gyxm, gyxp, wo, wy, proj = tied((gyxm, gyxp, wo, wy, proj))

    go = move_col(gxm, dx=1)
    gyo = move_col(gyxp, dx=-1)
    wyzm = move_row(wy, dz=1)
    wyzp = move_row(wy, dz=-1)
    wyo = move_row(wo, dyh=1)

    proj = project([gyxm, gyxp], a_pair, ints(gblock(1, -1), gblock(1, 1)), proj)

    go, gyo, wyzm, wyzp, wyo, proj = tied((go, gyo, wyzm, wyzp, wyo, proj))

    proj, give_up, give_dn, give_far = project(
        [go, gyo],
        a_pair,
        ints(gblock(0, 2), gblock(1, 2), wblock(1, 1), wblock(-1, 1), wblock(2, 1)),
        proj,
        3,
    )
    rup = move_row(give_up, dz=1)
    rdn = move_row(give_dn, dz=-1)
    ry = move_row(give_far, dyh=1)

    g_pieces = [g0, gxm, gxp, gy, gyxm, gyxp, go, gyo]
    gplan = [(i, p * h, i, p) for i in range(8) for p in range(2)]
    w_pieces = [out_proj, wzm, wzp, wy, wyzm, wyzp, wyo, wo]
    wplan = [(i, p * hw, i, p) for i in range(8) for p in range(2)]
    meta = ints(
        gblock(0, 0), gblock(0, -1), gblock(0, 1), gblock(1, 0),
        gblock(1, -1), gblock(1, 1), gblock(0, 2), gblock(1, 2),
        wblock(0, 0), wblock(-1, 0), wblock(1, 0), wblock(0, 1),
        wblock(-1, 1), wblock(1, 1), wblock(2, 1), wblock(2, 0),
    )
    (meta,) = tied((meta,), give_up)
    grad_own, grad_give = attn_grad_part(g_pieces, gplan, w_pieces, wplan, meta)

    rup, rdn, ry, grad_own, grad_give = tied((rup, rdn, ry, grad_own, grad_give))

    across, far_up, far_dn = add_blocks(
        proj,
        ints(wblock(0, 1), wblock(2, 0)),
        [rup, rdn, ry],
        [(0, None, ((0, None), (1, None))), (1, 0, ((2, None),)), (1, 1, ((2, None),))],
    )
    fup = move_row(far_up, dz=1)
    fdn = move_row(far_dn, dz=-1)
    across = move_row(across, dyh=1)
    grad_got = move_row(grad_give, dk=1)
    attn_grad = (grad_own + grad_got.astype(F32)).astype(BF)

    fup, fdn, attn_grad = tied((fup, fdn, attn_grad))

    near_up, near_dn = add_blocks(
        proj,
        ints(wblock(1, 0), wblock(-1, 0)),
        [fup, fdn],
        [(0, None, ((0, 0),)), (1, None, ((1, 1),))],
    )
    nup = move_row(near_up, dz=1)
    ndn = move_row(near_dn, dz=-1)

    (attn_grad,) = tied((attn_grad,), near_up)
    query_grad, dkey, dvalue = attend_back(
        query_rows, attn_grad, key_pair, key_t, value_pair, segq, segk, first, top, total
    )
    back = passed_along(
        jnp.concatenate([dkey[:count], dvalue[:count]], 1).astype(BF), "row", -1
    ).astype(F32)
    key_grad = (dkey[count:] + back[:, :HD]).astype(BF)
    value_grad = (dvalue[count:] + back[:, HD:]).astype(BF)

    (proj_grad,) = add_blocks(
        proj, ints(wblock(0, 0)), [nup, ndn, across], [(0, None, ((0, None), (1, None), (2, None)))]
    )
    return (query_grad, key_grad, value_grad, proj_grad.reshape(2 * hw, out_proj.shape[1]))


def solution(mesh):
    placed = (
        P("row", "col"),
        P("row", "col"),
        P("row", "col"),
        P("row", "col"),
        P("row", "col"),
        P(),
    )
    return jax.shard_map(
        local,
        mesh=mesh,
        in_specs=placed,
        out_specs=(P("row", "col"), P("row", "col"), P("row", "col"), P("row", "col")),
        check_vma=False,
    )
```

```python
import functools
import math

import jax
import jax.numpy as jnp
from jax import lax
from jax.experimental import pallas as pl
from jax.experimental.pallas import tpu as pltpu
from jax.sharding import PartitionSpec as P

HD = 128
SCALE = 1.0 / math.sqrt(HD)
NEG = -1e30
BF = jnp.bfloat16
F32 = jnp.float32

PLACES = 64

ZN, YN, KN, LN, XN = 4, 2, 2, 2, 4


def move_row(value, dz=0, dyh=0, dk=0):
    pairs = []
    for z in range(ZN):
        for y in range(YN):
            for k in range(KN):
                source = (z * YN + y) * KN + k
                target = ((z + dz) % ZN * YN + (y + dyh) % YN) * KN + (k + dk) % KN
                pairs.append((source, target))
    return lax.ppermute(value, "row", pairs)


def move_col(value, dx=0, dyl=0):
    pairs = []
    for y in range(LN):
        for x in range(XN):
            pairs.append((y * XN + x, (y + dyl) % LN * XN + (x + dx) % XN))
    return lax.ppermute(value, "col", pairs)


def passed_along(value, axis, steps):
    count = lax.axis_size(axis)
    first, last = (max(0, -steps), min(count, count - steps))
    return lax.ppermute(value, axis, [(source, source + steps) for source in range(first, last)])


def tied(values, *others):
    held = lax.optimization_barrier((tuple(values), tuple(others)))
    return held[0]


def params(mib, **kw):
    return pltpu.CompilerParams(vmem_limit_bytes=mib * 1024 * 1024, **kw)


def fill_bias(bias_ref, segq, segk, first_block, count):
    key = lax.broadcasted_iota(jnp.int32, (2 * count, count), 0)
    query = lax.broadcasted_iota(jnp.int32, (2 * count, count), 1)
    ok = (key <= query + count) & (segk == segq) & (key >= first_block * count)
    bias_ref[...] = jnp.where(ok, 0.0, NEG).astype(F32)


def chunk_list(count, width):
    return [(i * width, count + (i + 1) * width) for i in range(count // width)]


def fwd_kernel(meta_ref, q_ref, k_ref, vt_ref, segq_ref, segk_ref, out_ref, top_ref, sum_ref, bias_ref):
    count = q_ref.shape[0]

    @pl.when(pl.program_id(0) == 0)
    def _():
        fill_bias(bias_ref, segq_ref[...], segk_ref[...], meta_ref[0], count)

    for start, keys in chunk_list(count, 256):
        cols = slice(start, start + 256)
        s = lax.dot_general(
            k_ref[:keys, :], q_ref[cols, :], (((1,), (1,)), ((), ())), preferred_element_type=F32
        )
        s = s * SCALE + bias_ref[:keys, cols]
        top = jnp.max(s, axis=0, keepdims=True)
        e = jnp.exp(s - top)
        total = jnp.sum(e, axis=0, keepdims=True)
        inv = 1.0 / total
        p = (e * inv).astype(BF)
        a = jnp.dot(vt_ref[:, :keys], p, preferred_element_type=F32)
        out_ref[cols, :] = a.T.astype(BF)
        top_ref[0, :, cols] = top
        sum_ref[0, :, cols] = inv


def attend(query, key_pair, vt, segq, segk, first):
    count, width = query.shape
    heads = width // HD
    whole = lambda shape: pl.BlockSpec(shape, lambda h, m: (0,) * len(shape))
    head = pl.BlockSpec((count, HD), lambda h, m: (0, h))
    stat = pl.BlockSpec((1, 1, count), lambda h, m: (h, 0, 0))
    return pl.pallas_call(
        fwd_kernel,
        grid_spec=pltpu.PrefetchScalarGridSpec(
            num_scalar_prefetch=1,
            grid=(heads,),
            in_specs=[
                head,
                whole((2 * count, HD)),
                whole((HD, 2 * count)),
                whole((1, count)),
                whole((2 * count, 1)),
            ],
            out_specs=[head, stat, stat],
            scratch_shapes=[pltpu.VMEM((2 * count, count), F32)],
        ),
        out_shape=[
            jax.ShapeDtypeStruct((count, width), BF),
            jax.ShapeDtypeStruct((heads, 1, count), F32),
            jax.ShapeDtypeStruct((heads, 1, count), F32),
        ],
        compiler_params=params(16),
        cost_estimate=pl.CostEstimate(
            flops=heads * 4 * 2 * 2 * count * count * HD,
            bytes_accessed=8 * 2**20,
            transcendentals=heads * 2 * count * count,
        ),
        name="attend",
    )(first, query, key_pair, vt, segq, segk)


def bwd_kernel(
    n_held, last, meta_ref, q_ref, g_ref, k_ref, kt_ref, v_ref, segq_ref, segk_ref, top_ref, sum_ref,
    *refs,
):
    dk_in, dv_in = refs[:2] if n_held else (None, None)
    dq_ref, dk_ref, dv_ref, bias_ref = refs[n_held:]
    count = q_ref.shape[0]

    @pl.when(pl.program_id(0) == 0)
    def _():
        fill_bias(bias_ref, segq_ref[...], segk_ref[...], meta_ref[0], count)
        if n_held:
            dk_ref[...] = dk_in[...]
            dv_ref[...] = dv_in[...]
        else:
            dk_ref[...] = jnp.zeros_like(dk_ref)
            dv_ref[...] = jnp.zeros_like(dv_ref)

    for start, keys in chunk_list(count, 256):
        cols = slice(start, start + 256)
        q = q_ref[cols, :]
        g = g_ref[cols, :]
        s = lax.dot_general(
            k_ref[:keys, :], q, (((1,), (1,)), ((), ())), preferred_element_type=F32
        )
        s = s * SCALE + bias_ref[:keys, cols]
        p = jnp.exp(s - top_ref[0, :, cols]) * sum_ref[0, :, cols]
        dp = lax.dot_general(
            v_ref[:keys, :], g, (((1,), (1,)), ((), ())), preferred_element_type=F32
        )
        delta = jnp.sum(p * dp, axis=0, keepdims=True)
        ds = (p * (dp - delta)).astype(BF)
        dq = jnp.dot(kt_ref[:, :keys], ds, preferred_element_type=F32) * SCALE
        dq_ref[cols, :] = dq.T.astype(BF)
        dk_ref[:keys, :] += jnp.dot(ds, q, preferred_element_type=F32)
        dv_ref[:keys, :] += jnp.dot(p.astype(BF), g, preferred_element_type=F32)

    if last:

        @pl.when(pl.program_id(0) == pl.num_programs(0) - 1)
        def _():
            dk_ref[...] = dk_ref[...] * SCALE


def attend_back(query, grad, key_pair, kt, value_pair, segq, segk, first, top, total, heads, held):
    count, width = query.shape
    begin, end = heads
    last = end == width // HD
    whole = lambda shape: pl.BlockSpec(shape, lambda h, m: (0,) * len(shape))
    head = pl.BlockSpec((count, HD), lambda h, m: (0, h + begin))
    stat = pl.BlockSpec((1, 1, count), lambda h, m: (h + begin, 0, 0))
    pair = whole((2 * count, HD))
    earlier = () if held is None else (held[1], held[2], held[0])
    return pl.pallas_call(
        functools.partial(bwd_kernel, len(earlier), last),
        grid_spec=pltpu.PrefetchScalarGridSpec(
            num_scalar_prefetch=1,
            grid=(end - begin,),
            in_specs=[
                head,
                head,
                pair,
                whole((HD, 2 * count)),
                pair,
                whole((1, count)),
                whole((2 * count, 1)),
                stat,
                stat,
            ]
            + ([pair, pair, pl.BlockSpec(memory_space=pl.ANY)] if earlier else []),
            out_specs=[head, pair, pair],
            scratch_shapes=[pltpu.VMEM((2 * count, count), F32)],
        ),
        out_shape=[
            jax.ShapeDtypeStruct((count, width), BF),
            jax.ShapeDtypeStruct((2 * count, HD), F32),
            jax.ShapeDtypeStruct((2 * count, HD), F32),
        ],
        input_output_aliases={12: 0} if earlier else {},
        compiler_params=params(22),
        cost_estimate=pl.CostEstimate(
            flops=(end - begin) * 10 * 2 * 2 * count * count * HD,
            bytes_accessed=6 * 2**20,
            transcendentals=(end - begin) * 2 * count * count,
        ),
        name="attend_back",
    )(first, query, grad, key_pair, kt, value_pair, segq, segk, top, total, *earlier)


def proj_kernel(n_in, held, plan, meta_ref, *refs):
    pieces, a_ref = refs[:n_in], refs[n_in]
    refs = refs[n_in + 1 + held:]
    buffer_ref, taken = refs[0], refs[1:-3]
    done, sems, take_sems = refs[-3:]
    step = pl.program_id(0)
    rows = done.shape[2]

    def put(j):
        return pltpu.make_async_copy(done.at[j], buffer_ref.at[:, meta_ref[j]], sems.at[j])

    for j in range(n_in):

        @pl.when(step == j)
        def _():
            value = lax.dot_general(
                pieces[j][...], a_ref[...], (((0,), (0,)), ((), ())), preferred_element_type=F32
            ).astype(BF)
            done[j, 0] = value[:rows]
            done[j, 1] = value[rows:]
            put(j).start()

    @pl.when(step == n_in - 1)
    def _():
        for j in range(n_in):
            put(j).wait()
        takes = []
        for i, (out, start, at, half, first, count) in enumerate(plan):
            source = buffer_ref.at[half, meta_ref[n_in + at], pl.ds(first, count)]
            target = taken[out].at[pl.ds(start, count)]
            takes.append(pltpu.make_async_copy(source, target, take_sems.at[i]))
        for take in takes:
            take.start()
        for take in takes:
            take.wait()


def project(pieces, a_pair, blocks, buffer, plan=()):
    tokens, width = a_pair.shape
    depth = pieces[0].shape[1]
    n_blocks = len(pieces)
    held = int(buffer is not None)
    here = pl.BlockSpec(memory_space=pltpu.VMEM)
    there = pl.BlockSpec(memory_space=pltpu.HBM)
    operands = (*pieces, a_pair) + ((buffer,) if held else ())
    shape = (2, depth // 2, width)
    n_taken = 1 + max((entry[0] for entry in plan), default=-1)
    taken = [(sum(e[5] for e in plan if e[0] == i), width) for i in range(n_taken)]
    out = pl.pallas_call(
        functools.partial(proj_kernel, n_blocks, held, plan),
        grid_spec=pltpu.PrefetchScalarGridSpec(
            num_scalar_prefetch=1,
            grid=(n_blocks,),
            in_specs=[here] * (n_blocks + 1) + [there] * held,
            out_specs=[there] + [here] * n_taken,
            scratch_shapes=[
                pltpu.VMEM((n_blocks, *shape), BF),
                pltpu.SemaphoreType.DMA((n_blocks,)),
                pltpu.SemaphoreType.DMA((max(len(plan), 1),)),
            ],
        ),
        out_shape=[jax.ShapeDtypeStruct((2, PLACES, depth // 2, width), BF)]
        + [jax.ShapeDtypeStruct(t, BF) for t in taken],
        input_output_aliases={n_blocks + 2: 0} if held else {},
        compiler_params=params(16),
        cost_estimate=pl.CostEstimate(
            flops=2 * n_blocks * tokens * depth * width,
            bytes_accessed=(2 * n_blocks + 2) * 2**20,
            transcendentals=0,
        ),
        name="project",
    )(blocks, *operands)
    return out if n_taken else out[0]


def grad_kernel(gplan, wplan, n_g, n_w, meta_ref, *refs):
    g_in, w_in = refs[:n_g], refs[n_g:n_g + n_w]
    own_ref, other_ref = refs[n_g + n_w:n_g + n_w + 2]
    gbuf, wbuf, total, gsems, wsems = refs[n_g + n_w + 2:]
    step = pl.program_id(0)
    half = own_ref.shape[0]
    gh, wh = gbuf.shape[1] // 2, wbuf.shape[1] // 2

    def g_copy(n):
        ref, source, block, part = gplan[n]
        return pltpu.make_async_copy(
            g_in[ref].at[pl.ds(source, gh)], gbuf.at[block, pl.ds(part * gh, gh)], gsems.at[n]
        )

    def w_copy(n):
        ref, source, block, part = wplan[n]
        place = meta_ref[8 + block]
        return pltpu.make_async_copy(
            w_in[ref].at[pl.ds(source, wh)],
            wbuf.at[place, pl.ds(part * wh, wh)],
            wsems.at[part, place],
        )

    @pl.when(step == 0)
    def _():
        for n in range(16):
            w_copy(n).start()
            g_copy(n).start()

    for j in range(8):

        @pl.when(step == j)
        def _():
            for n in range(16):
                if gplan[n][2] == j:
                    g_copy(n).wait()

    place = meta_ref[step]
    for part in range(2):
        pltpu.make_async_copy(
            w_in[0].at[pl.ds(0, wh)], wbuf.at[place, pl.ds(part * wh, wh)], wsems.at[part, place]
        ).wait()

    @pl.when(step == 0)
    def _():
        total[...] = jnp.dot(gbuf[step], wbuf[place], preferred_element_type=F32)

    @pl.when(step > 0)
    def _():
        total[...] += jnp.dot(gbuf[step], wbuf[place], preferred_element_type=F32)

    @pl.when(step == 7)
    def _():
        own_ref[...] = total[:half, :]
        other_ref[...] = total[half:, :].astype(BF)


def attn_grad_part(g_pieces, gplan, w_pieces, wplan, meta):
    tokens, depth = g_pieces[0].shape
    width = w_pieces[0].shape[1]
    half = tokens // 2
    kernel = functools.partial(grad_kernel, gplan, wplan, len(g_pieces), len(w_pieces))
    whole = pl.BlockSpec((half, width), lambda j, m: (0, 0))
    return pl.pallas_call(
        kernel,
        grid_spec=pltpu.PrefetchScalarGridSpec(
            num_scalar_prefetch=1,
            grid=(8,),
            in_specs=[pl.BlockSpec(memory_space=pltpu.HBM)] * (len(g_pieces) + len(w_pieces)),
            out_specs=[whole, whole],
            scratch_shapes=[
                pltpu.VMEM((8, tokens, depth), BF),
                pltpu.VMEM((8, depth, width), BF),
                pltpu.VMEM((tokens, width), F32),
                pltpu.SemaphoreType.DMA((16,)),
                pltpu.SemaphoreType.DMA((2, 8)),
            ],
        ),
        out_shape=[
            jax.ShapeDtypeStruct((half, width), F32),
            jax.ShapeDtypeStruct((half, width), BF),
        ],
        compiler_params=params(34),
        cost_estimate=pl.CostEstimate(
            flops=16 * tokens * depth * width,
            bytes_accessed=20 * 2**20,
            transcendentals=0,
        ),
        name="attn_grad",
    )(meta, *g_pieces, *w_pieces)


def add_kernel(n_terms, plan, joined, meta_ref, buffer_ref, *refs):
    terms, outs = refs[:n_terms], refs[n_terms:-2]
    blocks, sems = refs[-2:]
    rows = blocks.shape[2]
    copies = [
        pltpu.make_async_copy(buffer_ref.at[:, meta_ref[n]], blocks.at[n], sems.at[n])
        for n in range(blocks.shape[0])
    ]
    for copy in copies:
        copy.start()
    for copy in copies:
        copy.wait()
    for n, (block, half, extra) in enumerate(plan):
        value = blocks[block, half].astype(F32)
        for term, first in extra:
            value = value + terms[term][first:first + rows, :].astype(F32)
        if joined:
            outs[0][n * rows:(n + 1) * rows, :] = value.astype(BF)
        else:
            outs[n][...] = value.astype(BF)


def add_blocks(buffer, blocks, terms, plan, joined=False):
    _, _, rows, width = buffer.shape
    here = pl.BlockSpec(memory_space=pltpu.VMEM)
    shapes = [(len(plan) * rows, width)] if joined else [(rows, width)] * len(plan)
    return pl.pallas_call(
        functools.partial(add_kernel, len(terms), plan, joined),
        grid_spec=pltpu.PrefetchScalarGridSpec(
            num_scalar_prefetch=1,
            grid=(1,),
            in_specs=[pl.BlockSpec(memory_space=pltpu.HBM)] + [here] * len(terms),
            out_specs=[here] * len(shapes),
            scratch_shapes=[
                pltpu.VMEM((blocks.shape[0], 2, rows, width), BF),
                pltpu.SemaphoreType.DMA((blocks.shape[0],)),
            ],
        ),
        out_shape=[jax.ShapeDtypeStruct(shape, BF) for shape in shapes],
        compiler_params=params(12),
        cost_estimate=pl.CostEstimate(
            flops=2**21, bytes_accessed=5 * 2**20, transcendentals=0
        ),
        name="add_blocks",
    )(blocks, buffer, *terms)


def last_kernel(meta_ref, buffer_ref, across, nup, ndn, rup, up2, rdn, dn2, out_ref, block, sem):
    copy = pltpu.make_async_copy(buffer_ref.at[:, meta_ref[0]], block, sem)
    copy.start()
    copy.wait()
    half, quarter = nup.shape[0], up2.shape[0]
    for part in range(2):
        for n in range(2):
            rows = slice(n * quarter, (n + 1) * quarter)
            place = slice(part * half + n * quarter, part * half + (n + 1) * quarter)
            up, dn = nup[rows, :], ndn[rows, :]
            if part == 1:
                up = up2[...] if n else rup[2 * half:, :]
            else:
                dn = dn2[...] if n else rdn[2 * half:, :]
            out_ref[place, :] = (
                block[part, rows].astype(F32)
                + across[place, :].astype(F32)
                + up.astype(F32)
                + dn.astype(F32)
            ).astype(BF)


def last_sum(buffer, place, *terms):
    _, _, rows, width = buffer.shape
    here = pl.BlockSpec(memory_space=pltpu.VMEM)
    return pl.pallas_call(
        last_kernel,
        grid_spec=pltpu.PrefetchScalarGridSpec(
            num_scalar_prefetch=1,
            grid=(1,),
            in_specs=[pl.BlockSpec(memory_space=pltpu.HBM)] + [here] * len(terms),
            out_specs=pl.BlockSpec((2 * rows, width), lambda i, m: (0, 0)),
            scratch_shapes=[pltpu.VMEM((2, rows, width), BF), pltpu.SemaphoreType.DMA],
        ),
        out_shape=jax.ShapeDtypeStruct((2 * rows, width), BF),
        compiler_params=params(12),
        cost_estimate=pl.CostEstimate(
            flops=2**21, bytes_accessed=5 * 2**20, transcendentals=0
        ),
        name="last_sum",
    )(place, buffer, *terms)


def local(query_rows, key_rows, value_rows, output_grad, out_proj, segment_ids):
    count = query_rows.shape[0]
    half_d = output_grad.shape[1] // 2
    row, col = lax.axis_index("row"), lax.axis_index("col")
    z, yh, k = row // 4, row // 2 % 2, row % 2
    yl, x = col // 4, col % 4

    def gblock(dyl, dx):
        return (yl + dyl) % 2 * 4 + (x + dx) % 4

    def wblock(dz, dy):
        return (z + dz) % 4 * 2 + (yh + dy) % 2

    def ints(*values):
        return jnp.stack([jnp.asarray(v, jnp.int32) for v in values])

    g_keep = lax.dynamic_slice_in_dim(output_grad, k * half_d, half_d, 1)
    g_give = lax.dynamic_slice_in_dim(output_grad, (1 - k) * half_d, half_d, 1)
    g0 = jnp.concatenate([g_keep, move_row(g_give, dk=1)], 0)
    kv = jnp.concatenate([key_rows, value_rows], 1)
    kv_earlier = passed_along(kv, "row", 1)

    gxm = move_col(g0, dx=1)
    gxp = move_col(g0, dx=-1)
    gy = move_col(g0, dyl=1)
    wzm = move_row(out_proj, dz=1)
    wzp = move_row(out_proj, dz=-1)

    kv_pair = jnp.concatenate([kv_earlier, kv], 0)
    key_pair, value_pair = kv_pair[:, :HD], kv_pair[:, HD:]
    key_t, value_t = key_pair.T, value_pair.T
    seg_query = lax.dynamic_slice_in_dim(segment_ids, row * count, count, 0)
    seg_earlier = lax.dynamic_slice_in_dim(
        segment_ids, jnp.maximum(row - 1, 0) * count, count, 0
    )
    segk = jnp.concatenate([seg_earlier, seg_query], 0)[:, None]
    segq = seg_query[None, :]
    first = ints(row == 0)
    (query_held,) = tied((query_rows,), g0)
    attn_out, top, total = attend(query_held, key_pair, value_t, segq, segk, first)

    gxm, gxp, gy, wzm, wzp, attn_out = tied((gxm, gxp, gy, wzm, wzp, attn_out))

    h = g0.shape[0] // 2
    hw = out_proj.shape[0] // 2
    gyxm = move_col(gy, dx=1)
    gyxp = move_col(gy, dx=-1)
    a_other = move_row(attn_out, dk=1)
    wo = move_row(wzm, dz=1)
    wy = move_row(out_proj, dyh=1)

    a_pair = jnp.concatenate([attn_out, a_other], 0)
    proj = project(
        [g0, gxm, gxp, gy],
        a_pair,
        ints(gblock(0, 0), gblock(0, -1), gblock(0, 1), gblock(1, 0)),
        None,
    )

    go = move_col(gxm, dx=1)
    gyxm, gyxp, wo, wy, proj = tied((gyxm, gyxp, wo, wy, proj))
    gyo = move_col(gyxp, dx=-1)
    wyzm = move_row(wy, dz=1)
    wyzp = move_row(wy, dz=-1)
    wyo = move_row(wo, dyh=1)

    proj = project([gyxm, gyxp], a_pair, ints(gblock(1, -1), gblock(1, 1)), proj)

    go, gyo, proj = tied((go, gyo, proj))

    q = hw // 2
    proj, give_far, give_up, give_dn, up2, dn2 = project(
        [go, gyo],
        a_pair,
        ints(
            gblock(0, 2), gblock(1, 2),
            wblock(2, 1), wblock(1, 1), wblock(-1, 1), wblock(1, 0), wblock(-1, 0),
        ),
        proj,
        (
            (0, 0, 0, 0, 0, hw), (0, hw, 0, 1, 0, hw),
            (1, 0, 1, 0, 0, hw), (1, hw, 1, 1, 0, hw), (1, 2 * hw, 3, 1, 0, q),
            (2, 0, 2, 0, 0, hw), (2, hw, 2, 1, 0, hw), (2, 2 * hw, 4, 0, 0, q),
            (3, 0, 3, 1, q, q),
            (4, 0, 4, 0, q, q),
        ),
    )
    give_far, give_up, give_dn, wyzm, wyzp, wyo = tied(
        (give_far, give_up, give_dn, wyzm, wyzp, wyo)
    )
    ry = move_row(give_far, dyh=1)
    rup = move_row(give_up, dz=1)
    rdn = move_row(give_dn, dz=-1)

    g_pieces = [g0, gxm, gxp, gy, gyxm, gyxp, go, gyo]
    gplan = [(i, p * h, i, p) for i in range(8) for p in range(2)]
    w_pieces = [out_proj, wzm, wzp, wy, wyzm, wyzp, wyo, wo]
    wplan = [(i, p * hw, i, p) for i in range(8) for p in range(2)]
    meta = ints(
        gblock(0, 0), gblock(0, -1), gblock(0, 1), gblock(1, 0),
        gblock(1, -1), gblock(1, 1), gblock(0, 2), gblock(1, 2),
        wblock(0, 0), wblock(-1, 0), wblock(1, 0), wblock(0, 1),
        wblock(-1, 1), wblock(1, 1), wblock(2, 1), wblock(2, 0),
    )
    (meta,) = tied((meta,), give_up)
    grad_own, grad_give = attn_grad_part(g_pieces, gplan, w_pieces, wplan, meta)

    ry, grad_own, grad_give = tied((ry, grad_own, grad_give))

    far_up, far_dn = add_blocks(proj, ints(wblock(2, 0)), [ry], ((0, 0, ((0, 0),)), (0, 1, ((0, hw),))))
    fup = move_row(far_up, dz=1)
    fdn = move_row(far_dn, dz=-1)
    grad_got = move_row(grad_give, dk=1)
    rup, rdn = tied((rup, rdn), far_up)
    (across,) = add_blocks(
        proj,
        ints(wblock(0, 1)),
        [rup, rdn],
        ((0, 0, ((0, 0), (1, 0))), (0, 1, ((0, hw), (1, hw)))),
        joined=True,
    )
    across = move_row(across, dyh=1)
    up2, dn2 = tied((up2, dn2), far_up)
    up2 = move_row(up2, dz=1)
    dn2 = move_row(dn2, dz=-1)

    attn_grad = (grad_own + grad_got.astype(F32)).astype(BF)
    (attn_grad,) = tied((attn_grad,), rup)
    part = functools.partial(
        attend_back, query_rows, attn_grad, key_pair, key_t, value_pair, segq, segk, first, top, total
    )
    heads = query_rows.shape[1] // HD
    cut = 3 * heads // 8
    held = part((0, cut), None)

    fup, fdn, *held = tied((fup, fdn, *held))

    near_up, near_dn = add_blocks(
        proj,
        ints(wblock(1, 0), wblock(-1, 0)),
        [fup, fdn],
        ((0, 0, ((0, 0),)), (1, 1, ((1, 0),))),
    )
    nup = move_row(near_up, dz=1)
    ndn = move_row(near_dn, dz=-1)

    *held, up2, dn2 = tied((*held, up2, dn2), near_up)
    query_grad, dkey, dvalue = part((cut, heads), held)
    dkey, dvalue, nup, ndn = tied((dkey, dvalue, nup, ndn))
    back = passed_along(
        jnp.concatenate([dkey[:count], dvalue[:count]], 1).astype(BF), "row", -1
    ).astype(F32)
    key_grad = (dkey[count:] + back[:, :HD]).astype(BF)
    value_grad = (dvalue[count:] + back[:, HD:]).astype(BF)

    proj_grad = last_sum(proj, ints(wblock(0, 0)), across, nup, ndn, rup, up2, rdn, dn2)
    return (query_grad, key_grad, value_grad, proj_grad)


def solution(mesh):
    placed = (
        P("row", "col"),
        P("row", "col"),
        P("row", "col"),
        P("row", "col"),
        P("row", "col"),
        P(),
    )
    return jax.shard_map(
        local,
        mesh=mesh,
        in_specs=placed,
        out_specs=(P("row", "col"), P("row", "col"), P("row", "col"), P("row", "col")),
        check_vma=False,
    )
```

```python
import functools
import math

import jax
import jax.numpy as jnp
from jax import lax
from jax.experimental import pallas as pl
from jax.experimental.pallas import tpu as pltpu
from jax.sharding import PartitionSpec as P

HD = 128
SCALE = 1.0 / math.sqrt(HD)
NEG = -1e30
BF = jnp.bfloat16
F32 = jnp.float32

PLACES = 64

ZN, YN, KN, LN, XN = 4, 2, 2, 2, 4


def move_row(value, dz=0, dyh=0, dk=0):
    pairs = []
    for z in range(ZN):
        for y in range(YN):
            for k in range(KN):
                source = (z * YN + y) * KN + k
                target = ((z + dz) % ZN * YN + (y + dyh) % YN) * KN + (k + dk) % KN
                pairs.append((source, target))
    return lax.ppermute(value, "row", pairs)


def move_col(value, dx=0, dyl=0):
    pairs = []
    for y in range(LN):
        for x in range(XN):
            pairs.append((y * XN + x, (y + dyl) % LN * XN + (x + dx) % XN))
    return lax.ppermute(value, "col", pairs)


def passed_along(value, axis, steps):
    count = lax.axis_size(axis)
    first, last = (max(0, -steps), min(count, count - steps))
    return lax.ppermute(value, axis, [(source, source + steps) for source in range(first, last)])


def tied(values, *others):
    held = lax.optimization_barrier((tuple(values), tuple(others)))
    return held[0]


def params(mib, **kw):
    return pltpu.CompilerParams(vmem_limit_bytes=mib * 1024 * 1024, **kw)


def fill_bias(bias_ref, segq, segk, first_block, count):
    key = lax.broadcasted_iota(jnp.int32, (2 * count, count), 0)
    query = lax.broadcasted_iota(jnp.int32, (2 * count, count), 1)
    ok = (key <= query + count) & (segk == segq) & (key >= first_block * count)
    bias_ref[...] = jnp.where(ok, 0.0, NEG).astype(F32)


def chunk_list(count, width):
    return [(i * width, count + (i + 1) * width) for i in range(count // width)]


def fwd_kernel(meta_ref, q_ref, k_ref, vt_ref, segq_ref, segk_ref, out_ref, top_ref, sum_ref, bias_ref):
    count = q_ref.shape[0]

    @pl.when(pl.program_id(0) == 0)
    def _():
        fill_bias(bias_ref, segq_ref[...], segk_ref[...], meta_ref[0], count)

    for start, keys in chunk_list(count, 256):
        cols = slice(start, start + 256)
        s = lax.dot_general(
            k_ref[:keys, :], q_ref[cols, :], (((1,), (1,)), ((), ())), preferred_element_type=F32
        )
        s = s * SCALE + bias_ref[:keys, cols]
        top = jnp.max(s, axis=0, keepdims=True)
        e = jnp.exp(s - top)
        total = jnp.sum(e, axis=0, keepdims=True)
        inv = 1.0 / total
        p = (e * inv).astype(BF)
        a = jnp.dot(vt_ref[:, :keys], p, preferred_element_type=F32)
        out_ref[cols, :] = a.T.astype(BF)
        top_ref[0, :, cols] = top
        sum_ref[0, :, cols] = inv


def attend(query, key_pair, vt, segq, segk, first):
    count, width = query.shape
    heads = width // HD
    whole = lambda shape: pl.BlockSpec(shape, lambda h, m: (0,) * len(shape))
    head = pl.BlockSpec((count, HD), lambda h, m: (0, h))
    stat = pl.BlockSpec((1, 1, count), lambda h, m: (h, 0, 0))
    return pl.pallas_call(
        fwd_kernel,
        grid_spec=pltpu.PrefetchScalarGridSpec(
            num_scalar_prefetch=1,
            grid=(heads,),
            in_specs=[
                head,
                whole((2 * count, HD)),
                whole((HD, 2 * count)),
                whole((1, count)),
                whole((2 * count, 1)),
            ],
            out_specs=[head, stat, stat],
            scratch_shapes=[pltpu.VMEM((2 * count, count), F32)],
        ),
        out_shape=[
            jax.ShapeDtypeStruct((count, width), BF),
            jax.ShapeDtypeStruct((heads, 1, count), F32),
            jax.ShapeDtypeStruct((heads, 1, count), F32),
        ],
        compiler_params=params(16),
        cost_estimate=pl.CostEstimate(
            flops=heads * 4 * 2 * 2 * count * count * HD,
            bytes_accessed=8 * 2**20,
            transcendentals=heads * 2 * count * count,
        ),
        name="attend",
    )(first, query, key_pair, vt, segq, segk)


def bwd_kernel(
    n_held, last, meta_ref, q_ref, g_ref, k_ref, kt_ref, v_ref, segq_ref, segk_ref, top_ref, sum_ref,
    *refs,
):
    dk_in, dv_in = refs[:2] if n_held else (None, None)
    dq_ref, dk_ref, dv_ref, bias_ref = refs[n_held:]
    count = q_ref.shape[0]

    @pl.when(pl.program_id(0) == 0)
    def _():
        fill_bias(bias_ref, segq_ref[...], segk_ref[...], meta_ref[0], count)
        if n_held:
            dk_ref[...] = dk_in[...]
            dv_ref[...] = dv_in[...]
        else:
            dk_ref[...] = jnp.zeros_like(dk_ref)
            dv_ref[...] = jnp.zeros_like(dv_ref)

    for start, keys in chunk_list(count, 256):
        cols = slice(start, start + 256)
        q = q_ref[cols, :]
        g = g_ref[cols, :]
        s = lax.dot_general(
            k_ref[:keys, :], q, (((1,), (1,)), ((), ())), preferred_element_type=F32
        )
        s = s * SCALE + bias_ref[:keys, cols]
        p = jnp.exp(s - top_ref[0, :, cols]) * sum_ref[0, :, cols]
        dp = lax.dot_general(
            v_ref[:keys, :], g, (((1,), (1,)), ((), ())), preferred_element_type=F32
        )
        delta = jnp.sum(p * dp, axis=0, keepdims=True)
        ds = (p * (dp - delta)).astype(BF)
        dq = jnp.dot(kt_ref[:, :keys], ds, preferred_element_type=F32) * SCALE
        dq_ref[cols, :] = dq.T.astype(BF)
        dk_ref[:keys, :] += jnp.dot(ds, q, preferred_element_type=F32)
        dv_ref[:keys, :] += jnp.dot(p.astype(BF), g, preferred_element_type=F32)

    if last:

        @pl.when(pl.program_id(0) == pl.num_programs(0) - 1)
        def _():
            dk_ref[...] = dk_ref[...] * SCALE


def attend_back(query, grad, key_pair, kt, value_pair, segq, segk, first, top, total, heads, held):
    count, width = query.shape
    begin, end = heads
    last = end == width // HD
    whole = lambda shape: pl.BlockSpec(shape, lambda h, m: (0,) * len(shape))
    head = pl.BlockSpec((count, HD), lambda h, m: (0, h + begin))
    stat = pl.BlockSpec((1, 1, count), lambda h, m: (h + begin, 0, 0))
    pair = whole((2 * count, HD))
    earlier = () if held is None else (held[1], held[2], held[0])
    return pl.pallas_call(
        functools.partial(bwd_kernel, len(earlier), last),
        grid_spec=pltpu.PrefetchScalarGridSpec(
            num_scalar_prefetch=1,
            grid=(end - begin,),
            in_specs=[
                head,
                head,
                pair,
                whole((HD, 2 * count)),
                pair,
                whole((1, count)),
                whole((2 * count, 1)),
                stat,
                stat,
            ]
            + ([pair, pair, pl.BlockSpec(memory_space=pl.ANY)] if earlier else []),
            out_specs=[head, pair, pair],
            scratch_shapes=[pltpu.VMEM((2 * count, count), F32)],
        ),
        out_shape=[
            jax.ShapeDtypeStruct((count, width), BF),
            jax.ShapeDtypeStruct((2 * count, HD), F32),
            jax.ShapeDtypeStruct((2 * count, HD), F32),
        ],
        input_output_aliases={12: 0} if earlier else {},
        compiler_params=params(22),
        cost_estimate=pl.CostEstimate(
            flops=(end - begin) * 10 * 2 * 2 * count * count * HD,
            bytes_accessed=6 * 2**20,
            transcendentals=(end - begin) * 2 * count * count,
        ),
        name="attend_back",
    )(first, query, grad, key_pair, kt, value_pair, segq, segk, top, total, *earlier)


def proj_kernel(n_in, held, plan, meta_ref, *refs):
    pieces, a_ref = refs[:n_in], refs[n_in]
    refs = refs[n_in + 1 + held:]
    buffer_ref, taken = refs[0], refs[1:-3]
    done, sems, take_sems = refs[-3:]
    step = pl.program_id(0)
    rows = done.shape[2]

    def put(j):
        return pltpu.make_async_copy(done.at[j], buffer_ref.at[:, meta_ref[j]], sems.at[j])

    def take(i, made):
        out, start, at, half, first, count = plan[i]
        if made is None:
            source = buffer_ref.at[half, meta_ref[n_in + at], pl.ds(first, count)]
        else:
            source = done.at[made, half, pl.ds(first, count)]
        target = taken[out].at[pl.ds(start, count)]
        return pltpu.make_async_copy(source, target, take_sems.at[i])

    def made_here(i, j):
        return meta_ref[n_in + plan[i][2]] == meta_ref[j]

    @pl.when(step == 0)
    def _():
        for i in range(len(plan)):
            here = made_here(i, 0)
            for j in range(1, n_in):
                here = here | made_here(i, j)

            @pl.when(jnp.logical_not(here))
            def _():
                take(i, None).start()

    for j in range(n_in):

        @pl.when(step == j)
        def _():
            value = lax.dot_general(
                pieces[j][...], a_ref[...], (((0,), (0,)), ((), ())), preferred_element_type=F32
            ).astype(BF)
            done[j, 0] = value[:rows]
            done[j, 1] = value[rows:]
            put(j).start()
            for i in range(len(plan)):

                @pl.when(made_here(i, j))
                def _():
                    take(i, j).start()

    @pl.when(step == n_in - 1)
    def _():
        for j in range(n_in):
            put(j).wait()
        for i in range(len(plan)):
            take(i, None).wait()


def project(pieces, a_pair, blocks, buffer, plan=()):
    tokens, width = a_pair.shape
    depth = pieces[0].shape[1]
    n_blocks = len(pieces)
    held = int(buffer is not None)
    here = pl.BlockSpec(memory_space=pltpu.VMEM)
    there = pl.BlockSpec(memory_space=pltpu.HBM)
    operands = (*pieces, a_pair) + ((buffer,) if held else ())
    shape = (2, depth // 2, width)
    n_taken = 1 + max((entry[0] for entry in plan), default=-1)
    taken = [(sum(e[5] for e in plan if e[0] == i), width) for i in range(n_taken)]
    out = pl.pallas_call(
        functools.partial(proj_kernel, n_blocks, held, plan),
        grid_spec=pltpu.PrefetchScalarGridSpec(
            num_scalar_prefetch=1,
            grid=(n_blocks,),
            in_specs=[here] * (n_blocks + 1) + [there] * held,
            out_specs=[there] + [here] * n_taken,
            scratch_shapes=[
                pltpu.VMEM((n_blocks, *shape), BF),
                pltpu.SemaphoreType.DMA((n_blocks,)),
                pltpu.SemaphoreType.DMA((max(len(plan), 1),)),
            ],
        ),
        out_shape=[jax.ShapeDtypeStruct((2, PLACES, depth // 2, width), BF)]
        + [jax.ShapeDtypeStruct(t, BF) for t in taken],
        input_output_aliases={n_blocks + 2: 0} if held else {},
        compiler_params=params(16),
        cost_estimate=pl.CostEstimate(
            flops=2 * n_blocks * tokens * depth * width,
            bytes_accessed=(2 * n_blocks + 2) * 2**20,
            transcendentals=0,
        ),
        name="project",
    )(blocks, *operands)
    return out if n_taken else out[0]


def grad_kernel(wplan, n_g, n_w, meta_ref, *refs):
    g_in, w_in = refs[:n_g], refs[n_g:n_g + n_w]
    own_ref, other_ref = refs[n_g + n_w:n_g + n_w + 2]
    gbuf, wbuf, total, gsems, wsems = refs[n_g + n_w + 2:]
    step = pl.program_id(0)
    half = own_ref.shape[0]
    wh = wbuf.shape[1] // 2

    slots = gbuf.shape[0]

    def g_copy(j):
        return pltpu.make_async_copy(g_in[j], gbuf.at[j % slots], gsems.at[j])

    def w_copy(n):
        ref, source, block, part = wplan[n]
        place = meta_ref[8 + block]
        return pltpu.make_async_copy(
            w_in[ref].at[pl.ds(source, wh)],
            wbuf.at[place, pl.ds(part * wh, wh)],
            wsems.at[part, place],
        )

    @pl.when(step == 0)
    def _():
        for j in range(slots):
            g_copy(j).start()
        for n in range(16):
            w_copy(n).start()

    for j in range(8):

        @pl.when(step == j)
        def _():
            g_copy(j).wait()

    place = meta_ref[step]
    for part in range(2):
        pltpu.make_async_copy(
            w_in[0].at[pl.ds(0, wh)], wbuf.at[place, pl.ds(part * wh, wh)], wsems.at[part, place]
        ).wait()

    @pl.when(step == 0)
    def _():
        total[...] = jnp.dot(gbuf[0], wbuf[place], preferred_element_type=F32)

    @pl.when(step > 0)
    def _():
        total[...] += jnp.dot(gbuf[step % slots], wbuf[place], preferred_element_type=F32)

    for j in range(8 - slots):

        @pl.when(step == j)
        def _():
            g_copy(j + slots).start()

    @pl.when(step == 7)
    def _():
        own_ref[...] = total[:half, :]
        other_ref[...] = total[half:, :].astype(BF)


def attn_grad_part(g_pieces, w_pieces, wplan, meta):
    tokens, depth = g_pieces[0].shape
    width = w_pieces[0].shape[1]
    half = tokens // 2
    kernel = functools.partial(grad_kernel, wplan, len(g_pieces), len(w_pieces))
    whole = pl.BlockSpec(memory_space=pltpu.VMEM)
    return pl.pallas_call(
        kernel,
        grid_spec=pltpu.PrefetchScalarGridSpec(
            num_scalar_prefetch=1,
            grid=(8,),
            in_specs=[pl.BlockSpec(memory_space=pltpu.HBM)] * (len(g_pieces) + len(w_pieces)),
            out_specs=[whole, whole],
            scratch_shapes=[
                pltpu.VMEM((3, tokens, depth), BF),
                pltpu.VMEM((8, depth, width), BF),
                pltpu.VMEM((tokens, width), F32),
                pltpu.SemaphoreType.DMA((8,)),
                pltpu.SemaphoreType.DMA((2, 8)),
            ],
        ),
        out_shape=[
            jax.ShapeDtypeStruct((half, width), F32),
            jax.ShapeDtypeStruct((half, width), BF),
        ],
        compiler_params=params(26),
        cost_estimate=pl.CostEstimate(
            flops=16 * tokens * depth * width,
            bytes_accessed=20 * 2**20,
            transcendentals=0,
        ),
        name="attn_grad",
    )(meta, *g_pieces, *w_pieces)


def add_kernel(n_terms, plan, joined, meta_ref, buffer_ref, *refs):
    terms, outs = refs[:n_terms], refs[n_terms:-2]
    blocks, sems = refs[-2:]
    rows = blocks.shape[2]
    copies = [
        pltpu.make_async_copy(buffer_ref.at[:, meta_ref[n]], blocks.at[n], sems.at[n])
        for n in range(blocks.shape[0])
    ]
    for copy in copies:
        copy.start()
    for copy in copies:
        copy.wait()
    for n, (block, half, extra) in enumerate(plan):
        value = blocks[block, half].astype(F32)
        for term, first in extra:
            value = value + terms[term][first:first + rows, :].astype(F32)
        if joined:
            outs[0][n * rows:(n + 1) * rows, :] = value.astype(BF)
        else:
            outs[n][...] = value.astype(BF)


def add_blocks(buffer, blocks, terms, plan, joined=False):
    _, _, rows, width = buffer.shape
    here = pl.BlockSpec(memory_space=pltpu.VMEM)
    shapes = [(len(plan) * rows, width)] if joined else [(rows, width)] * len(plan)
    return pl.pallas_call(
        functools.partial(add_kernel, len(terms), plan, joined),
        grid_spec=pltpu.PrefetchScalarGridSpec(
            num_scalar_prefetch=1,
            grid=(1,),
            in_specs=[pl.BlockSpec(memory_space=pltpu.HBM)] + [here] * len(terms),
            out_specs=[here] * len(shapes),
            scratch_shapes=[
                pltpu.VMEM((blocks.shape[0], 2, rows, width), BF),
                pltpu.SemaphoreType.DMA((blocks.shape[0],)),
            ],
        ),
        out_shape=[jax.ShapeDtypeStruct(shape, BF) for shape in shapes],
        compiler_params=params(12),
        cost_estimate=pl.CostEstimate(
            flops=2**21, bytes_accessed=5 * 2**20, transcendentals=0
        ),
        name="add_blocks",
    )(blocks, buffer, *terms)


def last_kernel(meta_ref, buffer_ref, across, nup, ndn, rup, up2, rdn, dn2, out_ref, block, sem):
    copy = pltpu.make_async_copy(buffer_ref.at[:, meta_ref[0]], block, sem)
    copy.start()
    copy.wait()
    half, quarter = nup.shape[0], up2.shape[0]
    for part in range(2):
        for n in range(2):
            rows = slice(n * quarter, (n + 1) * quarter)
            place = slice(part * half + n * quarter, part * half + (n + 1) * quarter)
            up, dn = nup[rows, :], ndn[rows, :]
            if part == 1:
                up = up2[...] if n else rup[2 * half:, :]
            else:
                dn = dn2[...] if n else rdn[2 * half:, :]
            out_ref[place, :] = (
                block[part, rows].astype(F32)
                + across[place, :].astype(F32)
                + up.astype(F32)
                + dn.astype(F32)
            ).astype(BF)


def last_sum(buffer, place, *terms):
    _, _, rows, width = buffer.shape
    here = pl.BlockSpec(memory_space=pltpu.VMEM)
    return pl.pallas_call(
        last_kernel,
        grid_spec=pltpu.PrefetchScalarGridSpec(
            num_scalar_prefetch=1,
            grid=(1,),
            in_specs=[pl.BlockSpec(memory_space=pltpu.HBM)] + [here] * len(terms),
            out_specs=pl.BlockSpec((2 * rows, width), lambda i, m: (0, 0)),
            scratch_shapes=[pltpu.VMEM((2, rows, width), BF), pltpu.SemaphoreType.DMA],
        ),
        out_shape=jax.ShapeDtypeStruct((2 * rows, width), BF),
        compiler_params=params(12),
        cost_estimate=pl.CostEstimate(
            flops=2**21, bytes_accessed=5 * 2**20, transcendentals=0
        ),
        name="last_sum",
    )(place, buffer, *terms)


def local(query_rows, key_rows, value_rows, output_grad, out_proj, segment_ids):
    count = query_rows.shape[0]
    half_d = output_grad.shape[1] // 2
    row, col = lax.axis_index("row"), lax.axis_index("col")
    z, yh, k = row // 4, row // 2 % 2, row % 2
    yl, x = col // 4, col % 4

    def gblock(dyl, dx):
        return (yl + dyl) % 2 * 4 + (x + dx) % 4

    def wblock(dz, dy):
        return (z + dz) % 4 * 2 + (yh + dy) % 2

    def ints(*values):
        return jnp.stack([jnp.asarray(v, jnp.int32) for v in values])

    g_keep = lax.dynamic_slice_in_dim(output_grad, k * half_d, half_d, 1)
    g_give = lax.dynamic_slice_in_dim(output_grad, (1 - k) * half_d, half_d, 1)
    g0 = jnp.concatenate([g_keep, move_row(g_give, dk=1)], 0)
    kv = jnp.concatenate([key_rows, value_rows], 1)
    kv_earlier = passed_along(kv, "row", 1)

    gxm = move_col(g0, dx=1)
    gxp = move_col(g0, dx=-1)
    gy = move_col(g0, dyl=1)
    wzm = move_row(out_proj, dz=1)
    wzp = move_row(out_proj, dz=-1)

    kv_pair = jnp.concatenate([kv_earlier, kv], 0)
    key_pair, value_pair = kv_pair[:, :HD], kv_pair[:, HD:]
    key_t, value_t = key_pair.T, value_pair.T
    seg_query = lax.dynamic_slice_in_dim(segment_ids, row * count, count, 0)
    seg_earlier = lax.dynamic_slice_in_dim(
        segment_ids, jnp.maximum(row - 1, 0) * count, count, 0
    )
    segk = jnp.concatenate([seg_earlier, seg_query], 0)[:, None]
    segq = seg_query[None, :]
    first = ints(row == 0)
    (query_held,) = tied((query_rows,), g0)
    attn_out, top, total = attend(query_held, key_pair, value_t, segq, segk, first)

    wzm, wzp, gxm, gxp, gy, attn_out = tied((wzm, wzp, gxm, gxp, gy, attn_out))

    hw = out_proj.shape[0] // 2
    gyxm = move_col(gy, dx=1)
    gyxp = move_col(gy, dx=-1)
    a_other = move_row(attn_out, dk=1)
    wo = move_row(wzm, dz=1)
    wy = move_row(out_proj, dyh=1)

    a_pair = jnp.concatenate([attn_out, a_other], 0)
    proj = project(
        [g0, gxm, gxp, gy],
        a_pair,
        ints(gblock(0, 0), gblock(0, -1), gblock(0, 1), gblock(1, 0)),
        None,
    )

    go = move_col(gxm, dx=1)
    wo, wy, gyxm, gyxp, proj = tied((wo, wy, gyxm, gyxp, proj))
    gyo = move_col(gyxp, dx=-1)
    wyzm = move_row(wy, dz=1)
    wyzp = move_row(wy, dz=-1)
    wyo = move_row(wo, dyh=1)

    proj = project([gyxm, gyxp], a_pair, ints(gblock(1, -1), gblock(1, 1)), proj)

    go, gyo, proj = tied((go, gyo, proj))

    q = hw // 2
    proj, give_far, give_up, give_dn, up2, dn2 = project(
        [go, gyo],
        a_pair,
        ints(
            gblock(0, 2), gblock(1, 2),
            wblock(2, 1), wblock(1, 1), wblock(-1, 1), wblock(1, 0), wblock(-1, 0),
        ),
        proj,
        (
            (0, 0, 0, 0, 0, hw), (0, hw, 0, 1, 0, hw),
            (1, 0, 1, 0, 0, hw), (1, hw, 1, 1, 0, hw), (1, 2 * hw, 3, 1, 0, q),
            (2, 0, 2, 0, 0, hw), (2, hw, 2, 1, 0, hw), (2, 2 * hw, 4, 0, 0, q),
            (3, 0, 3, 1, q, q),
            (4, 0, 4, 0, q, q),
        ),
    )
    give_far, give_up, give_dn, wyzm, wyzp, wyo = tied(
        (give_far, give_up, give_dn, wyzm, wyzp, wyo)
    )
    ry = move_row(give_far, dyh=1)
    rup = move_row(give_up, dz=1)
    rdn = move_row(give_dn, dz=-1)

    g_pieces = [g0, gxm, gxp, gy, gyxm, gyxp, go, gyo]
    w_pieces = [out_proj, wzm, wzp, wy, wyzm, wyzp, wyo, wo]
    wplan = [(i, p * hw, i, p) for i in range(8) for p in range(2)]
    meta = ints(
        gblock(0, 0), gblock(0, -1), gblock(0, 1), gblock(1, 0),
        gblock(1, -1), gblock(1, 1), gblock(0, 2), gblock(1, 2),
        wblock(0, 0), wblock(-1, 0), wblock(1, 0), wblock(0, 1),
        wblock(-1, 1), wblock(1, 1), wblock(2, 1), wblock(2, 0),
    )
    (meta,) = tied((meta,), give_up)
    grad_own, grad_give = attn_grad_part(g_pieces, w_pieces, wplan, meta)

    ry, grad_own, grad_give = tied((ry, grad_own, grad_give))

    far_up, far_dn = add_blocks(proj, ints(wblock(2, 0)), [ry], ((0, 0, ((0, 0),)), (0, 1, ((0, hw),))))
    fup = move_row(far_up, dz=1)
    fdn = move_row(far_dn, dz=-1)
    grad_got = move_row(grad_give, dk=1)
    rup, rdn = tied((rup, rdn), far_up)
    (across,) = add_blocks(
        proj,
        ints(wblock(0, 1)),
        [rup, rdn],
        ((0, 0, ((0, 0), (1, 0))), (0, 1, ((0, hw), (1, hw)))),
        joined=True,
    )
    across = move_row(across, dyh=1)
    up2, dn2 = tied((up2, dn2), far_up)
    up2 = move_row(up2, dz=1)
    dn2 = move_row(dn2, dz=-1)

    attn_grad = (grad_own + grad_got.astype(F32)).astype(BF)
    (attn_grad,) = tied((attn_grad,), rup)
    part = functools.partial(
        attend_back, query_rows, attn_grad, key_pair, key_t, value_pair, segq, segk, first, top, total
    )
    heads = query_rows.shape[1] // HD
    cut = 3 * heads // 8
    held = part((0, cut), None)

    fup, fdn, *held = tied((fup, fdn, *held))

    near_up, near_dn = add_blocks(
        proj,
        ints(wblock(1, 0), wblock(-1, 0)),
        [fup, fdn],
        ((0, 0, ((0, 0),)), (1, 1, ((1, 0),))),
    )
    nup = move_row(near_up, dz=1)
    ndn = move_row(near_dn, dz=-1)

    *held, up2, dn2 = tied((*held, up2, dn2), near_up)
    query_grad, dkey, dvalue = part((cut, heads), held)
    dkey, dvalue, nup, ndn = tied((dkey, dvalue, nup, ndn))
    back = passed_along(
        jnp.concatenate([dkey[:count], dvalue[:count]], 1).astype(BF), "row", -1
    ).astype(F32)
    key_grad = (dkey[count:] + back[:, :HD]).astype(BF)
    value_grad = (dvalue[count:] + back[:, HD:]).astype(BF)

    proj_grad = last_sum(proj, ints(wblock(0, 0)), across, nup, ndn, rup, up2, rdn, dn2)
    return (query_grad, key_grad, value_grad, proj_grad)


def solution(mesh):
    placed = (
        P("row", "col"),
        P("row", "col"),
        P("row", "col"),
        P("row", "col"),
        P("row", "col"),
        P(),
    )
    return jax.shard_map(
        local,
        mesh=mesh,
        in_specs=placed,
        out_specs=(P("row", "col"), P("row", "col"), P("row", "col"), P("row", "col")),
        check_vma=False,
    )
```

```python
import functools
import math

import jax
import jax.numpy as jnp
from jax import lax
from jax.experimental import pallas as pl
from jax.experimental.pallas import tpu as pltpu
from jax.sharding import PartitionSpec as P

HD = 128
SCALE = 1.0 / math.sqrt(HD)
NEG = -1e30
BF = jnp.bfloat16
F32 = jnp.float32

PLACES = 64

ZN, YN, KN, LN, XN = 4, 2, 2, 2, 4


AT_FIRST, AT_ROW, AT_EARLIER, AT_G, AT_W = 0, 1, 2, 8, 16
G_STEPS = [(0, 0), (0, -1), (0, 1), (1, 0), (1, -1), (1, 1), (0, 2), (1, 2)]
W_STEPS = [(0, 0), (-1, 0), (1, 0), (0, 1), (-1, 1), (1, 1), (2, 1), (2, 0)]
LANES = 128


def positions(row, col):
    z, yh, yl, x = row // 4, row // 2 % 2, col // 4, col % 4
    head = jnp.stack([(row == 0).astype(jnp.int32), row, jnp.maximum(row - 1, 0)] + [row] * 5)
    steps = [jnp.asarray([step[i] for step in order], jnp.int32) for order in (G_STEPS, W_STEPS) for i in (0, 1)]
    dyl, dx, dz, dyh = steps
    g = ((yl + dyl) & 1) * 4 + ((x + dx) & 3)
    w = ((z + dz) & 3) * 2 + ((yh + dyh) & 1)
    return jnp.concatenate([head, g, w])


def at_w(dz, dyh):
    return AT_W + W_STEPS.index((dz, dyh))


def move_row(value, dz=0, dyh=0, dk=0):
    pairs = []
    for z in range(ZN):
        for y in range(YN):
            for k in range(KN):
                source = (z * YN + y) * KN + k
                target = ((z + dz) % ZN * YN + (y + dyh) % YN) * KN + (k + dk) % KN
                pairs.append((source, target))
    return lax.ppermute(value, "row", pairs)


def move_col(value, dx=0, dyl=0):
    pairs = []
    for y in range(LN):
        for x in range(XN):
            pairs.append((y * XN + x, (y + dyl) % LN * XN + (x + dx) % XN))
    return lax.ppermute(value, "col", pairs)


def passed_along(value, axis, steps):
    count = lax.axis_size(axis)
    first, last = (max(0, -steps), min(count, count - steps))
    return lax.ppermute(value, axis, [(source, source + steps) for source in range(first, last)])


def tied(values, *others):
    held = lax.optimization_barrier((tuple(values), tuple(others)))
    return held[0]


def params(mib, **kw):
    return pltpu.CompilerParams(vmem_limit_bytes=mib * 1024 * 1024, **kw)


def prepare(meta_ref, seg_ref, kv_ref, k_ref, v_ref, bias_ref, k_pair, v_pair, turned, of_keys):
    count = k_ref.shape[0]
    parts = count // LANES
    first, row, earlier = meta_ref[AT_FIRST], meta_ref[AT_ROW], meta_ref[AT_EARLIER]
    own = [seg_ref[pl.ds(row * parts + i, 1), :] for i in range(parts)]
    before = [seg_ref[pl.ds(earlier * parts + i, 1), :] for i in range(parts)]
    key_at = lax.broadcasted_iota(jnp.int32, (LANES, LANES), 0)
    query_at = lax.broadcasted_iota(jnp.int32, (LANES, LANES), 1)
    for i, keys in enumerate(before + own):
        column = jnp.broadcast_to(keys.astype(F32), (LANES, LANES)).T
        for j in range(parts):
            ok = column == own[j].astype(F32)
            if i < parts:
                ok = ok & (first == 0)
            else:
                ok = ok & (key_at + (i - parts) * LANES <= query_at + j * LANES)
            bias_ref[i * LANES:(i + 1) * LANES, j * LANES:(j + 1) * LANES] = jnp.where(
                ok, 0.0, NEG
            ).astype(F32)
    k_pair[:count, :] = kv_ref[:, :HD]
    k_pair[count:, :] = k_ref[...]
    v_pair[:count, :] = kv_ref[:, HD:]
    v_pair[count:, :] = v_ref[...]
    turned[...] = (k_pair if of_keys else v_pair)[...].astype(F32).T.astype(BF)


def pair_scratch(count):
    return [
        pltpu.VMEM((2 * count, count), F32),
        pltpu.VMEM((2 * count, HD), BF),
        pltpu.VMEM((2 * count, HD), BF),
        pltpu.VMEM((HD, 2 * count), BF),
    ]


def chunk_list(count, width):
    return [(i * width, count + (i + 1) * width) for i in range(count // width)]


def fwd_kernel(
    meta_ref, q_ref, kv_ref, k_ref, v_ref, seg_ref, out_ref, top_ref, sum_ref,
    bias_ref, k_pair, v_pair, vt_ref,
):
    count = q_ref.shape[0]

    @pl.when(pl.program_id(0) == 0)
    def _():
        prepare(meta_ref, seg_ref, kv_ref, k_ref, v_ref, bias_ref, k_pair, v_pair, vt_ref, False)

    for start, keys in chunk_list(count, 256):
        cols = slice(start, start + 256)
        s = lax.dot_general(
            k_pair[:keys, :], q_ref[cols, :], (((1,), (1,)), ((), ())), preferred_element_type=F32
        )
        s = s * SCALE + bias_ref[:keys, cols]
        top = jnp.max(s, axis=0, keepdims=True)
        e = jnp.exp(s - top)
        total = jnp.sum(e, axis=0, keepdims=True)
        inv = 1.0 / total
        p = (e * inv).astype(BF)
        a = jnp.dot(vt_ref[:, :keys], p, preferred_element_type=F32)
        out_ref[cols, :] = a.T.astype(BF)
        top_ref[0, :, cols] = top
        sum_ref[0, :, cols] = inv


def attend(meta, query, kv_earlier, key_rows, value_rows, segments):
    count, width = query.shape
    heads = width // HD
    whole = lambda value: pl.BlockSpec(value.shape, lambda h, m: (0, 0))
    head = pl.BlockSpec((count, HD), lambda h, m: (0, h))
    stat = pl.BlockSpec((1, 1, count), lambda h, m: (h, 0, 0))
    return pl.pallas_call(
        fwd_kernel,
        grid_spec=pltpu.PrefetchScalarGridSpec(
            num_scalar_prefetch=1,
            grid=(heads,),
            in_specs=[head] + [whole(v) for v in (kv_earlier, key_rows, value_rows, segments)],
            out_specs=[head, stat, stat],
            scratch_shapes=pair_scratch(count),
        ),
        out_shape=[
            jax.ShapeDtypeStruct((count, width), BF),
            jax.ShapeDtypeStruct((heads, 1, count), F32),
            jax.ShapeDtypeStruct((heads, 1, count), F32),
        ],
        compiler_params=params(16),
        cost_estimate=pl.CostEstimate(
            flops=heads * 4 * 2 * 2 * count * count * HD,
            bytes_accessed=8 * 2**20,
            transcendentals=heads * 2 * count * count,
        ),
        name="attend",
    )(meta, query, kv_earlier, key_rows, value_rows, segments)


def bwd_kernel(
    n_held, last, meta_ref, q_ref, g_ref, kv_ref, k_ref, v_ref, seg_ref, top_ref, sum_ref, *refs
):
    dk_in, dv_in = refs[:2] if n_held else (None, None)
    dq_ref, dk_ref, dv_ref, bias_ref, k_pair, v_pair, kt_ref = refs[n_held:]
    count = q_ref.shape[0]

    @pl.when(pl.program_id(0) == 0)
    def _():
        prepare(meta_ref, seg_ref, kv_ref, k_ref, v_ref, bias_ref, k_pair, v_pair, kt_ref, True)
        if n_held:
            dk_ref[...] = dk_in[...]
            dv_ref[...] = dv_in[...]
        else:
            dk_ref[...] = jnp.zeros_like(dk_ref)
            dv_ref[...] = jnp.zeros_like(dv_ref)

    for start, keys in chunk_list(count, 256):
        cols = slice(start, start + 256)
        q = q_ref[cols, :]
        g = g_ref[cols, :]
        s = lax.dot_general(
            k_pair[:keys, :], q, (((1,), (1,)), ((), ())), preferred_element_type=F32
        )
        s = s * SCALE + bias_ref[:keys, cols]
        p = jnp.exp(s - top_ref[0, :, cols]) * sum_ref[0, :, cols]
        dp = lax.dot_general(
            v_pair[:keys, :], g, (((1,), (1,)), ((), ())), preferred_element_type=F32
        )
        delta = jnp.sum(p * dp, axis=0, keepdims=True)
        ds = (p * (dp - delta)).astype(BF)
        dq = jnp.dot(kt_ref[:, :keys], ds, preferred_element_type=F32) * SCALE
        dq_ref[cols, :] = dq.T.astype(BF)
        dk_ref[:keys, :] += jnp.dot(ds, q, preferred_element_type=F32)
        dv_ref[:keys, :] += jnp.dot(p.astype(BF), g, preferred_element_type=F32)

    if last:

        @pl.when(pl.program_id(0) == pl.num_programs(0) - 1)
        def _():
            dk_ref[...] = dk_ref[...] * SCALE


def attend_back(
    meta, query, grad, kv_earlier, key_rows, value_rows, segments, top, total, heads, held
):
    count, width = query.shape
    begin, end = heads
    last = end == width // HD
    whole = lambda value: pl.BlockSpec(value.shape, lambda h, m: (0, 0))
    head = pl.BlockSpec((count, HD), lambda h, m: (0, h + begin))
    stat = pl.BlockSpec((1, 1, count), lambda h, m: (h + begin, 0, 0))
    pair = pl.BlockSpec((2 * count, HD), lambda h, m: (0, 0))
    earlier = () if held is None else (held[1], held[2], held[0])
    return pl.pallas_call(
        functools.partial(bwd_kernel, len(earlier), last),
        grid_spec=pltpu.PrefetchScalarGridSpec(
            num_scalar_prefetch=1,
            grid=(end - begin,),
            in_specs=[head, head]
            + [whole(v) for v in (kv_earlier, key_rows, value_rows, segments)]
            + [stat, stat]
            + ([pair, pair, pl.BlockSpec(memory_space=pl.ANY)] if earlier else []),
            out_specs=[head, pair, pair],
            scratch_shapes=pair_scratch(count),
        ),
        out_shape=[
            jax.ShapeDtypeStruct((count, width), BF),
            jax.ShapeDtypeStruct((2 * count, HD), F32),
            jax.ShapeDtypeStruct((2 * count, HD), F32),
        ],
        input_output_aliases={11: 0} if earlier else {},
        compiler_params=params(22),
        cost_estimate=pl.CostEstimate(
            flops=(end - begin) * 10 * 2 * 2 * count * count * HD,
            bytes_accessed=6 * 2**20,
            transcendentals=(end - begin) * 2 * count * count,
        ),
        name="attend_back",
    )(meta, query, grad, kv_earlier, key_rows, value_rows, segments, top, total, *earlier)


def proj_kernel(slots, held, plan, meta_ref, *refs):
    n_in = len(slots)
    pieces, a_ref = refs[:n_in], refs[n_in]
    refs = refs[n_in + 1 + held:]
    buffer_ref, taken = refs[0], refs[1:-3]
    done, sems, take_sems = refs[-3:]
    step = pl.program_id(0)
    rows = done.shape[2]

    def put(j):
        return pltpu.make_async_copy(done.at[j], buffer_ref.at[:, meta_ref[AT_G + slots[j]]], sems.at[j])

    def take(i, made):
        out, start, at, half, first, count = plan[i]
        if made is None:
            source = buffer_ref.at[half, meta_ref[at], pl.ds(first, count)]
        else:
            source = done.at[made, half, pl.ds(first, count)]
        target = taken[out].at[pl.ds(start, count)]
        return pltpu.make_async_copy(source, target, take_sems.at[i])

    def made_here(i, j):
        return meta_ref[plan[i][2]] == meta_ref[AT_G + slots[j]]

    @pl.when(step == 0)
    def _():
        for i in range(len(plan)):
            here = made_here(i, 0)
            for j in range(1, n_in):
                here = here | made_here(i, j)

            @pl.when(jnp.logical_not(here))
            def _():
                take(i, None).start()

    for j in range(n_in):

        @pl.when(step == j)
        def _():
            value = lax.dot_general(
                pieces[j][...], a_ref[...], (((0,), (0,)), ((), ())), preferred_element_type=F32
            ).astype(BF)
            done[j, 0] = value[:rows]
            done[j, 1] = value[rows:]
            put(j).start()
            for i in range(len(plan)):

                @pl.when(made_here(i, j))
                def _():
                    take(i, j).start()

    @pl.when(step == n_in - 1)
    def _():
        for j in range(n_in):
            put(j).wait()
        for i in range(len(plan)):
            take(i, None).wait()


def project(pieces, a_pair, meta, slots, buffer, plan=()):
    tokens, width = a_pair.shape
    depth = pieces[0].shape[1]
    n_blocks = len(pieces)
    held = int(buffer is not None)
    here = pl.BlockSpec(memory_space=pltpu.VMEM)
    there = pl.BlockSpec(memory_space=pltpu.HBM)
    operands = (*pieces, a_pair) + ((buffer,) if held else ())
    shape = (2, depth // 2, width)
    n_taken = 1 + max((entry[0] for entry in plan), default=-1)
    taken = [(sum(e[5] for e in plan if e[0] == i), width) for i in range(n_taken)]
    out = pl.pallas_call(
        functools.partial(proj_kernel, tuple(slots), held, plan),
        grid_spec=pltpu.PrefetchScalarGridSpec(
            num_scalar_prefetch=1,
            grid=(n_blocks,),
            in_specs=[here] * (n_blocks + 1) + [there] * held,
            out_specs=[there] + [here] * n_taken,
            scratch_shapes=[
                pltpu.VMEM((n_blocks, *shape), BF),
                pltpu.SemaphoreType.DMA((n_blocks,)),
                pltpu.SemaphoreType.DMA((max(len(plan), 1),)),
            ],
        ),
        out_shape=[jax.ShapeDtypeStruct((2, PLACES, depth // 2, width), BF)]
        + [jax.ShapeDtypeStruct(t, BF) for t in taken],
        input_output_aliases={n_blocks + 2: 0} if held else {},
        compiler_params=params(16),
        cost_estimate=pl.CostEstimate(
            flops=2 * n_blocks * tokens * depth * width,
            bytes_accessed=(2 * n_blocks + 2) * 2**20,
            transcendentals=0,
        ),
        name="project",
    )(meta, *operands)
    return out if n_taken else out[0]


def grad_kernel(wplan, n_g, n_w, meta_ref, *refs):
    g_in, w_in = refs[:n_g], refs[n_g:n_g + n_w]
    own_ref, other_ref = refs[n_g + n_w:n_g + n_w + 2]
    gbuf, wbuf, total, gsems, wsems = refs[n_g + n_w + 2:]
    step = pl.program_id(0)
    half = own_ref.shape[0]
    wh = wbuf.shape[1] // 2

    slots = gbuf.shape[0]

    def g_copy(j):
        return pltpu.make_async_copy(g_in[j], gbuf.at[j % slots], gsems.at[j])

    def w_copy(n):
        ref, source, block, part = wplan[n]
        place = meta_ref[AT_W + block]
        return pltpu.make_async_copy(
            w_in[ref].at[pl.ds(source, wh)],
            wbuf.at[place, pl.ds(part * wh, wh)],
            wsems.at[part, place],
        )

    @pl.when(step == 0)
    def _():
        for j in range(slots):
            g_copy(j).start()
        for n in range(16):
            w_copy(n).start()

    for j in range(8):

        @pl.when(step == j)
        def _():
            g_copy(j).wait()

    place = meta_ref[AT_G + step]
    for part in range(2):
        pltpu.make_async_copy(
            w_in[0].at[pl.ds(0, wh)], wbuf.at[place, pl.ds(part * wh, wh)], wsems.at[part, place]
        ).wait()

    @pl.when(step == 0)
    def _():
        total[...] = jnp.dot(gbuf[0], wbuf[place], preferred_element_type=F32)

    @pl.when(step > 0)
    def _():
        total[...] += jnp.dot(gbuf[step % slots], wbuf[place], preferred_element_type=F32)

    for j in range(8 - slots):

        @pl.when(step == j)
        def _():
            g_copy(j + slots).start()

    @pl.when(step == 7)
    def _():
        own_ref[...] = total[:half, :]
        other_ref[...] = total[half:, :].astype(BF)


def attn_grad_part(g_pieces, w_pieces, wplan, meta):
    tokens, depth = g_pieces[0].shape
    width = w_pieces[0].shape[1]
    half = tokens // 2
    kernel = functools.partial(grad_kernel, wplan, len(g_pieces), len(w_pieces))
    whole = pl.BlockSpec(memory_space=pltpu.VMEM)
    return pl.pallas_call(
        kernel,
        grid_spec=pltpu.PrefetchScalarGridSpec(
            num_scalar_prefetch=1,
            grid=(8,),
            in_specs=[pl.BlockSpec(memory_space=pltpu.HBM)] * (len(g_pieces) + len(w_pieces)),
            out_specs=[whole, whole],
            scratch_shapes=[
                pltpu.VMEM((3, tokens, depth), BF),
                pltpu.VMEM((8, depth, width), BF),
                pltpu.VMEM((tokens, width), F32),
                pltpu.SemaphoreType.DMA((8,)),
                pltpu.SemaphoreType.DMA((2, 8)),
            ],
        ),
        out_shape=[
            jax.ShapeDtypeStruct((half, width), F32),
            jax.ShapeDtypeStruct((half, width), BF),
        ],
        compiler_params=params(26),
        cost_estimate=pl.CostEstimate(
            flops=16 * tokens * depth * width,
            bytes_accessed=20 * 2**20,
            transcendentals=0,
        ),
        name="attn_grad",
    )(meta, *g_pieces, *w_pieces)


def add_kernel(places, n_terms, plan, joined, meta_ref, buffer_ref, *refs):
    terms, outs = refs[:n_terms], refs[n_terms:-2]
    blocks, sems = refs[-2:]
    rows = blocks.shape[2]
    copies = [
        pltpu.make_async_copy(buffer_ref.at[:, meta_ref[places[n]]], blocks.at[n], sems.at[n])
        for n in range(blocks.shape[0])
    ]
    for copy in copies:
        copy.start()
    for copy in copies:
        copy.wait()
    for n, (block, half, extra) in enumerate(plan):
        value = blocks[block, half].astype(F32)
        for term, first in extra:
            value = value + terms[term][first:first + rows, :].astype(F32)
        if joined:
            outs[0][n * rows:(n + 1) * rows, :] = value.astype(BF)
        else:
            outs[n][...] = value.astype(BF)


def add_blocks(buffer, meta, places, terms, plan, joined=False):
    _, _, rows, width = buffer.shape
    here = pl.BlockSpec(memory_space=pltpu.VMEM)
    shapes = [(len(plan) * rows, width)] if joined else [(rows, width)] * len(plan)
    return pl.pallas_call(
        functools.partial(add_kernel, tuple(places), len(terms), plan, joined),
        grid_spec=pltpu.PrefetchScalarGridSpec(
            num_scalar_prefetch=1,
            grid=(1,),
            in_specs=[pl.BlockSpec(memory_space=pltpu.HBM)] + [here] * len(terms),
            out_specs=[here] * len(shapes),
            scratch_shapes=[
                pltpu.VMEM((len(places), 2, rows, width), BF),
                pltpu.SemaphoreType.DMA((len(places),)),
            ],
        ),
        out_shape=[jax.ShapeDtypeStruct(shape, BF) for shape in shapes],
        compiler_params=params(12),
        cost_estimate=pl.CostEstimate(
            flops=2**21, bytes_accessed=5 * 2**20, transcendentals=0
        ),
        name="add_blocks",
    )(meta, buffer, *terms)


def last_kernel(meta_ref, buffer_ref, across, nup, ndn, rup, up2, rdn, dn2, out_ref, block, sem):
    copy = pltpu.make_async_copy(buffer_ref.at[:, meta_ref[at_w(0, 0)]], block, sem)
    copy.start()
    copy.wait()
    half, quarter = nup.shape[0], up2.shape[0]
    for part in range(2):
        for n in range(2):
            rows = slice(n * quarter, (n + 1) * quarter)
            place = slice(part * half + n * quarter, part * half + (n + 1) * quarter)
            up, dn = nup[rows, :], ndn[rows, :]
            if part == 1:
                up = up2[...] if n else rup[2 * half:, :]
            else:
                dn = dn2[...] if n else rdn[2 * half:, :]
            out_ref[place, :] = (
                block[part, rows].astype(F32)
                + across[place, :].astype(F32)
                + up.astype(F32)
                + dn.astype(F32)
            ).astype(BF)


def last_sum(buffer, meta, *terms):
    _, _, rows, width = buffer.shape
    here = pl.BlockSpec(memory_space=pltpu.VMEM)
    return pl.pallas_call(
        last_kernel,
        grid_spec=pltpu.PrefetchScalarGridSpec(
            num_scalar_prefetch=1,
            grid=(1,),
            in_specs=[pl.BlockSpec(memory_space=pltpu.HBM)] + [here] * len(terms),
            out_specs=pl.BlockSpec((2 * rows, width), lambda i, m: (0, 0)),
            scratch_shapes=[pltpu.VMEM((2, rows, width), BF), pltpu.SemaphoreType.DMA],
        ),
        out_shape=jax.ShapeDtypeStruct((2 * rows, width), BF),
        compiler_params=params(12),
        cost_estimate=pl.CostEstimate(
            flops=2**21, bytes_accessed=5 * 2**20, transcendentals=0
        ),
        name="last_sum",
    )(meta, buffer, *terms)


def local(query_rows, key_rows, value_rows, output_grad, out_proj, segment_ids):
    count = query_rows.shape[0]
    half_d = output_grad.shape[1] // 2
    row, col = lax.axis_index("row"), lax.axis_index("col")
    meta = positions(row, col)
    k = row % 2

    g_keep = lax.dynamic_slice_in_dim(output_grad, k * half_d, half_d, 1)
    g_give = lax.dynamic_slice_in_dim(output_grad, (1 - k) * half_d, half_d, 1)
    g_got, meta = tied((move_row(g_give, dk=1), meta))
    g0 = jnp.concatenate([g_keep, g_got], 0)
    kv_earlier = passed_along(jnp.concatenate([key_rows, value_rows], 1), "row", 1)
    segments = segment_ids.reshape(-1, LANES)

    (out_proj,) = tied((out_proj,), g0)
    gxm = move_col(g0, dx=1)
    gxp = move_col(g0, dx=-1)
    gy = move_col(g0, dyl=1)
    wzm = move_row(out_proj, dz=1)
    wzp = move_row(out_proj, dz=-1)

    (query_held,) = tied((query_rows,), g0)
    attn_out, top, total = attend(meta, query_held, kv_earlier, key_rows, value_rows, segments)

    wzm, wzp, gxm, gxp, gy, attn_out = tied((wzm, wzp, gxm, gxp, gy, attn_out))

    hw = out_proj.shape[0] // 2
    gyxm = move_col(gy, dx=1)
    gyxp = move_col(gy, dx=-1)
    a_other = move_row(attn_out, dk=1)
    wo = move_row(wzm, dz=1)
    wy = move_row(out_proj, dyh=1)

    a_pair = jnp.concatenate([attn_out, a_other], 0)
    proj = project([g0, gxm, gxp, gy], a_pair, meta, range(4), None)

    go = move_col(gxm, dx=1)
    wo, wy, gyxm, gyxp, proj = tied((wo, wy, gyxm, gyxp, proj))
    gyo = move_col(gyxp, dx=-1)
    wyzm = move_row(wy, dz=1)
    wyzp = move_row(wy, dz=-1)
    wyo = move_row(wo, dyh=1)

    proj = project([gyxm, gyxp], a_pair, meta, (4, 5), proj)
    proj = project([go], a_pair, meta, (6,), proj)

    q = hw // 2
    far, up, dn = at_w(2, 1), at_w(1, 1), at_w(-1, 1)
    own_up, own_dn = at_w(1, 0), at_w(-1, 0)
    proj, give_far, give_up, give_dn, up2, dn2 = project(
        [gyo],
        a_pair,
        meta,
        (7,),
        proj,
        (
            (0, 0, far, 0, 0, hw), (0, hw, far, 1, 0, hw),
            (1, 0, up, 0, 0, hw), (1, hw, up, 1, 0, hw), (1, 2 * hw, own_up, 1, 0, q),
            (2, 0, dn, 0, 0, hw), (2, hw, dn, 1, 0, hw), (2, 2 * hw, own_dn, 0, 0, q),
            (3, 0, own_up, 1, q, q),
            (4, 0, own_dn, 0, q, q),
        ),
    )
    give_far, give_up, give_dn, wyzm, wyzp, wyo = tied(
        (give_far, give_up, give_dn, wyzm, wyzp, wyo)
    )
    ry = move_row(give_far, dyh=1)
    rup = move_row(give_up, dz=1)
    rdn = move_row(give_dn, dz=-1)

    g_pieces = [g0, gxm, gxp, gy, gyxm, gyxp, go, gyo]
    w_pieces = [out_proj, wzm, wzp, wy, wyzm, wyzp, wyo, wo]
    wplan = [(i, p * hw, i, p) for i in range(8) for p in range(2)]
    (meta,) = tied((meta,), give_up)
    grad_own, grad_give = attn_grad_part(g_pieces, w_pieces, wplan, meta)

    ry, grad_own, grad_give = tied((ry, grad_own, grad_give))

    far_up, far_dn = add_blocks(
        proj, meta, [at_w(2, 0)], [ry], ((0, 0, ((0, 0),)), (0, 1, ((0, hw),)))
    )
    fup = move_row(far_up, dz=1)
    fdn = move_row(far_dn, dz=-1)
    grad_got = move_row(grad_give, dk=1)
    rup, rdn = tied((rup, rdn), far_up)
    (across,) = add_blocks(
        proj,
        meta,
        [at_w(0, 1)],
        [rup, rdn],
        ((0, 0, ((0, 0), (1, 0))), (0, 1, ((0, hw), (1, hw)))),
        joined=True,
    )
    across = move_row(across, dyh=1)
    up2, dn2 = tied((up2, dn2), far_up)
    up2 = move_row(up2, dz=1)
    dn2 = move_row(dn2, dz=-1)

    attn_grad = (grad_own + grad_got.astype(F32)).astype(BF)
    (attn_grad,) = tied((attn_grad,), rup)
    part = functools.partial(
        attend_back, meta, query_rows, attn_grad, kv_earlier, key_rows, value_rows, segments, top, total
    )
    heads = query_rows.shape[1] // HD
    cut = 3 * heads // 8
    held = part((0, cut), None)

    fup, fdn, *held = tied((fup, fdn, *held))

    near_up, near_dn = add_blocks(
        proj,
        meta,
        [own_up, own_dn],
        [fup, fdn],
        ((0, 0, ((0, 0),)), (1, 1, ((1, 0),))),
    )
    nup = move_row(near_up, dz=1)
    ndn = move_row(near_dn, dz=-1)

    *held, up2, dn2 = tied((*held, up2, dn2), near_up)
    query_grad, dkey, dvalue = part((cut, heads), held)
    dkey, dvalue, nup, ndn = tied((dkey, dvalue, nup, ndn))
    back = passed_along(
        jnp.concatenate([dkey[:count], dvalue[:count]], 1).astype(BF), "row", -1
    ).astype(F32)
    key_grad = (dkey[count:] + back[:, :HD]).astype(BF)
    value_grad = (dvalue[count:] + back[:, HD:]).astype(BF)

    proj_grad = last_sum(proj, meta, across, nup, ndn, rup, up2, rdn, dn2)
    return (query_grad, key_grad, value_grad, proj_grad)


def solution(mesh):
    placed = (
        P("row", "col"),
        P("row", "col"),
        P("row", "col"),
        P("row", "col"),
        P("row", "col"),
        P(),
    )
    return jax.shard_map(
        local,
        mesh=mesh,
        in_specs=placed,
        out_specs=(P("row", "col"), P("row", "col"), P("row", "col"), P("row", "col")),
        check_vma=False,
    )
```

```python
import functools
import math

import jax
import jax.numpy as jnp
from jax import lax
from jax.experimental import pallas as pl
from jax.experimental.pallas import tpu as pltpu
from jax.sharding import PartitionSpec as P

HD = 128
SCALE = 1.0 / math.sqrt(HD)
NEG = -1e30
BF = jnp.bfloat16
F32 = jnp.float32

PLACES = 64

ZN, YN, KN, LN, XN = 4, 2, 2, 2, 4


AT_FIRST, AT_ROW, AT_EARLIER, AT_G, AT_W = 0, 1, 2, 8, 16
G_STEPS = [(0, 0), (0, -1), (0, 1), (1, 0), (1, -1), (1, 1), (0, 2), (1, 2)]
W_STEPS = [(0, 0), (-1, 0), (1, 0), (0, 1), (-1, 1), (1, 1), (2, 1), (2, 0)]
LANES = 128


def positions(row, col):
    z, yh, yl, x = row // 4, row // 2 % 2, col // 4, col % 4
    head = jnp.stack([(row == 0).astype(jnp.int32), row, jnp.maximum(row - 1, 0)] + [row] * 5)
    steps = [jnp.asarray([step[i] for step in order], jnp.int32) for order in (G_STEPS, W_STEPS) for i in (0, 1)]
    dyl, dx, dz, dyh = steps
    g = ((yl + dyl) & 1) * 4 + ((x + dx) & 3)
    w = ((z + dz) & 3) * 2 + ((yh + dyh) & 1)
    return jnp.concatenate([head, g, w])


def at_w(dz, dyh):
    return AT_W + W_STEPS.index((dz, dyh))


def move_row(value, dz=0, dyh=0, dk=0):
    pairs = []
    for z in range(ZN):
        for y in range(YN):
            for k in range(KN):
                source = (z * YN + y) * KN + k
                target = ((z + dz) % ZN * YN + (y + dyh) % YN) * KN + (k + dk) % KN
                pairs.append((source, target))
    return lax.ppermute(value, "row", pairs)


def move_col(value, dx=0, dyl=0):
    pairs = []
    for y in range(LN):
        for x in range(XN):
            pairs.append((y * XN + x, (y + dyl) % LN * XN + (x + dx) % XN))
    return lax.ppermute(value, "col", pairs)


def passed_along(value, axis, steps):
    count = lax.axis_size(axis)
    first, last = (max(0, -steps), min(count, count - steps))
    return lax.ppermute(value, axis, [(source, source + steps) for source in range(first, last)])


def tied(values, *others):
    held = lax.optimization_barrier((tuple(values), tuple(others)))
    return held[0]


def params(mib, **kw):
    return pltpu.CompilerParams(vmem_limit_bytes=mib * 1024 * 1024, **kw)


def prepare(meta_ref, seg_ref, kv_ref, k_ref, v_ref, bias_ref, k_pair, v_pair, turned, of_keys):
    count = k_ref.shape[0]
    parts = count // LANES
    first, row, earlier = meta_ref[AT_FIRST], meta_ref[AT_ROW], meta_ref[AT_EARLIER]
    own = [seg_ref[pl.ds(row * parts + i, 1), :] for i in range(parts)]
    before = [seg_ref[pl.ds(earlier * parts + i, 1), :] for i in range(parts)]
    key_at = lax.broadcasted_iota(jnp.int32, (LANES, LANES), 0)
    query_at = lax.broadcasted_iota(jnp.int32, (LANES, LANES), 1)
    for i, keys in enumerate(before + own):
        column = jnp.broadcast_to(keys.astype(F32), (LANES, LANES)).T
        for j in range(parts):
            ok = column == own[j].astype(F32)
            if i < parts:
                ok = ok & (first == 0)
            else:
                ok = ok & (key_at + (i - parts) * LANES <= query_at + j * LANES)
            bias_ref[i * LANES:(i + 1) * LANES, j * LANES:(j + 1) * LANES] = jnp.where(
                ok, 0.0, NEG
            ).astype(F32)
    k_pair[:count, :] = kv_ref[:, :HD]
    k_pair[count:, :] = k_ref[...]
    v_pair[:count, :] = kv_ref[:, HD:]
    v_pair[count:, :] = v_ref[...]
    turned[...] = (k_pair if of_keys else v_pair)[...].astype(F32).T.astype(BF)


def pair_scratch(count):
    return [
        pltpu.VMEM((2 * count, count), F32),
        pltpu.VMEM((2 * count, HD), BF),
        pltpu.VMEM((2 * count, HD), BF),
        pltpu.VMEM((HD, 2 * count), BF),
    ]


def chunk_list(count, width):
    return [(i * width, count + (i + 1) * width) for i in range(count // width)]


def fwd_kernel(
    meta_ref, q_ref, kv_ref, k_ref, v_ref, seg_ref, out_ref, top_ref, sum_ref,
    bias_ref, k_pair, v_pair, vt_ref,
):
    count = q_ref.shape[0]

    @pl.when(pl.program_id(0) == 0)
    def _():
        prepare(meta_ref, seg_ref, kv_ref, k_ref, v_ref, bias_ref, k_pair, v_pair, vt_ref, False)

    for start, keys in chunk_list(count, 256):
        cols = slice(start, start + 256)
        s = lax.dot_general(
            k_pair[:keys, :], q_ref[cols, :], (((1,), (1,)), ((), ())), preferred_element_type=F32
        )
        s = s * SCALE + bias_ref[:keys, cols]
        top = jnp.max(s, axis=0, keepdims=True)
        e = jnp.exp(s - top)
        total = jnp.sum(e, axis=0, keepdims=True)
        inv = 1.0 / total
        p = (e * inv).astype(BF)
        a = jnp.dot(vt_ref[:, :keys], p, preferred_element_type=F32)
        out_ref[cols, :] = a.T.astype(BF)
        top_ref[0, :, cols] = top
        sum_ref[0, :, cols] = inv


def attend(meta, query, kv_earlier, key_rows, value_rows, segments):
    count, width = query.shape
    heads = width // HD
    whole = lambda value: pl.BlockSpec(value.shape, lambda h, m: (0, 0))
    head = pl.BlockSpec((count, HD), lambda h, m: (0, h))
    stat = pl.BlockSpec((1, 1, count), lambda h, m: (h, 0, 0))
    return pl.pallas_call(
        fwd_kernel,
        grid_spec=pltpu.PrefetchScalarGridSpec(
            num_scalar_prefetch=1,
            grid=(heads,),
            in_specs=[head] + [whole(v) for v in (kv_earlier, key_rows, value_rows, segments)],
            out_specs=[head, stat, stat],
            scratch_shapes=pair_scratch(count),
        ),
        out_shape=[
            jax.ShapeDtypeStruct((count, width), BF),
            jax.ShapeDtypeStruct((heads, 1, count), F32),
            jax.ShapeDtypeStruct((heads, 1, count), F32),
        ],
        compiler_params=params(16),
        cost_estimate=pl.CostEstimate(
            flops=heads * 4 * 2 * 2 * count * count * HD,
            bytes_accessed=8 * 2**20,
            transcendentals=heads * 2 * count * count,
        ),
        name="attend",
    )(meta, query, kv_earlier, key_rows, value_rows, segments)


def bwd_kernel(
    n_held, last, meta_ref, q_ref, g_ref, kv_ref, k_ref, v_ref, seg_ref, top_ref, sum_ref, *refs
):
    dk_in, dv_in = refs[:2] if n_held else (None, None)
    dq_ref, dk_ref, dv_ref, bias_ref, k_pair, v_pair, kt_ref = refs[n_held:]
    count = q_ref.shape[0]

    @pl.when(pl.program_id(0) == 0)
    def _():
        prepare(meta_ref, seg_ref, kv_ref, k_ref, v_ref, bias_ref, k_pair, v_pair, kt_ref, True)
        if n_held:
            dk_ref[...] = dk_in[...]
            dv_ref[...] = dv_in[...]
        else:
            dk_ref[...] = jnp.zeros_like(dk_ref)
            dv_ref[...] = jnp.zeros_like(dv_ref)

    for start, keys in chunk_list(count, 256):
        cols = slice(start, start + 256)
        q = q_ref[cols, :]
        g = g_ref[cols, :]
        s = lax.dot_general(
            k_pair[:keys, :], q, (((1,), (1,)), ((), ())), preferred_element_type=F32
        )
        s = s * SCALE + bias_ref[:keys, cols]
        p = jnp.exp(s - top_ref[0, :, cols]) * sum_ref[0, :, cols]
        dp = lax.dot_general(
            v_pair[:keys, :], g, (((1,), (1,)), ((), ())), preferred_element_type=F32
        )
        delta = jnp.sum(p * dp, axis=0, keepdims=True)
        ds = (p * (dp - delta)).astype(BF)
        dq = jnp.dot(kt_ref[:, :keys], ds, preferred_element_type=F32) * SCALE
        dq_ref[cols, :] = dq.T.astype(BF)
        dk_ref[:keys, :] += jnp.dot(ds, q, preferred_element_type=F32)
        dv_ref[:keys, :] += jnp.dot(p.astype(BF), g, preferred_element_type=F32)

    if last:

        @pl.when(pl.program_id(0) == pl.num_programs(0) - 1)
        def _():
            dk_ref[...] = dk_ref[...] * SCALE


def attend_back(
    meta, query, grad, kv_earlier, key_rows, value_rows, segments, top, total, heads, held
):
    count, width = query.shape
    begin, end = heads
    last = end == width // HD
    whole = lambda value: pl.BlockSpec(value.shape, lambda h, m: (0, 0))
    head = pl.BlockSpec((count, HD), lambda h, m: (0, h + begin))
    stat = pl.BlockSpec((1, 1, count), lambda h, m: (h + begin, 0, 0))
    pair = pl.BlockSpec((2 * count, HD), lambda h, m: (0, 0))
    earlier = () if held is None else (held[1], held[2], held[0])
    return pl.pallas_call(
        functools.partial(bwd_kernel, len(earlier), last),
        grid_spec=pltpu.PrefetchScalarGridSpec(
            num_scalar_prefetch=1,
            grid=(end - begin,),
            in_specs=[head, head]
            + [whole(v) for v in (kv_earlier, key_rows, value_rows, segments)]
            + [stat, stat]
            + ([pair, pair, pl.BlockSpec(memory_space=pl.ANY)] if earlier else []),
            out_specs=[head, pair, pair],
            scratch_shapes=pair_scratch(count),
        ),
        out_shape=[
            jax.ShapeDtypeStruct((count, width), BF),
            jax.ShapeDtypeStruct((2 * count, HD), F32),
            jax.ShapeDtypeStruct((2 * count, HD), F32),
        ],
        input_output_aliases={11: 0} if earlier else {},
        compiler_params=params(22),
        cost_estimate=pl.CostEstimate(
            flops=(end - begin) * 10 * 2 * 2 * count * count * HD if begin else 2**20,
            bytes_accessed=6 * 2**20 if begin else 2**16,
            transcendentals=(end - begin) * 2 * count * count if begin else 0,
        ),
        name="attend_back",
    )(meta, query, grad, kv_earlier, key_rows, value_rows, segments, top, total, *earlier)


def proj_kernel(slots, held, plan, meta_ref, *refs):
    n_in = len(slots)
    pieces, a_ref = refs[:n_in], refs[n_in]
    refs = refs[n_in + 1 + held:]
    buffer_ref, taken = refs[0], refs[1:-3]
    done, sems, take_sems = refs[-3:]
    step = pl.program_id(0)
    rows = done.shape[2]

    def put(j):
        return pltpu.make_async_copy(done.at[j], buffer_ref.at[:, meta_ref[AT_G + slots[j]]], sems.at[j])

    def take(i, made):
        out, start, at, half, first, count = plan[i]
        if made is None:
            source = buffer_ref.at[half, meta_ref[at], pl.ds(first, count)]
        else:
            source = done.at[made, half, pl.ds(first, count)]
        target = taken[out].at[pl.ds(start, count)]
        return pltpu.make_async_copy(source, target, take_sems.at[i])

    def made_here(i, j):
        return meta_ref[plan[i][2]] == meta_ref[AT_G + slots[j]]

    @pl.when(step == 0)
    def _():
        for i in range(len(plan)):
            here = made_here(i, 0)
            for j in range(1, n_in):
                here = here | made_here(i, j)

            @pl.when(jnp.logical_not(here))
            def _():
                take(i, None).start()

    for j in range(n_in):

        @pl.when(step == j)
        def _():
            value = lax.dot_general(
                pieces[j][...], a_ref[...], (((0,), (0,)), ((), ())), preferred_element_type=F32
            ).astype(BF)
            done[j, 0] = value[:rows]
            done[j, 1] = value[rows:]
            put(j).start()
            for i in range(len(plan)):

                @pl.when(made_here(i, j))
                def _():
                    take(i, j).start()

    @pl.when(step == n_in - 1)
    def _():
        for j in range(n_in):
            put(j).wait()
        for i in range(len(plan)):
            take(i, None).wait()


def project(pieces, a_pair, meta, slots, buffer, plan=()):
    tokens, width = a_pair.shape
    depth = pieces[0].shape[1]
    n_blocks = len(pieces)
    held = int(buffer is not None)
    here = pl.BlockSpec(memory_space=pltpu.VMEM)
    there = pl.BlockSpec(memory_space=pltpu.HBM)
    operands = (*pieces, a_pair) + ((buffer,) if held else ())
    shape = (2, depth // 2, width)
    n_taken = 1 + max((entry[0] for entry in plan), default=-1)
    taken = [(sum(e[5] for e in plan if e[0] == i), width) for i in range(n_taken)]
    out = pl.pallas_call(
        functools.partial(proj_kernel, tuple(slots), held, plan),
        grid_spec=pltpu.PrefetchScalarGridSpec(
            num_scalar_prefetch=1,
            grid=(n_blocks,),
            in_specs=[here] * (n_blocks + 1) + [there] * held,
            out_specs=[there] + [here] * n_taken,
            scratch_shapes=[
                pltpu.VMEM((n_blocks, *shape), BF),
                pltpu.SemaphoreType.DMA((n_blocks,)),
                pltpu.SemaphoreType.DMA((max(len(plan), 1),)),
            ],
        ),
        out_shape=[jax.ShapeDtypeStruct((2, PLACES, depth // 2, width), BF)]
        + [jax.ShapeDtypeStruct(t, BF) for t in taken],
        input_output_aliases={n_blocks + 2: 0} if held else {},
        compiler_params=params(16),
        cost_estimate=pl.CostEstimate(
            flops=2 * n_blocks * tokens * depth * width,
            bytes_accessed=(2 * n_blocks + 2) * 2**20,
            transcendentals=0,
        ),
        name="project",
    )(meta, *operands)
    return out if n_taken else out[0]


def grad_kernel(wplan, n_g, n_w, meta_ref, *refs):
    g_in, w_in = refs[:n_g], refs[n_g:n_g + n_w]
    own_ref, lo_ref, hi_ref = refs[n_g + n_w:n_g + n_w + 3]
    gbuf, wbuf, total, gsems, wsems = refs[n_g + n_w + 3:]
    step = pl.program_id(0)
    half = own_ref.shape[0]
    wh = wbuf.shape[1] // 2

    slots = gbuf.shape[0]

    def g_copy(j):
        return pltpu.make_async_copy(g_in[j], gbuf.at[j % slots], gsems.at[j])

    def w_copy(n):
        ref, source, block, part = wplan[n]
        place = meta_ref[AT_W + block]
        return pltpu.make_async_copy(
            w_in[ref].at[pl.ds(source, wh)],
            wbuf.at[place, pl.ds(part * wh, wh)],
            wsems.at[part, place],
        )

    @pl.when(step == 0)
    def _():
        for j in range(slots):
            g_copy(j).start()
        for n in range(16):
            w_copy(n).start()

    for j in range(8):

        @pl.when(step == j)
        def _():
            g_copy(j).wait()

    place = meta_ref[AT_G + step]
    for part in range(2):
        pltpu.make_async_copy(
            w_in[0].at[pl.ds(0, wh)], wbuf.at[place, pl.ds(part * wh, wh)], wsems.at[part, place]
        ).wait()

    @pl.when(step == 0)
    def _():
        total[...] = jnp.dot(gbuf[0], wbuf[place], preferred_element_type=F32)

    @pl.when(step > 0)
    def _():
        total[...] += jnp.dot(gbuf[step % slots], wbuf[place], preferred_element_type=F32)

    for j in range(8 - slots):

        @pl.when(step == j)
        def _():
            g_copy(j + slots).start()

    @pl.when(step == 7)
    def _():
        own_ref[...] = total[:half, :]
        lo_ref[...] = total[half:half + half // 2, :].astype(BF)
        hi_ref[...] = total[half + half // 2:, :].astype(BF)


def attn_grad_part(g_pieces, w_pieces, wplan, meta):
    tokens, depth = g_pieces[0].shape
    width = w_pieces[0].shape[1]
    half = tokens // 2
    kernel = functools.partial(grad_kernel, wplan, len(g_pieces), len(w_pieces))
    whole = pl.BlockSpec(memory_space=pltpu.VMEM)
    return pl.pallas_call(
        kernel,
        grid_spec=pltpu.PrefetchScalarGridSpec(
            num_scalar_prefetch=1,
            grid=(8,),
            in_specs=[pl.BlockSpec(memory_space=pltpu.HBM)] * (len(g_pieces) + len(w_pieces)),
            out_specs=[whole] * 3,
            scratch_shapes=[
                pltpu.VMEM((3, tokens, depth), BF),
                pltpu.VMEM((8, depth, width), BF),
                pltpu.VMEM((tokens, width), F32),
                pltpu.SemaphoreType.DMA((8,)),
                pltpu.SemaphoreType.DMA((2, 8)),
            ],
        ),
        out_shape=[
            jax.ShapeDtypeStruct((half, width), F32),
            jax.ShapeDtypeStruct((half // 2, width), BF),
            jax.ShapeDtypeStruct((half // 2, width), BF),
        ],
        compiler_params=params(26),
        cost_estimate=pl.CostEstimate(
            flops=16 * tokens * depth * width,
            bytes_accessed=20 * 2**20,
            transcendentals=0,
        ),
        name="attn_grad",
    )(meta, *g_pieces, *w_pieces)


def fetch_kernel(plan, meta_ref, buffer_ref, *refs):
    outs, sems = refs[:-1], refs[-1]
    copies = []
    for n, (out, start, at, half) in enumerate(plan):
        source = buffer_ref.at[half, meta_ref[at]]
        target = outs[out].at[pl.ds(start, source.shape[0])]
        copies.append(pltpu.make_async_copy(source, target, sems.at[n]))
    for copy in copies:
        copy.start()
    for copy in copies:
        copy.wait()


def fetch(buffer, meta, plan):
    _, _, rows, width = buffer.shape
    n_out = 1 + plan[-1][0]
    here = pl.BlockSpec(memory_space=pltpu.VMEM)
    return pl.pallas_call(
        functools.partial(fetch_kernel, plan),
        grid_spec=pltpu.PrefetchScalarGridSpec(
            num_scalar_prefetch=1,
            grid=(1,),
            in_specs=[pl.BlockSpec(memory_space=pltpu.HBM)],
            out_specs=[here] * n_out,
            scratch_shapes=[pltpu.SemaphoreType.DMA((len(plan),))],
        ),
        out_shape=[jax.ShapeDtypeStruct((2 * rows, width), BF)] * n_out,
        compiler_params=params(8),
        cost_estimate=pl.CostEstimate(
            flops=0, bytes_accessed=2**16, transcendentals=0
        ),
        name="fetch",
    )(meta, buffer)


def add_kernel(n_terms, plan, *refs):
    terms, outs = refs[:n_terms], refs[n_terms:]
    for out, start, rows, parts in plan:
        value = None
        for term, first in parts:
            part = terms[term][first:first + rows, :].astype(F32)
            value = part if value is None else value + part
        outs[out][start:start + rows, :] = value.astype(BF)


def add_rows(terms, plan, result=False):
    width = terms[0].shape[1]
    n_out = 1 + plan[-1][0]
    shapes = [(sum(p[2] for p in plan if p[0] == n), width) for n in range(n_out)]
    here = pl.BlockSpec(memory_space=pltpu.VMEM)
    outs = [pl.BlockSpec(shape, lambda i: (0, 0)) if result else here for shape in shapes]
    return pl.pallas_call(
        functools.partial(add_kernel, len(terms), plan),
        grid=(1,),
        in_specs=[here] * len(terms),
        out_specs=outs,
        out_shape=[jax.ShapeDtypeStruct(shape, BF) for shape in shapes],
        compiler_params=params(12),
        cost_estimate=pl.CostEstimate(
            flops=2**21, bytes_accessed=5 * 2**20, transcendentals=0
        ),
        name="add_rows",
    )(*terms)


def local(query_rows, key_rows, value_rows, output_grad, out_proj, segment_ids):
    count = query_rows.shape[0]
    half_d = output_grad.shape[1] // 2
    row, col = lax.axis_index("row"), lax.axis_index("col")
    meta = positions(row, col)
    k = row % 2

    g_keep = lax.dynamic_slice_in_dim(output_grad, k * half_d, half_d, 1)
    g_give = lax.dynamic_slice_in_dim(output_grad, (1 - k) * half_d, half_d, 1)
    g_got, meta = tied((move_row(g_give, dk=1), meta))
    g0 = jnp.concatenate([g_keep, g_got], 0)
    kv_earlier = passed_along(jnp.concatenate([key_rows, value_rows], 1), "row", 1)
    segments = segment_ids.reshape(-1, LANES)

    (out_proj,) = tied((out_proj,), g0)
    gxm = move_col(g0, dx=1)
    gxp = move_col(g0, dx=-1)
    gy = move_col(g0, dyl=1)
    wzm = move_row(out_proj, dz=1)
    wzp = move_row(out_proj, dz=-1)

    (query_held,) = tied((query_rows,), g0)
    attn_out, top, total = attend(meta, query_held, kv_earlier, key_rows, value_rows, segments)

    gxm, gxp, gy, attn_out = tied((gxm, gxp, gy, attn_out))
    wzm, wzp, out_proj = tied((wzm, wzp, out_proj), gxm)

    hw = out_proj.shape[0] // 2
    gyxm = move_col(gy, dx=1)
    gyxp = move_col(gy, dx=-1)
    a_other = move_row(attn_out, dk=1)
    wo = move_row(wzm, dz=1)
    wy = move_row(out_proj, dyh=1)

    a_pair = jnp.concatenate([attn_out, a_other], 0)
    proj = project([g0, gxm, gxp, gy], a_pair, meta, range(4), None)

    go = move_col(gxm, dx=1)
    gyxm, gyxp, proj = tied((gyxm, gyxp, proj))
    gyo = move_col(gyxp, dx=-1)
    wo, wy = tied((wo, wy), gyxp)
    wyzm = move_row(wy, dz=1)
    wyzp = move_row(wy, dz=-1)
    wyo = move_row(wo, dyh=1)

    proj = project([gyxm, gyxp], a_pair, meta, (4, 5), proj)
    proj = project([go], a_pair, meta, (6,), proj)

    q = hw // 2
    far, up, dn = at_w(2, 1), at_w(1, 1), at_w(-1, 1)
    own_up, own_dn = at_w(1, 0), at_w(-1, 0)
    proj, give_far, give_up, give_dn, up2, dn2 = project(
        [gyo],
        a_pair,
        meta,
        (7,),
        proj,
        (
            (0, 0, far, 0, 0, hw), (0, hw, far, 1, 0, hw),
            (1, 0, up, 0, 0, hw), (1, hw, up, 1, 0, hw), (1, 2 * hw, own_up, 1, 0, q),
            (2, 0, dn, 0, 0, hw), (2, hw, dn, 1, 0, hw), (2, 2 * hw, own_dn, 0, 0, q),
            (3, 0, own_up, 1, q, q),
            (4, 0, own_dn, 0, q, q),
        ),
    )
    give_far, give_up, give_dn, wyzm, wyzp, wyo = tied(
        (give_far, give_up, give_dn, wyzm, wyzp, wyo)
    )
    ry = move_row(give_far, dyh=1)
    rup = move_row(give_up, dz=1)
    rdn = move_row(give_dn, dz=-1)

    g_pieces = [g0, gxm, gxp, gy, gyxm, gyxp, go, gyo]
    w_pieces = [out_proj, wzm, wzp, wy, wyzm, wyzp, wyo, wo]
    wplan = [(i, p * hw, i, p) for i in range(8) for p in range(2)]
    (meta,) = tied((meta,), give_up)
    grad_own, give_lo, give_hi = attn_grad_part(g_pieces, w_pieces, wplan, meta)
    got_lo, got_hi = move_row(give_lo, dk=1), move_row(give_hi, dk=1)
    far, middle, near, own = fetch(
        proj,
        meta,
        (
            (0, 0, at_w(2, 0), 0), (0, hw, at_w(2, 0), 1),
            (1, 0, at_w(0, 1), 0), (1, hw, at_w(0, 1), 1),
            (2, 0, own_up, 0), (2, hw, own_dn, 1),
            (3, 0, at_w(0, 0), 0), (3, hw, at_w(0, 0), 1),
        ),
    )
    (attn_grad,) = add_rows(
        [grad_own, got_lo, got_hi],
        ((0, 0, hw, ((0, 0), (1, 0))), (0, hw, hw, ((0, hw), (2, 0)))),
    )
    part = functools.partial(
        attend_back, meta, query_rows, attn_grad, kv_earlier, key_rows, value_rows, segments, top, total
    )
    heads = query_rows.shape[1] // HD
    cuts = heads // 4, 5 * heads // 8
    held = part((0, cuts[0]), None)

    ry, *held = tied((ry, *held))

    far_up, far_dn = add_rows(
        [far, ry], ((0, 0, hw, ((0, 0), (1, 0))), (1, 0, hw, ((0, hw), (1, hw))))
    )
    fup = move_row(far_up, dz=1)
    fdn = move_row(far_dn, dz=-1)
    rup, rdn, up2, dn2 = tied((rup, rdn, up2, dn2), far_up)
    (across,) = add_rows([middle, rup, rdn], ((0, 0, 2 * hw, ((0, 0), (1, 0), (2, 0))),))
    held = tied(held, across)
    across = move_row(across, dyh=1)
    up2 = move_row(up2, dz=1)
    dn2 = move_row(dn2, dz=-1)
    held = part(cuts, held)

    fup, fdn, *held = tied((fup, fdn, *held))

    near_up, near_dn = add_rows(
        [near, fup, fdn], ((0, 0, hw, ((0, 0), (1, 0))), (1, 0, hw, ((0, hw), (2, 0))))
    )
    nup = move_row(near_up, dz=1)
    ndn = move_row(near_dn, dz=-1)

    *held, up2, dn2 = tied((*held, up2, dn2), near_up)
    query_grad, dkey, dvalue = part((cuts[1], heads), held)
    back = passed_along(
        jnp.concatenate([dkey[:count], dvalue[:count]], 1).astype(BF), "row", -1
    ).astype(F32)
    key_grad = (dkey[count:] + back[:, :HD]).astype(BF)
    value_grad = (dvalue[count:] + back[:, HD:]).astype(BF)

    (proj_grad,) = add_rows(
        [own, across, nup, ndn, rup, up2, rdn, dn2],
        (
            (0, 0, q, ((0, 0), (1, 0), (2, 0), (6, 2 * hw))),
            (0, q, q, ((0, q), (1, q), (2, q), (7, 0))),
            (0, 2 * q, q, ((0, 2 * q), (1, 2 * q), (4, 2 * hw), (3, 0))),
            (0, 3 * q, q, ((0, 3 * q), (1, 3 * q), (5, 0), (3, q))),
        ),
        result=True,
    )
    return (query_grad, key_grad, value_grad, proj_grad)


def solution(mesh):
    placed = (
        P("row", "col"),
        P("row", "col"),
        P("row", "col"),
        P("row", "col"),
        P("row", "col"),
        P(),
    )
    return jax.shard_map(
        local,
        mesh=mesh,
        in_specs=placed,
        out_specs=(P("row", "col"), P("row", "col"), P("row", "col"), P("row", "col")),
        check_vma=False,
    )
```

```python
import functools
import math

import jax
import jax.numpy as jnp
from jax import lax
from jax.experimental import pallas as pl
from jax.experimental.pallas import tpu as pltpu
from jax.sharding import PartitionSpec as P

HD = 128
SCALE = 1.0 / math.sqrt(HD)
NEG = -1e30
BF = jnp.bfloat16
F32 = jnp.float32

PLACES = 64

ZN, YN, KN, LN, XN = 4, 2, 2, 2, 4


AT_FIRST, AT_ROW, AT_EARLIER, AT_G, AT_W = 0, 1, 2, 8, 16
G_STEPS = [(0, 0), (0, -1), (0, 1), (1, 0), (1, -1), (1, 1), (0, 2), (1, 2)]
W_STEPS = [(0, 0), (-1, 0), (1, 0), (0, 1), (-1, 1), (1, 1), (2, 1), (2, 0)]
LANES = 128


def positions(row, col):
    z, yh, yl, x = row // 4, row // 2 % 2, col // 4, col % 4
    head = jnp.stack([(row == 0).astype(jnp.int32), row, jnp.maximum(row - 1, 0)] + [row] * 5)
    steps = [jnp.asarray([step[i] for step in order], jnp.int32) for order in (G_STEPS, W_STEPS) for i in (0, 1)]
    dyl, dx, dz, dyh = steps
    g = ((yl + dyl) & 1) * 4 + ((x + dx) & 3)
    w = ((z + dz) & 3) * 2 + ((yh + dyh) & 1)
    return jnp.concatenate([head, g, w])


def at_w(dz, dyh):
    return AT_W + W_STEPS.index((dz, dyh))


def move_row(value, dz=0, dyh=0, dk=0):
    pairs = []
    for z in range(ZN):
        for y in range(YN):
            for k in range(KN):
                source = (z * YN + y) * KN + k
                target = ((z + dz) % ZN * YN + (y + dyh) % YN) * KN + (k + dk) % KN
                pairs.append((source, target))
    return lax.ppermute(value, "row", pairs)


def move_col(value, dx=0, dyl=0):
    pairs = []
    for y in range(LN):
        for x in range(XN):
            pairs.append((y * XN + x, (y + dyl) % LN * XN + (x + dx) % XN))
    return lax.ppermute(value, "col", pairs)


def passed_along(value, axis, steps):
    count = lax.axis_size(axis)
    first, last = (max(0, -steps), min(count, count - steps))
    return lax.ppermute(value, axis, [(source, source + steps) for source in range(first, last)])


def tied(values, *others):
    held = lax.optimization_barrier((tuple(values), tuple(others)))
    return held[0]


def params(mib, **kw):
    return pltpu.CompilerParams(vmem_limit_bytes=mib * 1024 * 1024, **kw)


def prepare(meta_ref, seg_ref, kv_ref, k_ref, v_ref, bias_ref, k_pair, v_pair, turned, of_keys):
    count = k_ref.shape[0]
    parts = count // LANES
    first, row, earlier = meta_ref[AT_FIRST], meta_ref[AT_ROW], meta_ref[AT_EARLIER]
    own = [seg_ref[pl.ds(row * parts + i, 1), :] for i in range(parts)]
    before = [seg_ref[pl.ds(earlier * parts + i, 1), :] for i in range(parts)]
    key_at = lax.broadcasted_iota(jnp.int32, (LANES, LANES), 0)
    query_at = lax.broadcasted_iota(jnp.int32, (LANES, LANES), 1)
    for i, keys in enumerate(before + own):
        column = jnp.broadcast_to(keys.astype(F32), (LANES, LANES)).T
        for j in range(parts):
            ok = column == own[j].astype(F32)
            if i < parts:
                ok = ok & (first == 0)
            else:
                ok = ok & (key_at + (i - parts) * LANES <= query_at + j * LANES)
            bias_ref[i * LANES:(i + 1) * LANES, j * LANES:(j + 1) * LANES] = jnp.where(
                ok, 0.0, NEG
            ).astype(F32)
    k_pair[:count, :] = kv_ref[:, :HD]
    k_pair[count:, :] = k_ref[...]
    v_pair[:count, :] = kv_ref[:, HD:]
    v_pair[count:, :] = v_ref[...]
    turned[...] = (k_pair if of_keys else v_pair)[...].astype(F32).T.astype(BF)


def pair_scratch(count):
    return [
        pltpu.VMEM((2 * count, count), F32),
        pltpu.VMEM((2 * count, HD), BF),
        pltpu.VMEM((2 * count, HD), BF),
        pltpu.VMEM((HD, 2 * count), BF),
    ]


def chunk_list(count, width):
    return [(i * width, count + (i + 1) * width) for i in range(count // width)]


def fwd_kernel(
    meta_ref, q_ref, kv_ref, k_ref, v_ref, seg_ref, out_ref, top_ref, sum_ref,
    bias_ref, k_pair, v_pair, vt_ref,
):
    count = q_ref.shape[0]

    @pl.when(pl.program_id(0) == 0)
    def _():
        prepare(meta_ref, seg_ref, kv_ref, k_ref, v_ref, bias_ref, k_pair, v_pair, vt_ref, False)

    for start, keys in chunk_list(count, 256):
        cols = slice(start, start + 256)
        s = lax.dot_general(
            k_pair[:keys, :], q_ref[cols, :], (((1,), (1,)), ((), ())), preferred_element_type=F32
        )
        s = s * SCALE + bias_ref[:keys, cols]
        top = jnp.max(s, axis=0, keepdims=True)
        e = jnp.exp(s - top)
        total = jnp.sum(e, axis=0, keepdims=True)
        inv = 1.0 / total
        p = (e * inv).astype(BF)
        a = jnp.dot(vt_ref[:, :keys], p, preferred_element_type=F32)
        out_ref[cols, :] = a.T.astype(BF)
        top_ref[0, :, cols] = top
        sum_ref[0, :, cols] = inv


def attend(meta, query, kv_earlier, key_rows, value_rows, segments):
    count, width = query.shape
    heads = width // HD
    whole = lambda value: pl.BlockSpec(value.shape, lambda h, m: (0, 0))
    head = pl.BlockSpec((count, HD), lambda h, m: (0, h))
    stat = pl.BlockSpec((1, 1, count), lambda h, m: (h, 0, 0))
    return pl.pallas_call(
        fwd_kernel,
        grid_spec=pltpu.PrefetchScalarGridSpec(
            num_scalar_prefetch=1,
            grid=(heads,),
            in_specs=[head] + [whole(v) for v in (kv_earlier, key_rows, value_rows, segments)],
            out_specs=[head, stat, stat],
            scratch_shapes=pair_scratch(count),
        ),
        out_shape=[
            jax.ShapeDtypeStruct((count, width), BF),
            jax.ShapeDtypeStruct((heads, 1, count), F32),
            jax.ShapeDtypeStruct((heads, 1, count), F32),
        ],
        compiler_params=params(16),
        cost_estimate=pl.CostEstimate(
            flops=heads * 4 * 2 * 2 * count * count * HD,
            bytes_accessed=8 * 2**20,
            transcendentals=heads * 2 * count * count,
        ),
        name="attend",
    )(meta, query, kv_earlier, key_rows, value_rows, segments)


def bwd_kernel(
    n_held, last, meta_ref, q_ref, g_ref, kv_ref, k_ref, v_ref, seg_ref, top_ref, sum_ref, *refs
):
    dk_in, dv_in = refs[:2] if n_held else (None, None)
    dq_ref, dk_ref, dv_ref, bias_ref, k_pair, v_pair, kt_ref = refs[n_held:]
    count = q_ref.shape[0]

    @pl.when(pl.program_id(0) == 0)
    def _():
        prepare(meta_ref, seg_ref, kv_ref, k_ref, v_ref, bias_ref, k_pair, v_pair, kt_ref, True)
        if n_held:
            dk_ref[...] = dk_in[...]
            dv_ref[...] = dv_in[...]
        else:
            dk_ref[...] = jnp.zeros_like(dk_ref)
            dv_ref[...] = jnp.zeros_like(dv_ref)

    for start, keys in chunk_list(count, 256):
        cols = slice(start, start + 256)
        q = q_ref[cols, :]
        g = g_ref[cols, :]
        s = lax.dot_general(
            k_pair[:keys, :], q, (((1,), (1,)), ((), ())), preferred_element_type=F32
        )
        s = s * SCALE + bias_ref[:keys, cols]
        p = jnp.exp(s - top_ref[0, :, cols]) * sum_ref[0, :, cols]
        dp = lax.dot_general(
            v_pair[:keys, :], g, (((1,), (1,)), ((), ())), preferred_element_type=F32
        )
        delta = jnp.sum(p * dp, axis=0, keepdims=True)
        ds = (p * (dp - delta)).astype(BF)
        dq = jnp.dot(kt_ref[:, :keys], ds, preferred_element_type=F32) * SCALE
        dq_ref[cols, :] = dq.T.astype(BF)
        dk_ref[:keys, :] += jnp.dot(ds, q, preferred_element_type=F32)
        dv_ref[:keys, :] += jnp.dot(p.astype(BF), g, preferred_element_type=F32)

    if last:

        @pl.when(pl.program_id(0) == pl.num_programs(0) - 1)
        def _():
            dk_ref[...] = dk_ref[...] * SCALE


def attend_back(
    meta, query, grad, kv_earlier, key_rows, value_rows, segments, top, total, heads, held
):
    count, width = query.shape
    begin, end = heads
    last = end == width // HD
    whole = lambda value: pl.BlockSpec(value.shape, lambda h, m: (0, 0))
    head = pl.BlockSpec((count, HD), lambda h, m: (0, h + begin))
    stat = pl.BlockSpec((1, 1, count), lambda h, m: (h + begin, 0, 0))
    pair = pl.BlockSpec((2 * count, HD), lambda h, m: (0, 0))
    earlier = () if held is None else (held[1], held[2], held[0])
    return pl.pallas_call(
        functools.partial(bwd_kernel, len(earlier), last),
        grid_spec=pltpu.PrefetchScalarGridSpec(
            num_scalar_prefetch=1,
            grid=(end - begin,),
            in_specs=[head, head]
            + [whole(v) for v in (kv_earlier, key_rows, value_rows, segments)]
            + [stat, stat]
            + ([pair, pair, pl.BlockSpec(memory_space=pl.ANY)] if earlier else []),
            out_specs=[head, pair, pair],
            scratch_shapes=pair_scratch(count),
        ),
        out_shape=[
            jax.ShapeDtypeStruct((count, width), BF),
            jax.ShapeDtypeStruct((2 * count, HD), F32),
            jax.ShapeDtypeStruct((2 * count, HD), F32),
        ],
        input_output_aliases={11: 0} if earlier else {},
        compiler_params=params(22),
        cost_estimate=pl.CostEstimate(
            flops=(end - begin) * 10 * 2 * 2 * count * count * HD if begin else 2**20,
            bytes_accessed=6 * 2**20 if begin else 2**16,
            transcendentals=(end - begin) * 2 * count * count if begin else 0,
        ),
        name="attend_back",
    )(meta, query, grad, kv_earlier, key_rows, value_rows, segments, top, total, *earlier)


def proj_kernel(slots, held, plan, meta_ref, *refs):
    n_in = len(slots)
    pieces, a_ref = refs[:n_in], refs[n_in]
    refs = refs[n_in + 1 + held:]
    buffer_ref, taken = refs[0], refs[1:-3]
    done, sems, take_sems = refs[-3:]
    step = pl.program_id(0)
    rows = done.shape[2]

    def put(j):
        return pltpu.make_async_copy(done.at[j], buffer_ref.at[:, meta_ref[AT_G + slots[j]]], sems.at[j])

    def take(i, made):
        out, start, at, half, first, count = plan[i]
        if made is None:
            source = buffer_ref.at[half, meta_ref[at], pl.ds(first, count)]
        else:
            source = done.at[made, half, pl.ds(first, count)]
        target = taken[out].at[pl.ds(start, count)]
        return pltpu.make_async_copy(source, target, take_sems.at[i])

    def made_here(i, j):
        return meta_ref[plan[i][2]] == meta_ref[AT_G + slots[j]]

    @pl.when(step == 0)
    def _():
        for i in range(len(plan)):
            here = made_here(i, 0)
            for j in range(1, n_in):
                here = here | made_here(i, j)

            @pl.when(jnp.logical_not(here))
            def _():
                take(i, None).start()

    for j in range(n_in):

        @pl.when(step == j)
        def _():
            value = lax.dot_general(
                pieces[j][...], a_ref[...], (((0,), (0,)), ((), ())), preferred_element_type=F32
            ).astype(BF)
            done[j, 0] = value[:rows]
            done[j, 1] = value[rows:]
            put(j).start()
            for i in range(len(plan)):

                @pl.when(made_here(i, j))
                def _():
                    take(i, j).start()

    @pl.when(step == n_in - 1)
    def _():
        for j in range(n_in):
            put(j).wait()
        for i in range(len(plan)):
            take(i, None).wait()


def project(pieces, a_pair, meta, slots, buffer, plan=()):
    tokens, width = a_pair.shape
    depth = pieces[0].shape[1]
    n_blocks = len(pieces)
    held = int(buffer is not None)
    here = pl.BlockSpec(memory_space=pltpu.VMEM)
    there = pl.BlockSpec(memory_space=pltpu.HBM)
    operands = (*pieces, a_pair) + ((buffer,) if held else ())
    shape = (2, depth // 2, width)
    n_taken = 1 + max((entry[0] for entry in plan), default=-1)
    taken = [(sum(e[5] for e in plan if e[0] == i), width) for i in range(n_taken)]
    out = pl.pallas_call(
        functools.partial(proj_kernel, tuple(slots), held, plan),
        grid_spec=pltpu.PrefetchScalarGridSpec(
            num_scalar_prefetch=1,
            grid=(n_blocks,),
            in_specs=[here] * (n_blocks + 1) + [there] * held,
            out_specs=[there] + [here] * n_taken,
            scratch_shapes=[
                pltpu.VMEM((n_blocks, *shape), BF),
                pltpu.SemaphoreType.DMA((n_blocks,)),
                pltpu.SemaphoreType.DMA((max(len(plan), 1),)),
            ],
        ),
        out_shape=[jax.ShapeDtypeStruct((2, PLACES, depth // 2, width), BF)]
        + [jax.ShapeDtypeStruct(t, BF) for t in taken],
        input_output_aliases={n_blocks + 2: 0} if held else {},
        compiler_params=params(16),
        cost_estimate=pl.CostEstimate(
            flops=2 * n_blocks * tokens * depth * width,
            bytes_accessed=(2 * n_blocks + 2) * 2**20,
            transcendentals=0,
        ),
        name="project",
    )(meta, *operands)
    return out if n_taken else out[0]


def grad_kernel(wplan, n_g, n_w, meta_ref, *refs):
    g_in, w_in = refs[:n_g], refs[n_g:n_g + n_w]
    own_ref, lo_ref, hi_ref = refs[n_g + n_w:n_g + n_w + 3]
    gbuf, wbuf, total, gsems, wsems = refs[n_g + n_w + 3:]
    step = pl.program_id(0)
    half = own_ref.shape[0]
    wh = wbuf.shape[1] // 2

    slots = gbuf.shape[0]

    def g_copy(j):
        return pltpu.make_async_copy(g_in[j], gbuf.at[j % slots], gsems.at[j])

    def w_copy(n):
        ref, source, block, part = wplan[n]
        place = meta_ref[AT_W + block]
        return pltpu.make_async_copy(
            w_in[ref].at[pl.ds(source, wh)],
            wbuf.at[place, pl.ds(part * wh, wh)],
            wsems.at[part, place],
        )

    @pl.when(step == 0)
    def _():
        for j in range(slots):
            g_copy(j).start()
        for n in range(16):
            w_copy(n).start()

    for j in range(8):

        @pl.when(step == j)
        def _():
            g_copy(j).wait()

    place = meta_ref[AT_G + step]
    for part in range(2):
        pltpu.make_async_copy(
            w_in[0].at[pl.ds(0, wh)], wbuf.at[place, pl.ds(part * wh, wh)], wsems.at[part, place]
        ).wait()

    @pl.when(step == 0)
    def _():
        total[...] = jnp.dot(gbuf[0], wbuf[place], preferred_element_type=F32)

    @pl.when(step > 0)
    def _():
        total[...] += jnp.dot(gbuf[step % slots], wbuf[place], preferred_element_type=F32)

    for j in range(8 - slots):

        @pl.when(step == j)
        def _():
            g_copy(j + slots).start()

    @pl.when(step == 7)
    def _():
        own_ref[...] = total[:half, :]
        lo_ref[...] = total[half:half + half // 2, :].astype(BF)
        hi_ref[...] = total[half + half // 2:, :].astype(BF)


def attn_grad_part(g_pieces, w_pieces, wplan, meta):
    tokens, depth = g_pieces[0].shape
    width = w_pieces[0].shape[1]
    half = tokens // 2
    kernel = functools.partial(grad_kernel, wplan, len(g_pieces), len(w_pieces))
    whole = pl.BlockSpec(memory_space=pltpu.VMEM)
    return pl.pallas_call(
        kernel,
        grid_spec=pltpu.PrefetchScalarGridSpec(
            num_scalar_prefetch=1,
            grid=(8,),
            in_specs=[pl.BlockSpec(memory_space=pltpu.HBM)] * (len(g_pieces) + len(w_pieces)),
            out_specs=[whole] * 3,
            scratch_shapes=[
                pltpu.VMEM((3, tokens, depth), BF),
                pltpu.VMEM((8, depth, width), BF),
                pltpu.VMEM((tokens, width), F32),
                pltpu.SemaphoreType.DMA((8,)),
                pltpu.SemaphoreType.DMA((2, 8)),
            ],
        ),
        out_shape=[
            jax.ShapeDtypeStruct((half, width), F32),
            jax.ShapeDtypeStruct((half // 2, width), BF),
            jax.ShapeDtypeStruct((half // 2, width), BF),
        ],
        compiler_params=params(26),
        cost_estimate=pl.CostEstimate(
            flops=16 * tokens * depth * width,
            bytes_accessed=20 * 2**20,
            transcendentals=0,
        ),
        name="attn_grad",
    )(meta, *g_pieces, *w_pieces)


def fetch_kernel(plan, meta_ref, buffer_ref, *refs):
    outs, sems = refs[:-1], refs[-1]
    copies = []
    for n, (out, start, at, half) in enumerate(plan):
        source = buffer_ref.at[half, meta_ref[at]]
        target = outs[out].at[pl.ds(start, source.shape[0])]
        copies.append(pltpu.make_async_copy(source, target, sems.at[n]))
    for copy in copies:
        copy.start()
    for copy in copies:
        copy.wait()


def fetch(buffer, meta, plan):
    _, _, rows, width = buffer.shape
    n_out = 1 + plan[-1][0]
    here = pl.BlockSpec(memory_space=pltpu.VMEM)
    return pl.pallas_call(
        functools.partial(fetch_kernel, plan),
        grid_spec=pltpu.PrefetchScalarGridSpec(
            num_scalar_prefetch=1,
            grid=(1,),
            in_specs=[pl.BlockSpec(memory_space=pltpu.HBM)],
            out_specs=[here] * n_out,
            scratch_shapes=[pltpu.SemaphoreType.DMA((len(plan),))],
        ),
        out_shape=[jax.ShapeDtypeStruct((2 * rows, width), BF)] * n_out,
        compiler_params=params(8),
        cost_estimate=pl.CostEstimate(
            flops=0, bytes_accessed=2**16, transcendentals=0
        ),
        name="fetch",
    )(meta, buffer)


def add_kernel(n_terms, plan, *refs):
    terms, outs = refs[:n_terms], refs[n_terms:]
    for out, start, rows, parts in plan:
        value = None
        for term, first in parts:
            part = terms[term][first:first + rows, :].astype(F32)
            value = part if value is None else value + part
        outs[out][start:start + rows, :] = value.astype(BF)


def add_rows(terms, plan, result=False):
    width = terms[0].shape[1]
    n_out = 1 + plan[-1][0]
    shapes = [(sum(p[2] for p in plan if p[0] == n), width) for n in range(n_out)]
    here = pl.BlockSpec(memory_space=pltpu.VMEM)
    outs = [pl.BlockSpec(shape, lambda i: (0, 0)) if result else here for shape in shapes]
    return pl.pallas_call(
        functools.partial(add_kernel, len(terms), plan),
        grid=(1,),
        in_specs=[here] * len(terms),
        out_specs=outs,
        out_shape=[jax.ShapeDtypeStruct(shape, BF) for shape in shapes],
        compiler_params=params(12),
        cost_estimate=pl.CostEstimate(
            flops=2**21, bytes_accessed=5 * 2**20, transcendentals=0
        ),
        name="add_rows",
    )(*terms)


def local(query_rows, key_rows, value_rows, output_grad, out_proj, segment_ids):
    count = query_rows.shape[0]
    half_d = output_grad.shape[1] // 2
    row, col = lax.axis_index("row"), lax.axis_index("col")
    meta = positions(row, col)
    k = row % 2

    g_keep = lax.dynamic_slice_in_dim(output_grad, k * half_d, half_d, 1)
    g_give = lax.dynamic_slice_in_dim(output_grad, (1 - k) * half_d, half_d, 1)
    kv_earlier = passed_along(jnp.concatenate([key_rows, value_rows], 1), "row", 1)
    g_got, kv_earlier, meta = tied((move_row(g_give, dk=1), kv_earlier, meta))
    g0 = jnp.concatenate([g_keep, g_got], 0)
    segments = segment_ids.reshape(-1, LANES)

    (out_proj,) = tied((out_proj,), g0)
    gxm = move_col(g0, dx=1)
    gxp = move_col(g0, dx=-1)
    gy = move_col(g0, dyl=1)
    wzm = move_row(out_proj, dz=1)
    wzp = move_row(out_proj, dz=-1)

    (query_held,) = tied((query_rows,), g0)
    attn_out, top, total = attend(meta, query_held, kv_earlier, key_rows, value_rows, segments)

    gxm, gxp, gy, attn_out = tied((gxm, gxp, gy, attn_out))
    wzm, wzp, out_proj = tied((wzm, wzp, out_proj), gxm)

    hw = out_proj.shape[0] // 2
    gyxm = move_col(gy, dx=1)
    gyxp = move_col(gy, dx=-1)
    a_other = move_row(attn_out, dk=1)
    wo = move_row(wzm, dz=1)
    wy = move_row(out_proj, dyh=1)

    a_pair = jnp.concatenate([attn_out, a_other], 0)
    proj = project([g0, gxm, gxp, gy], a_pair, meta, range(4), None)

    go = move_col(gxm, dx=1)
    gyxm, gyxp, proj = tied((gyxm, gyxp, proj))
    gyo = move_col(gyxp, dx=-1)
    wo, wy = tied((wo, wy), gyxp)
    wyzm = move_row(wy, dz=1)
    wyzp = move_row(wy, dz=-1)
    wyo = move_row(wo, dyh=1)

    proj = project([gyxm, gyxp], a_pair, meta, (4, 5), proj)
    proj = project([go], a_pair, meta, (6,), proj)

    q = hw // 2
    far, up, dn = at_w(2, 1), at_w(1, 1), at_w(-1, 1)
    own_up, own_dn = at_w(1, 0), at_w(-1, 0)
    proj, give_far, give_up, give_dn, up2, dn2 = project(
        [gyo],
        a_pair,
        meta,
        (7,),
        proj,
        (
            (0, 0, far, 0, 0, hw), (0, hw, far, 1, 0, hw),
            (1, 0, up, 0, 0, hw), (1, hw, up, 1, 0, hw), (1, 2 * hw, own_up, 1, 0, q),
            (2, 0, dn, 0, 0, hw), (2, hw, dn, 1, 0, hw), (2, 2 * hw, own_dn, 0, 0, q),
            (3, 0, own_up, 1, q, q),
            (4, 0, own_dn, 0, q, q),
        ),
    )
    give_far, give_up, give_dn, wyzm, wyzp, wyo = tied(
        (give_far, give_up, give_dn, wyzm, wyzp, wyo)
    )
    ry = move_row(give_far, dyh=1)
    rup = move_row(give_up, dz=1)
    rdn = move_row(give_dn, dz=-1)

    g_pieces = [g0, gxm, gxp, gy, gyxm, gyxp, go, gyo]
    w_pieces = [out_proj, wzm, wzp, wy, wyzm, wyzp, wyo, wo]
    wplan = [(i, p * hw, i, p) for i in range(8) for p in range(2)]
    (meta,) = tied((meta,), give_up)
    grad_own, give_lo, give_hi = attn_grad_part(g_pieces, w_pieces, wplan, meta)
    got_lo, got_hi = move_row(give_lo, dk=1), move_row(give_hi, dk=1)
    far, middle, near, own = fetch(
        proj,
        meta,
        (
            (0, 0, at_w(2, 0), 0), (0, hw, at_w(2, 0), 1),
            (1, 0, at_w(0, 1), 0), (1, hw, at_w(0, 1), 1),
            (2, 0, own_up, 0), (2, hw, own_dn, 1),
            (3, 0, at_w(0, 0), 0), (3, hw, at_w(0, 0), 1),
        ),
    )
    (attn_grad,) = add_rows(
        [grad_own, got_lo, got_hi],
        ((0, 0, hw, ((0, 0), (1, 0))), (0, hw, hw, ((0, hw), (2, 0)))),
    )
    part = functools.partial(
        attend_back, meta, query_rows, attn_grad, kv_earlier, key_rows, value_rows, segments, top, total
    )
    heads = query_rows.shape[1] // HD
    cuts = heads // 4, 5 * heads // 8
    held = part((0, cuts[0]), None)

    ry, *held = tied((ry, *held))

    far_up, far_dn = add_rows(
        [far, ry], ((0, 0, hw, ((0, 0), (1, 0))), (1, 0, hw, ((0, hw), (1, hw))))
    )
    fup = move_row(far_up, dz=1)
    fdn = move_row(far_dn, dz=-1)
    rup, rdn, up2, dn2 = tied((rup, rdn, up2, dn2), far_up)
    (across,) = add_rows([middle, rup, rdn], ((0, 0, 2 * hw, ((0, 0), (1, 0), (2, 0))),))
    held = tied(held, across)
    across = move_row(across, dyh=1)
    up2 = move_row(up2, dz=1)
    dn2 = move_row(dn2, dz=-1)
    held = part(cuts, held)

    fup, fdn, *held = tied((fup, fdn, *held))

    near_up, near_dn = add_rows(
        [near, fup, fdn], ((0, 0, hw, ((0, 0), (1, 0))), (1, 0, hw, ((0, hw), (2, 0))))
    )
    nup = move_row(near_up, dz=1)
    ndn = move_row(near_dn, dz=-1)

    *held, up2, dn2 = tied((*held, up2, dn2), near_up)
    query_grad, dkey, dvalue = part((cuts[1], heads), held)
    back = passed_along(
        jnp.concatenate([dkey[:count], dvalue[:count]], 1).astype(BF), "row", -1
    ).astype(F32)
    key_grad = (dkey[count:] + back[:, :HD]).astype(BF)
    value_grad = (dvalue[count:] + back[:, HD:]).astype(BF)

    (proj_grad,) = add_rows(
        [own, across, nup, ndn, rup, up2, rdn, dn2],
        (
            (0, 0, q, ((0, 0), (1, 0), (2, 0), (6, 2 * hw))),
            (0, q, q, ((0, q), (1, q), (2, q), (7, 0))),
            (0, 2 * q, q, ((0, 2 * q), (1, 2 * q), (4, 2 * hw), (3, 0))),
            (0, 3 * q, q, ((0, 3 * q), (1, 3 * q), (5, 0), (3, q))),
        ),
        result=True,
    )
    return (query_grad, key_grad, value_grad, proj_grad)


def solution(mesh):
    placed = (
        P("row", "col"),
        P("row", "col"),
        P("row", "col"),
        P("row", "col"),
        P("row", "col"),
        P(),
    )
    return jax.shard_map(
        local,
        mesh=mesh,
        in_specs=placed,
        out_specs=(P("row", "col"), P("row", "col"), P("row", "col"), P("row", "col")),
        check_vma=False,
    )
```

```python
import functools
import math

import jax
import jax.numpy as jnp
from jax import lax
from jax.experimental import pallas as pl
from jax.experimental.pallas import tpu as pltpu
from jax.sharding import PartitionSpec as P

HD = 128
SCALE = 1.0 / math.sqrt(HD)
NEG = -1e30
BF = jnp.bfloat16
F32 = jnp.float32

PLACES = 64

ZN, YN, KN, LN, XN = 4, 2, 2, 2, 4


AT_FIRST, AT_ROW, AT_EARLIER, AT_G, AT_W = 0, 1, 2, 8, 16
G_STEPS = [(0, 0), (0, -1), (0, 1), (1, 0), (1, -1), (1, 1), (0, 2), (1, 2)]
W_STEPS = [(0, 0), (-1, 0), (1, 0), (0, 1), (-1, 1), (1, 1), (2, 1), (2, 0)]
LANES = 128


def positions(row, col):
    z, yh, yl, x = row // 4, row // 2 % 2, col // 4, col % 4
    head = jnp.stack([(row == 0).astype(jnp.int32), row, jnp.maximum(row - 1, 0)] + [row] * 5)
    steps = [jnp.asarray([step[i] for step in order], jnp.int32) for order in (G_STEPS, W_STEPS) for i in (0, 1)]
    dyl, dx, dz, dyh = steps
    g = ((yl + dyl) & 1) * 4 + ((x + dx) & 3)
    w = ((z + dz) & 3) * 2 + ((yh + dyh) & 1)
    return jnp.concatenate([head, g, w])


def at_w(dz, dyh):
    return AT_W + W_STEPS.index((dz, dyh))


def move_row(value, dz=0, dyh=0, dk=0):
    pairs = []
    for z in range(ZN):
        for y in range(YN):
            for k in range(KN):
                source = (z * YN + y) * KN + k
                target = ((z + dz) % ZN * YN + (y + dyh) % YN) * KN + (k + dk) % KN
                pairs.append((source, target))
    return lax.ppermute(value, "row", pairs)


def move_col(value, dx=0, dyl=0):
    pairs = []
    for y in range(LN):
        for x in range(XN):
            pairs.append((y * XN + x, (y + dyl) % LN * XN + (x + dx) % XN))
    return lax.ppermute(value, "col", pairs)


def passed_along(value, axis, steps):
    count = lax.axis_size(axis)
    first, last = (max(0, -steps), min(count, count - steps))
    return lax.ppermute(value, axis, [(source, source + steps) for source in range(first, last)])


def tied(values, *others):
    held = lax.optimization_barrier((tuple(values), tuple(others)))
    return held[0]


def params(mib, **kw):
    return pltpu.CompilerParams(vmem_limit_bytes=mib * 1024 * 1024, **kw)


def prepare(meta_ref, seg_ref, kv_ref, k_ref, v_ref, bias_ref, k_pair, v_pair, turned, of_keys):
    count = k_ref.shape[0]
    parts = count // LANES
    first, row, earlier = meta_ref[AT_FIRST], meta_ref[AT_ROW], meta_ref[AT_EARLIER]
    own = [seg_ref[pl.ds(row * parts + i, 1), :] for i in range(parts)]
    before = [seg_ref[pl.ds(earlier * parts + i, 1), :] for i in range(parts)]
    key_at = lax.broadcasted_iota(jnp.int32, (LANES, LANES), 0)
    query_at = lax.broadcasted_iota(jnp.int32, (LANES, LANES), 1)
    for i, keys in enumerate(before + own):
        column = jnp.broadcast_to(keys.astype(F32), (LANES, LANES)).T
        for j in range(parts):
            ok = column == own[j].astype(F32)
            if i < parts:
                ok = ok & (first == 0)
            else:
                ok = ok & (key_at + (i - parts) * LANES <= query_at + j * LANES)
            bias_ref[i * LANES:(i + 1) * LANES, j * LANES:(j + 1) * LANES] = jnp.where(
                ok, 0.0, NEG
            ).astype(F32)
    k_pair[:count, :] = kv_ref[:, :HD]
    k_pair[count:, :] = k_ref[...]
    v_pair[:count, :] = kv_ref[:, HD:]
    v_pair[count:, :] = v_ref[...]
    turned[...] = (k_pair if of_keys else v_pair)[...].astype(F32).T.astype(BF)


def pair_scratch(count):
    return [
        pltpu.VMEM((2 * count, count), F32),
        pltpu.VMEM((2 * count, HD), BF),
        pltpu.VMEM((2 * count, HD), BF),
        pltpu.VMEM((HD, 2 * count), BF),
    ]


def chunk_list(count, width):
    return [(i * width, count + (i + 1) * width) for i in range(count // width)]


def fwd_kernel(
    meta_ref, q_ref, kv_ref, k_ref, v_ref, seg_ref, out_ref, top_ref, sum_ref,
    bias_ref, k_pair, v_pair, vt_ref,
):
    count = q_ref.shape[0]

    @pl.when(pl.program_id(0) == 0)
    def _():
        prepare(meta_ref, seg_ref, kv_ref, k_ref, v_ref, bias_ref, k_pair, v_pair, vt_ref, False)

    for start, keys in chunk_list(count, 256):
        cols = slice(start, start + 256)
        s = lax.dot_general(
            k_pair[:keys, :], q_ref[cols, :], (((1,), (1,)), ((), ())), preferred_element_type=F32
        )
        s = s * SCALE + bias_ref[:keys, cols]
        top = jnp.max(s, axis=0, keepdims=True)
        e = jnp.exp(s - top)
        total = jnp.sum(e, axis=0, keepdims=True)
        inv = 1.0 / total
        p = (e * inv).astype(BF)
        a = jnp.dot(vt_ref[:, :keys], p, preferred_element_type=F32)
        out_ref[cols, :] = a.T.astype(BF)
        top_ref[0, :, cols] = top
        sum_ref[0, :, cols] = inv


def attend(meta, query, kv_earlier, key_rows, value_rows, segments):
    count, width = query.shape
    heads = width // HD
    whole = lambda value: pl.BlockSpec(value.shape, lambda h, m: (0, 0))
    head = pl.BlockSpec((count, HD), lambda h, m: (0, h))
    stat = pl.BlockSpec((1, 1, count), lambda h, m: (h, 0, 0))
    return pl.pallas_call(
        fwd_kernel,
        grid_spec=pltpu.PrefetchScalarGridSpec(
            num_scalar_prefetch=1,
            grid=(heads,),
            in_specs=[head] + [whole(v) for v in (kv_earlier, key_rows, value_rows, segments)],
            out_specs=[head, stat, stat],
            scratch_shapes=pair_scratch(count),
        ),
        out_shape=[
            jax.ShapeDtypeStruct((count, width), BF),
            jax.ShapeDtypeStruct((heads, 1, count), F32),
            jax.ShapeDtypeStruct((heads, 1, count), F32),
        ],
        compiler_params=params(16),
        cost_estimate=pl.CostEstimate(
            flops=heads * 64 * 2 * 2 * count * count * HD,
            bytes_accessed=8 * 2**20,
            transcendentals=heads * 2 * count * count,
        ),
        name="attend",
    )(meta, query, kv_earlier, key_rows, value_rows, segments)


def bwd_kernel(
    n_held, last, meta_ref, q_ref, g_ref, kv_ref, k_ref, v_ref, seg_ref, top_ref, sum_ref, *refs
):
    dk_in, dv_in = refs[:2] if n_held else (None, None)
    dq_ref, dk_ref, dv_ref, bias_ref, k_pair, v_pair, kt_ref = refs[n_held:]
    count = q_ref.shape[0]

    @pl.when(pl.program_id(0) == 0)
    def _():
        prepare(meta_ref, seg_ref, kv_ref, k_ref, v_ref, bias_ref, k_pair, v_pair, kt_ref, True)
        if n_held:
            dk_ref[...] = dk_in[...]
            dv_ref[...] = dv_in[...]
        else:
            dk_ref[...] = jnp.zeros_like(dk_ref)
            dv_ref[...] = jnp.zeros_like(dv_ref)

    for start, keys in chunk_list(count, 256):
        cols = slice(start, start + 256)
        q = q_ref[cols, :]
        g = g_ref[cols, :]
        s = lax.dot_general(
            k_pair[:keys, :], q, (((1,), (1,)), ((), ())), preferred_element_type=F32
        )
        s = s * SCALE + bias_ref[:keys, cols]
        p = jnp.exp(s - top_ref[0, :, cols]) * sum_ref[0, :, cols]
        dp = lax.dot_general(
            v_pair[:keys, :], g, (((1,), (1,)), ((), ())), preferred_element_type=F32
        )
        delta = jnp.sum(p * dp, axis=0, keepdims=True)
        ds = (p * (dp - delta)).astype(BF)
        dq = jnp.dot(kt_ref[:, :keys], ds, preferred_element_type=F32) * SCALE
        dq_ref[cols, :] = dq.T.astype(BF)
        dk_ref[:keys, :] += jnp.dot(ds, q, preferred_element_type=F32)
        dv_ref[:keys, :] += jnp.dot(p.astype(BF), g, preferred_element_type=F32)

    if last:

        @pl.when(pl.program_id(0) == pl.num_programs(0) - 1)
        def _():
            dk_ref[...] = dk_ref[...] * SCALE


def attend_back(
    meta, query, grad, kv_earlier, key_rows, value_rows, segments, top, total, heads, held
):
    count, width = query.shape
    begin, end = heads
    last = end == width // HD
    whole = lambda value: pl.BlockSpec(value.shape, lambda h, m: (0, 0))
    head = pl.BlockSpec((count, HD), lambda h, m: (0, h + begin))
    stat = pl.BlockSpec((1, 1, count), lambda h, m: (h + begin, 0, 0))
    pair = pl.BlockSpec((2 * count, HD), lambda h, m: (0, 0))
    earlier = () if held is None else (held[1], held[2], held[0])
    return pl.pallas_call(
        functools.partial(bwd_kernel, len(earlier), last),
        grid_spec=pltpu.PrefetchScalarGridSpec(
            num_scalar_prefetch=1,
            grid=(end - begin,),
            in_specs=[head, head]
            + [whole(v) for v in (kv_earlier, key_rows, value_rows, segments)]
            + [stat, stat]
            + ([pair, pair, pl.BlockSpec(memory_space=pl.ANY)] if earlier else []),
            out_specs=[head, pair, pair],
            scratch_shapes=pair_scratch(count),
        ),
        out_shape=[
            jax.ShapeDtypeStruct((count, width), BF),
            jax.ShapeDtypeStruct((2 * count, HD), F32),
            jax.ShapeDtypeStruct((2 * count, HD), F32),
        ],
        input_output_aliases={11: 0} if earlier else {},
        compiler_params=params(22),
        cost_estimate=pl.CostEstimate(
            flops=(end - begin) * 10 * 2 * 2 * count * count * HD if begin else 2**20,
            bytes_accessed=6 * 2**20 if begin else 2**16,
            transcendentals=(end - begin) * 2 * count * count if begin else 0,
        ),
        name="attend_back",
    )(meta, query, grad, kv_earlier, key_rows, value_rows, segments, top, total, *earlier)


def proj_kernel(slots, held, plan, meta_ref, *refs):
    n_in = len(slots)
    pieces, a_ref = refs[:n_in], refs[n_in]
    refs = refs[n_in + 1 + held:]
    buffer_ref, taken = refs[0], refs[1:-3]
    done, sems, take_sems = refs[-3:]
    step = pl.program_id(0)
    rows = done.shape[2]

    def put(j):
        return pltpu.make_async_copy(done.at[j], buffer_ref.at[:, meta_ref[AT_G + slots[j]]], sems.at[j])

    def take(i, made):
        out, start, at, half, first, count = plan[i]
        if made is None:
            source = buffer_ref.at[half, meta_ref[at], pl.ds(first, count)]
        else:
            source = done.at[made, half, pl.ds(first, count)]
        target = taken[out].at[pl.ds(start, count)]
        return pltpu.make_async_copy(source, target, take_sems.at[i])

    def made_here(i, j):
        return meta_ref[plan[i][2]] == meta_ref[AT_G + slots[j]]

    @pl.when(step == 0)
    def _():
        for i in range(len(plan)):
            here = made_here(i, 0)
            for j in range(1, n_in):
                here = here | made_here(i, j)

            @pl.when(jnp.logical_not(here))
            def _():
                take(i, None).start()

    for j in range(n_in):

        @pl.when(step == j)
        def _():
            value = lax.dot_general(
                pieces[j][...], a_ref[...], (((0,), (0,)), ((), ())), preferred_element_type=F32
            ).astype(BF)
            done[j, 0] = value[:rows]
            done[j, 1] = value[rows:]
            put(j).start()
            for i in range(len(plan)):

                @pl.when(made_here(i, j))
                def _():
                    take(i, j).start()

    @pl.when(step == n_in - 1)
    def _():
        for j in range(n_in):
            put(j).wait()
        for i in range(len(plan)):
            take(i, None).wait()


def project(pieces, a_pair, meta, slots, buffer, plan=()):
    tokens, width = a_pair.shape
    depth = pieces[0].shape[1]
    n_blocks = len(pieces)
    held = int(buffer is not None)
    here = pl.BlockSpec(memory_space=pltpu.VMEM)
    there = pl.BlockSpec(memory_space=pltpu.HBM)
    operands = (*pieces, a_pair) + ((buffer,) if held else ())
    shape = (2, depth // 2, width)
    n_taken = 1 + max((entry[0] for entry in plan), default=-1)
    taken = [(sum(e[5] for e in plan if e[0] == i), width) for i in range(n_taken)]
    out = pl.pallas_call(
        functools.partial(proj_kernel, tuple(slots), held, plan),
        grid_spec=pltpu.PrefetchScalarGridSpec(
            num_scalar_prefetch=1,
            grid=(n_blocks,),
            in_specs=[here] * (n_blocks + 1) + [there] * held,
            out_specs=[there] + [here] * n_taken,
            scratch_shapes=[
                pltpu.VMEM((n_blocks, *shape), BF),
                pltpu.SemaphoreType.DMA((n_blocks,)),
                pltpu.SemaphoreType.DMA((max(len(plan), 1),)),
            ],
        ),
        out_shape=[jax.ShapeDtypeStruct((2, PLACES, depth // 2, width), BF)]
        + [jax.ShapeDtypeStruct(t, BF) for t in taken],
        input_output_aliases={n_blocks + 2: 0} if held else {},
        compiler_params=params(16),
        cost_estimate=pl.CostEstimate(
            flops=2 * n_blocks * tokens * depth * width,
            bytes_accessed=(2 * n_blocks + 2) * 2**20,
            transcendentals=0,
        ),
        name="project",
    )(meta, *operands)
    return out if n_taken else out[0]


def grad_kernel(wplan, n_g, n_w, meta_ref, *refs):
    g_in, w_in = refs[:n_g], refs[n_g:n_g + n_w]
    own_ref, lo_ref, hi_ref = refs[n_g + n_w:n_g + n_w + 3]
    gbuf, wbuf, total, gsems, wsems = refs[n_g + n_w + 3:]
    step = pl.program_id(0)
    half = own_ref.shape[0]
    wh = wbuf.shape[1] // 2

    slots = gbuf.shape[0]

    def g_copy(j):
        return pltpu.make_async_copy(g_in[j], gbuf.at[j % slots], gsems.at[j])

    def w_copy(n):
        ref, source, block, part = wplan[n]
        place = meta_ref[AT_W + block]
        return pltpu.make_async_copy(
            w_in[ref].at[pl.ds(source, wh)],
            wbuf.at[place, pl.ds(part * wh, wh)],
            wsems.at[part, place],
        )

    @pl.when(step == 0)
    def _():
        for j in range(slots):
            g_copy(j).start()
        for n in range(16):
            w_copy(n).start()

    for j in range(8):

        @pl.when(step == j)
        def _():
            g_copy(j).wait()

    place = meta_ref[AT_G + step]
    for part in range(2):
        pltpu.make_async_copy(
            w_in[0].at[pl.ds(0, wh)], wbuf.at[place, pl.ds(part * wh, wh)], wsems.at[part, place]
        ).wait()

    @pl.when(step == 0)
    def _():
        total[...] = jnp.dot(gbuf[0], wbuf[place], preferred_element_type=F32)

    @pl.when(step > 0)
    def _():
        total[...] += jnp.dot(gbuf[step % slots], wbuf[place], preferred_element_type=F32)

    for j in range(8 - slots):

        @pl.when(step == j)
        def _():
            g_copy(j + slots).start()

    @pl.when(step == 7)
    def _():
        own_ref[...] = total[:half, :]
        lo_ref[...] = total[half:half + half // 2, :].astype(BF)
        hi_ref[...] = total[half + half // 2:, :].astype(BF)


def attn_grad_part(g_pieces, w_pieces, wplan, meta):
    tokens, depth = g_pieces[0].shape
    width = w_pieces[0].shape[1]
    half = tokens // 2
    kernel = functools.partial(grad_kernel, wplan, len(g_pieces), len(w_pieces))
    whole = pl.BlockSpec(memory_space=pltpu.VMEM)
    return pl.pallas_call(
        kernel,
        grid_spec=pltpu.PrefetchScalarGridSpec(
            num_scalar_prefetch=1,
            grid=(8,),
            in_specs=[pl.BlockSpec(memory_space=pltpu.HBM)] * (len(g_pieces) + len(w_pieces)),
            out_specs=[whole] * 3,
            scratch_shapes=[
                pltpu.VMEM((3, tokens, depth), BF),
                pltpu.VMEM((8, depth, width), BF),
                pltpu.VMEM((tokens, width), F32),
                pltpu.SemaphoreType.DMA((8,)),
                pltpu.SemaphoreType.DMA((2, 8)),
            ],
        ),
        out_shape=[
            jax.ShapeDtypeStruct((half, width), F32),
            jax.ShapeDtypeStruct((half // 2, width), BF),
            jax.ShapeDtypeStruct((half // 2, width), BF),
        ],
        compiler_params=params(26),
        cost_estimate=pl.CostEstimate(
            flops=16 * tokens * depth * width,
            bytes_accessed=20 * 2**20,
            transcendentals=0,
        ),
        name="attn_grad",
    )(meta, *g_pieces, *w_pieces)


def fetch_kernel(plan, meta_ref, buffer_ref, *refs):
    outs, sems = refs[:-1], refs[-1]
    copies = []
    for n, (out, start, at, half) in enumerate(plan):
        source = buffer_ref.at[half, meta_ref[at]]
        target = outs[out].at[pl.ds(start, source.shape[0])]
        copies.append(pltpu.make_async_copy(source, target, sems.at[n]))
    for copy in copies:
        copy.start()
    for copy in copies:
        copy.wait()


def fetch(buffer, meta, plan):
    _, _, rows, width = buffer.shape
    n_out = 1 + plan[-1][0]
    here = pl.BlockSpec(memory_space=pltpu.VMEM)
    return pl.pallas_call(
        functools.partial(fetch_kernel, plan),
        grid_spec=pltpu.PrefetchScalarGridSpec(
            num_scalar_prefetch=1,
            grid=(1,),
            in_specs=[pl.BlockSpec(memory_space=pltpu.HBM)],
            out_specs=[here] * n_out,
            scratch_shapes=[pltpu.SemaphoreType.DMA((len(plan),))],
        ),
        out_shape=[jax.ShapeDtypeStruct((2 * rows, width), BF)] * n_out,
        compiler_params=params(8),
        cost_estimate=pl.CostEstimate(
            flops=0, bytes_accessed=2**16, transcendentals=0
        ),
        name="fetch",
    )(meta, buffer)


def add_kernel(n_terms, plan, *refs):
    terms, outs = refs[:n_terms], refs[n_terms:]
    for out, start, rows, parts in plan:
        value = None
        for term, first in parts:
            part = terms[term][first:first + rows, :].astype(F32)
            value = part if value is None else value + part
        outs[out][start:start + rows, :] = value.astype(BF)


def add_rows(terms, plan, result=False):
    width = terms[0].shape[1]
    n_out = 1 + plan[-1][0]
    shapes = [(sum(p[2] for p in plan if p[0] == n), width) for n in range(n_out)]
    here = pl.BlockSpec(memory_space=pltpu.VMEM)
    outs = [pl.BlockSpec(shape, lambda i: (0, 0)) if result else here for shape in shapes]
    return pl.pallas_call(
        functools.partial(add_kernel, len(terms), plan),
        grid=(1,),
        in_specs=[here] * len(terms),
        out_specs=outs,
        out_shape=[jax.ShapeDtypeStruct(shape, BF) for shape in shapes],
        compiler_params=params(12),
        cost_estimate=pl.CostEstimate(
            flops=2**21, bytes_accessed=5 * 2**20, transcendentals=0
        ),
        name="add_rows",
    )(*terms)


def local(query_rows, key_rows, value_rows, output_grad, out_proj, segment_ids):
    count = query_rows.shape[0]
    half_d = output_grad.shape[1] // 2
    row, col = lax.axis_index("row"), lax.axis_index("col")
    meta = positions(row, col)
    k = row % 2

    g_keep = lax.dynamic_slice_in_dim(output_grad, k * half_d, half_d, 1)
    g_give = lax.dynamic_slice_in_dim(output_grad, (1 - k) * half_d, half_d, 1)
    kv_earlier = passed_along(jnp.concatenate([key_rows, value_rows], 1), "row", 1)
    g_got, meta = tied((move_row(g_give, dk=1), meta))
    g0 = jnp.concatenate([g_keep, g_got], 0)
    segments = segment_ids.reshape(-1, LANES)

    out_proj, kv_earlier = tied((out_proj, kv_earlier), g0)
    gxm = move_col(g0, dx=1)
    gxp = move_col(g0, dx=-1)
    gy = move_col(g0, dyl=1)
    wzm = move_row(out_proj, dz=1)
    wzp = move_row(out_proj, dz=-1)

    (query_held,) = tied((query_rows,), g0)
    attn_out, top, total = attend(meta, query_held, kv_earlier, key_rows, value_rows, segments)

    gxm, gxp, gy, attn_out = tied((gxm, gxp, gy, attn_out))
    wzm, wzp, out_proj = tied((wzm, wzp, out_proj), gxm)

    hw = out_proj.shape[0] // 2
    gyxm = move_col(gy, dx=1)
    gyxp = move_col(gy, dx=-1)
    a_other = move_row(attn_out, dk=1)
    wo = move_row(wzm, dz=1)
    wy = move_row(out_proj, dyh=1)

    a_pair = jnp.concatenate([attn_out, a_other], 0)
    proj = project([g0, gxm, gxp, gy], a_pair, meta, range(4), None)

    go = move_col(gxm, dx=1)
    gyxm, gyxp, proj = tied((gyxm, gyxp, proj))
    gyo = move_col(gyxp, dx=-1)
    wo, wy = tied((wo, wy), gyxp)
    wyzm = move_row(wy, dz=1)
    wyzp = move_row(wy, dz=-1)
    wyo = move_row(wo, dyh=1)

    proj = project([gyxm, gyxp], a_pair, meta, (4, 5), proj)
    proj = project([go], a_pair, meta, (6,), proj)

    q = hw // 2
    far, up, dn = at_w(2, 1), at_w(1, 1), at_w(-1, 1)
    own_up, own_dn = at_w(1, 0), at_w(-1, 0)
    proj, give_far, give_up, give_dn, up2, dn2 = project(
        [gyo],
        a_pair,
        meta,
        (7,),
        proj,
        (
            (0, 0, far, 0, 0, hw), (0, hw, far, 1, 0, hw),
            (1, 0, up, 0, 0, hw), (1, hw, up, 1, 0, hw), (1, 2 * hw, own_up, 1, 0, q),
            (2, 0, dn, 0, 0, hw), (2, hw, dn, 1, 0, hw), (2, 2 * hw, own_dn, 0, 0, q),
            (3, 0, own_up, 1, q, q),
            (4, 0, own_dn, 0, q, q),
        ),
    )
    give_far, give_up, give_dn, wyzm, wyzp, wyo = tied(
        (give_far, give_up, give_dn, wyzm, wyzp, wyo)
    )
    ry = move_row(give_far, dyh=1)
    rup = move_row(give_up, dz=1)
    rdn = move_row(give_dn, dz=-1)

    g_pieces = [g0, gxm, gxp, gy, gyxm, gyxp, go, gyo]
    w_pieces = [out_proj, wzm, wzp, wy, wyzm, wyzp, wyo, wo]
    wplan = [(i, p * hw, i, p) for i in range(8) for p in range(2)]
    (meta,) = tied((meta,), give_up)
    grad_own, give_lo, give_hi = attn_grad_part(g_pieces, w_pieces, wplan, meta)
    got_lo, got_hi = move_row(give_lo, dk=1), move_row(give_hi, dk=1)
    far, middle, near, own = fetch(
        proj,
        meta,
        (
            (0, 0, at_w(2, 0), 0), (0, hw, at_w(2, 0), 1),
            (1, 0, at_w(0, 1), 0), (1, hw, at_w(0, 1), 1),
            (2, 0, own_up, 0), (2, hw, own_dn, 1),
            (3, 0, at_w(0, 0), 0), (3, hw, at_w(0, 0), 1),
        ),
    )
    (attn_grad,) = add_rows(
        [grad_own, got_lo, got_hi],
        ((0, 0, hw, ((0, 0), (1, 0))), (0, hw, hw, ((0, hw), (2, 0)))),
    )
    part = functools.partial(
        attend_back, meta, query_rows, attn_grad, kv_earlier, key_rows, value_rows, segments, top, total
    )
    heads = query_rows.shape[1] // HD
    cuts = heads // 4, 5 * heads // 8
    held = part((0, cuts[0]), None)

    ry, *held = tied((ry, *held))

    far_up, far_dn = add_rows(
        [far, ry], ((0, 0, hw, ((0, 0), (1, 0))), (1, 0, hw, ((0, hw), (1, hw))))
    )
    fup = move_row(far_up, dz=1)
    fdn = move_row(far_dn, dz=-1)
    rup, rdn, up2, dn2 = tied((rup, rdn, up2, dn2), far_up)
    (across,) = add_rows([middle, rup, rdn], ((0, 0, 2 * hw, ((0, 0), (1, 0), (2, 0))),))
    held = tied(held, across)
    across = move_row(across, dyh=1)
    up2 = move_row(up2, dz=1)
    dn2 = move_row(dn2, dz=-1)
    held = part(cuts, held)

    fup, fdn, *held = tied((fup, fdn, *held))

    near_up, near_dn = add_rows(
        [near, fup, fdn], ((0, 0, hw, ((0, 0), (1, 0))), (1, 0, hw, ((0, hw), (2, 0))))
    )
    nup = move_row(near_up, dz=1)
    ndn = move_row(near_dn, dz=-1)

    *held, up2, dn2 = tied((*held, up2, dn2), near_up)
    query_grad, dkey, dvalue = part((cuts[1], heads), held)
    back = passed_along(
        jnp.concatenate([dkey[:count], dvalue[:count]], 1).astype(BF), "row", -1
    ).astype(F32)
    key_grad = (dkey[count:] + back[:, :HD]).astype(BF)
    value_grad = (dvalue[count:] + back[:, HD:]).astype(BF)

    (proj_grad,) = add_rows(
        [own, across, nup, ndn, rup, up2, rdn, dn2],
        (
            (0, 0, q, ((0, 0), (1, 0), (2, 0), (6, 2 * hw))),
            (0, q, q, ((0, q), (1, q), (2, q), (7, 0))),
            (0, 2 * q, q, ((0, 2 * q), (1, 2 * q), (4, 2 * hw), (3, 0))),
            (0, 3 * q, q, ((0, 3 * q), (1, 3 * q), (5, 0), (3, q))),
        ),
        result=True,
    )
    return (query_grad, key_grad, value_grad, proj_grad)


def solution(mesh):
    placed = (
        P("row", "col"),
        P("row", "col"),
        P("row", "col"),
        P("row", "col"),
        P("row", "col"),
        P(),
    )
    return jax.shard_map(
        local,
        mesh=mesh,
        in_specs=placed,
        out_specs=(P("row", "col"), P("row", "col"), P("row", "col"), P("row", "col")),
        check_vma=False,
    )
```

```python
import functools
import math

import jax
import jax.numpy as jnp
from jax import lax
from jax.experimental import pallas as pl
from jax.experimental.pallas import tpu as pltpu
from jax.sharding import PartitionSpec as P

HD = 128
SCALE = 1.0 / math.sqrt(HD)
NEG = -1e30
BF = jnp.bfloat16
F32 = jnp.float32

PLACES = 64

ZN, YN, KN, LN, XN = 4, 2, 2, 2, 4


AT_FIRST, AT_ROW, AT_EARLIER, AT_G, AT_W = 0, 1, 2, 8, 16
G_STEPS = [(0, 0), (0, -1), (0, 1), (1, 0), (1, -1), (1, 1), (0, 2), (1, 2)]
W_STEPS = [(0, 0), (-1, 0), (1, 0), (0, 1), (-1, 1), (1, 1), (2, 1), (2, 0)]
LANES = 128


def positions(row, col):
    z, yh, yl, x = row // 4, row // 2 % 2, col // 4, col % 4
    head = jnp.stack([(row == 0).astype(jnp.int32), row, jnp.maximum(row - 1, 0)] + [row] * 5)
    steps = [jnp.asarray([step[i] for step in order], jnp.int32) for order in (G_STEPS, W_STEPS) for i in (0, 1)]
    dyl, dx, dz, dyh = steps
    g = ((yl + dyl) & 1) * 4 + ((x + dx) & 3)
    w = ((z + dz) & 3) * 2 + ((yh + dyh) & 1)
    return jnp.concatenate([head, g, w])


def at_w(dz, dyh):
    return AT_W + W_STEPS.index((dz, dyh))


def move_row(value, dz=0, dyh=0, dk=0):
    pairs = []
    for z in range(ZN):
        for y in range(YN):
            for k in range(KN):
                source = (z * YN + y) * KN + k
                target = ((z + dz) % ZN * YN + (y + dyh) % YN) * KN + (k + dk) % KN
                pairs.append((source, target))
    return lax.ppermute(value, "row", pairs)


def move_col(value, dx=0, dyl=0):
    pairs = []
    for y in range(LN):
        for x in range(XN):
            pairs.append((y * XN + x, (y + dyl) % LN * XN + (x + dx) % XN))
    return lax.ppermute(value, "col", pairs)


def passed_along(value, axis, steps):
    count = lax.axis_size(axis)
    first, last = (max(0, -steps), min(count, count - steps))
    return lax.ppermute(value, axis, [(source, source + steps) for source in range(first, last)])


def tied(values, *others):
    held = lax.optimization_barrier((tuple(values), tuple(others)))
    return held[0]


def params(mib, **kw):
    return pltpu.CompilerParams(vmem_limit_bytes=mib * 1024 * 1024, **kw)


def prepare(meta_ref, seg_ref, kv_ref, k_ref, v_ref, bias_ref, k_pair, v_pair, turned, of_keys):
    count = k_ref.shape[0]
    parts = count // LANES
    first, row, earlier = meta_ref[AT_FIRST], meta_ref[AT_ROW], meta_ref[AT_EARLIER]
    own = [seg_ref[pl.ds(row * parts + i, 1), :] for i in range(parts)]
    before = [seg_ref[pl.ds(earlier * parts + i, 1), :] for i in range(parts)]
    key_at = lax.broadcasted_iota(jnp.int32, (LANES, LANES), 0)
    query_at = lax.broadcasted_iota(jnp.int32, (LANES, LANES), 1)
    for i, keys in enumerate(before + own):
        column = jnp.broadcast_to(keys.astype(F32), (LANES, LANES)).T
        for j in range(parts):
            ok = column == own[j].astype(F32)
            if i < parts:
                ok = ok & (first == 0)
            else:
                ok = ok & (key_at + (i - parts) * LANES <= query_at + j * LANES)
            bias_ref[i * LANES:(i + 1) * LANES, j * LANES:(j + 1) * LANES] = jnp.where(
                ok, 0.0, NEG
            ).astype(F32)
    k_pair[:count, :] = kv_ref[:, :HD]
    k_pair[count:, :] = k_ref[...]
    v_pair[:count, :] = kv_ref[:, HD:]
    v_pair[count:, :] = v_ref[...]
    turned[...] = (k_pair if of_keys else v_pair)[...].astype(F32).T.astype(BF)


def pair_scratch(count):
    return [
        pltpu.VMEM((2 * count, count), F32),
        pltpu.VMEM((2 * count, HD), BF),
        pltpu.VMEM((2 * count, HD), BF),
        pltpu.VMEM((HD, 2 * count), BF),
    ]


def chunk_list(count, width):
    return [(i * width, count + (i + 1) * width) for i in range(count // width)]


def fwd_kernel(
    meta_ref, q_ref, kv_ref, k_ref, v_ref, seg_ref, out_ref, top_ref, sum_ref,
    bias_ref, k_pair, v_pair, vt_ref,
):
    count = q_ref.shape[0]

    @pl.when(pl.program_id(0) == 0)
    def _():
        prepare(meta_ref, seg_ref, kv_ref, k_ref, v_ref, bias_ref, k_pair, v_pair, vt_ref, False)

    for start, keys in chunk_list(count, 256):
        cols = slice(start, start + 256)
        s = lax.dot_general(
            k_pair[:keys, :], q_ref[cols, :], (((1,), (1,)), ((), ())), preferred_element_type=F32
        )
        s = s * SCALE + bias_ref[:keys, cols]
        top = jnp.max(s, axis=0, keepdims=True)
        e = jnp.exp(s - top)
        total = jnp.sum(e, axis=0, keepdims=True)
        inv = 1.0 / total
        p = (e * inv).astype(BF)
        a = jnp.dot(vt_ref[:, :keys], p, preferred_element_type=F32)
        out_ref[cols, :] = a.T.astype(BF)
        top_ref[0, :, cols] = top
        sum_ref[0, :, cols] = inv


def attend(meta, query, kv_earlier, key_rows, value_rows, segments):
    count, width = query.shape
    heads = width // HD
    whole = lambda value: pl.BlockSpec(value.shape, lambda h, m: (0, 0))
    head = pl.BlockSpec((count, HD), lambda h, m: (0, h))
    stat = pl.BlockSpec((1, 1, count), lambda h, m: (h, 0, 0))
    return pl.pallas_call(
        fwd_kernel,
        grid_spec=pltpu.PrefetchScalarGridSpec(
            num_scalar_prefetch=1,
            grid=(heads,),
            in_specs=[head] + [whole(v) for v in (kv_earlier, key_rows, value_rows, segments)],
            out_specs=[head, stat, stat],
            scratch_shapes=pair_scratch(count),
        ),
        out_shape=[
            jax.ShapeDtypeStruct((count, width), BF),
            jax.ShapeDtypeStruct((heads, 1, count), F32),
            jax.ShapeDtypeStruct((heads, 1, count), F32),
        ],
        compiler_params=params(16),
        cost_estimate=pl.CostEstimate(
            flops=heads * 64 * 2 * 2 * count * count * HD,
            bytes_accessed=8 * 2**20,
            transcendentals=heads * 2 * count * count,
        ),
        name="attend",
    )(meta, query, kv_earlier, key_rows, value_rows, segments)


def bwd_kernel(
    n_held, last, meta_ref, q_ref, g_ref, kv_ref, k_ref, v_ref, seg_ref, top_ref, sum_ref, *refs
):
    dk_in, dv_in = refs[:2] if n_held else (None, None)
    dq_ref, dk_ref, dv_ref, bias_ref, k_pair, v_pair, kt_ref = refs[n_held:]
    count = q_ref.shape[0]

    @pl.when(pl.program_id(0) == 0)
    def _():
        prepare(meta_ref, seg_ref, kv_ref, k_ref, v_ref, bias_ref, k_pair, v_pair, kt_ref, True)
        if n_held:
            dk_ref[...] = dk_in[...]
            dv_ref[...] = dv_in[...]
        else:
            dk_ref[...] = jnp.zeros_like(dk_ref)
            dv_ref[...] = jnp.zeros_like(dv_ref)

    for start, keys in chunk_list(count, 256):
        cols = slice(start, start + 256)
        q = q_ref[cols, :]
        g = g_ref[cols, :]
        s = lax.dot_general(
            k_pair[:keys, :], q, (((1,), (1,)), ((), ())), preferred_element_type=F32
        )
        s = s * SCALE + bias_ref[:keys, cols]
        p = jnp.exp(s - top_ref[0, :, cols]) * sum_ref[0, :, cols]
        dp = lax.dot_general(
            v_pair[:keys, :], g, (((1,), (1,)), ((), ())), preferred_element_type=F32
        )
        delta = jnp.sum(p * dp, axis=0, keepdims=True)
        ds = (p * (dp - delta)).astype(BF)
        dq = jnp.dot(kt_ref[:, :keys], ds, preferred_element_type=F32) * SCALE
        dq_ref[cols, :] = dq.T.astype(BF)
        dk_ref[:keys, :] += jnp.dot(ds, q, preferred_element_type=F32)
        dv_ref[:keys, :] += jnp.dot(p.astype(BF), g, preferred_element_type=F32)

    if last:

        @pl.when(pl.program_id(0) == pl.num_programs(0) - 1)
        def _():
            dk_ref[...] = dk_ref[...] * SCALE


def attend_back(
    meta, query, grad, kv_earlier, key_rows, value_rows, segments, top, total, heads, held
):
    count, width = query.shape
    begin, end = heads
    last = end == width // HD
    whole = lambda value: pl.BlockSpec(value.shape, lambda h, m: (0, 0))
    head = pl.BlockSpec((count, HD), lambda h, m: (0, h + begin))
    stat = pl.BlockSpec((1, 1, count), lambda h, m: (h + begin, 0, 0))
    pair = pl.BlockSpec((2 * count, HD), lambda h, m: (0, 0))
    earlier = () if held is None else (held[1], held[2], held[0])
    return pl.pallas_call(
        functools.partial(bwd_kernel, len(earlier), last),
        grid_spec=pltpu.PrefetchScalarGridSpec(
            num_scalar_prefetch=1,
            grid=(end - begin,),
            in_specs=[head, head]
            + [whole(v) for v in (kv_earlier, key_rows, value_rows, segments)]
            + [stat, stat]
            + ([pair, pair, pl.BlockSpec(memory_space=pl.ANY)] if earlier else []),
            out_specs=[head, pair, pair],
            scratch_shapes=pair_scratch(count),
        ),
        out_shape=[
            jax.ShapeDtypeStruct((count, width), BF),
            jax.ShapeDtypeStruct((2 * count, HD), F32),
            jax.ShapeDtypeStruct((2 * count, HD), F32),
        ],
        input_output_aliases={11: 0} if earlier else {},
        compiler_params=params(22),
        cost_estimate=pl.CostEstimate(
            flops=(end - begin) * 10 * 2 * 2 * count * count * HD if begin else 2**20,
            bytes_accessed=6 * 2**20 if begin else 2**16,
            transcendentals=(end - begin) * 2 * count * count if begin else 0,
        ),
        name="attend_back",
    )(meta, query, grad, kv_earlier, key_rows, value_rows, segments, top, total, *earlier)


def proj_kernel(slots, held, plan, meta_ref, *refs):
    n_in = len(slots)
    pieces, a_ref = refs[:n_in], refs[n_in]
    refs = refs[n_in + 1 + held:]
    buffer_ref, taken = refs[0], refs[1:-3]
    done, sems, take_sems = refs[-3:]
    step = pl.program_id(0)
    rows = done.shape[2]

    def put(j):
        return pltpu.make_async_copy(done.at[j], buffer_ref.at[:, meta_ref[AT_G + slots[j]]], sems.at[j])

    def take(i, made):
        out, start, at, half, first, count = plan[i]
        if made is None:
            source = buffer_ref.at[half, meta_ref[at], pl.ds(first, count)]
        else:
            source = done.at[made, half, pl.ds(first, count)]
        target = taken[out].at[pl.ds(start, count)]
        return pltpu.make_async_copy(source, target, take_sems.at[i])

    def made_here(i, j):
        return meta_ref[plan[i][2]] == meta_ref[AT_G + slots[j]]

    @pl.when(step == 0)
    def _():
        for i in range(len(plan)):
            here = made_here(i, 0)
            for j in range(1, n_in):
                here = here | made_here(i, j)

            @pl.when(jnp.logical_not(here))
            def _():
                take(i, None).start()

    for j in range(n_in):

        @pl.when(step == j)
        def _():
            value = lax.dot_general(
                pieces[j][...], a_ref[...], (((0,), (0,)), ((), ())), preferred_element_type=F32
            ).astype(BF)
            done[j, 0] = value[:rows]
            done[j, 1] = value[rows:]
            put(j).start()
            for i in range(len(plan)):

                @pl.when(made_here(i, j))
                def _():
                    take(i, j).start()

    @pl.when(step == n_in - 1)
    def _():
        for j in range(n_in):
            put(j).wait()
        for i in range(len(plan)):
            take(i, None).wait()


def project(pieces, a_pair, meta, slots, buffer, plan=()):
    tokens, width = a_pair.shape
    depth = pieces[0].shape[1]
    n_blocks = len(pieces)
    held = int(buffer is not None)
    here = pl.BlockSpec(memory_space=pltpu.VMEM)
    there = pl.BlockSpec(memory_space=pltpu.HBM)
    operands = (*pieces, a_pair) + ((buffer,) if held else ())
    shape = (2, depth // 2, width)
    n_taken = 1 + max((entry[0] for entry in plan), default=-1)
    taken = [(sum(e[5] for e in plan if e[0] == i), width) for i in range(n_taken)]
    out = pl.pallas_call(
        functools.partial(proj_kernel, tuple(slots), held, plan),
        grid_spec=pltpu.PrefetchScalarGridSpec(
            num_scalar_prefetch=1,
            grid=(n_blocks,),
            in_specs=[here] * (n_blocks + 1) + [there] * held,
            out_specs=[there] + [here] * n_taken,
            scratch_shapes=[
                pltpu.VMEM((n_blocks, *shape), BF),
                pltpu.SemaphoreType.DMA((n_blocks,)),
                pltpu.SemaphoreType.DMA((max(len(plan), 1),)),
            ],
        ),
        out_shape=[jax.ShapeDtypeStruct((2, PLACES, depth // 2, width), BF)]
        + [jax.ShapeDtypeStruct(t, BF) for t in taken],
        input_output_aliases={n_blocks + 2: 0} if held else {},
        compiler_params=params(16),
        cost_estimate=pl.CostEstimate(
            flops=2 * n_blocks * tokens * depth * width,
            bytes_accessed=(2 * n_blocks + 2) * 2**20,
            transcendentals=0,
        ),
        name="project",
    )(meta, *operands)
    return out if n_taken else out[0]


def grad_kernel(wplan, n_g, n_w, meta_ref, *refs):
    g_in, w_in = refs[:n_g], refs[n_g:n_g + n_w]
    own_ref, lo_ref, hi_ref = refs[n_g + n_w:n_g + n_w + 3]
    gbuf, wbuf, total, gsems, wsems = refs[n_g + n_w + 3:]
    step = pl.program_id(0)
    half = own_ref.shape[0]
    wh = wbuf.shape[1] // 2

    slots = gbuf.shape[0]

    def g_copy(j):
        return pltpu.make_async_copy(g_in[j], gbuf.at[j % slots], gsems.at[j])

    def w_copy(n):
        ref, source, block, part = wplan[n]
        place = meta_ref[AT_W + block]
        return pltpu.make_async_copy(
            w_in[ref].at[pl.ds(source, wh)],
            wbuf.at[place, pl.ds(part * wh, wh)],
            wsems.at[part, place],
        )

    @pl.when(step == 0)
    def _():
        for j in range(slots):
            g_copy(j).start()
        for n in range(16):
            w_copy(n).start()

    for j in range(8):

        @pl.when(step == j)
        def _():
            g_copy(j).wait()

    place = meta_ref[AT_G + step]
    for part in range(2):
        pltpu.make_async_copy(
            w_in[0].at[pl.ds(0, wh)], wbuf.at[place, pl.ds(part * wh, wh)], wsems.at[part, place]
        ).wait()

    @pl.when(step == 0)
    def _():
        total[...] = jnp.dot(gbuf[0], wbuf[place], preferred_element_type=F32)

    @pl.when(step > 0)
    def _():
        total[...] += jnp.dot(gbuf[step % slots], wbuf[place], preferred_element_type=F32)

    for j in range(8 - slots):

        @pl.when(step == j)
        def _():
            g_copy(j + slots).start()

    @pl.when(step == 7)
    def _():
        own_ref[...] = total[:half, :]
        lo_ref[...] = total[half:half + half // 2, :].astype(BF)
        hi_ref[...] = total[half + half // 2:, :].astype(BF)


def attn_grad_part(g_pieces, w_pieces, wplan, meta):
    tokens, depth = g_pieces[0].shape
    width = w_pieces[0].shape[1]
    half = tokens // 2
    kernel = functools.partial(grad_kernel, wplan, len(g_pieces), len(w_pieces))
    whole = pl.BlockSpec(memory_space=pltpu.VMEM)
    return pl.pallas_call(
        kernel,
        grid_spec=pltpu.PrefetchScalarGridSpec(
            num_scalar_prefetch=1,
            grid=(8,),
            in_specs=[pl.BlockSpec(memory_space=pltpu.HBM)] * (len(g_pieces) + len(w_pieces)),
            out_specs=[whole] * 3,
            scratch_shapes=[
                pltpu.VMEM((3, tokens, depth), BF),
                pltpu.VMEM((8, depth, width), BF),
                pltpu.VMEM((tokens, width), F32),
                pltpu.SemaphoreType.DMA((8,)),
                pltpu.SemaphoreType.DMA((2, 8)),
            ],
        ),
        out_shape=[
            jax.ShapeDtypeStruct((half, width), F32),
            jax.ShapeDtypeStruct((half // 2, width), BF),
            jax.ShapeDtypeStruct((half // 2, width), BF),
        ],
        compiler_params=params(26),
        cost_estimate=pl.CostEstimate(
            flops=16 * tokens * depth * width,
            bytes_accessed=20 * 2**20,
            transcendentals=0,
        ),
        name="attn_grad",
    )(meta, *g_pieces, *w_pieces)


def fetch_kernel(plan, meta_ref, buffer_ref, *refs):
    outs, sems = refs[:-1], refs[-1]
    copies = []
    for n, (out, start, at, half) in enumerate(plan):
        source = buffer_ref.at[half, meta_ref[at]]
        target = outs[out].at[pl.ds(start, source.shape[0])]
        copies.append(pltpu.make_async_copy(source, target, sems.at[n]))
    for copy in copies:
        copy.start()
    for copy in copies:
        copy.wait()


def fetch(buffer, meta, plan):
    _, _, rows, width = buffer.shape
    n_out = 1 + plan[-1][0]
    here = pl.BlockSpec(memory_space=pltpu.VMEM)
    return pl.pallas_call(
        functools.partial(fetch_kernel, plan),
        grid_spec=pltpu.PrefetchScalarGridSpec(
            num_scalar_prefetch=1,
            grid=(1,),
            in_specs=[pl.BlockSpec(memory_space=pltpu.HBM)],
            out_specs=[here] * n_out,
            scratch_shapes=[pltpu.SemaphoreType.DMA((len(plan),))],
        ),
        out_shape=[jax.ShapeDtypeStruct((2 * rows, width), BF)] * n_out,
        compiler_params=params(8),
        cost_estimate=pl.CostEstimate(
            flops=0, bytes_accessed=2**16, transcendentals=0
        ),
        name="fetch",
    )(meta, buffer)


def add_kernel(n_terms, plan, *refs):
    terms, outs = refs[:n_terms], refs[n_terms:]
    for out, start, rows, parts in plan:
        value = None
        for term, first in parts:
            part = terms[term][first:first + rows, :].astype(F32)
            value = part if value is None else value + part
        outs[out][start:start + rows, :] = value.astype(BF)


def add_rows(terms, plan, result=False):
    width = terms[0].shape[1]
    n_out = 1 + plan[-1][0]
    shapes = [(sum(p[2] for p in plan if p[0] == n), width) for n in range(n_out)]
    here = pl.BlockSpec(memory_space=pltpu.VMEM)
    outs = [pl.BlockSpec(shape, lambda i: (0, 0)) if result else here for shape in shapes]
    return pl.pallas_call(
        functools.partial(add_kernel, len(terms), plan),
        grid=(1,),
        in_specs=[here] * len(terms),
        out_specs=outs,
        out_shape=[jax.ShapeDtypeStruct(shape, BF) for shape in shapes],
        compiler_params=params(12),
        cost_estimate=pl.CostEstimate(
            flops=2**21, bytes_accessed=5 * 2**20, transcendentals=0
        ),
        name="add_rows",
    )(*terms)


def local(query_rows, key_rows, value_rows, output_grad, out_proj, segment_ids):
    count = query_rows.shape[0]
    half_d = output_grad.shape[1] // 2
    row, col = lax.axis_index("row"), lax.axis_index("col")
    meta = positions(row, col)
    k = row % 2

    g_give = lax.dynamic_slice_in_dim(output_grad, (1 - k) * half_d, half_d, 1)
    (output_grad,) = tied((output_grad,), g_give)
    g_keep = lax.dynamic_slice_in_dim(output_grad, k * half_d, half_d, 1)
    kv_earlier = passed_along(jnp.concatenate([key_rows, value_rows], 1), "row", 1)
    g_got, meta = tied((move_row(g_give, dk=1), meta))
    g0 = jnp.concatenate([g_keep, g_got], 0)
    segments = segment_ids.reshape(-1, LANES)

    out_proj, kv_earlier = tied((out_proj, kv_earlier), g0)
    gy = move_col(g0, dyl=1)
    gxm = move_col(g0, dx=1)
    gxp = move_col(g0, dx=-1)
    wzm = move_row(out_proj, dz=1)
    wzp = move_row(out_proj, dz=-1)

    (query_held,) = tied((query_rows,), g0)
    attn_out, top, total = attend(meta, query_held, kv_earlier, key_rows, value_rows, segments)

    gy, gxm, gxp, attn_out = tied((gy, gxm, gxp, attn_out))
    wzm, wzp, out_proj = tied((wzm, wzp, out_proj), gxm)

    hw = out_proj.shape[0] // 2
    gyxm = move_col(gy, dx=1)
    gyxp = move_col(gy, dx=-1)
    a_other = move_row(attn_out, dk=1)
    wo = move_row(wzm, dz=1)
    wy = move_row(out_proj, dyh=1)

    a_pair = jnp.concatenate([attn_out, a_other], 0)
    proj = project([g0, gxm, gxp, gy], a_pair, meta, range(4), None)

    go = move_col(gxm, dx=1)
    gyxm, gyxp, proj = tied((gyxm, gyxp, proj))
    gyo = move_col(gyxp, dx=-1)
    wo, wy = tied((wo, wy), gyxp)
    wyzm = move_row(wy, dz=1)
    wyzp = move_row(wy, dz=-1)
    wyo = move_row(wo, dyh=1)

    proj = project([gyxm, gyxp], a_pair, meta, (4, 5), proj)
    proj = project([go], a_pair, meta, (6,), proj)

    q = hw // 2
    far, up, dn = at_w(2, 1), at_w(1, 1), at_w(-1, 1)
    own_up, own_dn = at_w(1, 0), at_w(-1, 0)
    proj, give_far, give_up, give_dn, up2, dn2 = project(
        [gyo],
        a_pair,
        meta,
        (7,),
        proj,
        (
            (0, 0, far, 0, 0, hw), (0, hw, far, 1, 0, hw),
            (1, 0, up, 0, 0, hw), (1, hw, up, 1, 0, hw), (1, 2 * hw, own_up, 1, 0, q),
            (2, 0, dn, 0, 0, hw), (2, hw, dn, 1, 0, hw), (2, 2 * hw, own_dn, 0, 0, q),
            (3, 0, own_up, 1, q, q),
            (4, 0, own_dn, 0, q, q),
        ),
    )
    ry = move_row(give_far, dyh=1)
    rup = move_row(give_up, dz=1)
    rdn = move_row(give_dn, dz=-1)

    g_pieces = [g0, gxm, gxp, gy, gyxm, gyxp, go, gyo]
    w_pieces = [out_proj, wzm, wzp, wy, wyzm, wyzp, wyo, wo]
    wplan = [(i, p * hw, i, p) for i in range(8) for p in range(2)]
    (meta,) = tied((meta,), give_up)
    grad_own, give_lo, give_hi = attn_grad_part(g_pieces, w_pieces, wplan, meta)
    got_lo, got_hi = move_row(give_lo, dk=1), move_row(give_hi, dk=1)
    far, middle, near, own = fetch(
        proj,
        meta,
        (
            (0, 0, at_w(2, 0), 0), (0, hw, at_w(2, 0), 1),
            (1, 0, at_w(0, 1), 0), (1, hw, at_w(0, 1), 1),
            (2, 0, own_up, 0), (2, hw, own_dn, 1),
            (3, 0, at_w(0, 0), 0), (3, hw, at_w(0, 0), 1),
        ),
    )
    (attn_grad,) = add_rows(
        [grad_own, got_lo, got_hi],
        ((0, 0, hw, ((0, 0), (1, 0))), (0, hw, hw, ((0, hw), (2, 0)))),
    )
    part = functools.partial(
        attend_back, meta, query_rows, attn_grad, kv_earlier, key_rows, value_rows, segments, top, total
    )
    heads = query_rows.shape[1] // HD
    cuts = heads // 4, 5 * heads // 8
    held = part((0, cuts[0]), None)

    ry, *held = tied((ry, *held))

    far_up, far_dn = add_rows(
        [far, ry], ((0, 0, hw, ((0, 0), (1, 0))), (1, 0, hw, ((0, hw), (1, hw))))
    )
    fup = move_row(far_up, dz=1)
    fdn = move_row(far_dn, dz=-1)
    rup, rdn, up2, dn2 = tied((rup, rdn, up2, dn2), far_up)
    (across,) = add_rows([middle, rup, rdn], ((0, 0, 2 * hw, ((0, 0), (1, 0), (2, 0))),))
    held = tied(held, across)
    across = move_row(across, dyh=1)
    up2 = move_row(up2, dz=1)
    dn2 = move_row(dn2, dz=-1)
    held = part(cuts, held)

    fup, fdn, *held = tied((fup, fdn, *held))

    near_up, near_dn = add_rows(
        [near, fup, fdn], ((0, 0, hw, ((0, 0), (1, 0))), (1, 0, hw, ((0, hw), (2, 0))))
    )
    nup = move_row(near_up, dz=1)
    ndn = move_row(near_dn, dz=-1)

    *held, up2, dn2 = tied((*held, up2, dn2), near_up)
    query_grad, dkey, dvalue = part((cuts[1], heads), held)
    back = passed_along(
        jnp.concatenate([dkey[:count], dvalue[:count]], 1).astype(BF), "row", -1
    ).astype(F32)
    key_grad = (dkey[count:] + back[:, :HD]).astype(BF)
    value_grad = (dvalue[count:] + back[:, HD:]).astype(BF)

    (proj_grad,) = add_rows(
        [own, across, nup, ndn, rup, up2, rdn, dn2],
        (
            (0, 0, q, ((0, 0), (1, 0), (2, 0), (6, 2 * hw))),
            (0, q, q, ((0, q), (1, q), (2, q), (7, 0))),
            (0, 2 * q, q, ((0, 2 * q), (1, 2 * q), (4, 2 * hw), (3, 0))),
            (0, 3 * q, q, ((0, 3 * q), (1, 3 * q), (5, 0), (3, q))),
        ),
        result=True,
    )
    return (query_grad, key_grad, value_grad, proj_grad)


def solution(mesh):
    placed = (
        P("row", "col"),
        P("row", "col"),
        P("row", "col"),
        P("row", "col"),
        P("row", "col"),
        P(),
    )
    return jax.shard_map(
        local,
        mesh=mesh,
        in_specs=placed,
        out_specs=(P("row", "col"), P("row", "col"), P("row", "col"), P("row", "col")),
        check_vma=False,
    )
```

```python
import functools
import math

import jax
import jax.numpy as jnp
from jax import lax
from jax.experimental import pallas as pl
from jax.experimental.pallas import tpu as pltpu
from jax.sharding import PartitionSpec as P

HD = 128
SCALE = 1.0 / math.sqrt(HD)
NEG = -1e30
BF = jnp.bfloat16
F32 = jnp.float32

PLACES = 64

ZN, YN, KN, LN, XN = 4, 2, 2, 2, 4


AT_FIRST, AT_ROW, AT_EARLIER, AT_G, AT_W = 0, 1, 2, 8, 16
G_STEPS = [(0, 0), (0, -1), (0, 1), (1, 0), (1, -1), (1, 1), (0, 2), (1, 2)]
W_STEPS = [(0, 0), (-1, 0), (1, 0), (0, 1), (-1, 1), (1, 1), (2, 1), (2, 0)]
LANES = 128


def positions(row, col):
    z, yh, yl, x = row // 4, row // 2 % 2, col // 4, col % 4
    head = jnp.stack([(row == 0).astype(jnp.int32), row, jnp.maximum(row - 1, 0)] + [row] * 5)
    steps = [jnp.asarray([step[i] for step in order], jnp.int32) for order in (G_STEPS, W_STEPS) for i in (0, 1)]
    dyl, dx, dz, dyh = steps
    g = ((yl + dyl) & 1) * 4 + ((x + dx) & 3)
    w = ((z + dz) & 3) * 2 + ((yh + dyh) & 1)
    return jnp.concatenate([head, g, w])


def at_w(dz, dyh):
    return AT_W + W_STEPS.index((dz, dyh))


def move_row(value, dz=0, dyh=0, dk=0):
    pairs = []
    for z in range(ZN):
        for y in range(YN):
            for k in range(KN):
                source = (z * YN + y) * KN + k
                target = ((z + dz) % ZN * YN + (y + dyh) % YN) * KN + (k + dk) % KN
                pairs.append((source, target))
    return lax.ppermute(value, "row", pairs)


def move_col(value, dx=0, dyl=0):
    pairs = []
    for y in range(LN):
        for x in range(XN):
            pairs.append((y * XN + x, (y + dyl) % LN * XN + (x + dx) % XN))
    return lax.ppermute(value, "col", pairs)


def passed_along(value, axis, steps):
    count = lax.axis_size(axis)
    first, last = (max(0, -steps), min(count, count - steps))
    return lax.ppermute(value, axis, [(source, source + steps) for source in range(first, last)])


def tied(values, *others):
    held = lax.optimization_barrier((tuple(values), tuple(others)))
    return held[0]


def params(mib, **kw):
    return pltpu.CompilerParams(vmem_limit_bytes=mib * 1024 * 1024, **kw)


def prepare(meta_ref, seg_ref, kv_ref, k_ref, v_ref, bias_ref, k_pair, v_pair, turned, of_keys):
    count = k_ref.shape[0]
    parts = count // LANES
    first, row, earlier = meta_ref[AT_FIRST], meta_ref[AT_ROW], meta_ref[AT_EARLIER]
    own = [seg_ref[pl.ds(row * parts + i, 1), :] for i in range(parts)]
    before = [seg_ref[pl.ds(earlier * parts + i, 1), :] for i in range(parts)]
    key_at = lax.broadcasted_iota(jnp.int32, (LANES, LANES), 0)
    query_at = lax.broadcasted_iota(jnp.int32, (LANES, LANES), 1)
    for i, keys in enumerate(before + own):
        column = jnp.broadcast_to(keys.astype(F32), (LANES, LANES)).T
        for j in range(parts):
            ok = column == own[j].astype(F32)
            if i < parts:
                ok = ok & (first == 0)
            else:
                ok = ok & (key_at + (i - parts) * LANES <= query_at + j * LANES)
            bias_ref[i * LANES:(i + 1) * LANES, j * LANES:(j + 1) * LANES] = jnp.where(
                ok, 0.0, NEG
            ).astype(F32)
    k_pair[:count, :] = kv_ref[:, :HD]
    k_pair[count:, :] = k_ref[...]
    v_pair[:count, :] = kv_ref[:, HD:]
    v_pair[count:, :] = v_ref[...]
    turned[...] = (k_pair if of_keys else v_pair)[...].astype(F32).T.astype(BF)


def pair_scratch(count):
    return [
        pltpu.VMEM((2 * count, count), F32),
        pltpu.VMEM((2 * count, HD), BF),
        pltpu.VMEM((2 * count, HD), BF),
        pltpu.VMEM((HD, 2 * count), BF),
    ]


def chunk_list(count, width):
    return [(i * width, count + (i + 1) * width) for i in range(count // width)]


def fwd_kernel(
    meta_ref, q_ref, kv_ref, k_ref, v_ref, seg_ref, out_ref, top_ref, sum_ref,
    bias_ref, k_pair, v_pair, vt_ref,
):
    count = q_ref.shape[0]

    @pl.when(pl.program_id(0) == 0)
    def _():
        prepare(meta_ref, seg_ref, kv_ref, k_ref, v_ref, bias_ref, k_pair, v_pair, vt_ref, False)

    for start, keys in chunk_list(count, 256):
        cols = slice(start, start + 256)
        s = lax.dot_general(
            k_pair[:keys, :], q_ref[cols, :], (((1,), (1,)), ((), ())), preferred_element_type=F32
        )
        s = s * SCALE + bias_ref[:keys, cols]
        top = jnp.max(s, axis=0, keepdims=True)
        e = jnp.exp(s - top)
        total = jnp.sum(e, axis=0, keepdims=True)
        inv = 1.0 / total
        p = (e * inv).astype(BF)
        a = jnp.dot(vt_ref[:, :keys], p, preferred_element_type=F32)
        out_ref[cols, :] = a.T.astype(BF)
        top_ref[0, :, cols] = top
        sum_ref[0, :, cols] = inv


def attend(meta, query, kv_earlier, key_rows, value_rows, segments):
    count, width = query.shape
    heads = width // HD
    whole = lambda value: pl.BlockSpec(value.shape, lambda h, m: (0, 0))
    head = pl.BlockSpec((count, HD), lambda h, m: (0, h))
    stat = pl.BlockSpec((1, 1, count), lambda h, m: (h, 0, 0))
    return pl.pallas_call(
        fwd_kernel,
        grid_spec=pltpu.PrefetchScalarGridSpec(
            num_scalar_prefetch=1,
            grid=(heads,),
            in_specs=[head] + [whole(v) for v in (kv_earlier, key_rows, value_rows, segments)],
            out_specs=[head, stat, stat],
            scratch_shapes=pair_scratch(count),
        ),
        out_shape=[
            jax.ShapeDtypeStruct((count, width), BF),
            jax.ShapeDtypeStruct((heads, 1, count), F32),
            jax.ShapeDtypeStruct((heads, 1, count), F32),
        ],
        compiler_params=params(16),
        cost_estimate=pl.CostEstimate(
            flops=heads * 64 * 2 * 2 * count * count * HD,
            bytes_accessed=8 * 2**20,
            transcendentals=heads * 2 * count * count,
        ),
        name="attend",
    )(meta, query, kv_earlier, key_rows, value_rows, segments)


def bwd_kernel(
    n_held, last, meta_ref, q_ref, g_ref, kv_ref, k_ref, v_ref, seg_ref, top_ref, sum_ref, *refs
):
    dk_in, dv_in = refs[:2] if n_held else (None, None)
    dq_ref, dk_ref, dv_ref, bias_ref, k_pair, v_pair, kt_ref = refs[n_held:]
    count = q_ref.shape[0]

    @pl.when(pl.program_id(0) == 0)
    def _():
        prepare(meta_ref, seg_ref, kv_ref, k_ref, v_ref, bias_ref, k_pair, v_pair, kt_ref, True)
        if n_held:
            dk_ref[...] = dk_in[...]
            dv_ref[...] = dv_in[...]
        else:
            dk_ref[...] = jnp.zeros_like(dk_ref)
            dv_ref[...] = jnp.zeros_like(dv_ref)

    for start, keys in chunk_list(count, 256):
        cols = slice(start, start + 256)
        q = q_ref[cols, :]
        g = g_ref[cols, :]
        s = lax.dot_general(
            k_pair[:keys, :], q, (((1,), (1,)), ((), ())), preferred_element_type=F32
        )
        s = s * SCALE + bias_ref[:keys, cols]
        p = jnp.exp(s - top_ref[0, :, cols]) * sum_ref[0, :, cols]
        dp = lax.dot_general(
            v_pair[:keys, :], g, (((1,), (1,)), ((), ())), preferred_element_type=F32
        )
        delta = jnp.sum(p * dp, axis=0, keepdims=True)
        ds = (p * (dp - delta)).astype(BF)
        dq = jnp.dot(kt_ref[:, :keys], ds, preferred_element_type=F32) * SCALE
        dq_ref[cols, :] = dq.T.astype(BF)
        dk_ref[:keys, :] += jnp.dot(ds, q, preferred_element_type=F32)
        dv_ref[:keys, :] += jnp.dot(p.astype(BF), g, preferred_element_type=F32)

    if last:

        @pl.when(pl.program_id(0) == pl.num_programs(0) - 1)
        def _():
            dk_ref[...] = dk_ref[...] * SCALE


def attend_back(
    meta, query, grad, kv_earlier, key_rows, value_rows, segments, top, total, heads, held
):
    count, width = query.shape
    begin, end = heads
    last = end == width // HD
    whole = lambda value: pl.BlockSpec(value.shape, lambda h, m: (0, 0))
    head = pl.BlockSpec((count, HD), lambda h, m: (0, h + begin))
    stat = pl.BlockSpec((1, 1, count), lambda h, m: (h + begin, 0, 0))
    pair = pl.BlockSpec((2 * count, HD), lambda h, m: (0, 0))
    earlier = () if held is None else (held[1], held[2], held[0])
    return pl.pallas_call(
        functools.partial(bwd_kernel, len(earlier), last),
        grid_spec=pltpu.PrefetchScalarGridSpec(
            num_scalar_prefetch=1,
            grid=(end - begin,),
            in_specs=[head, head]
            + [whole(v) for v in (kv_earlier, key_rows, value_rows, segments)]
            + [stat, stat]
            + ([pair, pair, pl.BlockSpec(memory_space=pl.ANY)] if earlier else []),
            out_specs=[head, pair, pair],
            scratch_shapes=pair_scratch(count),
        ),
        out_shape=[
            jax.ShapeDtypeStruct((count, width), BF),
            jax.ShapeDtypeStruct((2 * count, HD), F32),
            jax.ShapeDtypeStruct((2 * count, HD), F32),
        ],
        input_output_aliases={11: 0} if earlier else {},
        compiler_params=params(22),
        cost_estimate=pl.CostEstimate(
            flops=(end - begin) * 10 * 2 * 2 * count * count * HD if begin else 2**20,
            bytes_accessed=6 * 2**20 if begin else 2**16,
            transcendentals=(end - begin) * 2 * count * count if begin else 0,
        ),
        name="attend_back",
    )(meta, query, grad, kv_earlier, key_rows, value_rows, segments, top, total, *earlier)


def proj_kernel(slots, held, plan, meta_ref, *refs):
    n_in = len(slots)
    pieces, a_ref = refs[:n_in], refs[n_in]
    refs = refs[n_in + 1 + held:]
    buffer_ref, taken = refs[0], refs[1:-3]
    done, sems, take_sems = refs[-3:]
    step = pl.program_id(0)
    rows = done.shape[2]

    def put(j):
        return pltpu.make_async_copy(done.at[j], buffer_ref.at[:, meta_ref[AT_G + slots[j]]], sems.at[j])

    def take(i, made):
        out, start, at, half, first, count = plan[i]
        if made is None:
            source = buffer_ref.at[half, meta_ref[at], pl.ds(first, count)]
        else:
            source = done.at[made, half, pl.ds(first, count)]
        target = taken[out].at[pl.ds(start, count)]
        return pltpu.make_async_copy(source, target, take_sems.at[i])

    def made_here(i, j):
        return meta_ref[plan[i][2]] == meta_ref[AT_G + slots[j]]

    @pl.when(step == 0)
    def _():
        for i in range(len(plan)):
            here = made_here(i, 0)
            for j in range(1, n_in):
                here = here | made_here(i, j)

            @pl.when(jnp.logical_not(here))
            def _():
                take(i, None).start()

    for j in range(n_in):

        @pl.when(step == j)
        def _():
            value = lax.dot_general(
                pieces[j][...], a_ref[...], (((0,), (0,)), ((), ())), preferred_element_type=F32
            ).astype(BF)
            done[j, 0] = value[:rows]
            done[j, 1] = value[rows:]
            put(j).start()
            for i in range(len(plan)):

                @pl.when(made_here(i, j))
                def _():
                    take(i, j).start()

    @pl.when(step == n_in - 1)
    def _():
        for j in range(n_in):
            put(j).wait()
        for i in range(len(plan)):
            take(i, None).wait()


def project(pieces, a_pair, meta, slots, buffer, plan=()):
    tokens, width = a_pair.shape
    depth = pieces[0].shape[1]
    n_blocks = len(pieces)
    held = int(buffer is not None)
    here = pl.BlockSpec(memory_space=pltpu.VMEM)
    there = pl.BlockSpec(memory_space=pltpu.HBM)
    operands = (*pieces, a_pair) + ((buffer,) if held else ())
    shape = (2, depth // 2, width)
    n_taken = 1 + max((entry[0] for entry in plan), default=-1)
    taken = [(sum(e[5] for e in plan if e[0] == i), width) for i in range(n_taken)]
    out = pl.pallas_call(
        functools.partial(proj_kernel, tuple(slots), held, plan),
        grid_spec=pltpu.PrefetchScalarGridSpec(
            num_scalar_prefetch=1,
            grid=(n_blocks,),
            in_specs=[here] * (n_blocks + 1) + [there] * held,
            out_specs=[there] + [here] * n_taken,
            scratch_shapes=[
                pltpu.VMEM((n_blocks, *shape), BF),
                pltpu.SemaphoreType.DMA((n_blocks,)),
                pltpu.SemaphoreType.DMA((max(len(plan), 1),)),
            ],
        ),
        out_shape=[jax.ShapeDtypeStruct((2, PLACES, depth // 2, width), BF)]
        + [jax.ShapeDtypeStruct(t, BF) for t in taken],
        input_output_aliases={n_blocks + 2: 0} if held else {},
        compiler_params=params(16),
        cost_estimate=pl.CostEstimate(
            flops=2 * n_blocks * tokens * depth * width,
            bytes_accessed=(2 * n_blocks + 2) * 2**20,
            transcendentals=0,
        ),
        name="project",
    )(meta, *operands)
    return out if n_taken else out[0]


def grad_kernel(wplan, n_g, n_w, meta_ref, *refs):
    g_in, w_in = refs[:n_g], refs[n_g:n_g + n_w]
    own_ref, lo_ref, hi_ref = refs[n_g + n_w:n_g + n_w + 3]
    gbuf, wbuf, total, gsems, wsems = refs[n_g + n_w + 3:]
    step = pl.program_id(0)
    half = own_ref.shape[0]
    wh = wbuf.shape[1] // 2

    slots = gbuf.shape[0]

    def g_copy(j):
        return pltpu.make_async_copy(g_in[j], gbuf.at[j % slots], gsems.at[j])

    def w_copy(n):
        ref, source, block, part = wplan[n]
        place = meta_ref[AT_W + block]
        return pltpu.make_async_copy(
            w_in[ref].at[pl.ds(source, wh)],
            wbuf.at[place, pl.ds(part * wh, wh)],
            wsems.at[part, place],
        )

    @pl.when(step == 0)
    def _():
        for j in range(slots):
            g_copy(j).start()
        for n in range(16):
            w_copy(n).start()

    for j in range(8):

        @pl.when(step == j)
        def _():
            g_copy(j).wait()

    place = meta_ref[AT_G + step]
    for part in range(2):
        pltpu.make_async_copy(
            w_in[0].at[pl.ds(0, wh)], wbuf.at[place, pl.ds(part * wh, wh)], wsems.at[part, place]
        ).wait()

    @pl.when(step == 0)
    def _():
        total[...] = jnp.dot(gbuf[0], wbuf[place], preferred_element_type=F32)

    @pl.when(step > 0)
    def _():
        total[...] += jnp.dot(gbuf[step % slots], wbuf[place], preferred_element_type=F32)

    for j in range(8 - slots):

        @pl.when(step == j)
        def _():
            g_copy(j + slots).start()

    @pl.when(step == 7)
    def _():
        own_ref[...] = total[:half, :]
        lo_ref[...] = total[half:half + half // 2, :].astype(BF)
        hi_ref[...] = total[half + half // 2:, :].astype(BF)


def attn_grad_part(g_pieces, w_pieces, wplan, meta):
    tokens, depth = g_pieces[0].shape
    width = w_pieces[0].shape[1]
    half = tokens // 2
    kernel = functools.partial(grad_kernel, wplan, len(g_pieces), len(w_pieces))
    whole = pl.BlockSpec(memory_space=pltpu.VMEM)
    return pl.pallas_call(
        kernel,
        grid_spec=pltpu.PrefetchScalarGridSpec(
            num_scalar_prefetch=1,
            grid=(8,),
            in_specs=[pl.BlockSpec(memory_space=pltpu.HBM)] * (len(g_pieces) + len(w_pieces)),
            out_specs=[whole] * 3,
            scratch_shapes=[
                pltpu.VMEM((3, tokens, depth), BF),
                pltpu.VMEM((8, depth, width), BF),
                pltpu.VMEM((tokens, width), F32),
                pltpu.SemaphoreType.DMA((8,)),
                pltpu.SemaphoreType.DMA((2, 8)),
            ],
        ),
        out_shape=[
            jax.ShapeDtypeStruct((half, width), F32),
            jax.ShapeDtypeStruct((half // 2, width), BF),
            jax.ShapeDtypeStruct((half // 2, width), BF),
        ],
        compiler_params=params(26),
        cost_estimate=pl.CostEstimate(
            flops=16 * tokens * depth * width,
            bytes_accessed=20 * 2**20,
            transcendentals=0,
        ),
        name="attn_grad",
    )(meta, *g_pieces, *w_pieces)


def fetch_kernel(plan, meta_ref, buffer_ref, *refs):
    outs, sems = refs[:-1], refs[-1]
    copies = []
    for n, (out, start, at, half) in enumerate(plan):
        source = buffer_ref.at[half, meta_ref[at]]
        target = outs[out].at[pl.ds(start, source.shape[0])]
        copies.append(pltpu.make_async_copy(source, target, sems.at[n]))
    for copy in copies:
        copy.start()
    for copy in copies:
        copy.wait()


def fetch(buffer, meta, plan):
    _, _, rows, width = buffer.shape
    n_out = 1 + plan[-1][0]
    here = pl.BlockSpec(memory_space=pltpu.VMEM)
    return pl.pallas_call(
        functools.partial(fetch_kernel, plan),
        grid_spec=pltpu.PrefetchScalarGridSpec(
            num_scalar_prefetch=1,
            grid=(1,),
            in_specs=[pl.BlockSpec(memory_space=pltpu.HBM)],
            out_specs=[here] * n_out,
            scratch_shapes=[pltpu.SemaphoreType.DMA((len(plan),))],
        ),
        out_shape=[jax.ShapeDtypeStruct((2 * rows, width), BF)] * n_out,
        compiler_params=params(8),
        cost_estimate=pl.CostEstimate(
            flops=0, bytes_accessed=2**16, transcendentals=0
        ),
        name="fetch",
    )(meta, buffer)


def add_kernel(n_terms, plan, *refs):
    terms, outs = refs[:n_terms], refs[n_terms:]
    for out, start, rows, parts in plan:
        value = None
        for term, first in parts:
            part = terms[term][first:first + rows, :].astype(F32)
            value = part if value is None else value + part
        outs[out][start:start + rows, :] = value.astype(BF)


def add_rows(terms, plan, result=False):
    width = terms[0].shape[1]
    n_out = 1 + plan[-1][0]
    shapes = [(sum(p[2] for p in plan if p[0] == n), width) for n in range(n_out)]
    here = pl.BlockSpec(memory_space=pltpu.VMEM)
    outs = [pl.BlockSpec(shape, lambda i: (0, 0)) if result else here for shape in shapes]
    return pl.pallas_call(
        functools.partial(add_kernel, len(terms), plan),
        grid=(1,),
        in_specs=[here] * len(terms),
        out_specs=outs,
        out_shape=[jax.ShapeDtypeStruct(shape, BF) for shape in shapes],
        compiler_params=params(12),
        cost_estimate=pl.CostEstimate(
            flops=2**21, bytes_accessed=5 * 2**20, transcendentals=0
        ),
        name="add_rows",
    )(*terms)


def local(query_rows, key_rows, value_rows, output_grad, out_proj, segment_ids):
    count = query_rows.shape[0]
    half_d = output_grad.shape[1] // 2
    row, col = lax.axis_index("row"), lax.axis_index("col")
    meta = positions(row, col)
    k = row % 2

    g_keep = lax.dynamic_slice_in_dim(output_grad, k * half_d, half_d, 1)
    g_give = lax.dynamic_slice_in_dim(output_grad, (1 - k) * half_d, half_d, 1)
    kv_earlier = passed_along(jnp.concatenate([key_rows, value_rows], 1), "row", 1)
    g_got, meta = tied((move_row(g_give, dk=1), meta))
    g0 = jnp.concatenate([g_keep, g_got], 0)
    segments = segment_ids.reshape(-1, LANES)

    out_proj, kv_earlier = tied((out_proj, kv_earlier), g0)
    gy = move_col(g0, dyl=1)
    gxm = move_col(g0, dx=1)
    gxp = move_col(g0, dx=-1)
    wzm = move_row(out_proj, dz=1)
    wzp = move_row(out_proj, dz=-1)

    (query_held,) = tied((query_rows,), g0)
    attn_out, top, total = attend(meta, query_held, kv_earlier, key_rows, value_rows, segments)

    gy, attn_out = tied((gy, attn_out))
    gxm, gxp = tied((gxm, gxp), gy)
    wzm, wzp, out_proj = tied((wzm, wzp, out_proj), gxm)

    hw = out_proj.shape[0] // 2
    gyxm = move_col(gy, dx=1)
    gyxp = move_col(gy, dx=-1)
    a_other = move_row(attn_out, dk=1)
    wo = move_row(wzm, dz=1)
    wy = move_row(out_proj, dyh=1)

    a_pair = jnp.concatenate([attn_out, a_other], 0)
    proj = project([g0, gxm, gxp, gy], a_pair, meta, range(4), None)

    go = move_col(gxm, dx=1)
    gyxm, gyxp, proj = tied((gyxm, gyxp, proj))
    gyo = move_col(gyxp, dx=-1)
    wo, wy = tied((wo, wy), gyxp)
    wyzm = move_row(wy, dz=1)
    wyzp = move_row(wy, dz=-1)
    wyo = move_row(wo, dyh=1)

    proj = project([gyxm, gyxp], a_pair, meta, (4, 5), proj)
    proj = project([go], a_pair, meta, (6,), proj)

    q = hw // 2
    far, up, dn = at_w(2, 1), at_w(1, 1), at_w(-1, 1)
    own_up, own_dn = at_w(1, 0), at_w(-1, 0)
    proj, give_far, give_up, give_dn, up2, dn2 = project(
        [gyo],
        a_pair,
        meta,
        (7,),
        proj,
        (
            (0, 0, far, 0, 0, hw), (0, hw, far, 1, 0, hw),
            (1, 0, up, 0, 0, hw), (1, hw, up, 1, 0, hw), (1, 2 * hw, own_up, 1, 0, q),
            (2, 0, dn, 0, 0, hw), (2, hw, dn, 1, 0, hw), (2, 2 * hw, own_dn, 0, 0, q),
            (3, 0, own_up, 1, q, q),
            (4, 0, own_dn, 0, q, q),
        ),
    )
    ry = move_row(give_far, dyh=1)
    rup = move_row(give_up, dz=1)
    rdn = move_row(give_dn, dz=-1)

    g_pieces = [g0, gxm, gxp, gy, gyxm, gyxp, go, gyo]
    w_pieces = [out_proj, wzm, wzp, wy, wyzm, wyzp, wyo, wo]
    wplan = [(i, p * hw, i, p) for i in range(8) for p in range(2)]
    (meta,) = tied((meta,), give_up)
    grad_own, give_lo, give_hi = attn_grad_part(g_pieces, w_pieces, wplan, meta)
    got_lo, got_hi = move_row(give_lo, dk=1), move_row(give_hi, dk=1)
    far, middle, near, own = fetch(
        proj,
        meta,
        (
            (0, 0, at_w(2, 0), 0), (0, hw, at_w(2, 0), 1),
            (1, 0, at_w(0, 1), 0), (1, hw, at_w(0, 1), 1),
            (2, 0, own_up, 0), (2, hw, own_dn, 1),
            (3, 0, at_w(0, 0), 0), (3, hw, at_w(0, 0), 1),
        ),
    )
    (attn_grad,) = add_rows(
        [grad_own, got_lo, got_hi],
        ((0, 0, hw, ((0, 0), (1, 0))), (0, hw, hw, ((0, hw), (2, 0)))),
    )
    part = functools.partial(
        attend_back, meta, query_rows, attn_grad, kv_earlier, key_rows, value_rows, segments, top, total
    )
    heads = query_rows.shape[1] // HD
    cuts = heads // 4, 5 * heads // 8
    held = part((0, cuts[0]), None)

    ry, *held = tied((ry, *held))

    far_up, far_dn = add_rows(
        [far, ry], ((0, 0, hw, ((0, 0), (1, 0))), (1, 0, hw, ((0, hw), (1, hw))))
    )
    fup = move_row(far_up, dz=1)
    fdn = move_row(far_dn, dz=-1)
    rup, rdn, up2, dn2 = tied((rup, rdn, up2, dn2), far_up)
    (across,) = add_rows([middle, rup, rdn], ((0, 0, 2 * hw, ((0, 0), (1, 0), (2, 0))),))
    held = tied(held, across)
    across = move_row(across, dyh=1)
    up2 = move_row(up2, dz=1)
    dn2 = move_row(dn2, dz=-1)
    held = part(cuts, held)

    fup, fdn, *held = tied((fup, fdn, *held))

    near_up, near_dn = add_rows(
        [near, fup, fdn], ((0, 0, hw, ((0, 0), (1, 0))), (1, 0, hw, ((0, hw), (2, 0))))
    )
    nup = move_row(near_up, dz=1)
    ndn = move_row(near_dn, dz=-1)

    *held, up2, dn2 = tied((*held, up2, dn2), near_up)
    query_grad, dkey, dvalue = part((cuts[1], heads), held)
    back = passed_along(
        jnp.concatenate([dkey[:count], dvalue[:count]], 1).astype(BF), "row", -1
    ).astype(F32)
    key_grad = (dkey[count:] + back[:, :HD]).astype(BF)
    value_grad = (dvalue[count:] + back[:, HD:]).astype(BF)

    (proj_grad,) = add_rows(
        [own, across, nup, ndn, rup, up2, rdn, dn2],
        (
            (0, 0, q, ((0, 0), (1, 0), (2, 0), (6, 2 * hw))),
            (0, q, q, ((0, q), (1, q), (2, q), (7, 0))),
            (0, 2 * q, q, ((0, 2 * q), (1, 2 * q), (4, 2 * hw), (3, 0))),
            (0, 3 * q, q, ((0, 3 * q), (1, 3 * q), (5, 0), (3, q))),
        ),
        result=True,
    )
    return (query_grad, key_grad, value_grad, proj_grad)


def solution(mesh):
    placed = (
        P("row", "col"),
        P("row", "col"),
        P("row", "col"),
        P("row", "col"),
        P("row", "col"),
        P(),
    )
    return jax.shard_map(
        local,
        mesh=mesh,
        in_specs=placed,
        out_specs=(P("row", "col"), P("row", "col"), P("row", "col"), P("row", "col")),
        check_vma=False,
    )
```

```python
import functools
import math

import jax
import jax.numpy as jnp
from jax import lax
from jax.experimental import pallas as pl
from jax.experimental.pallas import tpu as pltpu
from jax.sharding import PartitionSpec as P

HD = 128
SCALE = 1.0 / math.sqrt(HD)
NEG = -1e30
BF = jnp.bfloat16
F32 = jnp.float32

PLACES = 64

ZN, YN, KN, LN, XN = 4, 2, 2, 2, 4


AT_FIRST, AT_ROW, AT_EARLIER, AT_G, AT_W = 0, 1, 2, 8, 16
G_STEPS = [(0, 0), (0, -1), (0, 1), (1, 0), (1, -1), (1, 1), (0, 2), (1, 2)]
W_STEPS = [(0, 0), (-1, 0), (1, 0), (0, 1), (-1, 1), (1, 1), (2, 1), (2, 0)]
LANES = 128


def positions(row, col):
    z, yh, yl, x = row // 4, row // 2 % 2, col // 4, col % 4
    head = jnp.stack([(row == 0).astype(jnp.int32), row, jnp.maximum(row - 1, 0)] + [row] * 5)
    steps = [jnp.asarray([step[i] for step in order], jnp.int32) for order in (G_STEPS, W_STEPS) for i in (0, 1)]
    dyl, dx, dz, dyh = steps
    g = ((yl + dyl) & 1) * 4 + ((x + dx) & 3)
    w = ((z + dz) & 3) * 2 + ((yh + dyh) & 1)
    return jnp.concatenate([head, g, w])


def at_w(dz, dyh):
    return AT_W + W_STEPS.index((dz, dyh))


def move_row(value, dz=0, dyh=0, dk=0):
    pairs = []
    for z in range(ZN):
        for y in range(YN):
            for k in range(KN):
                source = (z * YN + y) * KN + k
                target = ((z + dz) % ZN * YN + (y + dyh) % YN) * KN + (k + dk) % KN
                pairs.append((source, target))
    return lax.ppermute(value, "row", pairs)


def move_col(value, dx=0, dyl=0):
    pairs = []
    for y in range(LN):
        for x in range(XN):
            pairs.append((y * XN + x, (y + dyl) % LN * XN + (x + dx) % XN))
    return lax.ppermute(value, "col", pairs)


def passed_along(value, axis, steps):
    count = lax.axis_size(axis)
    first, last = (max(0, -steps), min(count, count - steps))
    return lax.ppermute(value, axis, [(source, source + steps) for source in range(first, last)])


def tied(values, *others):
    held = lax.optimization_barrier((tuple(values), tuple(others)))
    return held[0]


def params(mib, **kw):
    return pltpu.CompilerParams(vmem_limit_bytes=mib * 1024 * 1024, **kw)


def prepare(meta_ref, seg_ref, kv_ref, k_ref, v_ref, bias_ref, k_pair, v_pair, turned, of_keys):
    count = k_ref.shape[0]
    parts = count // LANES
    first, row, earlier = meta_ref[AT_FIRST], meta_ref[AT_ROW], meta_ref[AT_EARLIER]
    own = [seg_ref[pl.ds(row * parts + i, 1), :] for i in range(parts)]
    before = [seg_ref[pl.ds(earlier * parts + i, 1), :] for i in range(parts)]
    key_at = lax.broadcasted_iota(jnp.int32, (LANES, LANES), 0)
    query_at = lax.broadcasted_iota(jnp.int32, (LANES, LANES), 1)
    for i, keys in enumerate(before + own):
        column = jnp.broadcast_to(keys.astype(F32), (LANES, LANES)).T
        for j in range(parts):
            ok = column == own[j].astype(F32)
            if i < parts:
                ok = ok & (first == 0)
            else:
                ok = ok & (key_at + (i - parts) * LANES <= query_at + j * LANES)
            bias_ref[i * LANES:(i + 1) * LANES, j * LANES:(j + 1) * LANES] = jnp.where(
                ok, 0.0, NEG
            ).astype(F32)
    k_pair[:count, :] = kv_ref[:, :HD]
    k_pair[count:, :] = k_ref[...]
    v_pair[:count, :] = kv_ref[:, HD:]
    v_pair[count:, :] = v_ref[...]
    turned[...] = (k_pair if of_keys else v_pair)[...].astype(F32).T.astype(BF)


def pair_scratch(count):
    return [
        pltpu.VMEM((2 * count, count), F32),
        pltpu.VMEM((2 * count, HD), BF),
        pltpu.VMEM((2 * count, HD), BF),
        pltpu.VMEM((HD, 2 * count), BF),
    ]


def chunk_list(count, width):
    return [(i * width, count + (i + 1) * width) for i in range(count // width)]


def fwd_kernel(
    meta_ref, q_ref, kv_ref, k_ref, v_ref, seg_ref, out_ref, top_ref, sum_ref,
    bias_ref, k_pair, v_pair, vt_ref,
):
    count = q_ref.shape[0]

    @pl.when(pl.program_id(0) == 0)
    def _():
        prepare(meta_ref, seg_ref, kv_ref, k_ref, v_ref, bias_ref, k_pair, v_pair, vt_ref, False)

    for start, keys in chunk_list(count, 256):
        cols = slice(start, start + 256)
        s = lax.dot_general(
            k_pair[:keys, :], q_ref[cols, :], (((1,), (1,)), ((), ())), preferred_element_type=F32
        )
        s = s * SCALE + bias_ref[:keys, cols]
        top = jnp.max(s, axis=0, keepdims=True)
        e = jnp.exp(s - top)
        total = jnp.sum(e, axis=0, keepdims=True)
        inv = 1.0 / total
        p = (e * inv).astype(BF)
        a = jnp.dot(vt_ref[:, :keys], p, preferred_element_type=F32)
        out_ref[cols, :] = a.T.astype(BF)
        top_ref[0, :, cols] = top
        sum_ref[0, :, cols] = inv


def attend(meta, query, kv_earlier, key_rows, value_rows, segments):
    count, width = query.shape
    heads = width // HD
    whole = lambda value: pl.BlockSpec(value.shape, lambda h, m: (0, 0))
    head = pl.BlockSpec((count, HD), lambda h, m: (0, h))
    stat = pl.BlockSpec((1, 1, count), lambda h, m: (h, 0, 0))
    return pl.pallas_call(
        fwd_kernel,
        grid_spec=pltpu.PrefetchScalarGridSpec(
            num_scalar_prefetch=1,
            grid=(heads,),
            in_specs=[head] + [whole(v) for v in (kv_earlier, key_rows, value_rows, segments)],
            out_specs=[head, stat, stat],
            scratch_shapes=pair_scratch(count),
        ),
        out_shape=[
            jax.ShapeDtypeStruct((count, width), BF),
            jax.ShapeDtypeStruct((heads, 1, count), F32),
            jax.ShapeDtypeStruct((heads, 1, count), F32),
        ],
        compiler_params=params(16),
        cost_estimate=pl.CostEstimate(
            flops=heads * 64 * 2 * 2 * count * count * HD,
            bytes_accessed=8 * 2**20,
            transcendentals=heads * 2 * count * count,
        ),
        name="attend",
    )(meta, query, kv_earlier, key_rows, value_rows, segments)


def bwd_kernel(
    n_held, last, meta_ref, q_ref, g_ref, kv_ref, k_ref, v_ref, seg_ref, top_ref, sum_ref, *refs
):
    dk_in, dv_in = refs[:2] if n_held else (None, None)
    dq_ref, dk_ref, dv_ref, bias_ref, k_pair, v_pair, kt_ref = refs[n_held:]
    count = q_ref.shape[0]

    @pl.when(pl.program_id(0) == 0)
    def _():
        prepare(meta_ref, seg_ref, kv_ref, k_ref, v_ref, bias_ref, k_pair, v_pair, kt_ref, True)
        if n_held:
            dk_ref[...] = dk_in[...]
            dv_ref[...] = dv_in[...]
        else:
            dk_ref[...] = jnp.zeros_like(dk_ref)
            dv_ref[...] = jnp.zeros_like(dv_ref)

    for start, keys in chunk_list(count, 256):
        cols = slice(start, start + 256)
        q = q_ref[cols, :]
        g = g_ref[cols, :]
        s = lax.dot_general(
            k_pair[:keys, :], q, (((1,), (1,)), ((), ())), preferred_element_type=F32
        )
        s = s * SCALE + bias_ref[:keys, cols]
        p = jnp.exp(s - top_ref[0, :, cols]) * sum_ref[0, :, cols]
        dp = lax.dot_general(
            v_pair[:keys, :], g, (((1,), (1,)), ((), ())), preferred_element_type=F32
        )
        delta = jnp.sum(p * dp, axis=0, keepdims=True)
        ds = (p * (dp - delta)).astype(BF)
        dq = jnp.dot(kt_ref[:, :keys], ds, preferred_element_type=F32) * SCALE
        dq_ref[cols, :] = dq.T.astype(BF)
        dk_ref[:keys, :] += jnp.dot(ds, q, preferred_element_type=F32)
        dv_ref[:keys, :] += jnp.dot(p.astype(BF), g, preferred_element_type=F32)

    if last:

        @pl.when(pl.program_id(0) == pl.num_programs(0) - 1)
        def _():
            dk_ref[...] = dk_ref[...] * SCALE


def attend_back(
    meta, query, grad, kv_earlier, key_rows, value_rows, segments, top, total, heads, held
):
    count, width = query.shape
    begin, end = heads
    last = end == width // HD
    whole = lambda value: pl.BlockSpec(value.shape, lambda h, m: (0, 0))
    head = pl.BlockSpec((count, HD), lambda h, m: (0, h + begin))
    stat = pl.BlockSpec((1, 1, count), lambda h, m: (h + begin, 0, 0))
    pair = pl.BlockSpec((2 * count, HD), lambda h, m: (0, 0))
    earlier = () if held is None else (held[1], held[2], held[0])
    return pl.pallas_call(
        functools.partial(bwd_kernel, len(earlier), last),
        grid_spec=pltpu.PrefetchScalarGridSpec(
            num_scalar_prefetch=1,
            grid=(end - begin,),
            in_specs=[head, head]
            + [whole(v) for v in (kv_earlier, key_rows, value_rows, segments)]
            + [stat, stat]
            + ([pair, pair, pl.BlockSpec(memory_space=pl.ANY)] if earlier else []),
            out_specs=[head, pair, pair],
            scratch_shapes=pair_scratch(count),
        ),
        out_shape=[
            jax.ShapeDtypeStruct((count, width), BF),
            jax.ShapeDtypeStruct((2 * count, HD), F32),
            jax.ShapeDtypeStruct((2 * count, HD), F32),
        ],
        input_output_aliases={11: 0} if earlier else {},
        compiler_params=params(22),
        cost_estimate=pl.CostEstimate(
            flops=(end - begin) * 10 * 2 * 2 * count * count * HD if begin else 2**20,
            bytes_accessed=6 * 2**20 if begin else 2**16,
            transcendentals=(end - begin) * 2 * count * count if begin else 0,
        ),
        name="attend_back",
    )(meta, query, grad, kv_earlier, key_rows, value_rows, segments, top, total, *earlier)


def proj_kernel(slots, held, plan, meta_ref, *refs):
    n_in = len(slots)
    pieces, a_ref = refs[:n_in], refs[n_in]
    refs = refs[n_in + 1 + held:]
    buffer_ref, taken = refs[0], refs[1:-3]
    done, sems, take_sems = refs[-3:]
    step = pl.program_id(0)
    rows = done.shape[2]

    def put(j):
        return pltpu.make_async_copy(done.at[j], buffer_ref.at[:, meta_ref[AT_G + slots[j]]], sems.at[j])

    def take(i, made):
        out, start, at, half, first, count = plan[i]
        if made is None:
            source = buffer_ref.at[half, meta_ref[at], pl.ds(first, count)]
        else:
            source = done.at[made, half, pl.ds(first, count)]
        target = taken[out].at[pl.ds(start, count)]
        return pltpu.make_async_copy(source, target, take_sems.at[i])

    def made_here(i, j):
        return meta_ref[plan[i][2]] == meta_ref[AT_G + slots[j]]

    @pl.when(step == 0)
    def _():
        for i in range(len(plan)):
            here = made_here(i, 0)
            for j in range(1, n_in):
                here = here | made_here(i, j)

            @pl.when(jnp.logical_not(here))
            def _():
                take(i, None).start()

    for j in range(n_in):

        @pl.when(step == j)
        def _():
            value = lax.dot_general(
                pieces[j][...], a_ref[...], (((0,), (0,)), ((), ())), preferred_element_type=F32
            ).astype(BF)
            done[j, 0] = value[:rows]
            done[j, 1] = value[rows:]
            put(j).start()
            for i in range(len(plan)):

                @pl.when(made_here(i, j))
                def _():
                    take(i, j).start()

    @pl.when(step == n_in - 1)
    def _():
        for j in range(n_in):
            put(j).wait()
        for i in range(len(plan)):
            take(i, None).wait()


def project(pieces, a_pair, meta, slots, buffer, plan=()):
    tokens, width = a_pair.shape
    depth = pieces[0].shape[1]
    n_blocks = len(pieces)
    held = int(buffer is not None)
    here = pl.BlockSpec(memory_space=pltpu.VMEM)
    there = pl.BlockSpec(memory_space=pltpu.HBM)
    operands = (*pieces, a_pair) + ((buffer,) if held else ())
    shape = (2, depth // 2, width)
    n_taken = 1 + max((entry[0] for entry in plan), default=-1)
    taken = [(sum(e[5] for e in plan if e[0] == i), width) for i in range(n_taken)]
    out = pl.pallas_call(
        functools.partial(proj_kernel, tuple(slots), held, plan),
        grid_spec=pltpu.PrefetchScalarGridSpec(
            num_scalar_prefetch=1,
            grid=(n_blocks,),
            in_specs=[here] * (n_blocks + 1) + [there] * held,
            out_specs=[there] + [here] * n_taken,
            scratch_shapes=[
                pltpu.VMEM((n_blocks, *shape), BF),
                pltpu.SemaphoreType.DMA((n_blocks,)),
                pltpu.SemaphoreType.DMA((max(len(plan), 1),)),
            ],
        ),
        out_shape=[jax.ShapeDtypeStruct((2, PLACES, depth // 2, width), BF)]
        + [jax.ShapeDtypeStruct(t, BF) for t in taken],
        input_output_aliases={n_blocks + 2: 0} if held else {},
        compiler_params=params(16),
        cost_estimate=pl.CostEstimate(
            flops=2 * n_blocks * tokens * depth * width,
            bytes_accessed=(2 * n_blocks + 2) * 2**20,
            transcendentals=0,
        ),
        name="project",
    )(meta, *operands)
    return out if n_taken else out[0]


def grad_kernel(wplan, n_g, n_w, meta_ref, *refs):
    g_in, w_in = refs[:n_g], refs[n_g:n_g + n_w]
    own_ref, lo_ref, hi_ref = refs[n_g + n_w:n_g + n_w + 3]
    gbuf, wbuf, total, gsems, wsems = refs[n_g + n_w + 3:]
    step = pl.program_id(0)
    half = own_ref.shape[0]
    wh = wbuf.shape[1] // 2

    slots = gbuf.shape[0]

    def g_copy(j):
        return pltpu.make_async_copy(g_in[j], gbuf.at[j % slots], gsems.at[j])

    def w_copy(n):
        ref, source, block, part = wplan[n]
        place = meta_ref[AT_W + block]
        return pltpu.make_async_copy(
            w_in[ref].at[pl.ds(source, wh)],
            wbuf.at[place, pl.ds(part * wh, wh)],
            wsems.at[part, place],
        )

    @pl.when(step == 0)
    def _():
        for j in range(slots):
            g_copy(j).start()
        for n in range(16):
            w_copy(n).start()

    for j in range(8):

        @pl.when(step == j)
        def _():
            g_copy(j).wait()

    place = meta_ref[AT_G + step]
    for part in range(2):
        pltpu.make_async_copy(
            w_in[0].at[pl.ds(0, wh)], wbuf.at[place, pl.ds(part * wh, wh)], wsems.at[part, place]
        ).wait()

    @pl.when(step == 0)
    def _():
        total[...] = jnp.dot(gbuf[0], wbuf[place], preferred_element_type=F32)

    @pl.when(step > 0)
    def _():
        total[...] += jnp.dot(gbuf[step % slots], wbuf[place], preferred_element_type=F32)

    for j in range(8 - slots):

        @pl.when(step == j)
        def _():
            g_copy(j + slots).start()

    @pl.when(step == 7)
    def _():
        own_ref[...] = total[:half, :]
        lo_ref[...] = total[half:half + half // 2, :].astype(BF)
        hi_ref[...] = total[half + half // 2:, :].astype(BF)


def attn_grad_part(g_pieces, w_pieces, wplan, meta):
    tokens, depth = g_pieces[0].shape
    width = w_pieces[0].shape[1]
    half = tokens // 2
    kernel = functools.partial(grad_kernel, wplan, len(g_pieces), len(w_pieces))
    whole = pl.BlockSpec(memory_space=pltpu.VMEM)
    return pl.pallas_call(
        kernel,
        grid_spec=pltpu.PrefetchScalarGridSpec(
            num_scalar_prefetch=1,
            grid=(8,),
            in_specs=[pl.BlockSpec(memory_space=pltpu.HBM)] * (len(g_pieces) + len(w_pieces)),
            out_specs=[whole] * 3,
            scratch_shapes=[
                pltpu.VMEM((3, tokens, depth), BF),
                pltpu.VMEM((8, depth, width), BF),
                pltpu.VMEM((tokens, width), F32),
                pltpu.SemaphoreType.DMA((8,)),
                pltpu.SemaphoreType.DMA((2, 8)),
            ],
        ),
        out_shape=[
            jax.ShapeDtypeStruct((half, width), F32),
            jax.ShapeDtypeStruct((half // 2, width), BF),
            jax.ShapeDtypeStruct((half // 2, width), BF),
        ],
        compiler_params=params(26),
        cost_estimate=pl.CostEstimate(
            flops=16 * tokens * depth * width,
            bytes_accessed=20 * 2**20,
            transcendentals=0,
        ),
        name="attn_grad",
    )(meta, *g_pieces, *w_pieces)


def fetch_kernel(plan, meta_ref, buffer_ref, *refs):
    outs, sems = refs[:-1], refs[-1]
    copies = []
    for n, (out, start, at, half) in enumerate(plan):
        source = buffer_ref.at[half, meta_ref[at]]
        target = outs[out].at[pl.ds(start, source.shape[0])]
        copies.append(pltpu.make_async_copy(source, target, sems.at[n]))
    for copy in copies:
        copy.start()
    for copy in copies:
        copy.wait()


def fetch(buffer, meta, plan):
    _, _, rows, width = buffer.shape
    n_out = 1 + plan[-1][0]
    here = pl.BlockSpec(memory_space=pltpu.VMEM)
    return pl.pallas_call(
        functools.partial(fetch_kernel, plan),
        grid_spec=pltpu.PrefetchScalarGridSpec(
            num_scalar_prefetch=1,
            grid=(1,),
            in_specs=[pl.BlockSpec(memory_space=pltpu.HBM)],
            out_specs=[here] * n_out,
            scratch_shapes=[pltpu.SemaphoreType.DMA((len(plan),))],
        ),
        out_shape=[jax.ShapeDtypeStruct((2 * rows, width), BF)] * n_out,
        compiler_params=params(8),
        cost_estimate=pl.CostEstimate(
            flops=0, bytes_accessed=2**16, transcendentals=0
        ),
        name="fetch",
    )(meta, buffer)


def add_kernel(n_terms, plan, *refs):
    terms, outs = refs[:n_terms], refs[n_terms:]
    for out, start, rows, parts in plan:
        value = None
        for term, first in parts:
            part = terms[term][first:first + rows, :].astype(F32)
            value = part if value is None else value + part
        outs[out][start:start + rows, :] = value.astype(BF)


def add_rows(terms, plan, result=False):
    width = terms[0].shape[1]
    n_out = 1 + plan[-1][0]
    shapes = [(sum(p[2] for p in plan if p[0] == n), width) for n in range(n_out)]
    here = pl.BlockSpec(memory_space=pltpu.VMEM)
    outs = [pl.BlockSpec(shape, lambda i: (0, 0)) if result else here for shape in shapes]
    return pl.pallas_call(
        functools.partial(add_kernel, len(terms), plan),
        grid=(1,),
        in_specs=[here] * len(terms),
        out_specs=outs,
        out_shape=[jax.ShapeDtypeStruct(shape, BF) for shape in shapes],
        compiler_params=params(12),
        cost_estimate=pl.CostEstimate(
            flops=2**21, bytes_accessed=5 * 2**20, transcendentals=0
        ),
        name="add_rows",
    )(*terms)


def local(query_rows, key_rows, value_rows, output_grad, out_proj, segment_ids):
    count = query_rows.shape[0]
    half_d = output_grad.shape[1] // 2
    row, col = lax.axis_index("row"), lax.axis_index("col")
    meta = positions(row, col)
    k = row % 2

    g_keep = lax.dynamic_slice_in_dim(output_grad, k * half_d, half_d, 1)
    g_give = lax.dynamic_slice_in_dim(output_grad, (1 - k) * half_d, half_d, 1)
    kv_earlier = passed_along(jnp.concatenate([key_rows, value_rows], 1), "row", 1)
    g_got, meta = tied((move_row(g_give, dk=1), meta))
    g0 = jnp.concatenate([g_keep, g_got], 0)
    segments = segment_ids.reshape(-1, LANES)

    out_proj, kv_earlier = tied((out_proj, kv_earlier), g0)
    gy = move_col(g0, dyl=1)
    gxm = move_col(g0, dx=1)
    gxp = move_col(g0, dx=-1)
    wzm = move_row(out_proj, dz=1)
    wzp = move_row(out_proj, dz=-1)

    (query_held,) = tied((query_rows,), g0)
    attn_out, top, total = attend(meta, query_held, kv_earlier, key_rows, value_rows, segments)

    gy, attn_out = tied((gy, attn_out))
    gxm, gxp = tied((gxm, gxp), gy)
    wzm, wzp, out_proj = tied((wzm, wzp, out_proj), gxm)

    hw = out_proj.shape[0] // 2
    gyxm = move_col(gy, dx=1)
    gyxp = move_col(gy, dx=-1)
    a_other = move_row(attn_out, dk=1)
    wo = move_row(wzm, dz=1)
    wy = move_row(out_proj, dyh=1)

    a_pair = jnp.concatenate([attn_out, a_other], 0)
    proj = project([g0, gxm, gxp, gy], a_pair, meta, range(4), None)

    go = move_col(gxm, dx=1)
    gyxm, gyxp, proj = tied((gyxm, gyxp, proj))
    gyo = move_col(gyxp, dx=-1)
    wo, wy = tied((wo, wy), gyxp)
    wyzm = move_row(wy, dz=1)
    wyzp = move_row(wy, dz=-1)
    wyo = move_row(wo, dyh=1)

    proj = project([gyxm, gyxp], a_pair, meta, (4, 5), proj)
    proj = project([go], a_pair, meta, (6,), proj)

    q = hw // 2
    far, up, dn = at_w(2, 1), at_w(1, 1), at_w(-1, 1)
    own_up, own_dn = at_w(1, 0), at_w(-1, 0)
    proj, give_far, give_up, give_dn, up2, dn2 = project(
        [gyo],
        a_pair,
        meta,
        (7,),
        proj,
        (
            (0, 0, far, 0, 0, hw), (0, hw, far, 1, 0, hw),
            (1, 0, up, 0, 0, hw), (1, hw, up, 1, 0, hw), (1, 2 * hw, own_up, 1, 0, q),
            (2, 0, dn, 0, 0, hw), (2, hw, dn, 1, 0, hw), (2, 2 * hw, own_dn, 0, 0, q),
            (3, 0, own_up, 1, q, q),
            (4, 0, own_dn, 0, q, q),
        ),
    )
    ry = move_row(give_far, dyh=1)
    rup = move_row(give_up, dz=1)
    rdn = move_row(give_dn, dz=-1)

    g_pieces = [g0, gxm, gxp, gy, gyxm, gyxp, go, gyo]
    w_pieces = [out_proj, wzm, wzp, wy, wyzm, wyzp, wyo, wo]
    wplan = [(i, p * hw, i, p) for i in range(8) for p in range(2)]
    (meta,) = tied((meta,), give_up)
    grad_own, give_lo, give_hi = attn_grad_part(g_pieces, w_pieces, wplan, meta)
    got_lo, got_hi = move_row(give_lo, dk=1), move_row(give_hi, dk=1)
    far, middle, near, own = fetch(
        proj,
        meta,
        (
            (0, 0, at_w(2, 0), 0), (0, hw, at_w(2, 0), 1),
            (1, 0, at_w(0, 1), 0), (1, hw, at_w(0, 1), 1),
            (2, 0, own_up, 0), (2, hw, own_dn, 1),
            (3, 0, at_w(0, 0), 0), (3, hw, at_w(0, 0), 1),
        ),
    )
    (attn_grad,) = add_rows(
        [grad_own, got_lo, got_hi],
        ((0, 0, hw, ((0, 0), (1, 0))), (0, hw, hw, ((0, hw), (2, 0)))),
    )
    part = functools.partial(
        attend_back, meta, query_rows, attn_grad, kv_earlier, key_rows, value_rows, segments, top, total
    )
    heads = query_rows.shape[1] // HD
    cuts = heads // 4, heads // 2
    held = part((0, cuts[0]), None)

    ry, *held = tied((ry, *held))

    far_up, far_dn = add_rows(
        [far, ry], ((0, 0, hw, ((0, 0), (1, 0))), (1, 0, hw, ((0, hw), (1, hw))))
    )
    fup = move_row(far_up, dz=1)
    fdn = move_row(far_dn, dz=-1)
    rup, rdn, up2, dn2 = tied((rup, rdn, up2, dn2), far_up)
    (across,) = add_rows([middle, rup, rdn], ((0, 0, 2 * hw, ((0, 0), (1, 0), (2, 0))),))
    held = tied(held, across)
    across = move_row(across, dyh=1)
    up2 = move_row(up2, dz=1)
    dn2 = move_row(dn2, dz=-1)
    held = part(cuts, held)

    fup, fdn, *held = tied((fup, fdn, *held))

    near_up, near_dn = add_rows(
        [near, fup, fdn], ((0, 0, hw, ((0, 0), (1, 0))), (1, 0, hw, ((0, hw), (2, 0))))
    )
    nup = move_row(near_up, dz=1)
    ndn = move_row(near_dn, dz=-1)

    *held, up2, dn2 = tied((*held, up2, dn2), near_up)
    query_grad, dkey, dvalue = part((cuts[1], heads), held)
    back = passed_along(
        jnp.concatenate([dkey[:count], dvalue[:count]], 1).astype(BF), "row", -1
    )
    (proj_grad,) = add_rows(
        [own, across, nup, ndn, rup, up2, rdn, dn2],
        (
            (0, 0, q, ((0, 0), (1, 0), (2, 0), (6, 2 * hw))),
            (0, q, q, ((0, q), (1, q), (2, q), (7, 0))),
            (0, 2 * q, q, ((0, 2 * q), (1, 2 * q), (4, 2 * hw), (3, 0))),
            (0, 3 * q, q, ((0, 3 * q), (1, 3 * q), (5, 0), (3, q))),
        ),
        result=True,
    )
    proj_grad, back = tied((proj_grad, back))
    back = back.astype(F32)
    key_grad = (dkey[count:] + back[:, :HD]).astype(BF)
    value_grad = (dvalue[count:] + back[:, HD:]).astype(BF)
    return (query_grad, key_grad, value_grad, proj_grad)


def solution(mesh):
    placed = (
        P("row", "col"),
        P("row", "col"),
        P("row", "col"),
        P("row", "col"),
        P("row", "col"),
        P(),
    )
    return jax.shard_map(
        local,
        mesh=mesh,
        in_specs=placed,
        out_specs=(P("row", "col"), P("row", "col"), P("row", "col"), P("row", "col")),
        check_vma=False,
    )
```

```python
import functools
import math

import jax
import jax.numpy as jnp
from jax import lax
from jax.experimental import pallas as pl
from jax.experimental.pallas import tpu as pltpu
from jax.sharding import PartitionSpec as P

HD = 128
SCALE = 1.0 / math.sqrt(HD)
NEG = -1e30
BF = jnp.bfloat16
F32 = jnp.float32

PLACES = 64

ZN, YN, KN, LN, XN = 4, 2, 2, 2, 4


AT_FIRST, AT_ROW, AT_EARLIER, AT_G, AT_W = 0, 1, 2, 8, 16
G_STEPS = [(0, 0), (0, -1), (0, 1), (1, 0), (1, -1), (1, 1), (0, 2), (1, 2)]
W_STEPS = [(0, 0), (-1, 0), (1, 0), (0, 1), (-1, 1), (1, 1), (2, 1), (2, 0)]
LANES = 128


def positions(row, col):
    z, yh, yl, x = row // 4, row // 2 % 2, col // 4, col % 4
    head = jnp.stack([(row == 0).astype(jnp.int32), row, jnp.maximum(row - 1, 0)] + [row] * 5)
    steps = [jnp.asarray([step[i] for step in order], jnp.int32) for order in (G_STEPS, W_STEPS) for i in (0, 1)]
    dyl, dx, dz, dyh = steps
    g = ((yl + dyl) & 1) * 4 + ((x + dx) & 3)
    w = ((z + dz) & 3) * 2 + ((yh + dyh) & 1)
    return jnp.concatenate([head, g, w])


def at_w(dz, dyh):
    return AT_W + W_STEPS.index((dz, dyh))


def move_row(value, dz=0, dyh=0, dk=0):
    pairs = []
    for z in range(ZN):
        for y in range(YN):
            for k in range(KN):
                source = (z * YN + y) * KN + k
                target = ((z + dz) % ZN * YN + (y + dyh) % YN) * KN + (k + dk) % KN
                pairs.append((source, target))
    return lax.ppermute(value, "row", pairs)


def move_col(value, dx=0, dyl=0):
    pairs = []
    for y in range(LN):
        for x in range(XN):
            pairs.append((y * XN + x, (y + dyl) % LN * XN + (x + dx) % XN))
    return lax.ppermute(value, "col", pairs)


def passed_along(value, axis, steps):
    count = lax.axis_size(axis)
    first, last = (max(0, -steps), min(count, count - steps))
    return lax.ppermute(value, axis, [(source, source + steps) for source in range(first, last)])


def tied(values, *others):
    held = lax.optimization_barrier((tuple(values), tuple(others)))
    return held[0]


def params(mib, **kw):
    return pltpu.CompilerParams(vmem_limit_bytes=mib * 1024 * 1024, **kw)


def prepare(meta_ref, seg_ref, kv_ref, k_ref, v_ref, bias_ref, k_pair, v_pair, turned, of_keys):
    count = k_ref.shape[0]
    parts = count // LANES
    first, row, earlier = meta_ref[AT_FIRST], meta_ref[AT_ROW], meta_ref[AT_EARLIER]
    own = [seg_ref[pl.ds(row * parts + i, 1), :] for i in range(parts)]
    before = [seg_ref[pl.ds(earlier * parts + i, 1), :] for i in range(parts)]
    key_at = lax.broadcasted_iota(jnp.int32, (LANES, LANES), 0)
    query_at = lax.broadcasted_iota(jnp.int32, (LANES, LANES), 1)
    for i, keys in enumerate(before + own):
        column = jnp.broadcast_to(keys.astype(F32), (LANES, LANES)).T
        for j in range(parts):
            ok = column == own[j].astype(F32)
            if i < parts:
                ok = ok & (first == 0)
            else:
                ok = ok & (key_at + (i - parts) * LANES <= query_at + j * LANES)
            bias_ref[i * LANES:(i + 1) * LANES, j * LANES:(j + 1) * LANES] = jnp.where(
                ok, 0.0, NEG
            ).astype(F32)
    k_pair[:count, :] = kv_ref[:, :HD]
    k_pair[count:, :] = k_ref[...]
    v_pair[:count, :] = kv_ref[:, HD:]
    v_pair[count:, :] = v_ref[...]
    turned[...] = (k_pair if of_keys else v_pair)[...].astype(F32).T.astype(BF)


def pair_scratch(count):
    return [
        pltpu.VMEM((2 * count, count), F32),
        pltpu.VMEM((2 * count, HD), BF),
        pltpu.VMEM((2 * count, HD), BF),
        pltpu.VMEM((HD, 2 * count), BF),
    ]


def chunk_list(count, width):
    return [(i * width, count + (i + 1) * width) for i in range(count // width)]


def fwd_kernel(
    meta_ref, q_ref, kv_ref, k_ref, v_ref, seg_ref, out_ref, top_ref, sum_ref,
    bias_ref, k_pair, v_pair, vt_ref,
):
    count = q_ref.shape[0]

    @pl.when(pl.program_id(0) == 0)
    def _():
        prepare(meta_ref, seg_ref, kv_ref, k_ref, v_ref, bias_ref, k_pair, v_pair, vt_ref, False)

    for start, keys in chunk_list(count, 256):
        cols = slice(start, start + 256)
        s = lax.dot_general(
            k_pair[:keys, :], q_ref[cols, :], (((1,), (1,)), ((), ())), preferred_element_type=F32
        )
        s = s * SCALE + bias_ref[:keys, cols]
        top = jnp.max(s, axis=0, keepdims=True)
        e = jnp.exp(s - top)
        total = jnp.sum(e, axis=0, keepdims=True)
        inv = 1.0 / total
        p = (e * inv).astype(BF)
        a = jnp.dot(vt_ref[:, :keys], p, preferred_element_type=F32)
        out_ref[cols, :] = a.T.astype(BF)
        top_ref[0, :, cols] = top
        sum_ref[0, :, cols] = inv


def attend(meta, query, kv_earlier, key_rows, value_rows, segments):
    count, width = query.shape
    heads = width // HD
    whole = lambda value: pl.BlockSpec(value.shape, lambda h, m: (0, 0))
    head = pl.BlockSpec((count, HD), lambda h, m: (0, h))
    stat = pl.BlockSpec((1, 1, count), lambda h, m: (h, 0, 0))
    return pl.pallas_call(
        fwd_kernel,
        grid_spec=pltpu.PrefetchScalarGridSpec(
            num_scalar_prefetch=1,
            grid=(heads,),
            in_specs=[head] + [whole(v) for v in (kv_earlier, key_rows, value_rows, segments)],
            out_specs=[head, stat, stat],
            scratch_shapes=pair_scratch(count),
        ),
        out_shape=[
            jax.ShapeDtypeStruct((count, width), BF),
            jax.ShapeDtypeStruct((heads, 1, count), F32),
            jax.ShapeDtypeStruct((heads, 1, count), F32),
        ],
        compiler_params=params(16),
        cost_estimate=pl.CostEstimate(
            flops=heads * 64 * 2 * 2 * count * count * HD,
            bytes_accessed=8 * 2**20,
            transcendentals=heads * 2 * count * count,
        ),
        name="attend",
    )(meta, query, kv_earlier, key_rows, value_rows, segments)


def bwd_kernel(
    n_held, last, meta_ref, q_ref, g_ref, kv_ref, k_ref, v_ref, seg_ref, top_ref, sum_ref, *refs
):
    dk_in, dv_in = refs[:2] if n_held else (None, None)
    dq_ref, dk_ref, dv_ref, bias_ref, k_pair, v_pair, kt_ref = refs[n_held:]
    count = q_ref.shape[0]

    @pl.when(pl.program_id(0) == 0)
    def _():
        prepare(meta_ref, seg_ref, kv_ref, k_ref, v_ref, bias_ref, k_pair, v_pair, kt_ref, True)
        if n_held:
            dk_ref[...] = dk_in[...]
            dv_ref[...] = dv_in[...]
        else:
            dk_ref[...] = jnp.zeros_like(dk_ref)
            dv_ref[...] = jnp.zeros_like(dv_ref)

    for start, keys in chunk_list(count, 256):
        cols = slice(start, start + 256)
        q = q_ref[cols, :]
        g = g_ref[cols, :]
        s = lax.dot_general(
            k_pair[:keys, :], q, (((1,), (1,)), ((), ())), preferred_element_type=F32
        )
        s = s * SCALE + bias_ref[:keys, cols]
        p = jnp.exp(s - top_ref[0, :, cols]) * sum_ref[0, :, cols]
        dp = lax.dot_general(
            v_pair[:keys, :], g, (((1,), (1,)), ((), ())), preferred_element_type=F32
        )
        delta = jnp.sum(p * dp, axis=0, keepdims=True)
        ds = (p * (dp - delta)).astype(BF)
        dq = jnp.dot(kt_ref[:, :keys], ds, preferred_element_type=F32) * SCALE
        dq_ref[cols, :] = dq.T.astype(BF)
        dk_ref[:keys, :] += jnp.dot(ds, q, preferred_element_type=F32)
        dv_ref[:keys, :] += jnp.dot(p.astype(BF), g, preferred_element_type=F32)

    if last:

        @pl.when(pl.program_id(0) == pl.num_programs(0) - 1)
        def _():
            dk_ref[...] = dk_ref[...] * SCALE


def attend_back(
    meta, query, grad, kv_earlier, key_rows, value_rows, segments, top, total, heads, held
):
    count, width = query.shape
    begin, end = heads
    last = end == width // HD
    whole = lambda value: pl.BlockSpec(value.shape, lambda h, m: (0, 0))
    head = pl.BlockSpec((count, HD), lambda h, m: (0, h + begin))
    stat = pl.BlockSpec((1, 1, count), lambda h, m: (h + begin, 0, 0))
    pair = pl.BlockSpec((2 * count, HD), lambda h, m: (0, 0))
    earlier = () if held is None else (held[1], held[2], held[0])
    return pl.pallas_call(
        functools.partial(bwd_kernel, len(earlier), last),
        grid_spec=pltpu.PrefetchScalarGridSpec(
            num_scalar_prefetch=1,
            grid=(end - begin,),
            in_specs=[head, head]
            + [whole(v) for v in (kv_earlier, key_rows, value_rows, segments)]
            + [stat, stat]
            + ([pair, pair, pl.BlockSpec(memory_space=pl.ANY)] if earlier else []),
            out_specs=[head, pair, pair],
            scratch_shapes=pair_scratch(count),
        ),
        out_shape=[
            jax.ShapeDtypeStruct((count, width), BF),
            jax.ShapeDtypeStruct((2 * count, HD), F32),
            jax.ShapeDtypeStruct((2 * count, HD), F32),
        ],
        input_output_aliases={11: 0} if earlier else {},
        compiler_params=params(22),
        cost_estimate=pl.CostEstimate(
            flops=(end - begin) * 10 * 2 * 2 * count * count * HD if begin else 2**20,
            bytes_accessed=6 * 2**20 if begin else 2**16,
            transcendentals=(end - begin) * 2 * count * count if begin else 0,
        ),
        name="attend_back",
    )(meta, query, grad, kv_earlier, key_rows, value_rows, segments, top, total, *earlier)


def proj_kernel(slots, held, plan, meta_ref, *refs):
    n_in = len(slots)
    pieces, a_ref = refs[:n_in], refs[n_in]
    refs = refs[n_in + 1 + held:]
    buffer_ref, taken = refs[0], refs[1:-3]
    done, sems, take_sems = refs[-3:]
    step = pl.program_id(0)
    rows = done.shape[2]

    def put(j):
        return pltpu.make_async_copy(done.at[j], buffer_ref.at[:, meta_ref[AT_G + slots[j]]], sems.at[j])

    def take(i, made):
        out, start, at, half, first, count = plan[i]
        if made is None:
            source = buffer_ref.at[half, meta_ref[at], pl.ds(first, count)]
        else:
            source = done.at[made, half, pl.ds(first, count)]
        target = taken[out].at[pl.ds(start, count)]
        return pltpu.make_async_copy(source, target, take_sems.at[i])

    def made_here(i, j):
        return meta_ref[plan[i][2]] == meta_ref[AT_G + slots[j]]

    @pl.when(step == 0)
    def _():
        for i in range(len(plan)):
            here = made_here(i, 0)
            for j in range(1, n_in):
                here = here | made_here(i, j)

            @pl.when(jnp.logical_not(here))
            def _():
                take(i, None).start()

    for j in range(n_in):

        @pl.when(step == j)
        def _():
            value = lax.dot_general(
                pieces[j][...], a_ref[...], (((0,), (0,)), ((), ())), preferred_element_type=F32
            ).astype(BF)
            done[j, 0] = value[:rows]
            done[j, 1] = value[rows:]
            put(j).start()
            for i in range(len(plan)):

                @pl.when(made_here(i, j))
                def _():
                    take(i, j).start()

    @pl.when(step == n_in - 1)
    def _():
        for j in range(n_in):
            put(j).wait()
        for i in range(len(plan)):
            take(i, None).wait()


def project(pieces, a_pair, meta, slots, buffer, plan=()):
    tokens, width = a_pair.shape
    depth = pieces[0].shape[1]
    n_blocks = len(pieces)
    held = int(buffer is not None)
    here = pl.BlockSpec(memory_space=pltpu.VMEM)
    there = pl.BlockSpec(memory_space=pltpu.HBM)
    operands = (*pieces, a_pair) + ((buffer,) if held else ())
    shape = (2, depth // 2, width)
    n_taken = 1 + max((entry[0] for entry in plan), default=-1)
    taken = [(sum(e[5] for e in plan if e[0] == i), width) for i in range(n_taken)]
    out = pl.pallas_call(
        functools.partial(proj_kernel, tuple(slots), held, plan),
        grid_spec=pltpu.PrefetchScalarGridSpec(
            num_scalar_prefetch=1,
            grid=(n_blocks,),
            in_specs=[here] * (n_blocks + 1) + [there] * held,
            out_specs=[there] + [here] * n_taken,
            scratch_shapes=[
                pltpu.VMEM((n_blocks, *shape), BF),
                pltpu.SemaphoreType.DMA((n_blocks,)),
                pltpu.SemaphoreType.DMA((max(len(plan), 1),)),
            ],
        ),
        out_shape=[jax.ShapeDtypeStruct((2, PLACES, depth // 2, width), BF)]
        + [jax.ShapeDtypeStruct(t, BF) for t in taken],
        input_output_aliases={n_blocks + 2: 0} if held else {},
        compiler_params=params(16),
        cost_estimate=pl.CostEstimate(
            flops=2 * n_blocks * tokens * depth * width,
            bytes_accessed=(2 * n_blocks + 2) * 2**20,
            transcendentals=0,
        ),
        name="project",
    )(meta, *operands)
    return out if n_taken else out[0]


def grad_kernel(wplan, n_g, n_w, meta_ref, *refs):
    g_in, w_in = refs[:n_g], refs[n_g:n_g + n_w]
    own_ref, lo_ref, hi_ref = refs[n_g + n_w:n_g + n_w + 3]
    gbuf, wbuf, total, gsems, wsems = refs[n_g + n_w + 3:]
    step = pl.program_id(0)
    half = own_ref.shape[0]
    wh = wbuf.shape[1] // 2

    slots = gbuf.shape[0]

    def g_copy(j):
        return pltpu.make_async_copy(g_in[j], gbuf.at[j % slots], gsems.at[j])

    def w_copy(n):
        ref, source, block, part = wplan[n]
        place = meta_ref[AT_W + block]
        return pltpu.make_async_copy(
            w_in[ref].at[pl.ds(source, wh)],
            wbuf.at[place, pl.ds(part * wh, wh)],
            wsems.at[part, place],
        )

    @pl.when(step == 0)
    def _():
        for j in range(slots):
            g_copy(j).start()
        for n in range(16):
            w_copy(n).start()

    for j in range(8):

        @pl.when(step == j)
        def _():
            g_copy(j).wait()

    place = meta_ref[AT_G + step]
    for part in range(2):
        pltpu.make_async_copy(
            w_in[0].at[pl.ds(0, wh)], wbuf.at[place, pl.ds(part * wh, wh)], wsems.at[part, place]
        ).wait()

    @pl.when(step == 0)
    def _():
        total[...] = jnp.dot(gbuf[0], wbuf[place], preferred_element_type=F32)

    @pl.when(step > 0)
    def _():
        total[...] += jnp.dot(gbuf[step % slots], wbuf[place], preferred_element_type=F32)

    for j in range(8 - slots):

        @pl.when(step == j)
        def _():
            g_copy(j + slots).start()

    @pl.when(step == 7)
    def _():
        own_ref[...] = total[:half, :]
        lo_ref[...] = total[half:half + half // 2, :].astype(BF)
        hi_ref[...] = total[half + half // 2:, :].astype(BF)


def attn_grad_part(g_pieces, w_pieces, wplan, meta):
    tokens, depth = g_pieces[0].shape
    width = w_pieces[0].shape[1]
    half = tokens // 2
    kernel = functools.partial(grad_kernel, wplan, len(g_pieces), len(w_pieces))
    whole = pl.BlockSpec(memory_space=pltpu.VMEM)
    return pl.pallas_call(
        kernel,
        grid_spec=pltpu.PrefetchScalarGridSpec(
            num_scalar_prefetch=1,
            grid=(8,),
            in_specs=[pl.BlockSpec(memory_space=pltpu.HBM)] * (len(g_pieces) + len(w_pieces)),
            out_specs=[whole] * 3,
            scratch_shapes=[
                pltpu.VMEM((3, tokens, depth), BF),
                pltpu.VMEM((8, depth, width), BF),
                pltpu.VMEM((tokens, width), F32),
                pltpu.SemaphoreType.DMA((8,)),
                pltpu.SemaphoreType.DMA((2, 8)),
            ],
        ),
        out_shape=[
            jax.ShapeDtypeStruct((half, width), F32),
            jax.ShapeDtypeStruct((half // 2, width), BF),
            jax.ShapeDtypeStruct((half // 2, width), BF),
        ],
        compiler_params=params(26),
        cost_estimate=pl.CostEstimate(
            flops=16 * tokens * depth * width,
            bytes_accessed=20 * 2**20,
            transcendentals=0,
        ),
        name="attn_grad",
    )(meta, *g_pieces, *w_pieces)


def fetch_kernel(plan, meta_ref, buffer_ref, *refs):
    outs, sems = refs[:-1], refs[-1]
    copies = []
    for n, (out, start, at, half) in enumerate(plan):
        source = buffer_ref.at[half, meta_ref[at]]
        target = outs[out].at[pl.ds(start, source.shape[0])]
        copies.append(pltpu.make_async_copy(source, target, sems.at[n]))
    for copy in copies:
        copy.start()
    for copy in copies:
        copy.wait()


def fetch(buffer, meta, plan):
    _, _, rows, width = buffer.shape
    n_out = 1 + plan[-1][0]
    here = pl.BlockSpec(memory_space=pltpu.VMEM)
    return pl.pallas_call(
        functools.partial(fetch_kernel, plan),
        grid_spec=pltpu.PrefetchScalarGridSpec(
            num_scalar_prefetch=1,
            grid=(1,),
            in_specs=[pl.BlockSpec(memory_space=pltpu.HBM)],
            out_specs=[here] * n_out,
            scratch_shapes=[pltpu.SemaphoreType.DMA((len(plan),))],
        ),
        out_shape=[jax.ShapeDtypeStruct((2 * rows, width), BF)] * n_out,
        compiler_params=params(8),
        cost_estimate=pl.CostEstimate(
            flops=0, bytes_accessed=2**16, transcendentals=0
        ),
        name="fetch",
    )(meta, buffer)


def add_kernel(n_terms, plan, *refs):
    terms, outs = refs[:n_terms], refs[n_terms:]
    for out, start, rows, parts in plan:
        value = None
        for term, first in parts:
            part = terms[term][first:first + rows, :].astype(F32)
            value = part if value is None else value + part
        outs[out][start:start + rows, :] = value.astype(BF)


def add_rows(terms, plan, result=False):
    width = terms[0].shape[1]
    n_out = 1 + plan[-1][0]
    shapes = [(sum(p[2] for p in plan if p[0] == n), width) for n in range(n_out)]
    here = pl.BlockSpec(memory_space=pltpu.VMEM)
    outs = [pl.BlockSpec(shape, lambda i: (0, 0)) if result else here for shape in shapes]
    return pl.pallas_call(
        functools.partial(add_kernel, len(terms), plan),
        grid=(1,),
        in_specs=[here] * len(terms),
        out_specs=outs,
        out_shape=[jax.ShapeDtypeStruct(shape, BF) for shape in shapes],
        compiler_params=params(12),
        cost_estimate=pl.CostEstimate(
            flops=2**21, bytes_accessed=5 * 2**20, transcendentals=0
        ),
        name="add_rows",
    )(*terms)


def local(query_rows, key_rows, value_rows, output_grad, out_proj, segment_ids):
    count = query_rows.shape[0]
    half_d = output_grad.shape[1] // 2
    row, col = lax.axis_index("row"), lax.axis_index("col")
    meta = positions(row, col)
    k = row % 2

    g_keep = lax.dynamic_slice_in_dim(output_grad, k * half_d, half_d, 1)
    g_give = lax.dynamic_slice_in_dim(output_grad, (1 - k) * half_d, half_d, 1)
    kv_earlier = passed_along(jnp.concatenate([key_rows, value_rows], 1), "row", 1)
    g_got, meta = tied((move_row(g_give, dk=1), meta))
    g0 = jnp.concatenate([g_keep, g_got], 0)
    segments = segment_ids.reshape(-1, LANES)

    out_proj, kv_earlier = tied((out_proj, kv_earlier), g0)
    gy = move_col(g0, dyl=1)
    gxm = move_col(g0, dx=1)
    gxp = move_col(g0, dx=-1)
    wzm = move_row(out_proj, dz=1)
    wzp = move_row(out_proj, dz=-1)

    (query_held,) = tied((query_rows,), g0)
    attn_out, top, total = attend(meta, query_held, kv_earlier, key_rows, value_rows, segments)

    gy, attn_out = tied((gy, attn_out))
    gxm, gxp = tied((gxm, gxp), gy)
    wzm, wzp, out_proj = tied((wzm, wzp, out_proj), gxm)

    hw = out_proj.shape[0] // 2
    gyxm = move_col(gy, dx=1)
    gyxp = move_col(gy, dx=-1)
    a_other = move_row(attn_out, dk=1)
    wo = move_row(wzm, dz=1)
    wy = move_row(out_proj, dyh=1)

    a_pair = jnp.concatenate([attn_out, a_other], 0)
    proj = project([g0, gxm, gxp, gy], a_pair, meta, range(4), None)

    go = move_col(gxm, dx=1)
    gyxm, gyxp, proj = tied((gyxm, gyxp, proj))
    gyo = move_col(gyxp, dx=-1)
    wo, wy = tied((wo, wy), gyxp)
    wyzm = move_row(wy, dz=1)
    wyzp = move_row(wy, dz=-1)
    wyo = move_row(wo, dyh=1)

    proj = project([gyxm, gyxp], a_pair, meta, (4, 5), proj)
    proj = project([go], a_pair, meta, (6,), proj)

    q = hw // 2
    far, up, dn = at_w(2, 1), at_w(1, 1), at_w(-1, 1)
    own_up, own_dn = at_w(1, 0), at_w(-1, 0)
    proj, give_far, give_up, give_dn, up2, dn2 = project(
        [gyo],
        a_pair,
        meta,
        (7,),
        proj,
        (
            (0, 0, far, 0, 0, hw), (0, hw, far, 1, 0, hw),
            (1, 0, up, 0, 0, hw), (1, hw, up, 1, 0, hw), (1, 2 * hw, own_up, 1, 0, q),
            (2, 0, dn, 0, 0, hw), (2, hw, dn, 1, 0, hw), (2, 2 * hw, own_dn, 0, 0, q),
            (3, 0, own_up, 1, q, q),
            (4, 0, own_dn, 0, q, q),
        ),
    )
    ry = move_row(give_far, dyh=1)
    rup = move_row(give_up, dz=1)
    rdn = move_row(give_dn, dz=-1)

    g_pieces = [g0, gxm, gxp, gy, gyxm, gyxp, go, gyo]
    w_pieces = [out_proj, wzm, wzp, wy, wyzm, wyzp, wyo, wo]
    wplan = [(i, p * hw, i, p) for i in range(8) for p in range(2)]
    (meta,) = tied((meta,), give_up)
    grad_own, give_lo, give_hi = attn_grad_part(g_pieces, w_pieces, wplan, meta)
    got_lo, got_hi = move_row(give_lo, dk=1), move_row(give_hi, dk=1)
    far, middle, near, own = fetch(
        proj,
        meta,
        (
            (0, 0, at_w(2, 0), 0), (0, hw, at_w(2, 0), 1),
            (1, 0, at_w(0, 1), 0), (1, hw, at_w(0, 1), 1),
            (2, 0, own_up, 0), (2, hw, own_dn, 1),
            (3, 0, at_w(0, 0), 0), (3, hw, at_w(0, 0), 1),
        ),
    )
    (attn_grad,) = add_rows(
        [grad_own, got_lo, got_hi],
        ((0, 0, hw, ((0, 0), (1, 0))), (0, hw, hw, ((0, hw), (2, 0)))),
    )
    part = functools.partial(
        attend_back, meta, query_rows, attn_grad, kv_earlier, key_rows, value_rows, segments, top, total
    )
    heads = query_rows.shape[1] // HD
    cuts = heads // 4, 5 * heads // 8
    held = part((0, cuts[0]), None)

    ry, *held = tied((ry, *held))

    far_up, far_dn = add_rows(
        [far, ry], ((0, 0, hw, ((0, 0), (1, 0))), (1, 0, hw, ((0, hw), (1, hw))))
    )
    fup = move_row(far_up, dz=1)
    fdn = move_row(far_dn, dz=-1)
    rup, rdn = tied((rup, rdn), far_up)
    up2, dn2 = tied((up2, dn2), far_up)
    (across,) = add_rows([middle, rup, rdn], ((0, 0, 2 * hw, ((0, 0), (1, 0), (2, 0))),))
    held = tied(held, across)
    across = move_row(across, dyh=1)
    up2 = move_row(up2, dz=1)
    dn2 = move_row(dn2, dz=-1)
    held = part(cuts, held)

    fup, fdn, *held = tied((fup, fdn, *held))

    near_up, near_dn = add_rows(
        [near, fup, fdn], ((0, 0, hw, ((0, 0), (1, 0))), (1, 0, hw, ((0, hw), (2, 0))))
    )
    nup = move_row(near_up, dz=1)
    ndn = move_row(near_dn, dz=-1)

    *held, up2, dn2 = tied((*held, up2, dn2), near_up)
    query_grad, dkey, dvalue = part((cuts[1], heads), held)
    back = passed_along(
        jnp.concatenate([dkey[:count], dvalue[:count]], 1).astype(BF), "row", -1
    )
    (proj_grad,) = add_rows(
        [own, across, nup, ndn, rup, up2, rdn, dn2],
        (
            (0, 0, q, ((0, 0), (1, 0), (2, 0), (6, 2 * hw))),
            (0, q, q, ((0, q), (1, q), (2, q), (7, 0))),
            (0, 2 * q, q, ((0, 2 * q), (1, 2 * q), (4, 2 * hw), (3, 0))),
            (0, 3 * q, q, ((0, 3 * q), (1, 3 * q), (5, 0), (3, q))),
        ),
        result=True,
    )
    proj_grad, back = tied((proj_grad, back))
    back = back.astype(F32)
    key_grad = (dkey[count:] + back[:, :HD]).astype(BF)
    value_grad = (dvalue[count:] + back[:, HD:]).astype(BF)
    return (query_grad, key_grad, value_grad, proj_grad)


def solution(mesh):
    placed = (
        P("row", "col"),
        P("row", "col"),
        P("row", "col"),
        P("row", "col"),
        P("row", "col"),
        P(),
    )
    return jax.shard_map(
        local,
        mesh=mesh,
        in_specs=placed,
        out_specs=(P("row", "col"), P("row", "col"), P("row", "col"), P("row", "col")),
        check_vma=False,
    )
```

```python
import functools
import math

import jax
import jax.numpy as jnp
from jax import lax
from jax.experimental import pallas as pl
from jax.experimental.pallas import tpu as pltpu
from jax.sharding import PartitionSpec as P

HD = 128
SCALE = 1.0 / math.sqrt(HD)
NEG = -1e30
BF = jnp.bfloat16
F32 = jnp.float32

PLACES = 64

ZN, YN, KN, LN, XN = 4, 2, 2, 2, 4


AT_FIRST, AT_ROW, AT_EARLIER, AT_G, AT_W = 0, 1, 2, 8, 16
G_STEPS = [(0, 0), (0, -1), (0, 1), (1, 0), (1, -1), (1, 1), (0, 2), (1, 2)]
W_STEPS = [(0, 0), (-1, 0), (1, 0), (0, 1), (-1, 1), (1, 1), (2, 1), (2, 0)]
LANES = 128


def positions(row, col):
    z, yh, yl, x = row // 4, row // 2 % 2, col // 4, col % 4
    head = jnp.stack([(row == 0).astype(jnp.int32), row, jnp.maximum(row - 1, 0)] + [row] * 5)
    steps = [jnp.asarray([step[i] for step in order], jnp.int32) for order in (G_STEPS, W_STEPS) for i in (0, 1)]
    dyl, dx, dz, dyh = steps
    g = ((yl + dyl) & 1) * 4 + ((x + dx) & 3)
    w = ((z + dz) & 3) * 2 + ((yh + dyh) & 1)
    return jnp.concatenate([head, g, w])


def at_w(dz, dyh):
    return AT_W + W_STEPS.index((dz, dyh))


def move_row(value, dz=0, dyh=0, dk=0):
    pairs = []
    for z in range(ZN):
        for y in range(YN):
            for k in range(KN):
                source = (z * YN + y) * KN + k
                target = ((z + dz) % ZN * YN + (y + dyh) % YN) * KN + (k + dk) % KN
                pairs.append((source, target))
    return lax.ppermute(value, "row", pairs)


def move_col(value, dx=0, dyl=0):
    pairs = []
    for y in range(LN):
        for x in range(XN):
            pairs.append((y * XN + x, (y + dyl) % LN * XN + (x + dx) % XN))
    return lax.ppermute(value, "col", pairs)


def passed_along(value, axis, steps):
    count = lax.axis_size(axis)
    first, last = (max(0, -steps), min(count, count - steps))
    return lax.ppermute(value, axis, [(source, source + steps) for source in range(first, last)])


def tied(values, *others):
    held = lax.optimization_barrier((tuple(values), tuple(others)))
    return held[0]


def params(mib, **kw):
    return pltpu.CompilerParams(vmem_limit_bytes=mib * 1024 * 1024, **kw)


def prepare(meta_ref, seg_ref, kv_ref, k_ref, v_ref, bias_ref, k_pair, v_pair, turned, of_keys):
    count = k_ref.shape[0]
    parts = count // LANES
    first, row, earlier = meta_ref[AT_FIRST], meta_ref[AT_ROW], meta_ref[AT_EARLIER]
    own = [seg_ref[pl.ds(row * parts + i, 1), :] for i in range(parts)]
    before = [seg_ref[pl.ds(earlier * parts + i, 1), :] for i in range(parts)]
    key_at = lax.broadcasted_iota(jnp.int32, (LANES, LANES), 0)
    query_at = lax.broadcasted_iota(jnp.int32, (LANES, LANES), 1)
    for i, keys in enumerate(before + own):
        column = jnp.broadcast_to(keys.astype(F32), (LANES, LANES)).T
        for j in range(parts):
            ok = column == own[j].astype(F32)
            if i < parts:
                ok = ok & (first == 0)
            else:
                ok = ok & (key_at + (i - parts) * LANES <= query_at + j * LANES)
            bias_ref[i * LANES:(i + 1) * LANES, j * LANES:(j + 1) * LANES] = jnp.where(
                ok, 0.0, NEG
            ).astype(F32)
    k_pair[:count, :] = kv_ref[:, :HD]
    k_pair[count:, :] = k_ref[...]
    v_pair[:count, :] = kv_ref[:, HD:]
    v_pair[count:, :] = v_ref[...]
    turned[...] = (k_pair if of_keys else v_pair)[...].astype(F32).T.astype(BF)


def pair_scratch(count):
    return [
        pltpu.VMEM((2 * count, count), F32),
        pltpu.VMEM((2 * count, HD), BF),
        pltpu.VMEM((2 * count, HD), BF),
        pltpu.VMEM((HD, 2 * count), BF),
    ]


def chunk_list(count, width):
    return [(i * width, count + (i + 1) * width) for i in range(count // width)]


def fwd_kernel(
    meta_ref, q_ref, kv_ref, k_ref, v_ref, seg_ref, out_ref, top_ref, sum_ref,
    bias_ref, k_pair, v_pair, vt_ref,
):
    count = q_ref.shape[0]

    @pl.when(pl.program_id(0) == 0)
    def _():
        prepare(meta_ref, seg_ref, kv_ref, k_ref, v_ref, bias_ref, k_pair, v_pair, vt_ref, False)

    for start, keys in chunk_list(count, 256):
        cols = slice(start, start + 256)
        s = lax.dot_general(
            k_pair[:keys, :], q_ref[cols, :], (((1,), (1,)), ((), ())), preferred_element_type=F32
        )
        s = s * SCALE + bias_ref[:keys, cols]
        top = jnp.max(s, axis=0, keepdims=True)
        e = jnp.exp(s - top)
        total = jnp.sum(e, axis=0, keepdims=True)
        inv = 1.0 / total
        p = (e * inv).astype(BF)
        a = jnp.dot(vt_ref[:, :keys], p, preferred_element_type=F32)
        out_ref[cols, :] = a.T.astype(BF)
        top_ref[0, :, cols] = top
        sum_ref[0, :, cols] = inv


def attend(meta, query, kv_earlier, key_rows, value_rows, segments):
    count, width = query.shape
    heads = width // HD
    whole = lambda value: pl.BlockSpec(value.shape, lambda h, m: (0, 0))
    head = pl.BlockSpec((count, HD), lambda h, m: (0, h))
    stat = pl.BlockSpec((1, 1, count), lambda h, m: (h, 0, 0))
    return pl.pallas_call(
        fwd_kernel,
        grid_spec=pltpu.PrefetchScalarGridSpec(
            num_scalar_prefetch=1,
            grid=(heads,),
            in_specs=[head] + [whole(v) for v in (kv_earlier, key_rows, value_rows, segments)],
            out_specs=[head, stat, stat],
            scratch_shapes=pair_scratch(count),
        ),
        out_shape=[
            jax.ShapeDtypeStruct((count, width), BF),
            jax.ShapeDtypeStruct((heads, 1, count), F32),
            jax.ShapeDtypeStruct((heads, 1, count), F32),
        ],
        compiler_params=params(16),
        cost_estimate=pl.CostEstimate(
            flops=heads * 64 * 2 * 2 * count * count * HD,
            bytes_accessed=8 * 2**20,
            transcendentals=heads * 2 * count * count,
        ),
        name="attend",
    )(meta, query, kv_earlier, key_rows, value_rows, segments)


def bwd_kernel(
    n_held, last, meta_ref, q_ref, g_ref, kv_ref, k_ref, v_ref, seg_ref, top_ref, sum_ref, *refs
):
    dk_in, dv_in = refs[:2] if n_held else (None, None)
    dq_ref, dk_ref, dv_ref, bias_ref, k_pair, v_pair, kt_ref = refs[n_held:]
    count = q_ref.shape[0]

    @pl.when(pl.program_id(0) == 0)
    def _():
        prepare(meta_ref, seg_ref, kv_ref, k_ref, v_ref, bias_ref, k_pair, v_pair, kt_ref, True)
        if n_held:
            dk_ref[...] = dk_in[...]
            dv_ref[...] = dv_in[...]
        else:
            dk_ref[...] = jnp.zeros_like(dk_ref)
            dv_ref[...] = jnp.zeros_like(dv_ref)

    for start, keys in chunk_list(count, 256):
        cols = slice(start, start + 256)
        q = q_ref[cols, :]
        g = g_ref[cols, :]
        s = lax.dot_general(
            k_pair[:keys, :], q, (((1,), (1,)), ((), ())), preferred_element_type=F32
        )
        s = s * SCALE + bias_ref[:keys, cols]
        p = jnp.exp(s - top_ref[0, :, cols]) * sum_ref[0, :, cols]
        dp = lax.dot_general(
            v_pair[:keys, :], g, (((1,), (1,)), ((), ())), preferred_element_type=F32
        )
        delta = jnp.sum(p * dp, axis=0, keepdims=True)
        ds = (p * (dp - delta)).astype(BF)
        dq = jnp.dot(kt_ref[:, :keys], ds, preferred_element_type=F32) * SCALE
        dq_ref[cols, :] = dq.T.astype(BF)
        dk_ref[:keys, :] += jnp.dot(ds, q, preferred_element_type=F32)
        dv_ref[:keys, :] += jnp.dot(p.astype(BF), g, preferred_element_type=F32)

    if last:

        @pl.when(pl.program_id(0) == pl.num_programs(0) - 1)
        def _():
            dk_ref[...] = dk_ref[...] * SCALE


def attend_back(
    meta, query, grad, kv_earlier, key_rows, value_rows, segments, top, total, heads, held
):
    count, width = query.shape
    begin, end = heads
    last = end == width // HD
    whole = lambda value: pl.BlockSpec(value.shape, lambda h, m: (0, 0))
    head = pl.BlockSpec((count, HD), lambda h, m: (0, h + begin))
    stat = pl.BlockSpec((1, 1, count), lambda h, m: (h + begin, 0, 0))
    pair = pl.BlockSpec((2 * count, HD), lambda h, m: (0, 0))
    earlier = () if held is None else (held[1], held[2], held[0])
    return pl.pallas_call(
        functools.partial(bwd_kernel, len(earlier), last),
        grid_spec=pltpu.PrefetchScalarGridSpec(
            num_scalar_prefetch=1,
            grid=(end - begin,),
            in_specs=[head, head]
            + [whole(v) for v in (kv_earlier, key_rows, value_rows, segments)]
            + [stat, stat]
            + ([pair, pair, pl.BlockSpec(memory_space=pl.ANY)] if earlier else []),
            out_specs=[head, pair, pair],
            scratch_shapes=pair_scratch(count),
        ),
        out_shape=[
            jax.ShapeDtypeStruct((count, width), BF),
            jax.ShapeDtypeStruct((2 * count, HD), F32),
            jax.ShapeDtypeStruct((2 * count, HD), F32),
        ],
        input_output_aliases={11: 0} if earlier else {},
        compiler_params=params(22),
        cost_estimate=pl.CostEstimate(
            flops=(end - begin) * 10 * 2 * 2 * count * count * HD if begin else 2**20,
            bytes_accessed=6 * 2**20 if begin else 2**16,
            transcendentals=(end - begin) * 2 * count * count if begin else 0,
        ),
        name="attend_back",
    )(meta, query, grad, kv_earlier, key_rows, value_rows, segments, top, total, *earlier)


def proj_kernel(slots, held, plan, meta_ref, *refs):
    n_in = len(slots)
    pieces, a_ref = refs[:n_in], refs[n_in]
    refs = refs[n_in + 1 + held:]
    buffer_ref, taken = refs[0], refs[1:-3]
    done, sems, take_sems = refs[-3:]
    step = pl.program_id(0)
    rows = done.shape[2]

    def put(j, half):
        place = meta_ref[AT_G + slots[j]]
        return pltpu.make_async_copy(done.at[j, half], buffer_ref.at[half, place], sems.at[j, half])

    def take(i, made):
        out, start, at, half, first, count = plan[i]
        if made is None:
            source = buffer_ref.at[half, meta_ref[at], pl.ds(first, count)]
        else:
            source = done.at[made, half, pl.ds(first, count)]
        target = taken[out].at[pl.ds(start, count)]
        return pltpu.make_async_copy(source, target, take_sems.at[i])

    def made_here(i, j):
        return meta_ref[plan[i][2]] == meta_ref[AT_G + slots[j]]

    @pl.when(step == 0)
    def _():
        for i in range(len(plan)):
            here = made_here(i, 0)
            for j in range(1, n_in):
                here = here | made_here(i, j)

            @pl.when(jnp.logical_not(here))
            def _():
                take(i, None).start()

    for j in range(n_in):

        @pl.when(step == j)
        def _():
            for half in range(2):
                part = pieces[j][:, half * rows:(half + 1) * rows]
                done[j, half] = lax.dot_general(
                    part, a_ref[...], (((0,), (0,)), ((), ())), preferred_element_type=F32
                ).astype(BF)
                put(j, half).start()
                for i in range(len(plan)):
                    if plan[i][3] == half:

                        @pl.when(made_here(i, j))
                        def _(i=i):
                            take(i, j).start()

    @pl.when(step == n_in - 1)
    def _():
        for j in range(n_in):
            for half in range(2):
                put(j, half).wait()
        for i in range(len(plan)):
            take(i, None).wait()


def project(pieces, a_pair, meta, slots, buffer, plan=()):
    tokens, width = a_pair.shape
    depth = pieces[0].shape[1]
    n_blocks = len(pieces)
    held = int(buffer is not None)
    here = pl.BlockSpec(memory_space=pltpu.VMEM)
    there = pl.BlockSpec(memory_space=pltpu.HBM)
    operands = (*pieces, a_pair) + ((buffer,) if held else ())
    shape = (2, depth // 2, width)
    n_taken = 1 + max((entry[0] for entry in plan), default=-1)
    taken = [(sum(e[5] for e in plan if e[0] == i), width) for i in range(n_taken)]
    out = pl.pallas_call(
        functools.partial(proj_kernel, tuple(slots), held, plan),
        grid_spec=pltpu.PrefetchScalarGridSpec(
            num_scalar_prefetch=1,
            grid=(n_blocks,),
            in_specs=[here] * (n_blocks + 1) + [there] * held,
            out_specs=[there] + [here] * n_taken,
            scratch_shapes=[
                pltpu.VMEM((n_blocks, *shape), BF),
                pltpu.SemaphoreType.DMA((n_blocks, 2)),
                pltpu.SemaphoreType.DMA((max(len(plan), 1),)),
            ],
        ),
        out_shape=[jax.ShapeDtypeStruct((2, PLACES, depth // 2, width), BF)]
        + [jax.ShapeDtypeStruct(t, BF) for t in taken],
        input_output_aliases={n_blocks + 2: 0} if held else {},
        compiler_params=params(16),
        cost_estimate=pl.CostEstimate(
            flops=2 * n_blocks * tokens * depth * width,
            bytes_accessed=(2 * n_blocks + 2) * 2**20,
            transcendentals=0,
        ),
        name="project",
    )(meta, *operands)
    return out if n_taken else out[0]


def grad_kernel(wplan, n_g, n_w, meta_ref, *refs):
    g_in, w_in = refs[:n_g], refs[n_g:n_g + n_w]
    own_ref, lo_ref, hi_ref = refs[n_g + n_w:n_g + n_w + 3]
    gbuf, wbuf, total, gsems, wsems = refs[n_g + n_w + 3:]
    step = pl.program_id(0)
    half = own_ref.shape[0]
    wh = wbuf.shape[1] // 2

    slots = gbuf.shape[0]

    def g_copy(j):
        return pltpu.make_async_copy(g_in[j], gbuf.at[j % slots], gsems.at[j])

    def w_copy(n):
        ref, source, block, part = wplan[n]
        place = meta_ref[AT_W + block]
        return pltpu.make_async_copy(
            w_in[ref].at[pl.ds(source, wh)],
            wbuf.at[place, pl.ds(part * wh, wh)],
            wsems.at[part, place],
        )

    @pl.when(step == 0)
    def _():
        for j in range(slots):
            g_copy(j).start()
        for n in range(16):
            w_copy(n).start()

    for j in range(8):

        @pl.when(step == j)
        def _():
            g_copy(j).wait()

    place = meta_ref[AT_G + step]
    for part in range(2):
        pltpu.make_async_copy(
            w_in[0].at[pl.ds(0, wh)], wbuf.at[place, pl.ds(part * wh, wh)], wsems.at[part, place]
        ).wait()

    @pl.when(step == 0)
    def _():
        total[...] = jnp.dot(gbuf[0], wbuf[place], preferred_element_type=F32)

    @pl.when(step > 0)
    def _():
        total[...] += jnp.dot(gbuf[step % slots], wbuf[place], preferred_element_type=F32)

    for j in range(8 - slots):

        @pl.when(step == j)
        def _():
            g_copy(j + slots).start()

    @pl.when(step == 7)
    def _():
        own_ref[...] = total[:half, :]
        lo_ref[...] = total[half:half + half // 2, :].astype(BF)
        hi_ref[...] = total[half + half // 2:, :].astype(BF)


def attn_grad_part(g_pieces, w_pieces, wplan, meta):
    tokens, depth = g_pieces[0].shape
    width = w_pieces[0].shape[1]
    half = tokens // 2
    kernel = functools.partial(grad_kernel, wplan, len(g_pieces), len(w_pieces))
    whole = pl.BlockSpec(memory_space=pltpu.VMEM)
    return pl.pallas_call(
        kernel,
        grid_spec=pltpu.PrefetchScalarGridSpec(
            num_scalar_prefetch=1,
            grid=(8,),
            in_specs=[pl.BlockSpec(memory_space=pltpu.HBM)] * (len(g_pieces) + len(w_pieces)),
            out_specs=[whole] * 3,
            scratch_shapes=[
                pltpu.VMEM((3, tokens, depth), BF),
                pltpu.VMEM((8, depth, width), BF),
                pltpu.VMEM((tokens, width), F32),
                pltpu.SemaphoreType.DMA((8,)),
                pltpu.SemaphoreType.DMA((2, 8)),
            ],
        ),
        out_shape=[
            jax.ShapeDtypeStruct((half, width), F32),
            jax.ShapeDtypeStruct((half // 2, width), BF),
            jax.ShapeDtypeStruct((half // 2, width), BF),
        ],
        compiler_params=params(26),
        cost_estimate=pl.CostEstimate(
            flops=16 * tokens * depth * width,
            bytes_accessed=20 * 2**20,
            transcendentals=0,
        ),
        name="attn_grad",
    )(meta, *g_pieces, *w_pieces)


def fetch_kernel(plan, meta_ref, buffer_ref, *refs):
    outs, sems = refs[:-1], refs[-1]
    copies = []
    for n, (out, start, at, half) in enumerate(plan):
        source = buffer_ref.at[half, meta_ref[at]]
        target = outs[out].at[pl.ds(start, source.shape[0])]
        copies.append(pltpu.make_async_copy(source, target, sems.at[n]))
    for copy in copies:
        copy.start()
    for copy in copies:
        copy.wait()


def fetch(buffer, meta, plan):
    _, _, rows, width = buffer.shape
    n_out = 1 + plan[-1][0]
    here = pl.BlockSpec(memory_space=pltpu.VMEM)
    return pl.pallas_call(
        functools.partial(fetch_kernel, plan),
        grid_spec=pltpu.PrefetchScalarGridSpec(
            num_scalar_prefetch=1,
            grid=(1,),
            in_specs=[pl.BlockSpec(memory_space=pltpu.HBM)],
            out_specs=[here] * n_out,
            scratch_shapes=[pltpu.SemaphoreType.DMA((len(plan),))],
        ),
        out_shape=[jax.ShapeDtypeStruct((2 * rows, width), BF)] * n_out,
        compiler_params=params(8),
        cost_estimate=pl.CostEstimate(
            flops=0, bytes_accessed=2**16, transcendentals=0
        ),
        name="fetch",
    )(meta, buffer)


def add_kernel(n_terms, plan, *refs):
    terms, outs = refs[:n_terms], refs[n_terms:]
    for out, start, rows, parts in plan:
        value = None
        for term, first in parts:
            part = terms[term][first:first + rows, :].astype(F32)
            value = part if value is None else value + part
        outs[out][start:start + rows, :] = value.astype(BF)


def add_rows(terms, plan, result=False):
    width = terms[0].shape[1]
    n_out = 1 + plan[-1][0]
    shapes = [(sum(p[2] for p in plan if p[0] == n), width) for n in range(n_out)]
    here = pl.BlockSpec(memory_space=pltpu.VMEM)
    outs = [pl.BlockSpec(shape, lambda i: (0, 0)) if result else here for shape in shapes]
    return pl.pallas_call(
        functools.partial(add_kernel, len(terms), plan),
        grid=(1,),
        in_specs=[here] * len(terms),
        out_specs=outs,
        out_shape=[jax.ShapeDtypeStruct(shape, BF) for shape in shapes],
        compiler_params=params(12),
        cost_estimate=pl.CostEstimate(
            flops=2**21, bytes_accessed=5 * 2**20, transcendentals=0
        ),
        name="add_rows",
    )(*terms)


def local(query_rows, key_rows, value_rows, output_grad, out_proj, segment_ids):
    count = query_rows.shape[0]
    half_d = output_grad.shape[1] // 2
    row, col = lax.axis_index("row"), lax.axis_index("col")
    meta = positions(row, col)
    k = row % 2

    g_keep = lax.dynamic_slice_in_dim(output_grad, k * half_d, half_d, 1)
    g_give = lax.dynamic_slice_in_dim(output_grad, (1 - k) * half_d, half_d, 1)
    kv_earlier = passed_along(jnp.concatenate([key_rows, value_rows], 1), "row", 1)
    g_got, meta = tied((move_row(g_give, dk=1), meta))
    g0 = jnp.concatenate([g_keep, g_got], 0)
    segments = segment_ids.reshape(-1, LANES)

    out_proj, kv_earlier = tied((out_proj, kv_earlier), g0)
    gy = move_col(g0, dyl=1)
    gxm = move_col(g0, dx=1)
    gxp = move_col(g0, dx=-1)
    wzm = move_row(out_proj, dz=1)
    wzp = move_row(out_proj, dz=-1)

    (query_held,) = tied((query_rows,), g0)
    attn_out, top, total = attend(meta, query_held, kv_earlier, key_rows, value_rows, segments)

    gy, attn_out = tied((gy, attn_out))
    gxm, gxp = tied((gxm, gxp), gy)
    wzm, wzp, out_proj = tied((wzm, wzp, out_proj), gxm)

    hw = out_proj.shape[0] // 2
    gyxm = move_col(gy, dx=1)
    gyxp = move_col(gy, dx=-1)
    a_other = move_row(attn_out, dk=1)
    wo = move_row(wzm, dz=1)
    wy = move_row(out_proj, dyh=1)

    a_pair = jnp.concatenate([attn_out, a_other], 0)
    proj = project([g0, gxm, gxp, gy], a_pair, meta, range(4), None)

    go = move_col(gxm, dx=1)
    gyxm, gyxp, proj = tied((gyxm, gyxp, proj))
    gyo = move_col(gyxp, dx=-1)
    wo, wy = tied((wo, wy), gyxp)
    wyzm = move_row(wy, dz=1)
    wyzp = move_row(wy, dz=-1)
    wyo = move_row(wo, dyh=1)

    proj = project([gyxm, gyxp], a_pair, meta, (4, 5), proj)
    proj = project([go], a_pair, meta, (6,), proj)

    q = hw // 2
    far, up, dn = at_w(2, 1), at_w(1, 1), at_w(-1, 1)
    own_up, own_dn = at_w(1, 0), at_w(-1, 0)
    proj, give_far, give_up, give_dn, up2, dn2 = project(
        [gyo],
        a_pair,
        meta,
        (7,),
        proj,
        (
            (0, 0, far, 0, 0, hw), (0, hw, far, 1, 0, hw),
            (1, 0, up, 0, 0, hw), (1, hw, up, 1, 0, hw), (1, 2 * hw, own_up, 1, 0, q),
            (2, 0, dn, 0, 0, hw), (2, hw, dn, 1, 0, hw), (2, 2 * hw, own_dn, 0, 0, q),
            (3, 0, own_up, 1, q, q),
            (4, 0, own_dn, 0, q, q),
        ),
    )
    ry = move_row(give_far, dyh=1)
    rup = move_row(give_up, dz=1)
    rdn = move_row(give_dn, dz=-1)

    g_pieces = [g0, gxm, gxp, gy, gyxm, gyxp, go, gyo]
    w_pieces = [out_proj, wzm, wzp, wy, wyzm, wyzp, wyo, wo]
    wplan = [(i, p * hw, i, p) for i in range(8) for p in range(2)]
    (meta,) = tied((meta,), give_up)
    grad_own, give_lo, give_hi = attn_grad_part(g_pieces, w_pieces, wplan, meta)
    got_lo, got_hi = move_row(give_lo, dk=1), move_row(give_hi, dk=1)
    far, middle, near, own = fetch(
        proj,
        meta,
        (
            (0, 0, at_w(2, 0), 0), (0, hw, at_w(2, 0), 1),
            (1, 0, at_w(0, 1), 0), (1, hw, at_w(0, 1), 1),
            (2, 0, own_up, 0), (2, hw, own_dn, 1),
            (3, 0, at_w(0, 0), 0), (3, hw, at_w(0, 0), 1),
        ),
    )
    (attn_grad,) = add_rows(
        [grad_own, got_lo, got_hi],
        ((0, 0, hw, ((0, 0), (1, 0))), (0, hw, hw, ((0, hw), (2, 0)))),
    )
    part = functools.partial(
        attend_back, meta, query_rows, attn_grad, kv_earlier, key_rows, value_rows, segments, top, total
    )
    heads = query_rows.shape[1] // HD
    cuts = heads // 4, 5 * heads // 8
    held = part((0, cuts[0]), None)

    ry, *held = tied((ry, *held))

    far_up, far_dn = add_rows(
        [far, ry], ((0, 0, hw, ((0, 0), (1, 0))), (1, 0, hw, ((0, hw), (1, hw))))
    )
    fup = move_row(far_up, dz=1)
    fdn = move_row(far_dn, dz=-1)
    rup, rdn = tied((rup, rdn), far_up)
    up2, dn2 = tied((up2, dn2), far_up)
    (across,) = add_rows([middle, rup, rdn], ((0, 0, 2 * hw, ((0, 0), (1, 0), (2, 0))),))
    held = tied(held, across)
    across = move_row(across, dyh=1)
    up2 = move_row(up2, dz=1)
    dn2 = move_row(dn2, dz=-1)
    held = part(cuts, held)

    fup, fdn, *held = tied((fup, fdn, *held))

    near_up, near_dn = add_rows(
        [near, fup, fdn], ((0, 0, hw, ((0, 0), (1, 0))), (1, 0, hw, ((0, hw), (2, 0))))
    )
    nup = move_row(near_up, dz=1)
    ndn = move_row(near_dn, dz=-1)

    *held, up2, dn2 = tied((*held, up2, dn2), near_up)
    query_grad, dkey, dvalue = part((cuts[1], heads), held)
    back = passed_along(
        jnp.concatenate([dkey[:count], dvalue[:count]], 1).astype(BF), "row", -1
    )
    (proj_grad,) = add_rows(
        [own, across, nup, ndn, rup, up2, rdn, dn2],
        (
            (0, 0, q, ((0, 0), (1, 0), (2, 0), (6, 2 * hw))),
            (0, q, q, ((0, q), (1, q), (2, q), (7, 0))),
            (0, 2 * q, q, ((0, 2 * q), (1, 2 * q), (4, 2 * hw), (3, 0))),
            (0, 3 * q, q, ((0, 3 * q), (1, 3 * q), (5, 0), (3, q))),
        ),
        result=True,
    )
    proj_grad, back = tied((proj_grad, back))
    back = back.astype(F32)
    key_grad = (dkey[count:] + back[:, :HD]).astype(BF)
    value_grad = (dvalue[count:] + back[:, HD:]).astype(BF)
    return (query_grad, key_grad, value_grad, proj_grad)


def solution(mesh):
    placed = (
        P("row", "col"),
        P("row", "col"),
        P("row", "col"),
        P("row", "col"),
        P("row", "col"),
        P(),
    )
    return jax.shard_map(
        local,
        mesh=mesh,
        in_specs=placed,
        out_specs=(P("row", "col"), P("row", "col"), P("row", "col"), P("row", "col")),
        check_vma=False,
    )
```

```python
import functools
import math

import jax
import jax.numpy as jnp
from jax import lax
from jax.experimental import pallas as pl
from jax.experimental.pallas import tpu as pltpu
from jax.sharding import PartitionSpec as P

HD = 128
SCALE = 1.0 / math.sqrt(HD)
NEG = -1e30
BF = jnp.bfloat16
F32 = jnp.float32

PLACES = 64

ZN, YN, KN, LN, XN = 4, 2, 2, 2, 4


AT_FIRST, AT_ROW, AT_EARLIER, AT_G, AT_W = 0, 1, 2, 8, 16
G_STEPS = [(0, 0), (0, -1), (0, 1), (1, 0), (1, -1), (1, 1), (0, 2), (1, 2)]
W_STEPS = [(0, 0), (-1, 0), (1, 0), (0, 1), (-1, 1), (1, 1), (2, 1), (2, 0)]
LANES = 128


def positions(row, col):
    z, yh, yl, x = row // 4, row // 2 % 2, col // 4, col % 4
    head = jnp.stack([(row == 0).astype(jnp.int32), row, jnp.maximum(row - 1, 0)] + [row] * 5)
    steps = [jnp.asarray([step[i] for step in order], jnp.int32) for order in (G_STEPS, W_STEPS) for i in (0, 1)]
    dyl, dx, dz, dyh = steps
    g = ((yl + dyl) & 1) * 4 + ((x + dx) & 3)
    w = ((z + dz) & 3) * 2 + ((yh + dyh) & 1)
    return jnp.concatenate([head, g, w])


def at_w(dz, dyh):
    return AT_W + W_STEPS.index((dz, dyh))


def move_row(value, dz=0, dyh=0, dk=0):
    pairs = []
    for z in range(ZN):
        for y in range(YN):
            for k in range(KN):
                source = (z * YN + y) * KN + k
                target = ((z + dz) % ZN * YN + (y + dyh) % YN) * KN + (k + dk) % KN
                pairs.append((source, target))
    return lax.ppermute(value, "row", pairs)


def move_col(value, dx=0, dyl=0):
    pairs = []
    for y in range(LN):
        for x in range(XN):
            pairs.append((y * XN + x, (y + dyl) % LN * XN + (x + dx) % XN))
    return lax.ppermute(value, "col", pairs)


def passed_along(value, axis, steps):
    count = lax.axis_size(axis)
    first, last = (max(0, -steps), min(count, count - steps))
    return lax.ppermute(value, axis, [(source, source + steps) for source in range(first, last)])


def tied(values, *others):
    held = lax.optimization_barrier((tuple(values), tuple(others)))
    return held[0]


def params(mib, **kw):
    return pltpu.CompilerParams(vmem_limit_bytes=mib * 1024 * 1024, **kw)


def prepare(meta_ref, seg_ref, kv_ref, k_ref, v_ref, bias_ref, k_pair, v_pair, turned, of_keys):
    count = k_ref.shape[0]
    parts = count // LANES
    first, row, earlier = meta_ref[AT_FIRST], meta_ref[AT_ROW], meta_ref[AT_EARLIER]
    own = [seg_ref[pl.ds(row * parts + i, 1), :] for i in range(parts)]
    before = [seg_ref[pl.ds(earlier * parts + i, 1), :] for i in range(parts)]
    key_at = lax.broadcasted_iota(jnp.int32, (LANES, LANES), 0)
    query_at = lax.broadcasted_iota(jnp.int32, (LANES, LANES), 1)
    for i, keys in enumerate(before + own):
        column = jnp.broadcast_to(keys.astype(F32), (LANES, LANES)).T
        for j in range(parts):
            ok = column == own[j].astype(F32)
            if i < parts:
                ok = ok & (first == 0)
            else:
                ok = ok & (key_at + (i - parts) * LANES <= query_at + j * LANES)
            bias_ref[i * LANES:(i + 1) * LANES, j * LANES:(j + 1) * LANES] = jnp.where(
                ok, 0.0, NEG
            ).astype(F32)
    k_pair[:count, :] = kv_ref[:, :HD]
    k_pair[count:, :] = k_ref[...]
    v_pair[:count, :] = kv_ref[:, HD:]
    v_pair[count:, :] = v_ref[...]
    turned[...] = (k_pair if of_keys else v_pair)[...].astype(F32).T.astype(BF)


def pair_scratch(count):
    return [
        pltpu.VMEM((2 * count, count), F32),
        pltpu.VMEM((2 * count, HD), BF),
        pltpu.VMEM((2 * count, HD), BF),
        pltpu.VMEM((HD, 2 * count), BF),
    ]


def chunk_list(count, width):
    return [(i * width, count + (i + 1) * width) for i in range(count // width)]


def fwd_kernel(
    meta_ref, q_ref, kv_ref, k_ref, v_ref, seg_ref, out_ref, top_ref, sum_ref,
    bias_ref, k_pair, v_pair, vt_ref,
):
    count = q_ref.shape[0]

    @pl.when(pl.program_id(0) == 0)
    def _():
        prepare(meta_ref, seg_ref, kv_ref, k_ref, v_ref, bias_ref, k_pair, v_pair, vt_ref, False)

    for start, keys in chunk_list(count, 256):
        cols = slice(start, start + 256)
        s = lax.dot_general(
            k_pair[:keys, :], q_ref[cols, :], (((1,), (1,)), ((), ())), preferred_element_type=F32
        )
        s = s * SCALE + bias_ref[:keys, cols]
        top = jnp.max(s, axis=0, keepdims=True)
        e = jnp.exp(s - top)
        total = jnp.sum(e, axis=0, keepdims=True)
        inv = 1.0 / total
        p = (e * inv).astype(BF)
        a = jnp.dot(vt_ref[:, :keys], p, preferred_element_type=F32)
        out_ref[cols, :] = a.T.astype(BF)
        top_ref[0, :, cols] = top
        sum_ref[0, :, cols] = inv


def attend(meta, query, kv_earlier, key_rows, value_rows, segments):
    count, width = query.shape
    heads = width // HD
    whole = lambda value: pl.BlockSpec(value.shape, lambda h, m: (0, 0))
    head = pl.BlockSpec((count, HD), lambda h, m: (0, h))
    stat = pl.BlockSpec((1, 1, count), lambda h, m: (h, 0, 0))
    return pl.pallas_call(
        fwd_kernel,
        grid_spec=pltpu.PrefetchScalarGridSpec(
            num_scalar_prefetch=1,
            grid=(heads,),
            in_specs=[head] + [whole(v) for v in (kv_earlier, key_rows, value_rows, segments)],
            out_specs=[head, stat, stat],
            scratch_shapes=pair_scratch(count),
        ),
        out_shape=[
            jax.ShapeDtypeStruct((count, width), BF),
            jax.ShapeDtypeStruct((heads, 1, count), F32),
            jax.ShapeDtypeStruct((heads, 1, count), F32),
        ],
        compiler_params=params(16),
        cost_estimate=pl.CostEstimate(
            flops=heads * 64 * 2 * 2 * count * count * HD,
            bytes_accessed=8 * 2**20,
            transcendentals=heads * 2 * count * count,
        ),
        name="attend",
    )(meta, query, kv_earlier, key_rows, value_rows, segments)


def bwd_kernel(
    n_held, last, meta_ref, q_ref, g_ref, kv_ref, k_ref, v_ref, seg_ref, top_ref, sum_ref, *refs
):
    dk_in, dv_in = refs[:2] if n_held else (None, None)
    dq_ref, dk_ref, dv_ref, bias_ref, k_pair, v_pair, kt_ref = refs[n_held:]
    count = q_ref.shape[0]

    @pl.when(pl.program_id(0) == 0)
    def _():
        prepare(meta_ref, seg_ref, kv_ref, k_ref, v_ref, bias_ref, k_pair, v_pair, kt_ref, True)
        if n_held:
            dk_ref[...] = dk_in[...]
            dv_ref[...] = dv_in[...]
        else:
            dk_ref[...] = jnp.zeros_like(dk_ref)
            dv_ref[...] = jnp.zeros_like(dv_ref)

    for start, keys in chunk_list(count, 256):
        cols = slice(start, start + 256)
        q = q_ref[cols, :]
        g = g_ref[cols, :]
        s = lax.dot_general(
            k_pair[:keys, :], q, (((1,), (1,)), ((), ())), preferred_element_type=F32
        )
        s = s * SCALE + bias_ref[:keys, cols]
        p = jnp.exp(s - top_ref[0, :, cols]) * sum_ref[0, :, cols]
        dp = lax.dot_general(
            v_pair[:keys, :], g, (((1,), (1,)), ((), ())), preferred_element_type=F32
        )
        delta = jnp.sum(p * dp, axis=0, keepdims=True)
        ds = (p * (dp - delta)).astype(BF)
        dq = jnp.dot(kt_ref[:, :keys], ds, preferred_element_type=F32) * SCALE
        dq_ref[cols, :] = dq.T.astype(BF)
        dk_ref[:keys, :] += jnp.dot(ds, q, preferred_element_type=F32)
        dv_ref[:keys, :] += jnp.dot(p.astype(BF), g, preferred_element_type=F32)

    if last:

        @pl.when(pl.program_id(0) == pl.num_programs(0) - 1)
        def _():
            dk_ref[...] = dk_ref[...] * SCALE


def attend_back(
    meta, query, grad, kv_earlier, key_rows, value_rows, segments, top, total, heads, held
):
    count, width = query.shape
    begin, end = heads
    last = end == width // HD
    whole = lambda value: pl.BlockSpec(value.shape, lambda h, m: (0, 0))
    head = pl.BlockSpec((count, HD), lambda h, m: (0, h + begin))
    stat = pl.BlockSpec((1, 1, count), lambda h, m: (h + begin, 0, 0))
    pair = pl.BlockSpec((2 * count, HD), lambda h, m: (0, 0))
    earlier = () if held is None else (held[1], held[2], held[0])
    return pl.pallas_call(
        functools.partial(bwd_kernel, len(earlier), last),
        grid_spec=pltpu.PrefetchScalarGridSpec(
            num_scalar_prefetch=1,
            grid=(end - begin,),
            in_specs=[head, head]
            + [whole(v) for v in (kv_earlier, key_rows, value_rows, segments)]
            + [stat, stat]
            + ([pair, pair, pl.BlockSpec(memory_space=pl.ANY)] if earlier else []),
            out_specs=[head, pair, pair],
            scratch_shapes=pair_scratch(count),
        ),
        out_shape=[
            jax.ShapeDtypeStruct((count, width), BF),
            jax.ShapeDtypeStruct((2 * count, HD), F32),
            jax.ShapeDtypeStruct((2 * count, HD), F32),
        ],
        input_output_aliases={11: 0} if earlier else {},
        compiler_params=params(22),
        cost_estimate=pl.CostEstimate(
            flops=(end - begin) * 10 * 2 * 2 * count * count * HD if begin else 2**20,
            bytes_accessed=6 * 2**20 if begin else 2**16,
            transcendentals=(end - begin) * 2 * count * count if begin else 0,
        ),
        name="attend_back",
    )(meta, query, grad, kv_earlier, key_rows, value_rows, segments, top, total, *earlier)


def proj_kernel(slots, held, plan, meta_ref, *refs):
    n_in = len(slots)
    pieces, a_ref = refs[:n_in], refs[n_in]
    refs = refs[n_in + 1 + held:]
    buffer_ref, taken = refs[0], refs[1:-3]
    done, sems, take_sems = refs[-3:]
    step = pl.program_id(0)
    rows = done.shape[2]

    def put(j, half):
        place = meta_ref[AT_G + slots[j]]
        return pltpu.make_async_copy(done.at[j, half], buffer_ref.at[half, place], sems.at[j, half])

    def take(i, made):
        out, start, at, half, first, count = plan[i]
        if made is None:
            source = buffer_ref.at[half, meta_ref[at], pl.ds(first, count)]
        else:
            source = done.at[made, half, pl.ds(first, count)]
        target = taken[out].at[pl.ds(start, count)]
        return pltpu.make_async_copy(source, target, take_sems.at[i])

    def made_here(i, j):
        return meta_ref[plan[i][2]] == meta_ref[AT_G + slots[j]]

    @pl.when(step == 0)
    def _():
        for i in range(len(plan)):
            here = made_here(i, 0)
            for j in range(1, n_in):
                here = here | made_here(i, j)

            @pl.when(jnp.logical_not(here))
            def _():
                take(i, None).start()

    for j in range(n_in):

        @pl.when(step == j)
        def _():
            for half in range(2):
                part = pieces[j][:, half * rows:(half + 1) * rows]
                done[j, half] = lax.dot_general(
                    part, a_ref[...], (((0,), (0,)), ((), ())), preferred_element_type=F32
                ).astype(BF)
                put(j, half).start()
                for i in range(len(plan)):
                    if plan[i][3] == half:

                        @pl.when(made_here(i, j))
                        def _(i=i):
                            take(i, j).start()

    @pl.when(step == n_in - 1)
    def _():
        for j in range(n_in):
            for half in range(2):
                put(j, half).wait()
        for i in range(len(plan)):
            take(i, None).wait()


def project(pieces, a_pair, meta, slots, buffer, plan=()):
    tokens, width = a_pair.shape
    depth = pieces[0].shape[1]
    n_blocks = len(pieces)
    held = int(buffer is not None)
    here = pl.BlockSpec(memory_space=pltpu.VMEM)
    there = pl.BlockSpec(memory_space=pltpu.HBM)
    operands = (*pieces, a_pair) + ((buffer,) if held else ())
    shape = (2, depth // 2, width)
    n_taken = 1 + max((entry[0] for entry in plan), default=-1)
    taken = [(sum(e[5] for e in plan if e[0] == i), width) for i in range(n_taken)]
    out = pl.pallas_call(
        functools.partial(proj_kernel, tuple(slots), held, plan),
        grid_spec=pltpu.PrefetchScalarGridSpec(
            num_scalar_prefetch=1,
            grid=(n_blocks,),
            in_specs=[here] * (n_blocks + 1) + [there] * held,
            out_specs=[there] + [here] * n_taken,
            scratch_shapes=[
                pltpu.VMEM((n_blocks, *shape), BF),
                pltpu.SemaphoreType.DMA((n_blocks, 2)),
                pltpu.SemaphoreType.DMA((max(len(plan), 1),)),
            ],
        ),
        out_shape=[jax.ShapeDtypeStruct((2, PLACES, depth // 2, width), BF)]
        + [jax.ShapeDtypeStruct(t, BF) for t in taken],
        input_output_aliases={n_blocks + 2: 0} if held else {},
        compiler_params=params(16),
        cost_estimate=pl.CostEstimate(
            flops=2 * n_blocks * tokens * depth * width,
            bytes_accessed=(2 * n_blocks + 2) * 2**20,
            transcendentals=0,
        ),
        name="project",
    )(meta, *operands)
    return out if n_taken else out[0]


def grad_kernel(wplan, n_g, n_w, meta_ref, *refs):
    g_in, w_in = refs[:n_g], refs[n_g:n_g + n_w]
    own_ref, lo_ref, hi_ref = refs[n_g + n_w:n_g + n_w + 3]
    gbuf, wbuf, total, gsems, wsems = refs[n_g + n_w + 3:]
    step = pl.program_id(0)
    half = own_ref.shape[0]
    wh = wbuf.shape[1] // 2

    slots = gbuf.shape[0]

    def g_copy(j):
        return pltpu.make_async_copy(g_in[j], gbuf.at[j % slots], gsems.at[j])

    def w_copy(n):
        ref, source, block, part = wplan[n]
        place = meta_ref[AT_W + block]
        return pltpu.make_async_copy(
            w_in[ref].at[pl.ds(source, wh)],
            wbuf.at[place, pl.ds(part * wh, wh)],
            wsems.at[part, place],
        )

    @pl.when(step == 0)
    def _():
        for j in range(slots):
            g_copy(j).start()
        for n in range(16):
            w_copy(n).start()

    for j in range(8):

        @pl.when(step == j)
        def _():
            g_copy(j).wait()

    place = meta_ref[AT_G + step]
    for part in range(2):
        pltpu.make_async_copy(
            w_in[0].at[pl.ds(0, wh)], wbuf.at[place, pl.ds(part * wh, wh)], wsems.at[part, place]
        ).wait()

    @pl.when(step == 0)
    def _():
        total[...] = jnp.dot(gbuf[0], wbuf[place], preferred_element_type=F32)

    @pl.when(step > 0)
    def _():
        total[...] += jnp.dot(gbuf[step % slots], wbuf[place], preferred_element_type=F32)

    for j in range(8 - slots):

        @pl.when(step == j)
        def _():
            g_copy(j + slots).start()

    @pl.when(step == 7)
    def _():
        own_ref[...] = total[:half, :]
        lo_ref[...] = total[half:half + half // 2, :].astype(BF)
        hi_ref[...] = total[half + half // 2:, :].astype(BF)


def attn_grad_part(g_pieces, w_pieces, wplan, meta):
    tokens, depth = g_pieces[0].shape
    width = w_pieces[0].shape[1]
    half = tokens // 2
    kernel = functools.partial(grad_kernel, wplan, len(g_pieces), len(w_pieces))
    whole = pl.BlockSpec(memory_space=pltpu.VMEM)
    return pl.pallas_call(
        kernel,
        grid_spec=pltpu.PrefetchScalarGridSpec(
            num_scalar_prefetch=1,
            grid=(8,),
            in_specs=[pl.BlockSpec(memory_space=pltpu.HBM)] * (len(g_pieces) + len(w_pieces)),
            out_specs=[whole] * 3,
            scratch_shapes=[
                pltpu.VMEM((3, tokens, depth), BF),
                pltpu.VMEM((8, depth, width), BF),
                pltpu.VMEM((tokens, width), F32),
                pltpu.SemaphoreType.DMA((8,)),
                pltpu.SemaphoreType.DMA((2, 8)),
            ],
        ),
        out_shape=[
            jax.ShapeDtypeStruct((half, width), F32),
            jax.ShapeDtypeStruct((half // 2, width), BF),
            jax.ShapeDtypeStruct((half // 2, width), BF),
        ],
        compiler_params=params(26),
        cost_estimate=pl.CostEstimate(
            flops=16 * tokens * depth * width,
            bytes_accessed=20 * 2**20,
            transcendentals=0,
        ),
        name="attn_grad",
    )(meta, *g_pieces, *w_pieces)


def fetch_kernel(plan, meta_ref, buffer_ref, *refs):
    outs, sems = refs[:-1], refs[-1]
    copies = []
    for n, (out, start, at, half) in enumerate(plan):
        source = buffer_ref.at[half, meta_ref[at]]
        target = outs[out].at[pl.ds(start, source.shape[0])]
        copies.append(pltpu.make_async_copy(source, target, sems.at[n]))
    for copy in copies:
        copy.start()
    for copy in copies:
        copy.wait()


def fetch(buffer, meta, plan):
    _, _, rows, width = buffer.shape
    n_out = 1 + plan[-1][0]
    here = pl.BlockSpec(memory_space=pltpu.VMEM)
    return pl.pallas_call(
        functools.partial(fetch_kernel, plan),
        grid_spec=pltpu.PrefetchScalarGridSpec(
            num_scalar_prefetch=1,
            grid=(1,),
            in_specs=[pl.BlockSpec(memory_space=pltpu.HBM)],
            out_specs=[here] * n_out,
            scratch_shapes=[pltpu.SemaphoreType.DMA((len(plan),))],
        ),
        out_shape=[jax.ShapeDtypeStruct((2 * rows, width), BF)] * n_out,
        compiler_params=params(8),
        cost_estimate=pl.CostEstimate(
            flops=0, bytes_accessed=2**16, transcendentals=0
        ),
        name="fetch",
    )(meta, buffer)


def add_kernel(n_terms, plan, *refs):
    terms, outs = refs[:n_terms], refs[n_terms:]
    for out, start, rows, parts in plan:
        value = None
        for term, first in parts:
            part = terms[term][first:first + rows, :].astype(F32)
            value = part if value is None else value + part
        outs[out][start:start + rows, :] = value.astype(BF)


def add_rows(terms, plan, result=False):
    width = terms[0].shape[1]
    n_out = 1 + plan[-1][0]
    shapes = [(sum(p[2] for p in plan if p[0] == n), width) for n in range(n_out)]
    here = pl.BlockSpec(memory_space=pltpu.VMEM)
    outs = [pl.BlockSpec(shape, lambda i: (0, 0)) if result else here for shape in shapes]
    return pl.pallas_call(
        functools.partial(add_kernel, len(terms), plan),
        grid=(1,),
        in_specs=[here] * len(terms),
        out_specs=outs,
        out_shape=[jax.ShapeDtypeStruct(shape, BF) for shape in shapes],
        compiler_params=params(12),
        cost_estimate=pl.CostEstimate(
            flops=2**21, bytes_accessed=5 * 2**20, transcendentals=0
        ),
        name="add_rows",
    )(*terms)


def local(query_rows, key_rows, value_rows, output_grad, out_proj, segment_ids):
    count = query_rows.shape[0]
    half_d = output_grad.shape[1] // 2
    row, col = lax.axis_index("row"), lax.axis_index("col")
    meta = positions(row, col)
    k = row % 2

    g_keep = lax.dynamic_slice_in_dim(output_grad, k * half_d, half_d, 1)
    g_give = lax.dynamic_slice_in_dim(output_grad, (1 - k) * half_d, half_d, 1)
    kv_earlier = passed_along(jnp.concatenate([key_rows, value_rows], 1), "row", 1)
    g_got, meta = tied((move_row(g_give, dk=1), meta))
    g0 = jnp.concatenate([g_keep, g_got], 0)
    segments = segment_ids.reshape(-1, LANES)

    out_proj, kv_earlier = tied((out_proj, kv_earlier), g0)
    gy = move_col(g0, dyl=1)
    gxm = move_col(g0, dx=1)
    gxp = move_col(g0, dx=-1)
    wzm = move_row(out_proj, dz=1)
    wzp = move_row(out_proj, dz=-1)

    (query_held,) = tied((query_rows,), g0)
    attn_out, top, total = attend(meta, query_held, kv_earlier, key_rows, value_rows, segments)

    gy, attn_out = tied((gy, attn_out))
    gxm, gxp = tied((gxm, gxp), gy)
    wzm, wzp, out_proj = tied((wzm, wzp, out_proj), gxm)

    hw = out_proj.shape[0] // 2
    gyxm = move_col(gy, dx=1)
    gyxp = move_col(gy, dx=-1)
    a_other = move_row(attn_out, dk=1)
    wo = move_row(wzm, dz=1)
    wy = move_row(out_proj, dyh=1)

    a_pair = jnp.concatenate([attn_out, a_other], 0)

    go = move_col(gxm, dx=1)
    gyxm, gyxp = tied((gyxm, gyxp))
    gyo = move_col(gyxp, dx=-1)
    wo, wy = tied((wo, wy), gyxp)
    wyzm = move_row(wy, dz=1)
    wyzp = move_row(wy, dz=-1)
    wyo = move_row(wo, dyh=1)

    (a_pair,) = tied((a_pair,), gyxp)
    proj = project([g0, gxm, gxp, gy], a_pair, meta, range(4), None)
    proj = project([gyxm, gyxp], a_pair, meta, (4, 5), proj)
    proj = project([go], a_pair, meta, (6,), proj)

    q = hw // 2
    far, up, dn = at_w(2, 1), at_w(1, 1), at_w(-1, 1)
    own_up, own_dn = at_w(1, 0), at_w(-1, 0)
    proj, give_far, give_up, give_dn, up2, dn2 = project(
        [gyo],
        a_pair,
        meta,
        (7,),
        proj,
        (
            (0, 0, far, 0, 0, hw), (0, hw, far, 1, 0, hw),
            (1, 0, up, 0, 0, hw), (1, hw, up, 1, 0, hw), (1, 2 * hw, own_up, 1, 0, q),
            (2, 0, dn, 0, 0, hw), (2, hw, dn, 1, 0, hw), (2, 2 * hw, own_dn, 0, 0, q),
            (3, 0, own_up, 1, q, q),
            (4, 0, own_dn, 0, q, q),
        ),
    )
    ry = move_row(give_far, dyh=1)
    rup = move_row(give_up, dz=1)
    rdn = move_row(give_dn, dz=-1)

    g_pieces = [g0, gxm, gxp, gy, gyxm, gyxp, go, gyo]
    w_pieces = [out_proj, wzm, wzp, wy, wyzm, wyzp, wyo, wo]
    wplan = [(i, p * hw, i, p) for i in range(8) for p in range(2)]
    (meta,) = tied((meta,), give_up)
    grad_own, give_lo, give_hi = attn_grad_part(g_pieces, w_pieces, wplan, meta)
    got_lo, got_hi = move_row(give_lo, dk=1), move_row(give_hi, dk=1)
    far, middle, near, own = fetch(
        proj,
        meta,
        (
            (0, 0, at_w(2, 0), 0), (0, hw, at_w(2, 0), 1),
            (1, 0, at_w(0, 1), 0), (1, hw, at_w(0, 1), 1),
            (2, 0, own_up, 0), (2, hw, own_dn, 1),
            (3, 0, at_w(0, 0), 0), (3, hw, at_w(0, 0), 1),
        ),
    )
    (attn_grad,) = add_rows(
        [grad_own, got_lo, got_hi],
        ((0, 0, hw, ((0, 0), (1, 0))), (0, hw, hw, ((0, hw), (2, 0)))),
    )
    part = functools.partial(
        attend_back, meta, query_rows, attn_grad, kv_earlier, key_rows, value_rows, segments, top, total
    )
    heads = query_rows.shape[1] // HD
    cuts = heads // 4, 5 * heads // 8
    held = part((0, cuts[0]), None)

    ry, *held = tied((ry, *held))

    far_up, far_dn = add_rows(
        [far, ry], ((0, 0, hw, ((0, 0), (1, 0))), (1, 0, hw, ((0, hw), (1, hw))))
    )
    fup = move_row(far_up, dz=1)
    fdn = move_row(far_dn, dz=-1)
    rup, rdn = tied((rup, rdn), far_up)
    up2, dn2 = tied((up2, dn2), far_up)
    (across,) = add_rows([middle, rup, rdn], ((0, 0, 2 * hw, ((0, 0), (1, 0), (2, 0))),))
    held = tied(held, across)
    across = move_row(across, dyh=1)
    up2 = move_row(up2, dz=1)
    dn2 = move_row(dn2, dz=-1)
    held = part(cuts, held)

    fup, fdn, *held = tied((fup, fdn, *held))

    near_up, near_dn = add_rows(
        [near, fup, fdn], ((0, 0, hw, ((0, 0), (1, 0))), (1, 0, hw, ((0, hw), (2, 0))))
    )
    nup = move_row(near_up, dz=1)
    ndn = move_row(near_dn, dz=-1)

    *held, up2, dn2 = tied((*held, up2, dn2), near_up)
    query_grad, dkey, dvalue = part((cuts[1], heads), held)
    back = passed_along(
        jnp.concatenate([dkey[:count], dvalue[:count]], 1).astype(BF), "row", -1
    )
    (proj_grad,) = add_rows(
        [own, across, nup, ndn, rup, up2, rdn, dn2],
        (
            (0, 0, q, ((0, 0), (1, 0), (2, 0), (6, 2 * hw))),
            (0, q, q, ((0, q), (1, q), (2, q), (7, 0))),
            (0, 2 * q, q, ((0, 2 * q), (1, 2 * q), (4, 2 * hw), (3, 0))),
            (0, 3 * q, q, ((0, 3 * q), (1, 3 * q), (5, 0), (3, q))),
        ),
        result=True,
    )
    proj_grad, back = tied((proj_grad, back))
    back = back.astype(F32)
    key_grad = (dkey[count:] + back[:, :HD]).astype(BF)
    value_grad = (dvalue[count:] + back[:, HD:]).astype(BF)
    return (query_grad, key_grad, value_grad, proj_grad)


def solution(mesh):
    placed = (
        P("row", "col"),
        P("row", "col"),
        P("row", "col"),
        P("row", "col"),
        P("row", "col"),
        P(),
    )
    return jax.shard_map(
        local,
        mesh=mesh,
        in_specs=placed,
        out_specs=(P("row", "col"), P("row", "col"), P("row", "col"), P("row", "col")),
        check_vma=False,
    )
```
